32 devices in a mesh: lat: 8 (over z, y), lon: 4 (over x, core).
Axes of the slice: x: 2, y: 2, z: 4, core: 2. Of those that a mesh axis runs over, the one named last changes fastest.
Arguments:
- initial_state: float32 [6, 384, 512], P(None, 'lat', 'lon'), may hold values from -6 to 6
- source: float32 [6, 384, 512], P(None, 'lat', 'lon'), may hold values from -3 to 3
- cotangent: float32 [6, 384, 512], P(None, 'lat', 'lon'), may hold values from -6 to 6
- face_coefs: float32 [2, 384, 512], P(None, 'lat', 'lon'), may hold values from 0.03 to 0.1
- land_mask: int32 [6, 384, 512], P(None, 'lat', 'lon'), may hold values 0 or 1
- bottom: int32 [384, 512], P('lat', 'lon'), may hold values from 1 to 6
Outputs:
- final_state: float32 [6, 384, 512], P(None, 'lat', 'lon')
- grad_initial: float32 [6, 384, 512], P(None, 'lat', 'lon')
- grad_source: float32 [6, 384, 512], P(None, 'lat', 'lon')
The draws below stay inside these ranges and needn't reach their ends.
All inputs are finite; a program needn't handle non-finite values. No bound on the sum of `land_mask` on one device may be relied on, other than what follows from the above.
Results may differ from the reference program's by a relative error of at most 0.00002.
Values sent between devices are 32-bit elements; how exact they have to be, the bound alone decides.
No kernel may reach another device: no remote copies, remote signals or barrier semaphores. Data moves between devices by JAX's collectives and lax.ppermute only.
A program may use at most 64 MiB of HBM per device.

```python
import math
import jax
import jax.numpy as jnp
from jax import lax

K = 6
STEPS = 4
NLAT = 384
NLON = 512


def touch_ends(entries, stream_key, least, top_value):
    index_at = [jax.random.randint(jax.random.fold_in(stream_key, axis), (), 0, length) for axis, length in enumerate(entries.shape)]
    widest = entries.shape.index(max(entries.shape))
    neighbour = index_at[:widest] + [(index_at[widest] + 1) % entries.shape[widest]] + index_at[widest + 1:]
    return entries.at[tuple(index_at)].set(least).at[tuple(neighbour)].set(top_value)


def shard_levels(own_key, dims, split, least, top_value):
    def one(dim, shards_of):
        draws = jax.random.uniform(jax.random.fold_in(jax.random.fold_in(own_key, 6), dim), (shards_of,), jnp.float32, least / len(split), top_value / len(split))
        return jnp.repeat(jnp.exp(draws), dims[dim] // shards_of).reshape((-1,) + (1,) * (len(dims) - dim - 1))

    loudness = one(*split[0])
    for cut in split[1:]:
        loudness = loudness * one(*cut)
    return loudness


def noise(rng, extent, width, bound, pieces=(), held_as=jnp.bfloat16):
    drawn = width * jax.random.normal(rng, extent, jnp.float32)
    if pieces:
        drawn = drawn * shard_levels(rng, extent, pieces, -0.22, 0.18)
    return jnp.clip(drawn, -bound, bound).astype(held_as)


def setup_inputs(seed: int = 0) -> dict:
    key_of = jax.random.split(jax.random.key(seed), 7)
    initial_state = noise(key_of[0], (K, NLAT, NLON), 1.0, 6.0, ((1, 8), (2, 4)), jnp.float32)
    source = noise(key_of[1], (K, NLAT, NLON), 0.5, 3.0, ((1, 8), (2, 4)), jnp.float32)
    cotangent = noise(key_of[2], (K, NLAT, NLON), 1.0, 6.0, ((1, 8), (2, 4)), jnp.float32)
    face_coefs = jnp.clip(jnp.exp(math.log(0.1) - 1.2039728 * jax.random.uniform(key_of[3], (2, NLAT, NLON), jnp.float32) ** shard_levels(key_of[3], (2, NLAT, NLON), ((1, 8), (2, 4)), -0.2, 0.2)), 0.03, 0.1)
    land_mask = touch_ends((jax.random.randint(key_of[4], (K, NLAT, NLON), 0, 5) < 4).astype(jnp.int32), jax.random.fold_in(key_of[4], 1), 0, 1)
    bottom = touch_ends(jax.random.randint(key_of[5], (NLAT, NLON), 1, K + 1), jax.random.fold_in(key_of[5], 1), 1, K).astype(jnp.int32)
    return dict(initial_state=initial_state, source=source, cotangent=cotangent, face_coefs=face_coefs, land_mask=land_mask, bottom=bottom)


vertical_coef = 0.04

def wet_cells(land_mask, bottom):
    levels = lax.broadcasted_iota(jnp.int32, land_mask.shape, 0)
    return jnp.where(levels < bottom[None, :, :], land_mask, 0).astype(jnp.float32)

def operate(values, wet_mask, coef_lon, coef_lat):
    east_values = jnp.roll(values, -1, axis=2)
    wet_east = jnp.roll(wet_mask, -1, axis=2)
    flux_east = coef_lon[None] * (wet_mask * wet_east) * (east_values - values)
    north_values = jnp.roll(values, -1, axis=1)
    wet_north = jnp.roll(wet_mask, -1, axis=1)
    flux_north = coef_lat[None] * (wet_mask * wet_north) * (north_values - values)
    flux_up = vertical_coef * (wet_mask[:-1] * wet_mask[1:]) * (values[1:] - values[:-1])
    zero_level = jnp.zeros_like(values[:1])
    vertical = jnp.concatenate([flux_up, zero_level], 0) - jnp.concatenate([zero_level, flux_up], 0)
    east_part = flux_east - jnp.roll(flux_east, 1, axis=2)
    north_part = flux_north - jnp.roll(flux_north, 1, axis=1)
    return values + east_part + north_part + vertical

def reference(initial_state, source, cotangent, face_coefs, land_mask, bottom):
    wet_mask = wet_cells(land_mask, bottom)
    row_index = lax.broadcasted_iota(jnp.int32, face_coefs.shape[1:], 0)
    coef_lat = jnp.where(row_index < NLAT - 1, face_coefs[1], jnp.float32(0.0))
    coef_lon = face_coefs[0]

    def forward(initial, forcing):
        tracer = initial
        for step_index in range(STEPS):
            tracer = wet_mask * (jnp.tanh(operate(tracer, wet_mask, coef_lon, coef_lat)) + forcing)
        return tracer
    final_state, pullback = jax.vjp(forward, initial_state, source)
    grad_initial, grad_source = pullback(cotangent)
    return (final_state, grad_initial, grad_source)
```

```python
import functools

import jax
import jax.numpy as jnp
from jax import lax
from jax.experimental import pallas as pl
from jax.experimental.pallas import tpu as pltpu
from jax.sharding import PartitionSpec as P

STEPS = 4
DEPTH = 2 * STEPS
LANES = 128
TILE = 8
PAD = TILE

vertical_coef = 0.04


def lane_iota():
    return lax.broadcasted_iota(jnp.int32, (TILE, LANES), 1)


def channel_shift(channel):
    place = channel % 16
    return (2 * DEPTH * (place % 8) + DEPTH * (place // 8)) % LANES


def is_odd(axis):
    return lax.rem(lax.axis_index(axis), 2) == 1


def pack_kernel(levels, u_ref, s_ref, a_ref, c_ref, land_ref, bottom_ref, f_ref, first_ref, second_ref):
    rows = u_ref.shape[1]
    last_lat = lax.axis_index("lat") == lax.axis_size("lat") - 1
    for k in range(levels):
        wet = jnp.where(k < bottom_ref[...], land_ref[k], 0).astype(jnp.float32)
        f_ref[k] = wet * u_ref[k]
        f_ref[levels + k] = wet * s_ref[k]
        f_ref[2 * levels + k] = wet
        f_ref[3 * levels + k] = a_ref[k]
    f_ref[4 * levels] = c_ref[0]
    row = lax.broadcasted_iota(jnp.int32, (rows, LANES), 0)
    f_ref[4 * levels + 1] = jnp.where(jnp.logical_and(last_lat, row == rows - 1), 0.0, c_ref[1])
    odd = is_odd("lon")
    channels = 4 * levels + 2
    group = lane_iota() // DEPTH
    for t in range(rows // TILE):
        at = pl.ds(t * TILE, TILE)
        for m in range(-(-channels // 16)):
            east = jnp.zeros((TILE, LANES), jnp.float32)
            west = east
            for channel in range(16 * m, min(16 * m + 16, channels)):
                shift = channel_shift(channel)
                tile = f_ref[channel, at, :]
                if shift:
                    tile = pltpu.roll(tile, shift, 1)
                east = jnp.where(group == shift // DEPTH, tile, east)
                west = jnp.where(group == (shift // DEPTH - 1) % 16, tile, west)
            first_ref[m, at, :] = jnp.where(odd, east, west)
            second_ref[m, at, :] = jnp.where(odd, west, east)


def lat_kernel(f_ref, one_ref, two_ref, first_ref, second_ref):
    channels, rows, _ = f_ref.shape
    parts = one_ref.shape[0]
    odd_lat, odd_lon = is_odd("lat"), is_odd("lon")
    low, high = pl.ds(0, TILE), pl.ds(rows - TILE, TILE)

    def fill(ref, at):
        for channel in range(channels):
            ref[channel] = f_ref[channel, at, :]
        for m in range(parts):
            one, two = one_ref[m, at, :], two_ref[m, at, :]
            ref[channels + m] = jnp.where(odd_lon, two, one)
            ref[channels + parts + m] = jnp.where(odd_lon, one, two)

    @pl.when(odd_lat)
    def _():
        fill(first_ref, low)
        fill(second_ref, high)

    @pl.when(jnp.logical_not(odd_lat))
    def _():
        fill(first_ref, high)
        fill(second_ref, low)


def sweep_kernel(
    levels, f_ref, one_ref, two_ref, lat_one_ref, lat_two_ref, state_ref, grad_ref, gsource_ref,
    e0, e1, d0, d1, w0, w1, p0, p1, q0, q1, m0, m1, acc,
):
    channels, rows, _ = f_ref.shape
    parts = one_ref.shape[0]
    tiles = rows // TILE + 2
    odd_lat, odd_lon = is_odd("lat"), is_odd("lon")
    lane = lane_iota()
    group = lane // DEPTH
    even_group = lax.rem(group, 2) == 0
    at_first, at_last = lane == 0, lane == LANES - 1
    zero = jnp.zeros((TILE, LANES), jnp.float32)
    U, S, W, A, CE, CN = 0, levels, 2 * levels, 3 * levels, 4 * levels, 4 * levels + 1

    ends = (pl.ds(0, TILE), pl.ds(PAD + tiles * TILE, TILE))
    for ref in (e0, e1):
        for end in ends:
            for k in range(levels):
                ref[U + k, end, :] = zero
                ref[W + k, end, :] = zero
            ref[CN, end, :] = zero
    for ref in (p0, p1, q0, q1):
        for end in ends:
            for k in range(levels):
                ref[k, end, :] = zero

    def spread(at, easts, wests):
        for m in range(parts):
            both = (
                jnp.where(even_group, easts[m], wests[m]),
                jnp.where(even_group, wests[m], easts[m]),
            )
            for channel in range(16 * m, min(16 * m + 16, channels)):
                shift = channel_shift(channel)
                tile = both[(channel % 16) // 8]
                if shift:
                    tile = pltpu.roll(tile, LANES - shift, 1)
                e1[channel, at, :] = tile

    for t in range(rows // TILE):
        at, to = pl.ds(t * TILE, TILE), pl.ds(PAD + (t + 1) * TILE, TILE)
        for channel in range(channels):
            e0[channel, to, :] = f_ref[channel, at, :]
        ones = [one_ref[m, at, :] for m in range(parts)]
        twos = [two_ref[m, at, :] for m in range(parts)]
        spread(
            to,
            [jnp.where(odd_lon, b, a) for a, b in zip(ones, twos)],
            [jnp.where(odd_lon, a, b) for a, b in zip(ones, twos)],
        )
    for t, low in ((0, True), (tiles - 1, False)):
        to = pl.ds(PAD + t * TILE, TILE)

        def got(index):
            one, two = lat_one_ref[index], lat_two_ref[index]
            return jnp.where(odd_lat, one, two) if low else jnp.where(odd_lat, two, one)

        for channel in range(channels):
            e0[channel, to, :] = got(channel)
        spread(
            to,
            [got(channels + m) for m in range(parts)],
            [got(channels + parts + m) for m in range(parts)],
        )

    def from_west(x0, x1):
        r0, r1 = pltpu.roll(x0, 1, 1), pltpu.roll(x1, 1, 1)
        return jnp.where(at_first, r1, r0), jnp.where(at_first, r0, r1)

    def from_east(x0, x1):
        r0, r1 = pltpu.roll(x0, LANES - 1, 1), pltpu.roll(x1, LANES - 1, 1)
        return jnp.where(at_last, r1, r0), jnp.where(at_last, r0, r1)

    def neighbours(x0, x1, base, row, halves, first_use=False):
        ce = (e0[CE, pl.ds(row, TILE), :], e1[CE, pl.ds(row, TILE), :])
        cw = (w0[pl.ds(row, TILE), :], w1[pl.ds(row, TILE), :])
        cn = (e0[CN, pl.ds(row, TILE), :], e1[CN, pl.ds(row, TILE), :])
        cs = (e0[CN, pl.ds(row - 1, TILE), :], e1[CN, pl.ds(row - 1, TILE), :])
        own = [(x0[base + k, pl.ds(row, TILE), :], x1[base + k, pl.ds(row, TILE), :]) for k in range(levels)]
        out = []
        for k in range(levels):
            east, west = from_east(*own[k]), from_west(*own[k])
            pair = []
            for h, ref in ((0, x0), (1, x1))[:halves]:
                north = ref[base + k, pl.ds(row + 1, TILE), :]
                south = ref[base + k, pl.ds(row - 1, TILE), :]
                total = (ce[h] * east[h] + cw[h] * west[h]) + (cn[h] * north + cs[h] * south)
                if k == 0:
                    column = own[1][h]
                elif k == levels - 1:
                    column = own[k - 1][h]
                else:
                    column = own[k - 1][h] + own[k + 1][h]
                pair.append((own[k][h], total + vertical_coef * column))
            out.append(pair)
        return out

    def over_tiles(body, inner=False):
        first, last = (1, tiles - 1) if inner else (0, tiles)

        def step(t, carry):
            body(pl.multiple_of(t * TILE, TILE))
            return carry

        lax.fori_loop(first, last, step, 0)

    def prepare(at):
        row = at + PAD
        w0[pl.ds(row, TILE), :], w1[pl.ds(row, TILE), :] = from_west(
            e0[CE, pl.ds(row, TILE), :], e1[CE, pl.ds(row, TILE), :]
        )
        for k, pair in enumerate(neighbours(e0, e1, W, row, 2)):
            for ref, (_, total) in zip((d0, d1), pair):
                ref[k, pl.ds(at, TILE), :] = 1.0 - total

    over_tiles(prepare)

    def forward(n, x, base, y):
        def body(at):
            row = at + PAD
            for k, pair in enumerate(neighbours(*x, base, row, 2)):
                for h, (own, total) in enumerate(pair):
                    e, d, m = ((e0, d0, m0), (e1, d1, m1))[h]
                    wet = e[W + k, pl.ds(row, TILE), :]
                    bounded = wet * jnp.tanh(d[k, pl.ds(at, TILE), :] * own + total)
                    slope = wet - bounded * bounded
                    if n < STEPS - 1:
                        y[h][k, pl.ds(row, TILE), :] = bounded + e[S + k, pl.ds(row, TILE), :]
                        m[n * levels + k, pl.ds(at, TILE), :] = slope
                    else:
                        if h == 0:
                            m[n * levels + k, pl.ds(at, TILE), :] = bounded + e[S + k, pl.ds(row, TILE), :]
                        y[h][k, pl.ds(row, TILE), :] = slope * e[A + k, pl.ds(row, TILE), :]

        over_tiles(body)

    def backward(n, x, y):
        def body(at):
            row = at + PAD
            for k, pair in enumerate(neighbours(*x, 0, row, 2)):
                for h, (own, total) in enumerate(pair):
                    d, m = ((d0, m0), (d1, m1))[h]
                    value = d[k, pl.ds(at, TILE), :] * own + total
                    if h == 0:
                        before = e0[A + k, pl.ds(row, TILE), :] if n == STEPS - 1 else acc[k, pl.ds(at, TILE), :]
                        acc[k, pl.ds(at, TILE), :] = before + value
                    y[h][k, pl.ds(row, TILE), :] = m[(n - 1) * levels + k, pl.ds(at, TILE), :] * value

        over_tiles(body)

    def finish(x):
        def body(at):
            row = at + PAD
            to = pl.ds(pl.multiple_of(at - TILE, TILE), TILE)
            for k, pair in enumerate(neighbours(*x, 0, row, 1)):
                own, total = pair[0]
                wet = e0[W + k, pl.ds(row, TILE), :]
                grad_ref[k, to, :] = wet * (d0[k, pl.ds(at, TILE), :] * own + total)
                gsource_ref[k, to, :] = wet * acc[k, pl.ds(at, TILE), :]
                state_ref[k, to, :] = m0[(STEPS - 1) * levels + k, pl.ds(at, TILE), :]

        over_tiles(body, inner=True)

    spaces = ((p0, p1), (q0, q1))
    here, base = (e0, e1), U
    for n in range(STEPS):
        forward(n, here, base, spaces[n % 2])
        here, base = spaces[n % 2], 0
    for n in range(STEPS - 1, 0, -1):
        there = spaces[0] if here is spaces[1] else spaces[1]
        backward(n, here, there)
        here = there
    finish(here)


def swaps(count, offset, wrap):
    pairs = []
    for i in range(offset, count, 2):
        j = i + 1
        if j < count or wrap:
            pairs += [(i, j % count), (j % count, i)]
    return pairs


def body(initial_state, source, cotangent, face_coefs, land_mask, bottom):
    levels, rows, _ = initial_state.shape
    channels = 4 * levels + 2
    parts = -(-channels // 16)
    tiles = rows // TILE + 2
    span, wide = tiles * TILE, tiles * TILE + 2 * PAD
    f32 = lambda *shape: jax.ShapeDtypeStruct(shape, jnp.float32)
    scratch = lambda *shape: pltpu.VMEM(shape, jnp.float32)
    vmem = pl.BlockSpec(memory_space=pltpu.VMEM)
    params = pltpu.CompilerParams(vmem_limit_bytes=16 * 1024 * 1024)

    fields, one, two = pl.pallas_call(
        functools.partial(pack_kernel, levels),
        out_shape=(f32(channels, rows, LANES), f32(parts, rows, LANES), f32(parts, rows, LANES)),
        in_specs=[vmem] * 6,
        out_specs=(vmem,) * 3,
        compiler_params=params,
        name="pack",
    )(initial_state, source, cotangent, face_coefs, land_mask, bottom)
    lon = lax.axis_size("lon")
    one = lax.ppermute(one, "lon", swaps(lon, 0, True))
    two = lax.ppermute(two, "lon", swaps(lon, 1, True))
    lat_one, lat_two = pl.pallas_call(
        lat_kernel,
        out_shape=(f32(channels + 2 * parts, TILE, LANES),) * 2,
        in_specs=[vmem] * 3,
        out_specs=(vmem,) * 2,
        compiler_params=params,
        name="lat_rows",
    )(fields, one, two)
    lat = lax.axis_size("lat")
    lat_two = lax.ppermute(lat_two, "lat", swaps(lat, 1, False))
    lat_one = lax.ppermute(lat_one, "lat", swaps(lat, 0, False))
    pair = lambda *shape: [scratch(*shape), scratch(*shape)]
    return pl.pallas_call(
        functools.partial(sweep_kernel, levels),
        out_shape=(f32(levels, rows, LANES),) * 3,
        in_specs=[vmem] * 5,
        out_specs=(vmem,) * 3,
        scratch_shapes=[
            *pair(channels, wide, LANES),
            *pair(levels, span, LANES),
            *pair(wide, LANES),
            *pair(levels, wide, LANES),
            *pair(levels, wide, LANES),
            *pair(STEPS * levels, span, LANES),
            scratch(levels, span, LANES),
        ],
        compiler_params=params,
        name="sweeps",
    )(fields, one, two, lat_one, lat_two)


def solution(mesh):
    block = P(None, "lat", "lon")
    return jax.shard_map(
        body,
        mesh=mesh,
        in_specs=(block, block, block, block, block, P("lat", "lon")),
        out_specs=(block, block, block),
        check_vma=False,
    )
```

```python
import functools

import jax
import jax.numpy as jnp
from jax import lax
from jax.experimental import pallas as pl
from jax.experimental.pallas import tpu as pltpu
from jax.sharding import PartitionSpec as P

STEPS = 4
DEPTH = 2 * STEPS
TILE = 8
HALO = TILE

vertical_coef = 0.04


class Names:
    def __init__(self, levels):
        self.levels = levels
        self.u, self.s, self.wet = 0, levels, 2 * levels
        self.ce, self.cn, self.cot = 3 * levels, 3 * levels + 1, 3 * levels + 2
        self.count = 4 * levels + 2
        self.paired = -(-levels // 2)
        self.main = self.cot + self.paired
        self.parts = -(-self.count // 16)


def lane_iota(lanes):
    return lax.broadcasted_iota(jnp.int32, (TILE, lanes), 1)


def channel_shift(channel, lanes):
    place = channel % 16
    return (2 * DEPTH * (place % 8) + DEPTH * (place // 8)) % lanes


def is_odd(axis):
    return lax.rem(lax.axis_index(axis), 2) == 1


def fill_rows(c, f_ref, ref, high):
    rows = f_ref.shape[1]
    at = pl.ds(rows - TILE if high else 0, TILE)
    for channel in range(c.cot):
        ref[channel] = f_ref[channel, at, :]
    row = lax.broadcasted_iota(jnp.int32, (TILE, f_ref.shape[2]), 0)
    half = TILE // 2
    for q in range(c.paired):
        one = f_ref[c.cot + 2 * q, at, :]
        two = f_ref[c.cot + min(2 * q + 1, c.levels - 1), at, :]
        if high:
            one = pltpu.roll(one, half, 0)
        else:
            two = pltpu.roll(two, half, 0)
        ref[c.cot + q] = jnp.where(row < half, one, two)


def pack_kernel(
    c, u_hbm, s_hbm, a_hbm, c_hbm, land_hbm, bottom_hbm, f_ref, first_ref, second_ref, lat_ref,
    u_ref, s_ref, c_ref, land_ref, bottom_ref, sems,
):
    levels = c.levels
    _, rows, lanes = u_ref.shape
    moves = [
        pltpu.make_async_copy(source, target, sems.at[i])
        for i, (source, target) in enumerate(
            (
                (bottom_hbm, bottom_ref),
                (land_hbm, land_ref),
                (u_hbm, u_ref),
                (s_hbm, s_ref),
                (c_hbm, c_ref),
                (a_hbm, f_ref.at[pl.ds(c.cot, levels)]),
            )
        )
    ]
    for move in moves:
        move.start()
    for move in moves:
        move.wait()
    last_lat = lax.axis_index("lat") == lax.axis_size("lat") - 1
    for k in range(levels):
        wet = jnp.where(k < bottom_ref[...], land_ref[k], 0).astype(jnp.float32)
        f_ref[c.u + k] = wet * u_ref[k]
        f_ref[c.s + k] = wet * s_ref[k]
        f_ref[c.wet + k] = wet
    f_ref[c.ce] = c_ref[0]
    row = lax.broadcasted_iota(jnp.int32, (rows, lanes), 0)
    f_ref[c.cn] = jnp.where(jnp.logical_and(last_lat, row == rows - 1), 0.0, c_ref[1])
    odd = is_odd("lon")
    group = lane_iota(lanes) // DEPTH
    groups = lanes // DEPTH
    for t in range(rows // TILE):
        at = pl.ds(t * TILE, TILE)
        for m in range(c.parts):
            east = jnp.zeros((TILE, lanes), jnp.float32)
            west = east
            for channel in range(16 * m, min(16 * m + 16, c.count)):
                shift = channel_shift(channel, lanes)
                tile = f_ref[channel, at, :]
                if shift:
                    tile = pltpu.roll(tile, shift, 1)
                east = jnp.where(group == shift // DEPTH, tile, east)
                west = jnp.where(group == (shift // DEPTH - 1) % groups, tile, west)
            first_ref[m, at, :] = jnp.where(odd, east, west)
            second_ref[m, at, :] = jnp.where(odd, west, east)
    odd_lat = is_odd("lat")

    @pl.when(odd_lat)
    def _():
        fill_rows(c, f_ref, lat_ref, False)

    @pl.when(jnp.logical_not(odd_lat))
    def _():
        fill_rows(c, f_ref, lat_ref, True)


def lat_kernel(c, f_ref, one_ref, two_ref, corner_ref, second_ref):
    rows = f_ref.shape[1]
    odd_lat, odd_lon = is_odd("lat"), is_odd("lon")

    def strips(ref, base, high):
        at = pl.ds(rows - TILE if high else 0, TILE)
        for m in range(c.parts):
            one, two = one_ref[m, at, :], two_ref[m, at, :]
            ref[base + m] = jnp.where(odd_lon, two, one)
            ref[base + c.parts + m] = jnp.where(odd_lon, one, two)

    @pl.when(odd_lat)
    def _():
        strips(corner_ref, 0, False)
        fill_rows(c, f_ref, second_ref, True)
        strips(second_ref, c.main, True)

    @pl.when(jnp.logical_not(odd_lat))
    def _():
        strips(corner_ref, 0, True)
        fill_rows(c, f_ref, second_ref, False)
        strips(second_ref, c.main, False)


class Sweeps:
    def __init__(self, c, e, w, d, x, m, adj, state):
        self.c, self.e, self.w, self.d, self.x, self.m, self.adj, self.state = c, e, w, d, x, m, adj, state
        self.lanes = e[0].shape[-1]
        lane = lane_iota(self.lanes)
        self.at_first, self.at_last = lane == 0, lane == self.lanes - 1
        self.even_group = lax.rem(lane // DEPTH, 2) == 0

    def from_west(self, x0, x1):
        r0, r1 = pltpu.roll(x0, 1, 1), pltpu.roll(x1, 1, 1)
        return jnp.where(self.at_first, r1, r0), jnp.where(self.at_first, r0, r1)

    def from_east(self, x0, x1):
        r0, r1 = pltpu.roll(x0, self.lanes - 1, 1), pltpu.roll(x1, self.lanes - 1, 1)
        return jnp.where(self.at_last, r1, r0), jnp.where(self.at_last, r0, r1)

    def spread(self, at, easts, wests):
        for m in range(self.c.parts):
            both = (
                jnp.where(self.even_group, easts[m], wests[m]),
                jnp.where(self.even_group, wests[m], easts[m]),
            )
            for channel in range(16 * m, min(16 * m + 16, self.c.count)):
                shift = channel_shift(channel, self.lanes)
                tile = both[(channel % 16) // 8]
                if shift:
                    tile = pltpu.roll(tile, self.lanes - shift, 1)
                self.e[1][channel, at, :] = tile

    def western(self, row):
        at = pl.ds(row, TILE)
        self.w[0][at, :], self.w[1][at, :] = self.from_west(self.e[0][self.c.ce, at, :], self.e[1][self.c.ce, at, :])

    def neighbours(self, load, row, halves=2):
        c, at = self.c, pl.ds(row, TILE)
        ce = [e[c.ce, at, :] for e in self.e]
        cw = [w[at, :] for w in self.w]
        cn = [e[c.cn, at, :] for e in self.e]
        cs = [e[c.cn, pl.ds(row - 1, TILE), :] for e in self.e]
        own = [(load(0, k, at), load(1, k, at)) for k in range(c.levels)]
        out = []
        for k in range(c.levels):
            east, west = self.from_east(*own[k]), self.from_west(*own[k])
            pair = []
            for h in range(halves):
                north, south = load(h, k, pl.ds(row + 1, TILE)), load(h, k, pl.ds(row - 1, TILE))
                total = (ce[h] * east[h] + cw[h] * west[h]) + (cn[h] * north + cs[h] * south)
                around = [own[j][h] for j in (k - 1, k + 1) if 0 <= j < c.levels]
                pair.append((own[k][h], total + vertical_coef * functools.reduce(jnp.add, around)))
            out.append(pair)
        return out

    def diagonal(self, row):
        load = lambda h, k, at: self.e[h][self.c.wet + k, at, :]
        for k, pair in enumerate(self.neighbours(load, row)):
            for h, (_, total) in enumerate(pair):
                self.d[h][k, pl.ds(row, TILE), :] = 1.0 - total

    def loader(self, index):
        if index == 0:
            return lambda h, k, at: self.e[h][self.c.u + k, at, :]
        base = (index - 1) * self.c.levels
        return lambda h, k, at: self.x[h][base + k, at, :]

    def forward(self, n, row):
        c, at = self.c, pl.ds(row, TILE)
        for k, pair in enumerate(self.neighbours(self.loader(n), row)):
            for h, (own, total) in enumerate(pair):
                e = self.e[h]
                wet = e[c.wet + k, at, :]
                bounded = wet * jnp.tanh(self.d[h][k, at, :] * own + total)
                slope = wet - bounded * bounded
                if n < STEPS - 1:
                    self.x[h][n * c.levels + k, at, :] = bounded + e[c.s + k, at, :]
                    self.m[h][n * c.levels + k, at, :] = slope
                else:
                    if h == 0:
                        self.state[k, at, :] = bounded + e[c.s + k, at, :]
                    self.x[h][n * c.levels + k, at, :] = slope * e[c.cot + k, at, :]

    def backward(self, n, row):
        c, at = self.c, pl.ds(row, TILE)
        index = 2 * STEPS - 1 - n
        for k, pair in enumerate(self.neighbours(self.loader(index), row)):
            for h, (own, total) in enumerate(pair):
                value = self.d[h][k, at, :] * own + total
                if h == 0:
                    self.adj[(n - 1) * c.levels + k, at, :] = value
                self.x[h][index * c.levels + k, at, :] = self.m[h][(n - 1) * c.levels + k, at, :] * value

    def gradient(self, row):
        c, at = self.c, pl.ds(row, TILE)
        for k, pair in enumerate(self.neighbours(self.loader(2 * STEPS - 1), row, 1)):
            own, total = pair[0]
            yield k, self.e[0][c.wet + k, at, :] * (self.d[0][k, at, :] * own + total)

    def source_gradient(self, row):
        c, at = self.c, pl.ds(row, TILE)
        for k in range(c.levels):
            total = self.e[0][c.cot + k, at, :]
            for n in range(STEPS - 1):
                total = total + self.adj[n * c.levels + k, at, :]
            yield k, self.e[0][c.wet + k, at, :] * total


def own_kernel(c, f_ref, one_ref, two_ref, e0, e1, w0, w1, d0, d1, x0, x1, m0, m1, adj, state, grad, gsource):
    rows = f_ref.shape[1]
    odd_lon = is_odd("lon")
    s = Sweeps(c, (e0, e1), (w0, w1), (d0, d1), (x0, x1), (m0, m1), adj, state)
    zero = jnp.zeros((TILE, f_ref.shape[2]), jnp.float32)
    for ref in (e0, e1):
        for end in (pl.ds(0, TILE), pl.ds(HALO + rows, TILE)):
            for channel in (*range(c.u, c.u + c.levels), *range(c.wet, c.wet + c.levels), c.cn):
                ref[channel, end, :] = zero
    places = [HALO + t * TILE for t in range(rows // TILE)]
    for row in places:
        at, to = pl.ds(row - HALO, TILE), pl.ds(row, TILE)
        for channel in range(c.count):
            e0[channel, to, :] = f_ref[channel, at, :]
        ones = [one_ref[m, at, :] for m in range(c.parts)]
        twos = [two_ref[m, at, :] for m in range(c.parts)]
        s.spread(
            to,
            [jnp.where(odd_lon, b, a) for a, b in zip(ones, twos)],
            [jnp.where(odd_lon, a, b) for a, b in zip(ones, twos)],
        )
        s.western(row)
    for row in places:
        s.diagonal(row)
    for n in range(STEPS):
        for row in places:
            s.forward(n, row)
    for n in range(STEPS - 1, 0, -1):
        for row in places:
            s.backward(n, row)
    for row in places[1:-1]:
        at = pl.ds(row - HALO, TILE)
        for k, value in s.source_gradient(row):
            gsource[k, at, :] = value
        for k, value in s.gradient(row):
            grad[k, at, :] = value


def edge_kernel(
    c, lat_one_ref, corner_ref, lat_two_ref, *refs,
):
    aliased = refs[: len(refs) // 2]
    del aliased
    e0, e1, w0, w1, d0, d1, x0, x1, m0, m1, adj, state, grad, gsource, state_hbm, grad_hbm, gsource_hbm, sems = refs[14:]
    rows = grad.shape[1]
    odd_lat = is_odd("lat")
    s = Sweeps(c, (e0, e1), (w0, w1), (d0, d1), (x0, x1), (m0, m1), adj, state)
    half = TILE // 2
    for row, low in ((0, True), (HALO + rows, False)):
        to = pl.ds(row, TILE)

        def choose(one, two):
            return jnp.where(odd_lat, one, two) if low else jnp.where(odd_lat, two, one)

        for channel in range(c.cot):
            e0[channel, to, :] = choose(lat_one_ref[channel], lat_two_ref[channel])
        for k in range(c.levels):
            tile = choose(lat_one_ref[c.cot + k // 2], lat_two_ref[c.cot + k // 2])
            if (k % 2 == 0) == low:
                tile = pltpu.roll(tile, half, 0)
            e0[c.cot + k, to, :] = tile
        strips = [choose(corner_ref[m], lat_two_ref[c.main + m]) for m in range(2 * c.parts)]
        s.spread(to, strips[: c.parts], strips[c.parts :])
        s.western(row)
    top = lambda i: HALO + i - (DEPTH - 1)
    bottom = lambda i: HALO + rows - 1 - i
    places = lambda i: (top(i), bottom(i))
    for row in places(0):
        s.diagonal(row)
    for n in range(STEPS):
        for row in places(n):
            s.forward(n, row)
    own = pl.ds(HALO, rows)
    moves = [
        pltpu.make_async_copy(state.at[:, own, :], state_hbm, sems.at[0]),
        pltpu.make_async_copy(gsource, gsource_hbm, sems.at[1]),
        pltpu.make_async_copy(grad, grad_hbm, sems.at[2]),
    ]
    moves[0].start()
    for n in range(STEPS - 1, 0, -1):
        for row in places(2 * STEPS - 1 - n):
            s.backward(n, row)
    for row in places(DEPTH - 1):
        for k, value in s.source_gradient(row):
            gsource[k, pl.ds(row - HALO, TILE), :] = value
    moves[1].start()
    for row in places(DEPTH - 1):
        for k, value in s.gradient(row):
            grad[k, pl.ds(row - HALO, TILE), :] = value
    moves[2].start()
    for move in moves:
        move.wait()


def swaps(count, offset, wrap):
    pairs = []
    for i in range(offset, count, 2):
        j = i + 1
        if j < count or wrap:
            pairs += [(i, j % count), (j % count, i)]
    return pairs


def body(initial_state, source, cotangent, face_coefs, land_mask, bottom):
    levels, rows, lanes = initial_state.shape
    c = Names(levels)
    span = rows + 2 * HALO
    f32 = lambda *shape: jax.ShapeDtypeStruct(shape, jnp.float32)
    vmem, hbm = pl.BlockSpec(memory_space=pltpu.VMEM), pl.BlockSpec(memory_space=pltpu.HBM)
    params = pltpu.CompilerParams(vmem_limit_bytes=8 * 1024 * 1024)

    fields, one, two, lat_one = pl.pallas_call(
        functools.partial(pack_kernel, c),
        out_shape=(f32(c.count, rows, lanes), f32(c.parts, rows, lanes), f32(c.parts, rows, lanes), f32(c.main, TILE, lanes)),
        in_specs=[hbm] * 6,
        out_specs=(vmem,) * 4,
        scratch_shapes=[
            pltpu.VMEM((levels, rows, lanes), jnp.float32),
            pltpu.VMEM((levels, rows, lanes), jnp.float32),
            pltpu.VMEM((2, rows, lanes), jnp.float32),
            pltpu.VMEM((levels, rows, lanes), jnp.int32),
            pltpu.VMEM((rows, lanes), jnp.int32),
            pltpu.SemaphoreType.DMA((6,)),
        ],
        compiler_params=params,
        name="pack",
    )(initial_state, source, cotangent, face_coefs, land_mask, bottom)
    lon, lat = lax.axis_size("lon"), lax.axis_size("lat")
    one = lax.ppermute(one, "lon", swaps(lon, 0, True))
    two = lax.ppermute(two, "lon", swaps(lon, 1, True))
    lat_one = lax.ppermute(lat_one, "lat", swaps(lat, 0, False))
    corner, lat_two = pl.pallas_call(
        functools.partial(lat_kernel, c),
        out_shape=(f32(2 * c.parts, TILE, lanes), f32(c.main + 2 * c.parts, TILE, lanes)),
        in_specs=[vmem] * 3,
        out_specs=(vmem,) * 2,
        compiler_params=params,
        name="lat_rows",
    )(fields, one, two)
    lat_two = lax.ppermute(lat_two, "lat", swaps(lat, 1, False))
    corner = lax.ppermute(corner, "lat", swaps(lat, 0, False))
    twice = lambda *shape: (f32(*shape), f32(*shape))
    shapes = (
        *twice(c.count, span, lanes),
        *twice(span, lanes),
        *twice(levels, span, lanes),
        *twice((2 * STEPS - 1) * levels, span, lanes),
        *twice((STEPS - 1) * levels, span, lanes),
        f32((STEPS - 1) * levels, span, lanes),
        f32(levels, span, lanes),
        f32(levels, rows, lanes),
        f32(levels, rows, lanes),
    )
    own = pl.pallas_call(
        functools.partial(own_kernel, c),
        out_shape=shapes,
        in_specs=[vmem] * 3,
        out_specs=(vmem,) * len(shapes),
        compiler_params=params,
        cost_estimate=pl.CostEstimate(
            flops=2 * STEPS * levels * rows * lanes * 40, bytes_accessed=16 * 2**20, transcendentals=0
        ),
        name="own_rows",
    )(fields, one, two)
    out = pl.pallas_call(
        functools.partial(edge_kernel, c),
        out_shape=(*shapes, *(f32(levels, rows, lanes),) * 3),
        in_specs=[vmem] * (3 + len(shapes)),
        out_specs=(*(vmem,) * len(shapes), hbm, hbm, hbm),
        input_output_aliases={3 + i: i for i in range(len(shapes))},
        scratch_shapes=[pltpu.SemaphoreType.DMA((3,))],
        compiler_params=params,
        name="edge_rows",
    )(lat_one, corner, lat_two, *own)
    return tuple(out[len(shapes) :])


def solution(mesh):
    block = P(None, "lat", "lon")
    return jax.shard_map(
        body,
        mesh=mesh,
        in_specs=(block, block, block, block, block, P("lat", "lon")),
        out_specs=(block, block, block),
        check_vma=False,
    )
```

```python
import functools

import jax
import jax.numpy as jnp
from jax import lax
from jax.experimental import pallas as pl
from jax.experimental.pallas import tpu as pltpu
from jax.sharding import PartitionSpec as P

STEPS = 4
DEPTH = 2 * STEPS
TILE = 8
HALO = TILE

vertical_coef = 0.04


class Names:
    def __init__(self, levels):
        self.levels = levels
        self.u, self.s, self.wet = 0, levels, 2 * levels
        self.ce, self.cn, self.cot = 3 * levels, 3 * levels + 1, 3 * levels + 2
        self.count = 4 * levels + 2
        self.paired = -(-levels // 2)
        self.main = self.cot + self.paired
        self.parts = -(-self.count // 16)


def lane_iota(lanes):
    return lax.broadcasted_iota(jnp.int32, (TILE, lanes), 1)


def channel_shift(channel, lanes):
    place = channel % 16
    return (2 * DEPTH * (place % 8) + DEPTH * (place // 8)) % lanes


def is_odd(axis):
    return lax.rem(lax.axis_index(axis), 2) == 1


def fill_rows(c, f_ref, ref, high):
    rows = f_ref.shape[1]
    at = pl.ds(rows - TILE if high else 0, TILE)
    for channel in range(c.cot):
        ref[channel] = f_ref[channel, at, :]
    row = lax.broadcasted_iota(jnp.int32, (TILE, f_ref.shape[2]), 0)
    half = TILE // 2
    for q in range(c.paired):
        one = f_ref[c.cot + 2 * q, at, :]
        two = f_ref[c.cot + min(2 * q + 1, c.levels - 1), at, :]
        if high:
            one = pltpu.roll(one, half, 0)
        else:
            two = pltpu.roll(two, half, 0)
        ref[c.cot + q] = jnp.where(row < half, one, two)


def pack_kernel(
    c, u_hbm, s_hbm, a_hbm, c_hbm, land_hbm, bottom_hbm, f_ref, first_ref, second_ref, lat_ref,
    u_ref, s_ref, c_ref, land_ref, bottom_ref, sems,
):
    levels = c.levels
    _, rows, lanes = u_ref.shape
    moves = [
        pltpu.make_async_copy(source, target, sems.at[i])
        for i, (source, target) in enumerate(
            (
                (bottom_hbm, bottom_ref),
                (land_hbm, land_ref),
                (u_hbm, u_ref),
                (s_hbm, s_ref),
                (c_hbm, c_ref),
                (a_hbm, f_ref.at[pl.ds(c.cot, levels)]),
            )
        )
    ]
    for move in moves:
        move.start()
    for move in moves:
        move.wait()
    last_lat = lax.axis_index("lat") == lax.axis_size("lat") - 1
    for k in range(levels):
        wet = jnp.where(k < bottom_ref[...], land_ref[k], 0).astype(jnp.float32)
        f_ref[c.u + k] = wet * u_ref[k]
        f_ref[c.s + k] = wet * s_ref[k]
        f_ref[c.wet + k] = wet
    f_ref[c.ce] = c_ref[0]
    row = lax.broadcasted_iota(jnp.int32, (rows, lanes), 0)
    f_ref[c.cn] = jnp.where(jnp.logical_and(last_lat, row == rows - 1), 0.0, c_ref[1])
    odd = is_odd("lon")
    group = lane_iota(lanes) // DEPTH
    groups = lanes // DEPTH
    for t in range(rows // TILE):
        at = pl.ds(t * TILE, TILE)
        for m in range(c.parts):
            east = jnp.zeros((TILE, lanes), jnp.float32)
            west = east
            for channel in range(16 * m, min(16 * m + 16, c.count)):
                shift = channel_shift(channel, lanes)
                tile = f_ref[channel, at, :]
                if shift:
                    tile = pltpu.roll(tile, shift, 1)
                east = jnp.where(group == shift // DEPTH, tile, east)
                west = jnp.where(group == (shift // DEPTH - 1) % groups, tile, west)
            first_ref[m, at, :] = jnp.where(odd, east, west)
            second_ref[m, at, :] = jnp.where(odd, west, east)
    odd_lat = is_odd("lat")

    @pl.when(odd_lat)
    def _():
        fill_rows(c, f_ref, lat_ref, False)

    @pl.when(jnp.logical_not(odd_lat))
    def _():
        fill_rows(c, f_ref, lat_ref, True)


def lat_kernel(c, f_ref, one_ref, two_ref, corner_ref, second_ref):
    rows = f_ref.shape[1]
    odd_lat, odd_lon = is_odd("lat"), is_odd("lon")

    def strips(ref, base, high):
        at = pl.ds(rows - TILE if high else 0, TILE)
        for m in range(c.parts):
            one, two = one_ref[m, at, :], two_ref[m, at, :]
            ref[base + m] = jnp.where(odd_lon, two, one)
            ref[base + c.parts + m] = jnp.where(odd_lon, one, two)

    @pl.when(odd_lat)
    def _():
        strips(corner_ref, 0, False)
        fill_rows(c, f_ref, second_ref, True)
        strips(second_ref, c.main, True)

    @pl.when(jnp.logical_not(odd_lat))
    def _():
        strips(corner_ref, 0, True)
        fill_rows(c, f_ref, second_ref, False)
        strips(second_ref, c.main, False)


class Sweeps:
    def __init__(self, c, e, w, d, x, m, adj, state):
        self.c, self.e, self.w, self.d, self.x, self.m, self.adj, self.state = c, e, w, d, x, m, adj, state
        self.lanes = e[0].shape[-1]
        lane = lane_iota(self.lanes)
        self.at_first, self.at_last = lane == 0, lane == self.lanes - 1
        self.even_group = lax.rem(lane // DEPTH, 2) == 0

    def from_west(self, x0, x1):
        r0, r1 = pltpu.roll(x0, 1, 1), pltpu.roll(x1, 1, 1)
        return jnp.where(self.at_first, r1, r0), jnp.where(self.at_first, r0, r1)

    def from_east(self, x0, x1):
        r0, r1 = pltpu.roll(x0, self.lanes - 1, 1), pltpu.roll(x1, self.lanes - 1, 1)
        return jnp.where(self.at_last, r1, r0), jnp.where(self.at_last, r0, r1)

    def spread(self, at, easts, wests):
        for m in range(self.c.parts):
            both = (
                jnp.where(self.even_group, easts[m], wests[m]),
                jnp.where(self.even_group, wests[m], easts[m]),
            )
            for channel in range(16 * m, min(16 * m + 16, self.c.count)):
                shift = channel_shift(channel, self.lanes)
                tile = both[(channel % 16) // 8]
                if shift:
                    tile = pltpu.roll(tile, self.lanes - shift, 1)
                self.e[1][channel, at, :] = tile

    def western(self, row):
        at = pl.ds(row, TILE)
        self.w[0][at, :], self.w[1][at, :] = self.from_west(self.e[0][self.c.ce, at, :], self.e[1][self.c.ce, at, :])

    def neighbours(self, load, row, halves=2):
        c, at = self.c, pl.ds(row, TILE)
        ce = [e[c.ce, at, :] for e in self.e]
        cw = [w[at, :] for w in self.w]
        cn = [e[c.cn, at, :] for e in self.e]
        cs = [e[c.cn, pl.ds(row - 1, TILE), :] for e in self.e]
        own = [(load(0, k, at), load(1, k, at)) for k in range(c.levels)]
        out = []
        for k in range(c.levels):
            east, west = self.from_east(*own[k]), self.from_west(*own[k])
            pair = []
            for h in range(halves):
                north, south = load(h, k, pl.ds(row + 1, TILE)), load(h, k, pl.ds(row - 1, TILE))
                total = (ce[h] * east[h] + cw[h] * west[h]) + (cn[h] * north + cs[h] * south)
                around = [own[j][h] for j in (k - 1, k + 1) if 0 <= j < c.levels]
                pair.append((own[k][h], total + vertical_coef * functools.reduce(jnp.add, around)))
            out.append(pair)
        return out

    def diagonal(self, row):
        load = lambda h, k, at: self.e[h][self.c.wet + k, at, :]
        for k, pair in enumerate(self.neighbours(load, row)):
            for h, (_, total) in enumerate(pair):
                self.d[h][k, pl.ds(row, TILE), :] = 1.0 - total

    def loader(self, index):
        if index == 0:
            return lambda h, k, at: self.e[h][self.c.u + k, at, :]
        base = (index - 1) * self.c.levels
        return lambda h, k, at: self.x[h][base + k, at, :]

    def forward(self, n, row):
        c, at = self.c, pl.ds(row, TILE)
        for k, pair in enumerate(self.neighbours(self.loader(n), row)):
            for h, (own, total) in enumerate(pair):
                e = self.e[h]
                wet = e[c.wet + k, at, :]
                bounded = wet * jnp.tanh(self.d[h][k, at, :] * own + total)
                slope = wet - bounded * bounded
                if n < STEPS - 1:
                    self.x[h][n * c.levels + k, at, :] = bounded + e[c.s + k, at, :]
                    self.m[h][n * c.levels + k, at, :] = slope
                else:
                    if h == 0:
                        self.state[k, at, :] = bounded + e[c.s + k, at, :]
                    self.x[h][n * c.levels + k, at, :] = slope * e[c.cot + k, at, :]

    def backward(self, n, row):
        c, at = self.c, pl.ds(row, TILE)
        index = 2 * STEPS - 1 - n
        for k, pair in enumerate(self.neighbours(self.loader(index), row)):
            for h, (own, total) in enumerate(pair):
                value = self.d[h][k, at, :] * own + total
                if h == 0:
                    self.adj[(n - 1) * c.levels + k, at, :] = value
                self.x[h][index * c.levels + k, at, :] = self.m[h][(n - 1) * c.levels + k, at, :] * value

    def gradient(self, row):
        c, at = self.c, pl.ds(row, TILE)
        for k, pair in enumerate(self.neighbours(self.loader(2 * STEPS - 1), row, 1)):
            own, total = pair[0]
            yield k, self.e[0][c.wet + k, at, :] * (self.d[0][k, at, :] * own + total)

    def source_gradient(self, row):
        c, at = self.c, pl.ds(row, TILE)
        for k in range(c.levels):
            total = self.e[0][c.cot + k, at, :]
            for n in range(STEPS - 1):
                total = total + self.adj[n * c.levels + k, at, :]
            yield k, self.e[0][c.wet + k, at, :] * total


def fill_halo(c, e0, message, row, low):
    to = pl.ds(row, TILE)
    for channel in range(c.cot):
        e0[channel, to, :] = message(channel)
    for k in range(c.levels):
        tile = message(c.cot + k // 2)
        if (k % 2 == 0) == low:
            tile = pltpu.roll(tile, TILE // 2, 0)
        e0[c.cot + k, to, :] = tile


def own_kernel(c, f_ref, one_ref, two_ref, lat_one_ref, e0, e1, w0, w1, d0, d1, x0, x1, m0, m1, adj, state, grad, gsource):
    rows = f_ref.shape[1]
    odd_lon = is_odd("lon")
    s = Sweeps(c, (e0, e1), (w0, w1), (d0, d1), (x0, x1), (m0, m1), adj, state)
    zero = jnp.zeros((TILE, f_ref.shape[2]), jnp.float32)
    for ref in (e0, e1):
        for end in (pl.ds(0, TILE), pl.ds(HALO + rows, TILE)):
            for channel in (*range(c.u, c.u + c.levels), *range(c.wet, c.wet + c.levels), c.cn):
                ref[channel, end, :] = zero
    odd_lat = is_odd("lat")

    @pl.when(odd_lat)
    def _():
        fill_halo(c, e0, lambda i: lat_one_ref[i], 0, True)

    @pl.when(jnp.logical_not(odd_lat))
    def _():
        fill_halo(c, e0, lambda i: lat_one_ref[i], HALO + rows, False)

    places = [HALO + t * TILE for t in range(rows // TILE)]
    for row in places:
        at, to = pl.ds(row - HALO, TILE), pl.ds(row, TILE)
        for channel in range(c.count):
            e0[channel, to, :] = f_ref[channel, at, :]
        ones = [one_ref[m, at, :] for m in range(c.parts)]
        twos = [two_ref[m, at, :] for m in range(c.parts)]
        s.spread(
            to,
            [jnp.where(odd_lon, b, a) for a, b in zip(ones, twos)],
            [jnp.where(odd_lon, a, b) for a, b in zip(ones, twos)],
        )
        s.western(row)
    for row in places:
        s.diagonal(row)
    for n in range(STEPS):
        for row in places:
            s.forward(n, row)
    for n in range(STEPS - 1, 0, -1):
        for row in places:
            s.backward(n, row)
    for row in places[1:-1]:
        at = pl.ds(row - HALO, TILE)
        for k, value in s.source_gradient(row):
            gsource[k, at, :] = value
        for k, value in s.gradient(row):
            grad[k, at, :] = value


def edge_kernel(
    c, corner_ref, lat_two_ref, *refs,
):
    aliased = refs[: len(refs) // 2]
    del aliased
    e0, e1, w0, w1, d0, d1, x0, x1, m0, m1, adj, state, grad, gsource, state_hbm, grad_hbm, gsource_hbm, sems = refs[14:]
    rows = grad.shape[1]
    odd_lat = is_odd("lat")
    s = Sweeps(c, (e0, e1), (w0, w1), (d0, d1), (x0, x1), (m0, m1), adj, state)

    @pl.when(odd_lat)
    def _():
        fill_halo(c, e0, lambda i: lat_two_ref[i], HALO + rows, False)

    @pl.when(jnp.logical_not(odd_lat))
    def _():
        fill_halo(c, e0, lambda i: lat_two_ref[i], 0, True)

    for row, low in ((0, True), (HALO + rows, False)):
        near = odd_lat if low else jnp.logical_not(odd_lat)
        strips = [jnp.where(near, corner_ref[m], lat_two_ref[c.main + m]) for m in range(2 * c.parts)]
        s.spread(pl.ds(row, TILE), strips[: c.parts], strips[c.parts :])
        s.western(row)
    top = lambda i: HALO + i - (DEPTH - 1)
    bottom = lambda i: HALO + rows - 1 - i
    places = lambda i: (top(i), bottom(i))
    for row in places(0):
        s.diagonal(row)
    for n in range(STEPS):
        for row in places(n):
            s.forward(n, row)
    own = pl.ds(HALO, rows)
    moves = [
        pltpu.make_async_copy(state.at[:, own, :], state_hbm, sems.at[0]),
        pltpu.make_async_copy(gsource, gsource_hbm, sems.at[1]),
        pltpu.make_async_copy(grad, grad_hbm, sems.at[2]),
    ]
    moves[0].start()
    for n in range(STEPS - 1, 0, -1):
        for row in places(2 * STEPS - 1 - n):
            s.backward(n, row)
    for row in places(DEPTH - 1):
        for k, value in s.source_gradient(row):
            gsource[k, pl.ds(row - HALO, TILE), :] = value
    moves[1].start()
    for row in places(DEPTH - 1):
        for k, value in s.gradient(row):
            grad[k, pl.ds(row - HALO, TILE), :] = value
    moves[2].start()
    for move in moves:
        move.wait()


def swaps(count, offset, wrap):
    pairs = []
    for i in range(offset, count, 2):
        j = i + 1
        if j < count or wrap:
            pairs += [(i, j % count), (j % count, i)]
    return pairs


def body(initial_state, source, cotangent, face_coefs, land_mask, bottom):
    arguments = (initial_state, source, cotangent, face_coefs, land_mask, bottom)
    levels, rows, lanes = initial_state.shape
    c = Names(levels)
    span = rows + 2 * HALO
    f32 = lambda *shape: jax.ShapeDtypeStruct(shape, jnp.float32)
    vmem, hbm = pl.BlockSpec(memory_space=pltpu.VMEM), pl.BlockSpec(memory_space=pltpu.HBM)
    params = pltpu.CompilerParams(vmem_limit_bytes=8 * 1024 * 1024)

    fields, one, two, lat_one = pl.pallas_call(
        functools.partial(pack_kernel, c),
        out_shape=(f32(c.count, rows, lanes), f32(c.parts, rows, lanes), f32(c.parts, rows, lanes), f32(c.main, TILE, lanes)),
        in_specs=[hbm] * 6,
        out_specs=(vmem,) * 4,
        scratch_shapes=[
            pltpu.VMEM((levels, rows, lanes), jnp.float32),
            pltpu.VMEM((levels, rows, lanes), jnp.float32),
            pltpu.VMEM((2, rows, lanes), jnp.float32),
            pltpu.VMEM((levels, rows, lanes), jnp.int32),
            pltpu.VMEM((rows, lanes), jnp.int32),
            pltpu.SemaphoreType.DMA((6,)),
        ],
        compiler_params=params,
        name="pack",
    )(*(pltpu.with_memory_space_constraint(x, pltpu.HBM) for x in arguments))
    lon, lat = lax.axis_size("lon"), lax.axis_size("lat")
    one = lax.ppermute(one, "lon", swaps(lon, 0, True))
    two = lax.ppermute(two, "lon", swaps(lon, 1, True))
    lat_one = lax.ppermute(lat_one, "lat", swaps(lat, 0, False))
    corner, lat_two = pl.pallas_call(
        functools.partial(lat_kernel, c),
        out_shape=(f32(2 * c.parts, TILE, lanes), f32(c.main + 2 * c.parts, TILE, lanes)),
        in_specs=[vmem] * 3,
        out_specs=(vmem,) * 2,
        compiler_params=params,
        name="lat_rows",
    )(fields, one, two)
    lat_two = lax.ppermute(lat_two, "lat", swaps(lat, 1, False))
    corner = lax.ppermute(corner, "lat", swaps(lat, 0, False))
    twice = lambda *shape: (f32(*shape), f32(*shape))
    shapes = (
        *twice(c.count, span, lanes),
        *twice(span, lanes),
        *twice(levels, span, lanes),
        *twice((2 * STEPS - 1) * levels, span, lanes),
        *twice((STEPS - 1) * levels, span, lanes),
        f32((STEPS - 1) * levels, span, lanes),
        f32(levels, span, lanes),
        f32(levels, rows, lanes),
        f32(levels, rows, lanes),
    )
    own = pl.pallas_call(
        functools.partial(own_kernel, c),
        out_shape=shapes,
        in_specs=[vmem] * 4,
        out_specs=(vmem,) * len(shapes),
        compiler_params=params,
        cost_estimate=pl.CostEstimate(
            flops=2 * STEPS * levels * rows * lanes * 40, bytes_accessed=16 * 2**20, transcendentals=0
        ),
        name="own_rows",
    )(fields, one, two, lat_one)
    out = pl.pallas_call(
        functools.partial(edge_kernel, c),
        out_shape=(*shapes, *(f32(levels, rows, lanes),) * 3),
        in_specs=[vmem] * (2 + len(shapes)),
        out_specs=(*(vmem,) * len(shapes), hbm, hbm, hbm),
        input_output_aliases={2 + i: i for i in range(len(shapes))},
        scratch_shapes=[pltpu.SemaphoreType.DMA((3,))],
        compiler_params=params,
        name="edge_rows",
    )(corner, lat_two, *own)
    return tuple(out[len(shapes) :])


def solution(mesh):
    block = P(None, "lat", "lon")
    return jax.shard_map(
        body,
        mesh=mesh,
        in_specs=(block, block, block, block, block, P("lat", "lon")),
        out_specs=(block, block, block),
        check_vma=False,
    )
```

```python
import functools

import jax
import jax.numpy as jnp
from jax import lax
from jax.experimental import pallas as pl
from jax.experimental.pallas import tpu as pltpu
from jax.sharding import PartitionSpec as P

STEPS = 4
DEPTH = 2 * STEPS
TILE = 8
HALO = TILE

vertical_coef = 0.04


class Names:
    def __init__(self, levels):
        self.levels = levels
        self.u, self.s, self.wet = 0, levels, 2 * levels
        self.ce, self.cn, self.cot = 3 * levels, 3 * levels + 1, 3 * levels + 2
        self.count = 4 * levels + 2
        self.paired = -(-levels // 2)
        self.main = self.cot + self.paired
        self.parts = -(-self.count // 16)


def lane_iota(lanes):
    return lax.broadcasted_iota(jnp.int32, (TILE, lanes), 1)


def channel_shift(channel, lanes):
    place = channel % 16
    return (2 * DEPTH * (place % 8) + DEPTH * (place // 8)) % lanes


def is_odd(axis):
    return lax.rem(lax.axis_index(axis), 2) == 1


def fill_rows(c, f_ref, ref, high):
    rows = f_ref.shape[1]
    at = pl.ds(rows - TILE if high else 0, TILE)
    for channel in range(c.cot):
        ref[channel] = f_ref[channel, at, :]
    row = lax.broadcasted_iota(jnp.int32, (TILE, f_ref.shape[2]), 0)
    half = TILE // 2
    for q in range(c.paired):
        one = f_ref[c.cot + 2 * q, at, :]
        two = f_ref[c.cot + min(2 * q + 1, c.levels - 1), at, :]
        if high:
            one = pltpu.roll(one, half, 0)
        else:
            two = pltpu.roll(two, half, 0)
        ref[c.cot + q] = jnp.where(row < half, one, two)


def pack_kernel(
    c, u_hbm, s_hbm, a_hbm, c_hbm, land_hbm, bottom_hbm, f_ref, first_ref, second_ref, lat_ref,
    u_ref, s_ref, c_ref, land_ref, bottom_ref, sems,
):
    levels = c.levels
    _, rows, lanes = u_ref.shape
    moves = [
        pltpu.make_async_copy(source, target, sems.at[i])
        for i, (source, target) in enumerate(
            (
                (bottom_hbm, bottom_ref),
                (land_hbm, land_ref),
                (u_hbm, u_ref),
                (s_hbm, s_ref),
                (c_hbm, c_ref),
                (a_hbm, f_ref.at[pl.ds(c.cot, levels)]),
            )
        )
    ]
    for move in moves:
        move.start()
    for move in moves:
        move.wait()
    last_lat = lax.axis_index("lat") == lax.axis_size("lat") - 1
    for k in range(levels):
        wet = jnp.where(k < bottom_ref[...], land_ref[k], 0).astype(jnp.float32)
        f_ref[c.u + k] = wet * u_ref[k]
        f_ref[c.s + k] = wet * s_ref[k]
        f_ref[c.wet + k] = wet
    f_ref[c.ce] = c_ref[0]
    row = lax.broadcasted_iota(jnp.int32, (rows, lanes), 0)
    f_ref[c.cn] = jnp.where(jnp.logical_and(last_lat, row == rows - 1), 0.0, c_ref[1])
    odd = is_odd("lon")
    group = lane_iota(lanes) // DEPTH
    groups = lanes // DEPTH
    for t in range(rows // TILE):
        at = pl.ds(t * TILE, TILE)
        for m in range(c.parts):
            east = jnp.zeros((TILE, lanes), jnp.float32)
            west = east
            for channel in range(16 * m, min(16 * m + 16, c.count)):
                shift = channel_shift(channel, lanes)
                tile = f_ref[channel, at, :]
                if shift:
                    tile = pltpu.roll(tile, shift, 1)
                east = jnp.where(group == shift // DEPTH, tile, east)
                west = jnp.where(group == (shift // DEPTH - 1) % groups, tile, west)
            first_ref[m, at, :] = jnp.where(odd, east, west)
            second_ref[m, at, :] = jnp.where(odd, west, east)
    odd_lat = is_odd("lat")

    @pl.when(odd_lat)
    def _():
        fill_rows(c, f_ref, lat_ref, False)

    @pl.when(jnp.logical_not(odd_lat))
    def _():
        fill_rows(c, f_ref, lat_ref, True)


def lat_kernel(c, f_ref, one_ref, two_ref, lat_one_ref, corner_ref, second_ref):
    del lat_one_ref
    rows = f_ref.shape[1]
    odd_lat, odd_lon = is_odd("lat"), is_odd("lon")

    def strips(ref, base, high):
        at = pl.ds(rows - TILE if high else 0, TILE)
        for m in range(c.parts):
            one, two = one_ref[m, at, :], two_ref[m, at, :]
            ref[base + m] = jnp.where(odd_lon, two, one)
            ref[base + c.parts + m] = jnp.where(odd_lon, one, two)

    @pl.when(odd_lat)
    def _():
        strips(corner_ref, 0, False)
        fill_rows(c, f_ref, second_ref, True)
        strips(second_ref, c.main, True)

    @pl.when(jnp.logical_not(odd_lat))
    def _():
        strips(corner_ref, 0, True)
        fill_rows(c, f_ref, second_ref, False)
        strips(second_ref, c.main, False)


class Sweeps:
    def __init__(self, c, e, w, d, x, m, adj, state):
        self.c, self.e, self.w, self.d, self.x, self.m, self.adj, self.state = c, e, w, d, x, m, adj, state
        self.lanes = e[0].shape[-1]
        lane = lane_iota(self.lanes)
        self.at_first, self.at_last = lane == 0, lane == self.lanes - 1
        self.even_group = lax.rem(lane // DEPTH, 2) == 0

    def from_west(self, x0, x1):
        r0, r1 = pltpu.roll(x0, 1, 1), pltpu.roll(x1, 1, 1)
        return jnp.where(self.at_first, r1, r0), jnp.where(self.at_first, r0, r1)

    def from_east(self, x0, x1):
        r0, r1 = pltpu.roll(x0, self.lanes - 1, 1), pltpu.roll(x1, self.lanes - 1, 1)
        return jnp.where(self.at_last, r1, r0), jnp.where(self.at_last, r0, r1)

    def spread(self, at, easts, wests):
        for m in range(self.c.parts):
            both = (
                jnp.where(self.even_group, easts[m], wests[m]),
                jnp.where(self.even_group, wests[m], easts[m]),
            )
            for channel in range(16 * m, min(16 * m + 16, self.c.count)):
                shift = channel_shift(channel, self.lanes)
                tile = both[(channel % 16) // 8]
                if shift:
                    tile = pltpu.roll(tile, self.lanes - shift, 1)
                self.e[1][channel, at, :] = tile

    def western(self, row):
        at = pl.ds(row, TILE)
        self.w[0][at, :], self.w[1][at, :] = self.from_west(self.e[0][self.c.ce, at, :], self.e[1][self.c.ce, at, :])

    def neighbours(self, load, row, halves=2):
        c, at = self.c, pl.ds(row, TILE)
        ce = [e[c.ce, at, :] for e in self.e]
        cw = [w[at, :] for w in self.w]
        cn = [e[c.cn, at, :] for e in self.e]
        cs = [e[c.cn, pl.ds(row - 1, TILE), :] for e in self.e]
        own = [(load(0, k, at), load(1, k, at)) for k in range(c.levels)]
        out = []
        for k in range(c.levels):
            east, west = self.from_east(*own[k]), self.from_west(*own[k])
            pair = []
            for h in range(halves):
                north, south = load(h, k, pl.ds(row + 1, TILE)), load(h, k, pl.ds(row - 1, TILE))
                total = (ce[h] * east[h] + cw[h] * west[h]) + (cn[h] * north + cs[h] * south)
                around = [own[j][h] for j in (k - 1, k + 1) if 0 <= j < c.levels]
                pair.append((own[k][h], total + vertical_coef * functools.reduce(jnp.add, around)))
            out.append(pair)
        return out

    def diagonal(self, row):
        load = lambda h, k, at: self.e[h][self.c.wet + k, at, :]
        for k, pair in enumerate(self.neighbours(load, row)):
            for h, (_, total) in enumerate(pair):
                self.d[h][k, pl.ds(row, TILE), :] = 1.0 - total

    def loader(self, index):
        if index == 0:
            return lambda h, k, at: self.e[h][self.c.u + k, at, :]
        base = (index - 1) * self.c.levels
        return lambda h, k, at: self.x[h][base + k, at, :]

    def forward(self, n, row):
        c, at = self.c, pl.ds(row, TILE)
        for k, pair in enumerate(self.neighbours(self.loader(n), row)):
            for h, (own, total) in enumerate(pair):
                e = self.e[h]
                wet = e[c.wet + k, at, :]
                bounded = wet * jnp.tanh(self.d[h][k, at, :] * own + total)
                slope = wet - bounded * bounded
                if n < STEPS - 1:
                    self.x[h][n * c.levels + k, at, :] = bounded + e[c.s + k, at, :]
                    self.m[h][n * c.levels + k, at, :] = slope
                else:
                    if h == 0:
                        self.state[k, at, :] = bounded + e[c.s + k, at, :]
                    self.x[h][n * c.levels + k, at, :] = slope * e[c.cot + k, at, :]

    def backward(self, n, row):
        c, at = self.c, pl.ds(row, TILE)
        index = 2 * STEPS - 1 - n
        for k, pair in enumerate(self.neighbours(self.loader(index), row)):
            for h, (own, total) in enumerate(pair):
                value = self.d[h][k, at, :] * own + total
                if h == 0:
                    self.adj[(n - 1) * c.levels + k, at, :] = value
                self.x[h][index * c.levels + k, at, :] = self.m[h][(n - 1) * c.levels + k, at, :] * value

    def gradient(self, row):
        c, at = self.c, pl.ds(row, TILE)
        for k, pair in enumerate(self.neighbours(self.loader(2 * STEPS - 1), row, 1)):
            own, total = pair[0]
            yield k, self.e[0][c.wet + k, at, :] * (self.d[0][k, at, :] * own + total)

    def source_gradient(self, row):
        c, at = self.c, pl.ds(row, TILE)
        for k in range(c.levels):
            total = self.e[0][c.cot + k, at, :]
            for n in range(STEPS - 1):
                total = total + self.adj[n * c.levels + k, at, :]
            yield k, self.e[0][c.wet + k, at, :] * total


def fill_halo(c, e0, message, row, low):
    to = pl.ds(row, TILE)
    for channel in range(c.cot):
        e0[channel, to, :] = message(channel)
    for k in range(c.levels):
        tile = message(c.cot + k // 2)
        if (k % 2 == 0) == low:
            tile = pltpu.roll(tile, TILE // 2, 0)
        e0[c.cot + k, to, :] = tile


def own_kernel(c, f_ref, one_ref, two_ref, lat_one_ref, e0, e1, w0, w1, d0, d1, x0, x1, m0, m1, adj, state, grad, gsource):
    rows = f_ref.shape[1]
    odd_lon = is_odd("lon")
    s = Sweeps(c, (e0, e1), (w0, w1), (d0, d1), (x0, x1), (m0, m1), adj, state)
    zero = jnp.zeros((TILE, f_ref.shape[2]), jnp.float32)
    for ref in (e0, e1):
        for end in (pl.ds(0, TILE), pl.ds(HALO + rows, TILE)):
            for channel in (*range(c.u, c.u + c.levels), *range(c.wet, c.wet + c.levels), c.cn):
                ref[channel, end, :] = zero
    odd_lat = is_odd("lat")

    @pl.when(odd_lat)
    def _():
        fill_halo(c, e0, lambda i: lat_one_ref[i], 0, True)

    @pl.when(jnp.logical_not(odd_lat))
    def _():
        fill_halo(c, e0, lambda i: lat_one_ref[i], HALO + rows, False)

    places = [HALO + t * TILE for t in range(rows // TILE)]
    for row in places:
        at, to = pl.ds(row - HALO, TILE), pl.ds(row, TILE)
        for channel in range(c.count):
            e0[channel, to, :] = f_ref[channel, at, :]
        ones = [one_ref[m, at, :] for m in range(c.parts)]
        twos = [two_ref[m, at, :] for m in range(c.parts)]
        s.spread(
            to,
            [jnp.where(odd_lon, b, a) for a, b in zip(ones, twos)],
            [jnp.where(odd_lon, a, b) for a, b in zip(ones, twos)],
        )
        s.western(row)
    for row in places:
        s.diagonal(row)
    for n in range(STEPS):
        for row in places:
            s.forward(n, row)
    for n in range(STEPS - 1, 0, -1):
        for row in places:
            s.backward(n, row)
    for row in places[1:-1]:
        at = pl.ds(row - HALO, TILE)
        for k, value in s.source_gradient(row):
            gsource[k, at, :] = value
        for k, value in s.gradient(row):
            grad[k, at, :] = value


def edge_kernel(
    c, corner_ref, lat_two_ref, *refs,
):
    aliased = refs[: len(refs) // 2]
    del aliased
    e0, e1, w0, w1, d0, d1, x0, x1, m0, m1, adj, state, grad, gsource, state_hbm, grad_hbm, gsource_hbm, sems = refs[14:]
    rows = grad.shape[1]
    odd_lat = is_odd("lat")
    s = Sweeps(c, (e0, e1), (w0, w1), (d0, d1), (x0, x1), (m0, m1), adj, state)

    @pl.when(odd_lat)
    def _():
        fill_halo(c, e0, lambda i: lat_two_ref[i], HALO + rows, False)

    @pl.when(jnp.logical_not(odd_lat))
    def _():
        fill_halo(c, e0, lambda i: lat_two_ref[i], 0, True)

    for row, low in ((0, True), (HALO + rows, False)):
        near = odd_lat if low else jnp.logical_not(odd_lat)
        strips = [jnp.where(near, corner_ref[m], lat_two_ref[c.main + m]) for m in range(2 * c.parts)]
        s.spread(pl.ds(row, TILE), strips[: c.parts], strips[c.parts :])
        s.western(row)
    top = lambda i: HALO + i - (DEPTH - 1)
    bottom = lambda i: HALO + rows - 1 - i
    places = lambda i: (top(i), bottom(i))
    for row in places(0):
        s.diagonal(row)
    for n in range(STEPS):
        for row in places(n):
            s.forward(n, row)
    own = pl.ds(HALO, rows)
    moves = [
        pltpu.make_async_copy(state.at[:, own, :], state_hbm, sems.at[0]),
        pltpu.make_async_copy(gsource, gsource_hbm, sems.at[1]),
        pltpu.make_async_copy(grad, grad_hbm, sems.at[2]),
    ]
    moves[0].start()
    for n in range(STEPS - 1, 0, -1):
        for row in places(2 * STEPS - 1 - n):
            s.backward(n, row)
    for row in places(DEPTH - 1):
        for k, value in s.source_gradient(row):
            gsource[k, pl.ds(row - HALO, TILE), :] = value
    moves[1].start()
    for row in places(DEPTH - 1):
        for k, value in s.gradient(row):
            grad[k, pl.ds(row - HALO, TILE), :] = value
    moves[2].start()
    for move in moves:
        move.wait()


def swaps(count, offset, wrap):
    pairs = []
    for i in range(offset, count, 2):
        j = i + 1
        if j < count or wrap:
            pairs += [(i, j % count), (j % count, i)]
    return pairs


def body(initial_state, source, cotangent, face_coefs, land_mask, bottom):
    arguments = (initial_state, source, cotangent, face_coefs, land_mask, bottom)
    levels, rows, lanes = initial_state.shape
    c = Names(levels)
    span = rows + 2 * HALO
    f32 = lambda *shape: jax.ShapeDtypeStruct(shape, jnp.float32)
    vmem, hbm = pl.BlockSpec(memory_space=pltpu.VMEM), pl.BlockSpec(memory_space=pltpu.HBM)
    params = pltpu.CompilerParams(vmem_limit_bytes=8 * 1024 * 1024)

    fields, one, two, lat_one = pl.pallas_call(
        functools.partial(pack_kernel, c),
        out_shape=(f32(c.count, rows, lanes), f32(c.parts, rows, lanes), f32(c.parts, rows, lanes), f32(c.main, TILE, lanes)),
        in_specs=[hbm] * 6,
        out_specs=(vmem,) * 4,
        scratch_shapes=[
            pltpu.VMEM((levels, rows, lanes), jnp.float32),
            pltpu.VMEM((levels, rows, lanes), jnp.float32),
            pltpu.VMEM((2, rows, lanes), jnp.float32),
            pltpu.VMEM((levels, rows, lanes), jnp.int32),
            pltpu.VMEM((rows, lanes), jnp.int32),
            pltpu.SemaphoreType.DMA((6,)),
        ],
        compiler_params=params,
        name="pack",
    )(*(pltpu.with_memory_space_constraint(x, pltpu.HBM) for x in arguments))
    lon, lat = lax.axis_size("lon"), lax.axis_size("lat")
    one = lax.ppermute(one, "lon", swaps(lon, 0, True))
    two = lax.ppermute(two, "lon", swaps(lon, 1, True))
    lat_one = lax.ppermute(lat_one, "lat", swaps(lat, 0, False))
    corner, lat_two = pl.pallas_call(
        functools.partial(lat_kernel, c),
        out_shape=(f32(2 * c.parts, TILE, lanes), f32(c.main + 2 * c.parts, TILE, lanes)),
        in_specs=[vmem] * 4,
        out_specs=(vmem,) * 2,
        compiler_params=params,
        name="lat_rows",
    )(fields, one, two, lat_one)
    lat_two = lax.ppermute(lat_two, "lat", swaps(lat, 1, False))
    corner = lax.ppermute(corner, "lat", swaps(lat, 0, False))
    twice = lambda *shape: (f32(*shape), f32(*shape))
    shapes = (
        *twice(c.count, span, lanes),
        *twice(span, lanes),
        *twice(levels, span, lanes),
        *twice((2 * STEPS - 1) * levels, span, lanes),
        *twice((STEPS - 1) * levels, span, lanes),
        f32((STEPS - 1) * levels, span, lanes),
        f32(levels, span, lanes),
        f32(levels, rows, lanes),
        f32(levels, rows, lanes),
    )
    own = pl.pallas_call(
        functools.partial(own_kernel, c),
        out_shape=shapes,
        in_specs=[vmem] * 4,
        out_specs=(vmem,) * len(shapes),
        compiler_params=params,
        cost_estimate=pl.CostEstimate(
            flops=2 * STEPS * levels * rows * lanes * 40, bytes_accessed=16 * 2**20, transcendentals=0
        ),
        name="own_rows",
    )(fields, one, two, lat_one)
    out = pl.pallas_call(
        functools.partial(edge_kernel, c),
        out_shape=(*shapes, *(f32(levels, rows, lanes),) * 3),
        in_specs=[vmem] * (2 + len(shapes)),
        out_specs=(*(vmem,) * len(shapes), hbm, hbm, hbm),
        input_output_aliases={2 + i: i for i in range(len(shapes))},
        scratch_shapes=[pltpu.SemaphoreType.DMA((3,))],
        compiler_params=params,
        name="edge_rows",
    )(corner, lat_two, *own)
    return tuple(out[len(shapes) :])


def solution(mesh):
    block = P(None, "lat", "lon")
    return jax.shard_map(
        body,
        mesh=mesh,
        in_specs=(block, block, block, block, block, P("lat", "lon")),
        out_specs=(block, block, block),
        check_vma=False,
    )
```

```python
import functools

import jax
import jax.numpy as jnp
from jax import lax
from jax.experimental import pallas as pl
from jax.experimental.pallas import tpu as pltpu
from jax.sharding import PartitionSpec as P

STEPS = 4
DEPTH = 2 * STEPS
TILE = 8
HALO = TILE

vertical_coef = 0.04


class Names:
    def __init__(self, levels):
        self.levels = levels
        self.u, self.s, self.wet = 0, levels, 2 * levels
        self.ce, self.cn, self.cot = 3 * levels, 3 * levels + 1, 3 * levels + 2
        self.count = 4 * levels + 2
        self.paired = -(-levels // 2)
        self.main = self.cot + self.paired
        assert 16 < self.main <= 24
        self.strips = 3


def lane_iota(lanes):
    return lax.broadcasted_iota(jnp.int32, (TILE, lanes), 1)


def shift_of(place):
    return 2 * DEPTH * (place % 8) + DEPTH * (place // 8)


def strip_tiles(c, tiles):
    folded = -(-tiles // 2)
    whole = [[(channel, t) for channel in range(16)] for t in range(tiles)]
    shared = [
        {p + 8 * half: (16 + p, t + half * folded) for half in (0, 1) if t + half * folded < tiles for p in range(c.main - 16)}
        for t in range(folded)
    ]
    return [dict(enumerate(places)) for places in whole] + shared


def even_groups(lanes):
    return lax.rem(lane_iota(lanes) // DEPTH, 2) == 0


def is_odd(axis):
    return lax.rem(lax.axis_index(axis), 2) == 1


def fill_rows(c, f_ref, ref, high):
    rows = f_ref.shape[1]
    at = pl.ds(rows - TILE if high else 0, TILE)
    for channel in range(c.cot):
        ref[channel] = f_ref[channel, at, :]
    row = lax.broadcasted_iota(jnp.int32, (TILE, f_ref.shape[2]), 0)
    half = TILE // 2
    for q in range(c.paired):
        one = f_ref[c.cot + 2 * q, at, :]
        two = f_ref[c.cot + min(2 * q + 1, c.levels - 1), at, :]
        if high:
            one = pltpu.roll(one, half, 0)
        else:
            two = pltpu.roll(two, half, 0)
        ref[c.cot + q] = jnp.where(row < half, one, two)


def pack_kernel(
    c, u_hbm, s_hbm, a_hbm, c_hbm, land_hbm, bottom_hbm, f_ref, first_ref, second_ref, lat_ref,
    u_ref, s_ref, c_ref, land_ref, bottom_ref, sems,
):
    levels = c.levels
    _, rows, lanes = u_ref.shape
    moves = [
        pltpu.make_async_copy(source, target, sems.at[i])
        for i, (source, target) in enumerate(
            (
                (bottom_hbm, bottom_ref),
                (land_hbm, land_ref),
                (u_hbm, u_ref),
                (s_hbm, s_ref),
                (c_hbm, c_ref),
                (a_hbm, f_ref.at[pl.ds(c.cot, levels)]),
            )
        )
    ]
    for move in moves:
        move.start()
    for move in moves:
        move.wait()
    last_lat = lax.axis_index("lat") == lax.axis_size("lat") - 1
    for k in range(levels):
        wet = jnp.where(k < bottom_ref[...], land_ref[k], 0).astype(jnp.float32)
        f_ref[c.u + k] = wet * u_ref[k]
        f_ref[c.s + k] = wet * s_ref[k]
        f_ref[c.wet + k] = wet
    f_ref[c.ce] = c_ref[0]
    row = lax.broadcasted_iota(jnp.int32, (rows, lanes), 0)
    f_ref[c.cn] = jnp.where(jnp.logical_and(last_lat, row == rows - 1), 0.0, c_ref[1])
    odd = is_odd("lon")
    lane = lane_iota(lanes)
    group, groups = lane // DEPTH, lanes // DEPTH
    half = DEPTH // 2

    def columns(channel, t):
        at = pl.ds(t * TILE, TILE)
        if channel < c.cot:
            return f_ref[channel, at, :]
        first = c.cot + 2 * (channel - c.cot)
        one, two = f_ref[first, at, :], f_ref[min(first + 1, c.count - 1), at, :]
        moved = jnp.where(lane < lanes // 2, pltpu.roll(two, half, 1), pltpu.roll(two, lanes - half, 1))
        return jnp.where(jnp.logical_or(lane < half, lane >= lanes - half), one, moved)

    for i, places in enumerate(strip_tiles(c, rows // TILE)):
        east = jnp.zeros((TILE, lanes), jnp.float32)
        west = east
        for place, (channel, t) in places.items():
            shift = shift_of(place)
            tile = columns(channel, t)
            if shift:
                tile = pltpu.roll(tile, shift, 1)
            east = jnp.where(group == shift // DEPTH, tile, east)
            west = jnp.where(group == (shift // DEPTH - 1) % groups, tile, west)
        first_ref[i] = jnp.where(odd, east, west)
        second_ref[i] = jnp.where(odd, west, east)
    odd_lat = is_odd("lat")

    @pl.when(odd_lat)
    def _():
        fill_rows(c, f_ref, lat_ref, False)

    @pl.when(jnp.logical_not(odd_lat))
    def _():
        fill_rows(c, f_ref, lat_ref, True)


def lat_kernel(c, f_ref, one_ref, two_ref, lat_one_ref, corner_ref, second_ref):
    del lat_one_ref
    rows = f_ref.shape[1]
    odd_lat, odd_lon = is_odd("lat"), is_odd("lon")

    tiles = rows // TILE
    folded = -(-tiles // 2)
    even_group = even_groups(f_ref.shape[2])

    def pair(i):
        one, two = one_ref[i], two_ref[i]
        return jnp.where(odd_lon, two, one), jnp.where(odd_lon, one, two)

    def strips(ref, base, high):
        t = tiles - 1 if high else 0
        ref[base], ref[base + 1] = pair(t)
        east, west = pair(tiles + t % folded)
        if t < folded:
            ref[base + 2] = jnp.where(even_group, east, west)
        else:
            ref[base + 2] = pltpu.roll(jnp.where(even_group, west, east), f_ref.shape[2] - DEPTH, 1)

    @pl.when(odd_lat)
    def _():
        strips(corner_ref, 0, False)
        fill_rows(c, f_ref, second_ref, True)
        strips(second_ref, c.main, True)

    @pl.when(jnp.logical_not(odd_lat))
    def _():
        strips(corner_ref, 0, True)
        fill_rows(c, f_ref, second_ref, False)
        strips(second_ref, c.main, False)


class Sweeps:
    def __init__(self, c, e, w, d, x, m, adj, state):
        self.c, self.e, self.w, self.d, self.x, self.m, self.adj, self.state = c, e, w, d, x, m, adj, state
        self.lanes = e[0].shape[-1]
        lane = lane_iota(self.lanes)
        self.at_first, self.at_last = lane == 0, lane == self.lanes - 1
        self.left = lane < self.lanes // 2
        self.even_group = even_groups(self.lanes)

    def from_west(self, x0, x1):
        r0, r1 = pltpu.roll(x0, 1, 1), pltpu.roll(x1, 1, 1)
        return jnp.where(self.at_first, r1, r0), jnp.where(self.at_first, r0, r1)

    def from_east(self, x0, x1):
        r0, r1 = pltpu.roll(x0, self.lanes - 1, 1), pltpu.roll(x1, self.lanes - 1, 1)
        return jnp.where(self.at_last, r1, r0), jnp.where(self.at_last, r0, r1)

    def mixed(self, east, west):
        return jnp.where(self.even_group, east, west), jnp.where(self.even_group, west, east)

    def spread(self, row, channel, tile, shift):
        c, at = self.c, pl.ds(row, TILE)
        if shift:
            tile = pltpu.roll(tile, self.lanes - shift, 1)
        if channel < c.cot:
            self.e[1][channel, at, :] = tile
            return
        first, half = c.cot + 2 * (channel - c.cot), DEPTH // 2
        self.e[1][first, at, :] = tile
        if first + 1 < c.count:
            moved = jnp.where(self.left, pltpu.roll(tile, self.lanes - half, 1), pltpu.roll(tile, half, 1))
            self.e[1][first + 1, at, :] = moved

    def western(self, row):
        at = pl.ds(row, TILE)
        self.w[0][at, :], self.w[1][at, :] = self.from_west(self.e[0][self.c.ce, at, :], self.e[1][self.c.ce, at, :])

    def neighbours(self, load, row, halves=2):
        c, at = self.c, pl.ds(row, TILE)
        ce = [e[c.ce, at, :] for e in self.e]
        cw = [w[at, :] for w in self.w]
        cn = [e[c.cn, at, :] for e in self.e]
        cs = [e[c.cn, pl.ds(row - 1, TILE), :] for e in self.e]
        own = [(load(0, k, at), load(1, k, at)) for k in range(c.levels)]
        out = []
        for k in range(c.levels):
            east, west = self.from_east(*own[k]), self.from_west(*own[k])
            pair = []
            for h in range(halves):
                north, south = load(h, k, pl.ds(row + 1, TILE)), load(h, k, pl.ds(row - 1, TILE))
                total = (ce[h] * east[h] + cw[h] * west[h]) + (cn[h] * north + cs[h] * south)
                around = [own[j][h] for j in (k - 1, k + 1) if 0 <= j < c.levels]
                pair.append((own[k][h], total + vertical_coef * functools.reduce(jnp.add, around)))
            out.append(pair)
        return out

    def diagonal(self, row):
        load = lambda h, k, at: self.e[h][self.c.wet + k, at, :]
        for k, pair in enumerate(self.neighbours(load, row)):
            for h, (_, total) in enumerate(pair):
                self.d[h][k, pl.ds(row, TILE), :] = 1.0 - total

    def loader(self, index):
        if index == 0:
            return lambda h, k, at: self.e[h][self.c.u + k, at, :]
        base = (index - 1) * self.c.levels
        return lambda h, k, at: self.x[h][base + k, at, :]

    def forward(self, n, row):
        c, at = self.c, pl.ds(row, TILE)
        for k, pair in enumerate(self.neighbours(self.loader(n), row)):
            for h, (own, total) in enumerate(pair):
                e = self.e[h]
                wet = e[c.wet + k, at, :]
                bounded = wet * jnp.tanh(self.d[h][k, at, :] * own + total)
                slope = wet - bounded * bounded
                if n < STEPS - 1:
                    self.x[h][n * c.levels + k, at, :] = bounded + e[c.s + k, at, :]
                    self.m[h][n * c.levels + k, at, :] = slope
                else:
                    if h == 0:
                        self.state[k, at, :] = bounded + e[c.s + k, at, :]
                    self.x[h][n * c.levels + k, at, :] = slope * e[c.cot + k, at, :]

    def backward(self, n, row):
        c, at = self.c, pl.ds(row, TILE)
        index = 2 * STEPS - 1 - n
        for k, pair in enumerate(self.neighbours(self.loader(index), row)):
            for h, (own, total) in enumerate(pair):
                value = self.d[h][k, at, :] * own + total
                if h == 0:
                    self.adj[(n - 1) * c.levels + k, at, :] = value
                self.x[h][index * c.levels + k, at, :] = self.m[h][(n - 1) * c.levels + k, at, :] * value

    def gradient(self, row):
        c, at = self.c, pl.ds(row, TILE)
        for k, pair in enumerate(self.neighbours(self.loader(2 * STEPS - 1), row, 1)):
            own, total = pair[0]
            yield k, self.e[0][c.wet + k, at, :] * (self.d[0][k, at, :] * own + total)

    def source_gradient(self, row):
        c, at = self.c, pl.ds(row, TILE)
        for k in range(c.levels):
            total = self.e[0][c.cot + k, at, :]
            for n in range(STEPS - 1):
                total = total + self.adj[n * c.levels + k, at, :]
            yield k, self.e[0][c.wet + k, at, :] * total


def beyond_pole(low):
    return lax.axis_index("lat") == (0 if low else lax.axis_size("lat") - 1)


def fill_halo(c, e0, ref, row, low):
    to = pl.ds(row, TILE)
    pole = beyond_pole(low)
    message = lambda i: jnp.where(pole, 0.0, ref[i])
    for channel in range(c.cot):
        e0[channel, to, :] = message(channel)
    for k in range(c.levels):
        tile = message(c.cot + k // 2)
        if (k % 2 == 0) == low:
            tile = pltpu.roll(tile, TILE // 2, 0)
        e0[c.cot + k, to, :] = tile


def own_kernel(c, f_ref, one_ref, two_ref, lat_one_ref, e0, e1, w0, w1, d0, d1, x0, x1, m0, m1, adj, state, grad, gsource):
    rows = f_ref.shape[1]
    odd_lon = is_odd("lon")
    s = Sweeps(c, (e0, e1), (w0, w1), (d0, d1), (x0, x1), (m0, m1), adj, state)
    zero = jnp.zeros((TILE, f_ref.shape[2]), jnp.float32)
    for ref in (e0, e1):
        for end in (pl.ds(0, TILE), pl.ds(HALO + rows, TILE)):
            for channel in (*range(c.u, c.u + c.levels), *range(c.wet, c.wet + c.levels), c.cn):
                ref[channel, end, :] = zero
    odd_lat = is_odd("lat")

    @pl.when(odd_lat)
    def _():
        fill_halo(c, e0, lat_one_ref, 0, True)

    @pl.when(jnp.logical_not(odd_lat))
    def _():
        fill_halo(c, e0, lat_one_ref, HALO + rows, False)

    places = [HALO + t * TILE for t in range(rows // TILE)]
    for row in places:
        at, to = pl.ds(row - HALO, TILE), pl.ds(row, TILE)
        for channel in range(c.count):
            e0[channel, to, :] = f_ref[channel, at, :]
    for i, held in enumerate(strip_tiles(c, rows // TILE)):
        one, two = one_ref[i], two_ref[i]
        both = s.mixed(jnp.where(odd_lon, two, one), jnp.where(odd_lon, one, two))
        for place, (channel, t) in held.items():
            s.spread(HALO + t * TILE, channel, both[place // 8], shift_of(place))
    for row in places:
        s.western(row)
    for row in places:
        s.diagonal(row)
    for n in range(STEPS):
        for row in places:
            s.forward(n, row)
    for n in range(STEPS - 1, 0, -1):
        for row in places:
            s.backward(n, row)
    for row in places[1:-1]:
        at = pl.ds(row - HALO, TILE)
        for k, value in s.source_gradient(row):
            gsource[k, at, :] = value
        for k, value in s.gradient(row):
            grad[k, at, :] = value


def edge_kernel(
    c, corner_ref, lat_two_ref, *refs,
):
    aliased = refs[: len(refs) // 2]
    del aliased
    e0, e1, w0, w1, d0, d1, x0, x1, m0, m1, adj, state, grad, gsource, state_hbm, grad_hbm, gsource_hbm, sems = refs[14:]
    rows = grad.shape[1]
    odd_lat = is_odd("lat")
    s = Sweeps(c, (e0, e1), (w0, w1), (d0, d1), (x0, x1), (m0, m1), adj, state)

    @pl.when(odd_lat)
    def _():
        fill_halo(c, e0, lat_two_ref, HALO + rows, False)

    @pl.when(jnp.logical_not(odd_lat))
    def _():
        fill_halo(c, e0, lat_two_ref, 0, True)

    for row, low in ((0, True), (HALO + rows, False)):
        near = odd_lat if low else jnp.logical_not(odd_lat)
        pole = beyond_pole(low)
        east, west, shared = (
            jnp.where(pole, 0.0, jnp.where(near, corner_ref[i], lat_two_ref[c.main + i])) for i in range(c.strips)
        )
        both = s.mixed(east, west)
        for channel in range(c.main):
            place = channel % 16
            s.spread(row, channel, both[place // 8] if channel < 16 else shared, shift_of(place))
        s.western(row)
    top = lambda i: HALO + i - (DEPTH - 1)
    bottom = lambda i: HALO + rows - 1 - i
    places = lambda i: (top(i), bottom(i))
    for row in places(0):
        s.diagonal(row)
    for n in range(STEPS):
        for row in places(n):
            s.forward(n, row)
    own = pl.ds(HALO, rows)
    moves = [
        pltpu.make_async_copy(state.at[:, own, :], state_hbm, sems.at[0]),
        pltpu.make_async_copy(gsource, gsource_hbm, sems.at[1]),
        pltpu.make_async_copy(grad, grad_hbm, sems.at[2]),
    ]
    moves[0].start()
    for n in range(STEPS - 1, 0, -1):
        for row in places(2 * STEPS - 1 - n):
            s.backward(n, row)
    for row in places(DEPTH - 1):
        for k, value in s.source_gradient(row):
            gsource[k, pl.ds(row - HALO, TILE), :] = value
    moves[1].start()
    for row in places(DEPTH - 1):
        for k, value in s.gradient(row):
            grad[k, pl.ds(row - HALO, TILE), :] = value
    moves[2].start()
    for move in moves:
        move.wait()


def swaps(count, offset, wrap):
    pairs = []
    for i in range(offset, count, 2):
        j = i + 1
        if j < count or wrap:
            pairs += [(i, j % count), (j % count, i)]
    paired = {i for i, _ in pairs}
    return pairs + [(i, i) for i in range(count) if i not in paired]


def body(initial_state, source, cotangent, face_coefs, land_mask, bottom):
    arguments = (initial_state, source, cotangent, face_coefs, land_mask, bottom)
    levels, rows, lanes = initial_state.shape
    c = Names(levels)
    span = rows + 2 * HALO
    strips = len(strip_tiles(c, rows // TILE))
    f32 = lambda *shape: jax.ShapeDtypeStruct(shape, jnp.float32)
    vmem, hbm = pl.BlockSpec(memory_space=pltpu.VMEM), pl.BlockSpec(memory_space=pltpu.HBM)
    params = pltpu.CompilerParams(vmem_limit_bytes=8 * 1024 * 1024)

    fields, one, two, lat_one = pl.pallas_call(
        functools.partial(pack_kernel, c),
        out_shape=(f32(c.count, rows, lanes), *(f32(strips, TILE, lanes),) * 2, f32(c.main, TILE, lanes)),
        in_specs=[hbm] * 6,
        out_specs=(vmem,) * 4,
        scratch_shapes=[
            pltpu.VMEM((levels, rows, lanes), jnp.float32),
            pltpu.VMEM((levels, rows, lanes), jnp.float32),
            pltpu.VMEM((2, rows, lanes), jnp.float32),
            pltpu.VMEM((levels, rows, lanes), jnp.int32),
            pltpu.VMEM((rows, lanes), jnp.int32),
            pltpu.SemaphoreType.DMA((6,)),
        ],
        compiler_params=params,
        name="pack",
    )(*(pltpu.with_memory_space_constraint(x, pltpu.HBM) for x in arguments))
    lon, lat = lax.axis_size("lon"), lax.axis_size("lat")
    one = lax.ppermute(one, "lon", swaps(lon, 0, True))
    two = lax.ppermute(two, "lon", swaps(lon, 1, True))
    lat_one = lax.ppermute(lat_one, "lat", swaps(lat, 0, False))
    corner, lat_two = pl.pallas_call(
        functools.partial(lat_kernel, c),
        out_shape=(f32(c.strips, TILE, lanes), f32(c.main + c.strips, TILE, lanes)),
        in_specs=[vmem] * 4,
        out_specs=(vmem,) * 2,
        compiler_params=params,
        name="lat_rows",
    )(fields, one, two, lat_one)
    lat_two = lax.ppermute(lat_two, "lat", swaps(lat, 1, False))
    corner = lax.ppermute(corner, "lat", swaps(lat, 0, False))
    twice = lambda *shape: (f32(*shape), f32(*shape))
    shapes = (
        *twice(c.count, span, lanes),
        *twice(span, lanes),
        *twice(levels, span, lanes),
        *twice((2 * STEPS - 1) * levels, span, lanes),
        *twice((STEPS - 1) * levels, span, lanes),
        f32((STEPS - 1) * levels, span, lanes),
        f32(levels, span, lanes),
        f32(levels, rows, lanes),
        f32(levels, rows, lanes),
    )
    own = pl.pallas_call(
        functools.partial(own_kernel, c),
        out_shape=shapes,
        in_specs=[vmem] * 4,
        out_specs=(vmem,) * len(shapes),
        compiler_params=params,
        cost_estimate=pl.CostEstimate(
            flops=2 * STEPS * levels * rows * lanes * 40, bytes_accessed=16 * 2**20, transcendentals=0
        ),
        name="own_rows",
    )(fields, one, two, lat_one)
    out = pl.pallas_call(
        functools.partial(edge_kernel, c),
        out_shape=(*shapes, *(f32(levels, rows, lanes),) * 3),
        in_specs=[vmem] * (2 + len(shapes)),
        out_specs=(*(vmem,) * len(shapes), hbm, hbm, hbm),
        input_output_aliases={2 + i: i for i in range(len(shapes))},
        scratch_shapes=[pltpu.SemaphoreType.DMA((3,))],
        compiler_params=params,
        name="edge_rows",
    )(corner, lat_two, *own)
    return tuple(out[len(shapes) :])


def solution(mesh):
    block = P(None, "lat", "lon")
    return jax.shard_map(
        body,
        mesh=mesh,
        in_specs=(block, block, block, block, block, P("lat", "lon")),
        out_specs=(block, block, block),
        check_vma=False,
    )
```

```python
import functools

import jax
import jax.numpy as jnp
from jax import lax
from jax.experimental import pallas as pl
from jax.experimental.pallas import tpu as pltpu
from jax.sharding import PartitionSpec as P

STEPS = 4
DEPTH = 2 * STEPS
TILE = 8
HALO = TILE

vertical_coef = 0.04


class Names:
    def __init__(self, levels):
        self.levels = levels
        self.u, self.s, self.wet = 0, levels, 2 * levels
        self.ce, self.cn, self.cot = 3 * levels, 3 * levels + 1, 3 * levels + 2
        self.count = 4 * levels + 2
        self.paired = -(-levels // 2)
        self.main = self.cot + self.paired
        assert 16 < self.main <= 24
        self.strips = 3


def lane_iota(lanes):
    return lax.broadcasted_iota(jnp.int32, (TILE, lanes), 1)


def shift_of(place):
    return 2 * DEPTH * (place % 8) + DEPTH * (place // 8)


def strip_tiles(c, tiles):
    folded = -(-tiles // 2)
    whole = [[(channel, t) for channel in range(16)] for t in range(tiles)]
    shared = [
        {p + 8 * half: (16 + p, t + half * folded) for half in (0, 1) if t + half * folded < tiles for p in range(c.main - 16)}
        for t in range(folded)
    ]
    return [dict(enumerate(places)) for places in whole] + shared


def even_groups(lanes):
    return lax.rem(lane_iota(lanes) // DEPTH, 2) == 0


def is_odd(axis):
    return lax.rem(lax.axis_index(axis), 2) == 1


def fill_rows(c, f_ref, ref, high):
    rows = f_ref.shape[1]
    at = pl.ds(rows - TILE if high else 0, TILE)
    for channel in range(c.cot):
        ref[channel] = f_ref[channel, at, :]
    row = lax.broadcasted_iota(jnp.int32, (TILE, f_ref.shape[2]), 0)
    half = TILE // 2
    for q in range(c.paired):
        one = f_ref[c.cot + 2 * q, at, :]
        two = f_ref[c.cot + min(2 * q + 1, c.levels - 1), at, :]
        if high:
            one = pltpu.roll(one, half, 0)
        else:
            two = pltpu.roll(two, half, 0)
        ref[c.cot + q] = jnp.where(row < half, one, two)


def pack_kernel(
    c, u_hbm, s_hbm, a_hbm, c_hbm, land_hbm, bottom_hbm, f_ref, first_ref, second_ref, north_ref, south_ref,
    u_ref, s_ref, c_ref, land_ref, bottom_ref, sems,
):
    levels = c.levels
    _, rows, lanes = u_ref.shape
    moves = [
        pltpu.make_async_copy(source, target, sems.at[i])
        for i, (source, target) in enumerate(
            (
                (bottom_hbm, bottom_ref),
                (land_hbm, land_ref),
                (u_hbm, u_ref),
                (s_hbm, s_ref),
                (c_hbm, c_ref),
                (a_hbm, f_ref.at[pl.ds(c.cot, levels)]),
            )
        )
    ]
    for move in moves:
        move.start()
    for move in moves:
        move.wait()
    last_lat = lax.axis_index("lat") == lax.axis_size("lat") - 1
    for k in range(levels):
        wet = jnp.where(k < bottom_ref[...], land_ref[k], 0).astype(jnp.float32)
        f_ref[c.u + k] = wet * u_ref[k]
        f_ref[c.s + k] = wet * s_ref[k]
        f_ref[c.wet + k] = wet
    f_ref[c.ce] = c_ref[0]
    row = lax.broadcasted_iota(jnp.int32, (rows, lanes), 0)
    f_ref[c.cn] = jnp.where(jnp.logical_and(last_lat, row == rows - 1), 0.0, c_ref[1])
    odd = is_odd("lon")
    lane = lane_iota(lanes)
    group, groups = lane // DEPTH, lanes // DEPTH
    half = DEPTH // 2

    def columns(channel, t):
        at = pl.ds(t * TILE, TILE)
        if channel < c.cot:
            return f_ref[channel, at, :]
        first = c.cot + 2 * (channel - c.cot)
        one, two = f_ref[first, at, :], f_ref[min(first + 1, c.count - 1), at, :]
        moved = jnp.where(lane < lanes // 2, pltpu.roll(two, half, 1), pltpu.roll(two, lanes - half, 1))
        return jnp.where(jnp.logical_or(lane < half, lane >= lanes - half), one, moved)

    for i, places in enumerate(strip_tiles(c, rows // TILE)):
        east = jnp.zeros((TILE, lanes), jnp.float32)
        west = east
        for place, (channel, t) in places.items():
            shift = shift_of(place)
            tile = columns(channel, t)
            if shift:
                tile = pltpu.roll(tile, shift, 1)
            east = jnp.where(group == shift // DEPTH, tile, east)
            west = jnp.where(group == (shift // DEPTH - 1) % groups, tile, west)
        first_ref[i] = jnp.where(odd, east, west)
        second_ref[i] = jnp.where(odd, west, east)
    fill_rows(c, f_ref, north_ref, True)
    fill_rows(c, f_ref, south_ref, False)


def corner_kernel(c, rows, one_ref, two_ref, north_ref, south_ref):
    odd_lon = is_odd("lon")
    lanes = one_ref.shape[-1]
    tiles = rows // TILE
    folded = -(-tiles // 2)
    even_group = even_groups(lanes)

    def pair(i):
        one, two = one_ref[i], two_ref[i]
        return jnp.where(odd_lon, two, one), jnp.where(odd_lon, one, two)

    for ref, t in ((north_ref, tiles - 1), (south_ref, 0)):
        ref[0], ref[1] = pair(t)
        east, west = pair(tiles + t % folded)
        if t < folded:
            ref[2] = jnp.where(even_group, east, west)
        else:
            ref[2] = pltpu.roll(jnp.where(even_group, west, east), lanes - DEPTH, 1)


class Sweeps:
    def __init__(self, c, e, w, d, x, m, adj, state):
        self.c, self.e, self.w, self.d, self.x, self.m, self.adj, self.state = c, e, w, d, x, m, adj, state
        self.lanes = e[0].shape[-1]
        lane = lane_iota(self.lanes)
        self.at_first, self.at_last = lane == 0, lane == self.lanes - 1
        self.left = lane < self.lanes // 2
        self.even_group = even_groups(self.lanes)

    def from_west(self, x0, x1):
        r0, r1 = pltpu.roll(x0, 1, 1), pltpu.roll(x1, 1, 1)
        return jnp.where(self.at_first, r1, r0), jnp.where(self.at_first, r0, r1)

    def from_east(self, x0, x1):
        r0, r1 = pltpu.roll(x0, self.lanes - 1, 1), pltpu.roll(x1, self.lanes - 1, 1)
        return jnp.where(self.at_last, r1, r0), jnp.where(self.at_last, r0, r1)

    def mixed(self, east, west):
        return jnp.where(self.even_group, east, west), jnp.where(self.even_group, west, east)

    def spread(self, row, channel, tile, shift):
        c, at = self.c, pl.ds(row, TILE)
        if shift:
            tile = pltpu.roll(tile, self.lanes - shift, 1)
        if channel < c.cot:
            self.e[1][channel, at, :] = tile
            return
        first, half = c.cot + 2 * (channel - c.cot), DEPTH // 2
        self.e[1][first, at, :] = tile
        if first + 1 < c.count:
            moved = jnp.where(self.left, pltpu.roll(tile, self.lanes - half, 1), pltpu.roll(tile, half, 1))
            self.e[1][first + 1, at, :] = moved

    def western(self, row):
        at = pl.ds(row, TILE)
        self.w[0][at, :], self.w[1][at, :] = self.from_west(self.e[0][self.c.ce, at, :], self.e[1][self.c.ce, at, :])

    def neighbours(self, load, row, halves=2):
        c, at = self.c, pl.ds(row, TILE)
        ce = [e[c.ce, at, :] for e in self.e]
        cw = [w[at, :] for w in self.w]
        cn = [e[c.cn, at, :] for e in self.e]
        cs = [e[c.cn, pl.ds(row - 1, TILE), :] for e in self.e]
        own = [(load(0, k, at), load(1, k, at)) for k in range(c.levels)]
        out = []
        for k in range(c.levels):
            east, west = self.from_east(*own[k]), self.from_west(*own[k])
            pair = []
            for h in range(halves):
                north, south = load(h, k, pl.ds(row + 1, TILE)), load(h, k, pl.ds(row - 1, TILE))
                total = (ce[h] * east[h] + cw[h] * west[h]) + (cn[h] * north + cs[h] * south)
                around = [own[j][h] for j in (k - 1, k + 1) if 0 <= j < c.levels]
                pair.append((own[k][h], total + vertical_coef * functools.reduce(jnp.add, around)))
            out.append(pair)
        return out

    def diagonal(self, row):
        load = lambda h, k, at: self.e[h][self.c.wet + k, at, :]
        for k, pair in enumerate(self.neighbours(load, row)):
            for h, (_, total) in enumerate(pair):
                self.d[h][k, pl.ds(row, TILE), :] = 1.0 - total

    def loader(self, index):
        if index == 0:
            return lambda h, k, at: self.e[h][self.c.u + k, at, :]
        base = (index - 1) * self.c.levels
        return lambda h, k, at: self.x[h][base + k, at, :]

    def forward(self, n, row):
        c, at = self.c, pl.ds(row, TILE)
        for k, pair in enumerate(self.neighbours(self.loader(n), row)):
            for h, (own, total) in enumerate(pair):
                e = self.e[h]
                wet = e[c.wet + k, at, :]
                bounded = wet * jnp.tanh(self.d[h][k, at, :] * own + total)
                slope = wet - bounded * bounded
                if n < STEPS - 1:
                    self.x[h][n * c.levels + k, at, :] = bounded + e[c.s + k, at, :]
                    self.m[h][n * c.levels + k, at, :] = slope
                else:
                    if h == 0:
                        self.state[k, at, :] = bounded + e[c.s + k, at, :]
                    self.x[h][n * c.levels + k, at, :] = slope * e[c.cot + k, at, :]

    def backward(self, n, row):
        c, at = self.c, pl.ds(row, TILE)
        index = 2 * STEPS - 1 - n
        for k, pair in enumerate(self.neighbours(self.loader(index), row)):
            for h, (own, total) in enumerate(pair):
                value = self.d[h][k, at, :] * own + total
                if h == 0:
                    self.adj[(n - 1) * c.levels + k, at, :] = value
                self.x[h][index * c.levels + k, at, :] = self.m[h][(n - 1) * c.levels + k, at, :] * value

    def gradient(self, row):
        c, at = self.c, pl.ds(row, TILE)
        for k, pair in enumerate(self.neighbours(self.loader(2 * STEPS - 1), row, 1)):
            own, total = pair[0]
            yield k, self.e[0][c.wet + k, at, :] * (self.d[0][k, at, :] * own + total)

    def source_gradient(self, row):
        c, at = self.c, pl.ds(row, TILE)
        for k in range(c.levels):
            total = self.e[0][c.cot + k, at, :]
            for n in range(STEPS - 1):
                total = total + self.adj[n * c.levels + k, at, :]
            yield k, self.e[0][c.wet + k, at, :] * total


def fill_halo(c, e0, ref, row, low):
    to = pl.ds(row, TILE)
    for channel in range(c.cot):
        e0[channel, to, :] = ref[channel]
    for k in range(c.levels):
        tile = ref[c.cot + k // 2]
        if (k % 2 == 0) == low:
            tile = pltpu.roll(tile, TILE // 2, 0)
        e0[c.cot + k, to, :] = tile


def own_kernel(c, f_ref, one_ref, two_ref, e0, e1, w0, w1, d0, d1, x0, x1, m0, m1, adj, state, grad, gsource):
    rows = f_ref.shape[1]
    odd_lon = is_odd("lon")
    s = Sweeps(c, (e0, e1), (w0, w1), (d0, d1), (x0, x1), (m0, m1), adj, state)
    zero = jnp.zeros((TILE, f_ref.shape[2]), jnp.float32)
    for ref in (e0, e1):
        for end in (pl.ds(0, TILE), pl.ds(HALO + rows, TILE)):
            for channel in (*range(c.u, c.u + c.levels), *range(c.wet, c.wet + c.levels), c.cn):
                ref[channel, end, :] = zero
    tiles = rows // TILE
    places = [HALO + t * TILE for t in range(tiles)]
    held = strip_tiles(c, tiles)
    for t, row in enumerate(places):
        at, to = pl.ds(t * TILE, TILE), pl.ds(row, TILE)
        for channel in range(c.count):
            e0[channel, to, :] = f_ref[channel, at, :]
        for i in (t, tiles + t % (len(held) - tiles)):
            one, two = one_ref[i], two_ref[i]
            both = s.mixed(jnp.where(odd_lon, two, one), jnp.where(odd_lon, one, two))
            for place, (channel, of) in held[i].items():
                if of == t:
                    s.spread(row, channel, both[place // 8], shift_of(place))
        s.western(row)
    for row in places:
        s.diagonal(row)
    for n in range(STEPS):
        for row in places:
            s.forward(n, row)
    for n in range(STEPS - 1, 0, -1):
        for row in places:
            s.backward(n, row)
    for row in places[1:-1]:
        at = pl.ds(row - HALO, TILE)
        for k, value in s.source_gradient(row):
            gsource[k, at, :] = value
        for k, value in s.gradient(row):
            grad[k, at, :] = value


def edge_kernel(
    c, low_ref, high_ref, low_strips, high_strips, *refs,
):
    aliased = refs[: len(refs) // 2]
    del aliased
    e0, e1, w0, w1, d0, d1, x0, x1, m0, m1, adj, state, grad, gsource, state_hbm, grad_hbm, gsource_hbm, sems = refs[14:]
    rows = grad.shape[1]
    s = Sweeps(c, (e0, e1), (w0, w1), (d0, d1), (x0, x1), (m0, m1), adj, state)
    for row, ref, strips, low in ((0, low_ref, low_strips, True), (HALO + rows, high_ref, high_strips, False)):
        fill_halo(c, e0, ref, row, low)
        both = s.mixed(strips[0], strips[1])
        for channel in range(c.main):
            place = channel % 16
            s.spread(row, channel, both[place // 8] if channel < 16 else strips[2], shift_of(place))
        s.western(row)
    top = lambda i: HALO + i - (DEPTH - 1)
    bottom = lambda i: HALO + rows - 1 - i
    places = lambda i: (top(i), bottom(i))
    for row in places(0):
        s.diagonal(row)
    for n in range(STEPS):
        for row in places(n):
            s.forward(n, row)
    own = pl.ds(HALO, rows)
    moves = [
        pltpu.make_async_copy(state.at[:, own, :], state_hbm, sems.at[0]),
        pltpu.make_async_copy(gsource, gsource_hbm, sems.at[1]),
        pltpu.make_async_copy(grad, grad_hbm, sems.at[2]),
    ]
    moves[0].start()
    for n in range(STEPS - 1, 0, -1):
        for row in places(2 * STEPS - 1 - n):
            s.backward(n, row)
    for row in places(DEPTH - 1):
        for k, value in s.source_gradient(row):
            gsource[k, pl.ds(row - HALO, TILE), :] = value
    moves[1].start()
    for row in places(DEPTH - 1):
        for k, value in s.gradient(row):
            grad[k, pl.ds(row - HALO, TILE), :] = value
    moves[2].start()
    for move in moves:
        move.wait()


def swaps(count, offset):
    pairs = [(i, (i + 1) % count) for i in range(offset, count, 2)]
    return pairs + [(j, i) for i, j in pairs]


def body(initial_state, source, cotangent, face_coefs, land_mask, bottom):
    arguments = (initial_state, source, cotangent, face_coefs, land_mask, bottom)
    levels, rows, lanes = initial_state.shape
    c = Names(levels)
    span = rows + 2 * HALO
    strips = len(strip_tiles(c, rows // TILE))
    f32 = lambda *shape: jax.ShapeDtypeStruct(shape, jnp.float32)
    vmem, hbm = pl.BlockSpec(memory_space=pltpu.VMEM), pl.BlockSpec(memory_space=pltpu.HBM)
    params = pltpu.CompilerParams(vmem_limit_bytes=8 * 1024 * 1024)

    fields, one, two, north, south = pl.pallas_call(
        functools.partial(pack_kernel, c),
        out_shape=(f32(c.count, rows, lanes), *(f32(strips, TILE, lanes),) * 2, *(f32(c.main, TILE, lanes),) * 2),
        in_specs=[hbm] * 6,
        out_specs=(vmem,) * 5,
        scratch_shapes=[
            pltpu.VMEM((levels, rows, lanes), jnp.float32),
            pltpu.VMEM((levels, rows, lanes), jnp.float32),
            pltpu.VMEM((2, rows, lanes), jnp.float32),
            pltpu.VMEM((levels, rows, lanes), jnp.int32),
            pltpu.VMEM((rows, lanes), jnp.int32),
            pltpu.SemaphoreType.DMA((6,)),
        ],
        compiler_params=params,
        name="pack",
    )(*(pltpu.with_memory_space_constraint(x, pltpu.HBM) for x in arguments))
    lon, lat = lax.axis_size("lon"), lax.axis_size("lat")
    one = lax.ppermute(one, "lon", swaps(lon, 0))
    two = lax.ppermute(two, "lon", swaps(lon, 1))
    to_north = [(i, i + 1) for i in range(lat - 1)]
    to_south = [(j, i) for i, j in to_north]
    low, high = lax.ppermute(north, "lat", to_north), lax.ppermute(south, "lat", to_south)
    north, south = pl.pallas_call(
        functools.partial(corner_kernel, c, rows),
        out_shape=(f32(c.strips, TILE, lanes),) * 2,
        in_specs=[vmem] * 2,
        out_specs=(vmem,) * 2,
        compiler_params=params,
        name="corners",
    )(one, two)
    low_strips, high_strips = lax.ppermute(north, "lat", to_north), lax.ppermute(south, "lat", to_south)
    twice = lambda *shape: (f32(*shape), f32(*shape))
    shapes = (
        *twice(c.count, span, lanes),
        *twice(span, lanes),
        *twice(levels, span, lanes),
        *twice((2 * STEPS - 1) * levels, span, lanes),
        *twice((STEPS - 1) * levels, span, lanes),
        f32((STEPS - 1) * levels, span, lanes),
        f32(levels, span, lanes),
        f32(levels, rows, lanes),
        f32(levels, rows, lanes),
    )
    own = pl.pallas_call(
        functools.partial(own_kernel, c),
        out_shape=shapes,
        in_specs=[vmem] * 3,
        out_specs=(vmem,) * len(shapes),
        compiler_params=params,
        cost_estimate=pl.CostEstimate(
            flops=2 * STEPS * levels * rows * lanes * 40, bytes_accessed=16 * 2**20, transcendentals=0
        ),
        name="own_rows",
    )(fields, one, two)
    out = pl.pallas_call(
        functools.partial(edge_kernel, c),
        out_shape=(*shapes, *(f32(levels, rows, lanes),) * 3),
        in_specs=[vmem] * (4 + len(shapes)),
        out_specs=(*(vmem,) * len(shapes), hbm, hbm, hbm),
        input_output_aliases={4 + i: i for i in range(len(shapes))},
        scratch_shapes=[pltpu.SemaphoreType.DMA((3,))],
        compiler_params=params,
        name="edge_rows",
    )(low, high, low_strips, high_strips, *own)
    return tuple(out[len(shapes) :])


def solution(mesh):
    block = P(None, "lat", "lon")
    return jax.shard_map(
        body,
        mesh=mesh,
        in_specs=(block, block, block, block, block, P("lat", "lon")),
        out_specs=(block, block, block),
        check_vma=False,
    )
```

```python
import functools

import jax
import jax.numpy as jnp
from jax import lax
from jax.experimental import pallas as pl
from jax.experimental.pallas import tpu as pltpu
from jax.sharding import PartitionSpec as P

STEPS = 4
DEPTH = 2 * STEPS
TILE = 8
HALO = TILE

vertical_coef = 0.04


class Names:
    def __init__(self, levels):
        self.levels = levels
        self.u, self.s, self.wet = 0, levels, 2 * levels
        self.ce, self.cn, self.cot = 3 * levels, 3 * levels + 1, 3 * levels + 2
        self.count = 4 * levels + 2
        self.parts = -(-self.count // 16)
        self.strips = 2 * self.parts
        self.second = self.strips + -(-levels // 2)


def lane_iota(lanes):
    return lax.broadcasted_iota(jnp.int32, (TILE, lanes), 1)


def shift_of(channel):
    place = channel % 16
    return 2 * DEPTH * (place % 8) + DEPTH * (place // 8)


def even_groups(lanes):
    return lax.rem(lane_iota(lanes) // DEPTH, 2) == 0


def is_odd(axis):
    return lax.rem(lax.axis_index(axis), 2) == 1


def strip_rows(c, m):
    return range(16 * m, min(16 * m + 16, c.count))


def pack_kernel(
    c, u_hbm, s_hbm, a_hbm, c_hbm, land_hbm, bottom_hbm, f_ref, first_ref, second_ref, north_ref, south_ref,
    u_ref, s_ref, c_ref, land_ref, bottom_ref, sems,
):
    levels = c.levels
    _, rows, lanes = u_ref.shape
    moves = [
        pltpu.make_async_copy(source, target, sems.at[i])
        for i, (source, target) in enumerate(
            (
                (bottom_hbm, bottom_ref),
                (land_hbm, land_ref),
                (u_hbm, u_ref),
                (s_hbm, s_ref),
                (c_hbm, c_ref),
                (a_hbm, f_ref.at[pl.ds(c.cot, levels)]),
            )
        )
    ]
    for move in moves:
        move.start()
    for move in moves:
        move.wait()
    last_lat = lax.axis_index("lat") == lax.axis_size("lat") - 1
    for k in range(levels):
        wet = jnp.where(k < bottom_ref[...], land_ref[k], 0).astype(jnp.float32)
        f_ref[c.u + k] = wet * u_ref[k]
        f_ref[c.s + k] = wet * s_ref[k]
        f_ref[c.wet + k] = wet
    f_ref[c.ce] = c_ref[0]
    row = lax.broadcasted_iota(jnp.int32, (rows, lanes), 0)
    f_ref[c.cn] = jnp.where(jnp.logical_and(last_lat, row == rows - 1), 0.0, c_ref[1])
    odd = is_odd("lon")
    group, groups = lane_iota(lanes) // DEPTH, lanes // DEPTH
    for t in range(rows // TILE):
        at = pl.ds(t * TILE, TILE)
        for m in range(c.parts):
            east = jnp.zeros((TILE, lanes), jnp.float32)
            west = east
            for channel in strip_rows(c, m):
                shift = shift_of(channel)
                tile = f_ref[channel, at, :]
                if shift:
                    tile = pltpu.roll(tile, shift, 1)
                east = jnp.where(group == shift // DEPTH, tile, east)
                west = jnp.where(group == (shift // DEPTH - 1) % groups, tile, west)
            first_ref[m, at, :] = jnp.where(odd, east, west)
            second_ref[m, at, :] = jnp.where(odd, west, east)
    for channel in range(c.cot):
        north_ref[channel] = f_ref[channel, pl.ds(rows - TILE, TILE), :]
        south_ref[channel] = f_ref[channel, pl.ds(0, TILE), :]


def corner_kernel(c, f_ref, one_ref, two_ref, north_ref, south_ref):
    odd_lon = is_odd("lon")
    _, rows, lanes = f_ref.shape
    half = TILE // 2
    first_half = lax.broadcasted_iota(jnp.int32, (TILE, lanes), 0) < half
    for ref, high in ((north_ref, True), (south_ref, False)):
        at = pl.ds(rows - TILE if high else 0, TILE)
        for m in range(c.parts):
            one, two = one_ref[m, at, :], two_ref[m, at, :]
            ref[m] = jnp.where(odd_lon, two, one)
            ref[c.parts + m] = jnp.where(odd_lon, one, two)
        for q in range(c.second - c.strips):
            one = f_ref[c.cot + 2 * q, at, :]
            two = f_ref[c.cot + min(2 * q + 1, c.levels - 1), at, :]
            if high:
                one = pltpu.roll(one, half, 0)
            else:
                two = pltpu.roll(two, half, 0)
            ref[c.strips + q] = jnp.where(first_half, one, two)


class Sweeps:
    def __init__(self, c, e, w, d, x, m, adj, state):
        self.c, self.e, self.w, self.d, self.x, self.m, self.adj, self.state = c, e, w, d, x, m, adj, state
        self.lanes = e[0].shape[-1]
        lane = lane_iota(self.lanes)
        self.at_first, self.at_last = lane == 0, lane == self.lanes - 1
        self.even_group = even_groups(self.lanes)

    def from_west(self, x0, x1):
        r0, r1 = pltpu.roll(x0, 1, 1), pltpu.roll(x1, 1, 1)
        return jnp.where(self.at_first, r1, r0), jnp.where(self.at_first, r0, r1)

    def from_east(self, x0, x1):
        r0, r1 = pltpu.roll(x0, self.lanes - 1, 1), pltpu.roll(x1, self.lanes - 1, 1)
        return jnp.where(self.at_last, r1, r0), jnp.where(self.at_last, r0, r1)

    def spread(self, row, easts, wests):
        for m, (east, west) in enumerate(zip(easts, wests)):
            both = jnp.where(self.even_group, east, west), jnp.where(self.even_group, west, east)
            for channel in strip_rows(self.c, m):
                shift = shift_of(channel)
                tile = both[(channel % 16) // 8]
                if shift:
                    tile = pltpu.roll(tile, self.lanes - shift, 1)
                self.e[1][channel, pl.ds(row, TILE), :] = tile

    def western(self, row):
        at = pl.ds(row, TILE)
        self.w[0][at, :], self.w[1][at, :] = self.from_west(self.e[0][self.c.ce, at, :], self.e[1][self.c.ce, at, :])

    def neighbours(self, load, row, halves=2):
        c, at = self.c, pl.ds(row, TILE)
        ce = [e[c.ce, at, :] for e in self.e]
        cw = [w[at, :] for w in self.w]
        cn = [e[c.cn, at, :] for e in self.e]
        cs = [e[c.cn, pl.ds(row - 1, TILE), :] for e in self.e]
        own = [(load(0, k, at), load(1, k, at)) for k in range(c.levels)]
        out = []
        for k in range(c.levels):
            east, west = self.from_east(*own[k]), self.from_west(*own[k])
            pair = []
            for h in range(halves):
                north, south = load(h, k, pl.ds(row + 1, TILE)), load(h, k, pl.ds(row - 1, TILE))
                total = (ce[h] * east[h] + cw[h] * west[h]) + (cn[h] * north + cs[h] * south)
                around = [own[j][h] for j in (k - 1, k + 1) if 0 <= j < c.levels]
                pair.append((own[k][h], total + vertical_coef * functools.reduce(jnp.add, around)))
            out.append(pair)
        return out

    def diagonal(self, row):
        load = lambda h, k, at: self.e[h][self.c.wet + k, at, :]
        for k, pair in enumerate(self.neighbours(load, row)):
            for h, (_, total) in enumerate(pair):
                self.d[h][k, pl.ds(row, TILE), :] = 1.0 - total

    def loader(self, index):
        if index == 0:
            return lambda h, k, at: self.e[h][self.c.u + k, at, :]
        base = (index - 1) * self.c.levels
        return lambda h, k, at: self.x[h][base + k, at, :]

    def forward(self, n, row):
        c, at = self.c, pl.ds(row, TILE)
        for k, pair in enumerate(self.neighbours(self.loader(n), row)):
            for h, (own, total) in enumerate(pair):
                e = self.e[h]
                wet = e[c.wet + k, at, :]
                bounded = wet * jnp.tanh(self.d[h][k, at, :] * own + total)
                slope = wet - bounded * bounded
                if n < STEPS - 1:
                    self.x[h][n * c.levels + k, at, :] = bounded + e[c.s + k, at, :]
                    self.m[h][n * c.levels + k, at, :] = slope
                else:
                    if h == 0:
                        self.state[k, at, :] = bounded + e[c.s + k, at, :]
                    self.x[h][n * c.levels + k, at, :] = slope * e[c.cot + k, at, :]

    def backward(self, n, row):
        c, at = self.c, pl.ds(row, TILE)
        index = 2 * STEPS - 1 - n
        for k, pair in enumerate(self.neighbours(self.loader(index), row)):
            for h, (own, total) in enumerate(pair):
                value = self.d[h][k, at, :] * own + total
                if h == 0:
                    self.adj[(n - 1) * c.levels + k, at, :] = value
                self.x[h][index * c.levels + k, at, :] = self.m[h][(n - 1) * c.levels + k, at, :] * value

    def gradient(self, row):
        c, at = self.c, pl.ds(row, TILE)
        for k, pair in enumerate(self.neighbours(self.loader(2 * STEPS - 1), row, 1)):
            own, total = pair[0]
            yield k, self.e[0][c.wet + k, at, :] * (self.d[0][k, at, :] * own + total)

    def source_gradient(self, row):
        c, at = self.c, pl.ds(row, TILE)
        for k in range(c.levels):
            total = self.e[0][c.cot + k, at, :]
            for n in range(STEPS - 1):
                total = total + self.adj[n * c.levels + k, at, :]
            yield k, self.e[0][c.wet + k, at, :] * total


def own_kernel(c, f_ref, one_ref, two_ref, e0, e1, w0, w1, d0, d1, x0, x1, m0, m1, adj, state, grad, gsource):
    rows = f_ref.shape[1]
    odd_lon = is_odd("lon")
    s = Sweeps(c, (e0, e1), (w0, w1), (d0, d1), (x0, x1), (m0, m1), adj, state)
    zero = jnp.zeros((TILE, f_ref.shape[2]), jnp.float32)
    for ref in (e0, e1):
        for end in (pl.ds(0, TILE), pl.ds(HALO + rows, TILE)):
            for channel in (*range(c.u, c.u + c.levels), *range(c.wet, c.wet + c.levels), c.cn):
                ref[channel, end, :] = zero
    tiles = rows // TILE
    places = [HALO + t * TILE for t in range(tiles)]
    for t, row in enumerate(places):
        at, to = pl.ds(t * TILE, TILE), pl.ds(row, TILE)
        for channel in range(c.count):
            e0[channel, to, :] = f_ref[channel, at, :]
        pairs = [(one_ref[m, at, :], two_ref[m, at, :]) for m in range(c.parts)]
        s.spread(
            row,
            [jnp.where(odd_lon, two, one) for one, two in pairs],
            [jnp.where(odd_lon, one, two) for one, two in pairs],
        )
        s.western(row)
    for row in places:
        s.diagonal(row)
    for n in range(STEPS):
        for row in places:
            s.forward(n, row)
    for n in range(STEPS - 1, 0, -1):
        for row in places:
            s.backward(n, row)
    for row in places[1:-1]:
        at = pl.ds(row - HALO, TILE)
        for k, value in s.source_gradient(row):
            gsource[k, at, :] = value
        for k, value in s.gradient(row):
            grad[k, at, :] = value


def edge_kernel(
    c, low_ref, high_ref, low_second, high_second, *refs,
):
    aliased = refs[: len(refs) // 2]
    del aliased
    e0, e1, w0, w1, d0, d1, x0, x1, m0, m1, adj, state, grad, gsource, state_hbm, grad_hbm, gsource_hbm, sems = refs[14:]
    rows = grad.shape[1]
    s = Sweeps(c, (e0, e1), (w0, w1), (d0, d1), (x0, x1), (m0, m1), adj, state)
    for row, ref, second, low in ((0, low_ref, low_second, True), (HALO + rows, high_ref, high_second, False)):
        pole = lax.axis_index("lat") == (0 if low else lax.axis_size("lat") - 1)

        def got(tile):
            return jnp.where(pole, 0.0, tile)

        to = pl.ds(row, TILE)
        for channel in range(c.cot):
            e0[channel, to, :] = got(ref[channel])
        for k in range(c.levels):
            tile = got(second[c.strips + k // 2])
            if (k % 2 == 0) == low:
                tile = pltpu.roll(tile, TILE // 2, 0)
            e0[c.cot + k, to, :] = tile
        strips = [got(second[i]) for i in range(c.strips)]
        s.spread(row, strips[: c.parts], strips[c.parts :])
        s.western(row)
    top = lambda i: HALO + i - (DEPTH - 1)
    bottom = lambda i: HALO + rows - 1 - i
    places = lambda i: (top(i), bottom(i))
    for row in places(0):
        s.diagonal(row)
    for n in range(STEPS):
        for row in places(n):
            s.forward(n, row)
    own = pl.ds(HALO, rows)
    moves = [
        pltpu.make_async_copy(state.at[:, own, :], state_hbm, sems.at[0]),
        pltpu.make_async_copy(gsource, gsource_hbm, sems.at[1]),
        pltpu.make_async_copy(grad, grad_hbm, sems.at[2]),
    ]
    moves[0].start()
    for n in range(STEPS - 1, 0, -1):
        for row in places(2 * STEPS - 1 - n):
            s.backward(n, row)
    for row in places(DEPTH - 1):
        for k, value in s.source_gradient(row):
            gsource[k, pl.ds(row - HALO, TILE), :] = value
    moves[1].start()
    for row in places(DEPTH - 1):
        for k, value in s.gradient(row):
            grad[k, pl.ds(row - HALO, TILE), :] = value
    moves[2].start()
    for move in moves:
        move.wait()


def swaps(count, offset):
    pairs = [(i, (i + 1) % count) for i in range(offset, count, 2)]
    return pairs + [(j, i) for i, j in pairs]


def body(initial_state, source, cotangent, face_coefs, land_mask, bottom):
    arguments = (initial_state, source, cotangent, face_coefs, land_mask, bottom)
    levels, rows, lanes = initial_state.shape
    c = Names(levels)
    span = rows + 2 * HALO
    f32 = lambda *shape: jax.ShapeDtypeStruct(shape, jnp.float32)
    vmem, hbm = pl.BlockSpec(memory_space=pltpu.VMEM), pl.BlockSpec(memory_space=pltpu.HBM)
    params = pltpu.CompilerParams(vmem_limit_bytes=8 * 1024 * 1024)

    fields, one, two, north, south = pl.pallas_call(
        functools.partial(pack_kernel, c),
        out_shape=(f32(c.count, rows, lanes), *(f32(c.parts, rows, lanes),) * 2, *(f32(c.cot, TILE, lanes),) * 2),
        in_specs=[hbm] * 6,
        out_specs=(vmem,) * 5,
        scratch_shapes=[
            pltpu.VMEM((levels, rows, lanes), jnp.float32),
            pltpu.VMEM((levels, rows, lanes), jnp.float32),
            pltpu.VMEM((2, rows, lanes), jnp.float32),
            pltpu.VMEM((levels, rows, lanes), jnp.int32),
            pltpu.VMEM((rows, lanes), jnp.int32),
            pltpu.SemaphoreType.DMA((6,)),
        ],
        compiler_params=params,
        name="pack",
    )(*(pltpu.with_memory_space_constraint(x, pltpu.HBM) for x in arguments))
    lon, lat = lax.axis_size("lon"), lax.axis_size("lat")
    one = lax.ppermute(one, "lon", swaps(lon, 0))
    two = lax.ppermute(two, "lon", swaps(lon, 1))
    to_north = [(i, (i + 1) % lat) for i in range(lat)]
    to_south = [(j, i) for i, j in to_north]
    low, high = lax.ppermute(north, "lat", to_north), lax.ppermute(south, "lat", to_south)
    north, south = pl.pallas_call(
        functools.partial(corner_kernel, c),
        out_shape=(f32(c.second, TILE, lanes),) * 2,
        in_specs=[vmem] * 3,
        out_specs=(vmem,) * 2,
        compiler_params=params,
        name="corners",
    )(fields, one, two)
    low_second, high_second = lax.ppermute(north, "lat", to_north), lax.ppermute(south, "lat", to_south)
    twice = lambda *shape: (f32(*shape), f32(*shape))
    shapes = (
        *twice(c.count, span, lanes),
        *twice(span, lanes),
        *twice(levels, span, lanes),
        *twice((2 * STEPS - 1) * levels, span, lanes),
        *twice((STEPS - 1) * levels, span, lanes),
        f32((STEPS - 1) * levels, span, lanes),
        f32(levels, span, lanes),
        f32(levels, rows, lanes),
        f32(levels, rows, lanes),
    )
    own = pl.pallas_call(
        functools.partial(own_kernel, c),
        out_shape=shapes,
        in_specs=[vmem] * 3,
        out_specs=(vmem,) * len(shapes),
        compiler_params=params,
        cost_estimate=pl.CostEstimate(
            flops=2 * STEPS * levels * rows * lanes * 40, bytes_accessed=16 * 2**20, transcendentals=0
        ),
        name="own_rows",
    )(fields, one, two)
    out = pl.pallas_call(
        functools.partial(edge_kernel, c),
        out_shape=(*shapes, *(f32(levels, rows, lanes),) * 3),
        in_specs=[vmem] * (4 + len(shapes)),
        out_specs=(*(vmem,) * len(shapes), hbm, hbm, hbm),
        input_output_aliases={4 + i: i for i in range(len(shapes))},
        scratch_shapes=[pltpu.SemaphoreType.DMA((3,))],
        compiler_params=params,
        name="edge_rows",
    )(low, high, low_second, high_second, *own)
    return tuple(out[len(shapes) :])


def solution(mesh):
    block = P(None, "lat", "lon")
    return jax.shard_map(
        body,
        mesh=mesh,
        in_specs=(block, block, block, block, block, P("lat", "lon")),
        out_specs=(block, block, block),
        check_vma=False,
    )
```

```python
import functools

import jax
import jax.numpy as jnp
from jax import lax
from jax.experimental import pallas as pl
from jax.experimental.pallas import tpu as pltpu
from jax.sharding import PartitionSpec as P

STEPS = 4
DEPTH = 2 * STEPS
TILE = 8
HALO = TILE

vertical_coef = 0.04


class Names:
    def __init__(self, levels):
        self.levels = levels
        self.u, self.s, self.wet = 0, levels, 2 * levels
        self.ce, self.cn, self.cot = 3 * levels, 3 * levels + 1, 3 * levels + 2
        self.count = 4 * levels + 2
        self.parts = -(-self.count // 16)
        self.strips = 2 * self.parts
        self.first = self.ce
        self.cot_at = self.strips + 2
        self.second = self.cot_at + -(-levels // 2)


def lane_iota(lanes):
    return lax.broadcasted_iota(jnp.int32, (TILE, lanes), 1)


def shift_of(channel):
    place = channel % 16
    return 2 * DEPTH * (place % 8) + DEPTH * (place // 8)


def even_groups(lanes):
    return lax.rem(lane_iota(lanes) // DEPTH, 2) == 0


def is_odd(axis):
    return lax.rem(lax.axis_index(axis), 2) == 1


def strip_rows(c, m):
    return range(16 * m, min(16 * m + 16, c.count))


def pack_kernel(
    c, u_hbm, s_hbm, a_hbm, c_hbm, land_hbm, bottom_hbm, f_ref, first_ref, second_ref, lat_one_ref, lat_two_ref,
    u_ref, s_ref, c_ref, land_ref, bottom_ref, sems,
):
    levels = c.levels
    _, rows, lanes = u_ref.shape
    moves = [
        pltpu.make_async_copy(source, target, sems.at[i])
        for i, (source, target) in enumerate(
            (
                (bottom_hbm, bottom_ref),
                (land_hbm, land_ref),
                (u_hbm, u_ref),
                (s_hbm, s_ref),
                (c_hbm, c_ref),
                (a_hbm, f_ref.at[pl.ds(c.cot, levels)]),
            )
        )
    ]
    for move in moves:
        move.start()
    for move in moves:
        move.wait()
    last_lat = lax.axis_index("lat") == lax.axis_size("lat") - 1
    for k in range(levels):
        wet = jnp.where(k < bottom_ref[...], land_ref[k], 0).astype(jnp.float32)
        f_ref[c.u + k] = wet * u_ref[k]
        f_ref[c.s + k] = wet * s_ref[k]
        f_ref[c.wet + k] = wet
    f_ref[c.ce] = c_ref[0]
    row = lax.broadcasted_iota(jnp.int32, (rows, lanes), 0)
    f_ref[c.cn] = jnp.where(jnp.logical_and(last_lat, row == rows - 1), 0.0, c_ref[1])
    odd = is_odd("lon")
    group, groups = lane_iota(lanes) // DEPTH, lanes // DEPTH
    for t in range(rows // TILE):
        at = pl.ds(t * TILE, TILE)
        for m in range(c.parts):
            east = jnp.zeros((TILE, lanes), jnp.float32)
            west = east
            for channel in strip_rows(c, m):
                shift = shift_of(channel)
                tile = f_ref[channel, at, :]
                if shift:
                    tile = pltpu.roll(tile, shift, 1)
                east = jnp.where(group == shift // DEPTH, tile, east)
                west = jnp.where(group == (shift // DEPTH - 1) % groups, tile, west)
            first_ref[m, at, :] = jnp.where(odd, east, west)
            second_ref[m, at, :] = jnp.where(odd, west, east)
    odd_lat = is_odd("lat")
    for channel in range(c.first):
        high, low = f_ref[channel, pl.ds(rows - TILE, TILE), :], f_ref[channel, pl.ds(0, TILE), :]
        lat_one_ref[channel] = jnp.where(odd_lat, low, high)
        lat_two_ref[channel] = jnp.where(odd_lat, high, low)


def corner_kernel(c, f_ref, one_ref, two_ref, lat_one_ref, lat_two_ref):
    odd_lat, odd_lon = is_odd("lat"), is_odd("lon")
    _, rows, lanes = f_ref.shape
    half = TILE // 2
    first_half = lax.broadcasted_iota(jnp.int32, (TILE, lanes), 0) < half
    low, high = pl.ds(0, TILE), pl.ds(rows - TILE, TILE)

    def put(i, low_tile, high_tile):
        lat_one_ref[i] = jnp.where(odd_lat, low_tile, high_tile)
        lat_two_ref[i] = jnp.where(odd_lat, high_tile, low_tile)

    for m in range(c.parts):
        ends = [(one_ref[m, at, :], two_ref[m, at, :]) for at in (low, high)]
        put(m, *(jnp.where(odd_lon, two, one) for one, two in ends))
        put(c.parts + m, *(jnp.where(odd_lon, one, two) for one, two in ends))
    put(c.strips, f_ref[c.ce, low, :], f_ref[c.ce, high, :])
    put(c.strips + 1, f_ref[c.cn, low, :], f_ref[c.cn, high, :])
    for q in range(c.second - c.cot_at):
        one, two = c.cot + 2 * q, c.cot + min(2 * q + 1, c.levels - 1)
        put(
            c.cot_at + q,
            jnp.where(first_half, f_ref[one, low, :], pltpu.roll(f_ref[two, low, :], half, 0)),
            jnp.where(first_half, pltpu.roll(f_ref[one, high, :], half, 0), f_ref[two, high, :]),
        )


class Sweeps:
    def __init__(self, c, e, w, d, x, m, adj, state):
        self.c, self.e, self.w, self.d, self.x, self.m, self.adj, self.state = c, e, w, d, x, m, adj, state
        self.lanes = e[0].shape[-1]
        lane = lane_iota(self.lanes)
        self.at_first, self.at_last = lane == 0, lane == self.lanes - 1
        self.even_group = even_groups(self.lanes)

    def from_west(self, x0, x1):
        r0, r1 = pltpu.roll(x0, 1, 1), pltpu.roll(x1, 1, 1)
        return jnp.where(self.at_first, r1, r0), jnp.where(self.at_first, r0, r1)

    def from_east(self, x0, x1):
        r0, r1 = pltpu.roll(x0, self.lanes - 1, 1), pltpu.roll(x1, self.lanes - 1, 1)
        return jnp.where(self.at_last, r1, r0), jnp.where(self.at_last, r0, r1)

    def spread(self, row, easts, wests):
        for m, (east, west) in enumerate(zip(easts, wests)):
            both = jnp.where(self.even_group, east, west), jnp.where(self.even_group, west, east)
            for channel in strip_rows(self.c, m):
                shift = shift_of(channel)
                tile = both[(channel % 16) // 8]
                if shift:
                    tile = pltpu.roll(tile, self.lanes - shift, 1)
                self.e[1][channel, pl.ds(row, TILE), :] = tile

    def western(self, row):
        at = pl.ds(row, TILE)
        self.w[0][at, :], self.w[1][at, :] = self.from_west(self.e[0][self.c.ce, at, :], self.e[1][self.c.ce, at, :])

    def neighbours(self, load, row, halves=2):
        c, at = self.c, pl.ds(row, TILE)
        ce = [e[c.ce, at, :] for e in self.e]
        cw = [w[at, :] for w in self.w]
        cn = [e[c.cn, at, :] for e in self.e]
        cs = [e[c.cn, pl.ds(row - 1, TILE), :] for e in self.e]
        own = [(load(0, k, at), load(1, k, at)) for k in range(c.levels)]
        out = []
        for k in range(c.levels):
            east, west = self.from_east(*own[k]), self.from_west(*own[k])
            pair = []
            for h in range(halves):
                north, south = load(h, k, pl.ds(row + 1, TILE)), load(h, k, pl.ds(row - 1, TILE))
                total = (ce[h] * east[h] + cw[h] * west[h]) + (cn[h] * north + cs[h] * south)
                around = [own[j][h] for j in (k - 1, k + 1) if 0 <= j < c.levels]
                pair.append((own[k][h], total + vertical_coef * functools.reduce(jnp.add, around)))
            out.append(pair)
        return out

    def diagonal(self, row):
        load = lambda h, k, at: self.e[h][self.c.wet + k, at, :]
        for k, pair in enumerate(self.neighbours(load, row)):
            for h, (_, total) in enumerate(pair):
                self.d[h][k, pl.ds(row, TILE), :] = 1.0 - total

    def loader(self, index):
        if index == 0:
            return lambda h, k, at: self.e[h][self.c.u + k, at, :]
        base = (index - 1) * self.c.levels
        return lambda h, k, at: self.x[h][base + k, at, :]

    def forward(self, n, row):
        c, at = self.c, pl.ds(row, TILE)
        for k, pair in enumerate(self.neighbours(self.loader(n), row)):
            for h, (own, total) in enumerate(pair):
                e = self.e[h]
                wet = e[c.wet + k, at, :]
                bounded = wet * jnp.tanh(self.d[h][k, at, :] * own + total)
                slope = wet - bounded * bounded
                if n < STEPS - 1:
                    self.x[h][n * c.levels + k, at, :] = bounded + e[c.s + k, at, :]
                    self.m[h][n * c.levels + k, at, :] = slope
                else:
                    if h == 0:
                        self.state[k, at, :] = bounded + e[c.s + k, at, :]
                    self.x[h][n * c.levels + k, at, :] = slope * e[c.cot + k, at, :]

    def backward(self, n, row):
        c, at = self.c, pl.ds(row, TILE)
        index = 2 * STEPS - 1 - n
        for k, pair in enumerate(self.neighbours(self.loader(index), row)):
            for h, (own, total) in enumerate(pair):
                value = self.d[h][k, at, :] * own + total
                if h == 0:
                    self.adj[(n - 1) * c.levels + k, at, :] = value
                self.x[h][index * c.levels + k, at, :] = self.m[h][(n - 1) * c.levels + k, at, :] * value

    def gradient(self, row):
        c, at = self.c, pl.ds(row, TILE)
        for k, pair in enumerate(self.neighbours(self.loader(2 * STEPS - 1), row, 1)):
            own, total = pair[0]
            yield k, self.e[0][c.wet + k, at, :] * (self.d[0][k, at, :] * own + total)

    def source_gradient(self, row):
        c, at = self.c, pl.ds(row, TILE)
        for k in range(c.levels):
            total = self.e[0][c.cot + k, at, :]
            for n in range(STEPS - 1):
                total = total + self.adj[n * c.levels + k, at, :]
            yield k, self.e[0][c.wet + k, at, :] * total


def own_kernel(c, f_ref, one_ref, two_ref, e0, e1, w0, w1, d0, d1, x0, x1, m0, m1, adj, state, grad, gsource):
    rows = f_ref.shape[1]
    odd_lon = is_odd("lon")
    s = Sweeps(c, (e0, e1), (w0, w1), (d0, d1), (x0, x1), (m0, m1), adj, state)
    zero = jnp.zeros((TILE, f_ref.shape[2]), jnp.float32)
    for ref in (e0, e1):
        for end in (pl.ds(0, TILE), pl.ds(HALO + rows, TILE)):
            for channel in (*range(c.u, c.u + c.levels), *range(c.wet, c.wet + c.levels), c.cn):
                ref[channel, end, :] = zero
    tiles = rows // TILE
    places = [HALO + t * TILE for t in range(tiles)]
    for t, row in enumerate(places):
        at, to = pl.ds(t * TILE, TILE), pl.ds(row, TILE)
        for channel in range(c.count):
            e0[channel, to, :] = f_ref[channel, at, :]
        pairs = [(one_ref[m, at, :], two_ref[m, at, :]) for m in range(c.parts)]
        s.spread(
            row,
            [jnp.where(odd_lon, two, one) for one, two in pairs],
            [jnp.where(odd_lon, one, two) for one, two in pairs],
        )
        s.western(row)
    for row in places:
        s.diagonal(row)
    for n in range(STEPS):
        for row in places:
            s.forward(n, row)
    for n in range(STEPS - 1, 0, -1):
        for row in places:
            s.backward(n, row)
    for row in places[1:-1]:
        at = pl.ds(row - HALO, TILE)
        for k, value in s.source_gradient(row):
            gsource[k, at, :] = value
        for k, value in s.gradient(row):
            grad[k, at, :] = value


def edge_kernel(
    c, first_one, first_two, second_one, second_two, *refs,
):
    aliased = refs[: len(refs) // 2]
    del aliased
    e0, e1, w0, w1, d0, d1, x0, x1, m0, m1, adj, state, grad, gsource, state_hbm, grad_hbm, gsource_hbm, sems = refs[14:]
    rows = grad.shape[1]
    s = Sweeps(c, (e0, e1), (w0, w1), (d0, d1), (x0, x1), (m0, m1), adj, state)
    odd_lat = is_odd("lat")
    for row, low in ((0, True), (HALO + rows, False)):
        pole = lax.axis_index("lat") == (0 if low else lax.axis_size("lat") - 1)
        from_one = odd_lat if low else jnp.logical_not(odd_lat)
        to = pl.ds(row, TILE)

        def got(one, two, i):
            return jnp.where(pole, 0.0, jnp.where(from_one, one[i], two[i]))

        second = [got(second_one, second_two, i) for i in range(c.second)]
        for channel in range(c.first):
            e0[channel, to, :] = got(first_one, first_two, channel)
        e0[c.ce, to, :], e0[c.cn, to, :] = second[c.strips : c.cot_at]
        for k in range(c.levels):
            tile = second[c.cot_at + k // 2]
            if (k % 2 == 0) == low:
                tile = pltpu.roll(tile, TILE // 2, 0)
            e0[c.cot + k, to, :] = tile
        s.spread(row, second[: c.parts], second[c.parts : c.strips])
        s.western(row)
    top = lambda i: HALO + i - (DEPTH - 1)
    bottom = lambda i: HALO + rows - 1 - i
    places = lambda i: (top(i), bottom(i))
    for row in places(0):
        s.diagonal(row)
    for n in range(STEPS):
        for row in places(n):
            s.forward(n, row)
    own = pl.ds(HALO, rows)
    moves = [
        pltpu.make_async_copy(state.at[:, own, :], state_hbm, sems.at[0]),
        pltpu.make_async_copy(gsource, gsource_hbm, sems.at[1]),
        pltpu.make_async_copy(grad, grad_hbm, sems.at[2]),
    ]
    moves[0].start()
    for n in range(STEPS - 1, 0, -1):
        for row in places(2 * STEPS - 1 - n):
            s.backward(n, row)
    for row in places(DEPTH - 1):
        for k, value in s.source_gradient(row):
            gsource[k, pl.ds(row - HALO, TILE), :] = value
    moves[1].start()
    for row in places(DEPTH - 1):
        for k, value in s.gradient(row):
            grad[k, pl.ds(row - HALO, TILE), :] = value
    moves[2].start()
    for move in moves:
        move.wait()


def swaps(count, offset):
    pairs = [(i, (i + 1) % count) for i in range(offset, count, 2)]
    return pairs + [(j, i) for i, j in pairs]


def lat_swaps(lat, lon, offset):
    pairs, alone = [], set(range(lat))
    for i in range(offset, lat - 1, 2):
        alone -= {i, i + 1}
        pairs += [(i * lon + j, (i + 1) * lon + j) for j in range(lon)]
    for i in sorted(alone):
        pairs += [(i * lon + j, i * lon + j + 1) for j in range(0, lon, 2)]
    return pairs + [(j, i) for i, j in pairs]


def body(initial_state, source, cotangent, face_coefs, land_mask, bottom):
    arguments = (initial_state, source, cotangent, face_coefs, land_mask, bottom)
    levels, rows, lanes = initial_state.shape
    c = Names(levels)
    span = rows + 2 * HALO
    f32 = lambda *shape: jax.ShapeDtypeStruct(shape, jnp.float32)
    vmem, hbm = pl.BlockSpec(memory_space=pltpu.VMEM), pl.BlockSpec(memory_space=pltpu.HBM)
    params = pltpu.CompilerParams(vmem_limit_bytes=8 * 1024 * 1024)

    fields, one, two, lat_one, lat_two = pl.pallas_call(
        functools.partial(pack_kernel, c),
        out_shape=(f32(c.count, rows, lanes), *(f32(c.parts, rows, lanes),) * 2, *(f32(c.first, TILE, lanes),) * 2),
        in_specs=[hbm] * 6,
        out_specs=(vmem,) * 5,
        scratch_shapes=[
            pltpu.VMEM((levels, rows, lanes), jnp.float32),
            pltpu.VMEM((levels, rows, lanes), jnp.float32),
            pltpu.VMEM((2, rows, lanes), jnp.float32),
            pltpu.VMEM((levels, rows, lanes), jnp.int32),
            pltpu.VMEM((rows, lanes), jnp.int32),
            pltpu.SemaphoreType.DMA((6,)),
        ],
        compiler_params=params,
        name="pack",
    )(*(pltpu.with_memory_space_constraint(x, pltpu.HBM) for x in arguments))
    lon, lat = lax.axis_size("lon"), lax.axis_size("lat")
    one = lax.ppermute(one, "lon", swaps(lon, 0))
    two = lax.ppermute(two, "lon", swaps(lon, 1))
    both = ("lat", "lon")
    lat_pairs, other_pairs = lat_swaps(lat, lon, 0), lat_swaps(lat, lon, 1)
    first = lax.ppermute(lat_one, both, lat_pairs), lax.ppermute(lat_two, both, other_pairs)
    lat_one, lat_two = pl.pallas_call(
        functools.partial(corner_kernel, c),
        out_shape=(f32(c.second, TILE, lanes),) * 2,
        in_specs=[vmem] * 3,
        out_specs=(vmem,) * 2,
        compiler_params=params,
        name="corners",
    )(fields, one, two)
    second = lax.ppermute(lat_one, both, lat_pairs), lax.ppermute(lat_two, both, other_pairs)
    twice = lambda *shape: (f32(*shape), f32(*shape))
    shapes = (
        *twice(c.count, span, lanes),
        *twice(span, lanes),
        *twice(levels, span, lanes),
        *twice((2 * STEPS - 1) * levels, span, lanes),
        *twice((STEPS - 1) * levels, span, lanes),
        f32((STEPS - 1) * levels, span, lanes),
        f32(levels, span, lanes),
        f32(levels, rows, lanes),
        f32(levels, rows, lanes),
    )
    own = pl.pallas_call(
        functools.partial(own_kernel, c),
        out_shape=shapes,
        in_specs=[vmem] * 3,
        out_specs=(vmem,) * len(shapes),
        compiler_params=params,
        cost_estimate=pl.CostEstimate(
            flops=2 * STEPS * levels * rows * lanes * 40, bytes_accessed=16 * 2**20, transcendentals=0
        ),
        name="own_rows",
    )(fields, one, two)
    out = pl.pallas_call(
        functools.partial(edge_kernel, c),
        out_shape=(*shapes, *(f32(levels, rows, lanes),) * 3),
        in_specs=[vmem] * (4 + len(shapes)),
        out_specs=(*(vmem,) * len(shapes), hbm, hbm, hbm),
        input_output_aliases={4 + i: i for i in range(len(shapes))},
        scratch_shapes=[pltpu.SemaphoreType.DMA((3,))],
        compiler_params=params,
        name="edge_rows",
    )(*first, *second, *own)
    return tuple(out[len(shapes) :])


def solution(mesh):
    block = P(None, "lat", "lon")
    return jax.shard_map(
        body,
        mesh=mesh,
        in_specs=(block, block, block, block, block, P("lat", "lon")),
        out_specs=(block, block, block),
        check_vma=False,
    )
```

```python
import functools

import jax
import jax.numpy as jnp
from jax import lax
from jax.experimental import pallas as pl
from jax.experimental.pallas import tpu as pltpu
from jax.sharding import PartitionSpec as P

STEPS = 4
DEPTH = 2 * STEPS
TILE = 8
HALO = TILE

vertical_coef = 0.04


class Names:
    def __init__(self, levels):
        self.levels = levels
        self.u, self.s, self.wet = 0, levels, 2 * levels
        self.ce, self.cn, self.cot = 3 * levels, 3 * levels + 1, 3 * levels + 2
        self.count = 4 * levels + 2
        self.parts = -(-self.count // 16)
        self.strips = 2 * self.parts
        self.first = self.ce
        self.cot_at = self.strips + 2
        self.second = self.cot_at + -(-levels // 2)


def lane_iota(lanes):
    return lax.broadcasted_iota(jnp.int32, (TILE, lanes), 1)


def shift_of(channel):
    place = channel % 16
    return 2 * DEPTH * (place % 8) + DEPTH * (place // 8)


def even_groups(lanes):
    return lax.rem(lane_iota(lanes) // DEPTH, 2) == 0


def is_odd(axis):
    return lax.rem(lax.axis_index(axis), 2) == 1


def strip_rows(c, m):
    return range(16 * m, min(16 * m + 16, c.count))


def pack_kernel(
    c, u_hbm, s_hbm, a_hbm, c_hbm, land_hbm, bottom_hbm, f_ref, first_ref, second_ref, lat_one_ref, lat_two_ref,
    u_ref, s_ref, c_ref, land_ref, bottom_ref, sems,
):
    levels = c.levels
    _, rows, lanes = u_ref.shape
    moves = [
        pltpu.make_async_copy(source, target, sems.at[i])
        for i, (source, target) in enumerate(
            (
                (bottom_hbm, bottom_ref),
                (land_hbm, land_ref),
                (u_hbm, u_ref),
                (s_hbm, s_ref),
                (c_hbm, c_ref),
                (a_hbm, f_ref.at[pl.ds(c.cot, levels)]),
            )
        )
    ]
    for move in moves:
        move.start()
    for move in moves:
        move.wait()
    last_lat = lax.axis_index("lat") == lax.axis_size("lat") - 1
    for k in range(levels):
        wet = jnp.where(k < bottom_ref[...], land_ref[k], 0).astype(jnp.float32)
        f_ref[c.u + k] = wet * u_ref[k]
        f_ref[c.s + k] = wet * s_ref[k]
        f_ref[c.wet + k] = wet
    f_ref[c.ce] = c_ref[0]
    row = lax.broadcasted_iota(jnp.int32, (rows, lanes), 0)
    f_ref[c.cn] = jnp.where(jnp.logical_and(last_lat, row == rows - 1), 0.0, c_ref[1])
    odd = is_odd("lon")
    group, groups = lane_iota(lanes) // DEPTH, lanes // DEPTH
    for t in range(rows // TILE):
        at = pl.ds(t * TILE, TILE)
        for m in range(c.parts):
            east = jnp.zeros((TILE, lanes), jnp.float32)
            west = east
            for channel in strip_rows(c, m):
                shift = shift_of(channel)
                tile = f_ref[channel, at, :]
                if shift:
                    tile = pltpu.roll(tile, shift, 1)
                east = jnp.where(group == shift // DEPTH, tile, east)
                west = jnp.where(group == (shift // DEPTH - 1) % groups, tile, west)
            first_ref[m, at, :] = jnp.where(odd, east, west)
            second_ref[m, at, :] = jnp.where(odd, west, east)
    odd_lat = is_odd("lat")
    for channel in range(c.first):
        high, low = f_ref[channel, pl.ds(rows - TILE, TILE), :], f_ref[channel, pl.ds(0, TILE), :]
        lat_one_ref[channel] = jnp.where(odd_lat, low, high)
        lat_two_ref[channel] = jnp.where(odd_lat, high, low)


def corner_kernel(c, f_ref, one_ref, two_ref, lat_one_ref, lat_two_ref):
    odd_lat, odd_lon = is_odd("lat"), is_odd("lon")
    _, rows, lanes = f_ref.shape
    half = TILE // 2
    first_half = lax.broadcasted_iota(jnp.int32, (TILE, lanes), 0) < half
    low, high = pl.ds(0, TILE), pl.ds(rows - TILE, TILE)

    def put(i, low_tile, high_tile):
        lat_one_ref[i] = jnp.where(odd_lat, low_tile, high_tile)
        lat_two_ref[i] = jnp.where(odd_lat, high_tile, low_tile)

    for m in range(c.parts):
        ends = [(one_ref[m, at, :], two_ref[m, at, :]) for at in (low, high)]
        put(m, *(jnp.where(odd_lon, two, one) for one, two in ends))
        put(c.parts + m, *(jnp.where(odd_lon, one, two) for one, two in ends))
    put(c.strips, f_ref[c.ce, low, :], f_ref[c.ce, high, :])
    put(c.strips + 1, f_ref[c.cn, low, :], f_ref[c.cn, high, :])
    for q in range(c.second - c.cot_at):
        one, two = c.cot + 2 * q, c.cot + min(2 * q + 1, c.levels - 1)
        put(
            c.cot_at + q,
            jnp.where(first_half, f_ref[one, low, :], pltpu.roll(f_ref[two, low, :], half, 0)),
            jnp.where(first_half, pltpu.roll(f_ref[one, high, :], half, 0), f_ref[two, high, :]),
        )


class Sweeps:
    def __init__(self, c, e, w, d, x, m, adj, state):
        self.c, self.e, self.w, self.d, self.x, self.m, self.adj, self.state = c, e, w, d, x, m, adj, state
        self.lanes = e[0].shape[-1]
        lane = lane_iota(self.lanes)
        self.at_first, self.at_last = lane == 0, lane == self.lanes - 1
        self.even_group = even_groups(self.lanes)

    def from_west(self, x0, x1):
        r0, r1 = pltpu.roll(x0, 1, 1), pltpu.roll(x1, 1, 1)
        return jnp.where(self.at_first, r1, r0), jnp.where(self.at_first, r0, r1)

    def from_east(self, x0, x1):
        r0, r1 = pltpu.roll(x0, self.lanes - 1, 1), pltpu.roll(x1, self.lanes - 1, 1)
        return jnp.where(self.at_last, r1, r0), jnp.where(self.at_last, r0, r1)

    def spread(self, row, easts, wests):
        for m, (east, west) in enumerate(zip(easts, wests)):
            both = jnp.where(self.even_group, east, west), jnp.where(self.even_group, west, east)
            for channel in strip_rows(self.c, m):
                shift = shift_of(channel)
                tile = both[(channel % 16) // 8]
                if shift:
                    tile = pltpu.roll(tile, self.lanes - shift, 1)
                self.e[1][channel, pl.ds(row, TILE), :] = tile

    def western(self, row):
        at = pl.ds(row, TILE)
        self.w[0][at, :], self.w[1][at, :] = self.from_west(self.e[0][self.c.ce, at, :], self.e[1][self.c.ce, at, :])

    def neighbours(self, load, row, halves=2):
        c, at = self.c, pl.ds(row, TILE)
        ce = [e[c.ce, at, :] for e in self.e]
        cw = [w[at, :] for w in self.w]
        cn = [e[c.cn, at, :] for e in self.e]
        cs = [e[c.cn, pl.ds(row - 1, TILE), :] for e in self.e]
        own = [(load(0, k, at), load(1, k, at)) for k in range(c.levels)]
        out = []
        for k in range(c.levels):
            east, west = self.from_east(*own[k]), self.from_west(*own[k])
            pair = []
            for h in range(halves):
                north, south = load(h, k, pl.ds(row + 1, TILE)), load(h, k, pl.ds(row - 1, TILE))
                total = (ce[h] * east[h] + cw[h] * west[h]) + (cn[h] * north + cs[h] * south)
                around = [own[j][h] for j in (k - 1, k + 1) if 0 <= j < c.levels]
                pair.append((own[k][h], total + vertical_coef * functools.reduce(jnp.add, around)))
            out.append(pair)
        return out

    def diagonal(self, row):
        load = lambda h, k, at: self.e[h][self.c.wet + k, at, :]
        for k, pair in enumerate(self.neighbours(load, row)):
            for h, (_, total) in enumerate(pair):
                self.d[h][k, pl.ds(row, TILE), :] = 1.0 - total

    def loader(self, index):
        if index == 0:
            return lambda h, k, at: self.e[h][self.c.u + k, at, :]
        base = (index - 1) * self.c.levels
        return lambda h, k, at: self.x[h][base + k, at, :]

    def forward(self, n, row):
        c, at = self.c, pl.ds(row, TILE)
        for k, pair in enumerate(self.neighbours(self.loader(n), row)):
            for h, (own, total) in enumerate(pair):
                e = self.e[h]
                wet = e[c.wet + k, at, :]
                bounded = wet * jnp.tanh(self.d[h][k, at, :] * own + total)
                slope = wet - bounded * bounded
                if n < STEPS - 1:
                    self.x[h][n * c.levels + k, at, :] = bounded + e[c.s + k, at, :]
                    self.m[h][n * c.levels + k, at, :] = slope
                else:
                    if h == 0:
                        self.state[k, at, :] = bounded + e[c.s + k, at, :]
                    self.x[h][n * c.levels + k, at, :] = slope * e[c.cot + k, at, :]

    def backward(self, n, row):
        c, at = self.c, pl.ds(row, TILE)
        index = 2 * STEPS - 1 - n
        for k, pair in enumerate(self.neighbours(self.loader(index), row)):
            for h, (own, total) in enumerate(pair):
                value = self.d[h][k, at, :] * own + total
                if h == 0:
                    self.adj[(n - 1) * c.levels + k, at, :] = value
                self.x[h][index * c.levels + k, at, :] = self.m[h][(n - 1) * c.levels + k, at, :] * value

    def gradient(self, row):
        c, at = self.c, pl.ds(row, TILE)
        for k, pair in enumerate(self.neighbours(self.loader(2 * STEPS - 1), row, 1)):
            own, total = pair[0]
            yield k, self.e[0][c.wet + k, at, :] * (self.d[0][k, at, :] * own + total)

    def source_gradient(self, row):
        c, at = self.c, pl.ds(row, TILE)
        for k in range(c.levels):
            total = self.e[0][c.cot + k, at, :]
            for n in range(STEPS - 1):
                total = total + self.adj[n * c.levels + k, at, :]
            yield k, self.e[0][c.wet + k, at, :] * total


def own_kernel(c, f_ref, one_ref, two_ref, e0, e1, w0, w1, d0, d1, x0, x1, m0, m1, adj, state, grad, gsource):
    rows = f_ref.shape[1]
    odd_lon = is_odd("lon")
    s = Sweeps(c, (e0, e1), (w0, w1), (d0, d1), (x0, x1), (m0, m1), adj, state)
    zero = jnp.zeros((TILE, f_ref.shape[2]), jnp.float32)
    for ref in (e0, e1):
        for end in (pl.ds(0, TILE), pl.ds(HALO + rows, TILE)):
            for channel in (*range(c.u, c.u + c.levels), *range(c.wet, c.wet + c.levels), c.cn):
                ref[channel, end, :] = zero
    tiles = rows // TILE
    places = [HALO + t * TILE for t in range(tiles)]
    for t, row in enumerate(places):
        at, to = pl.ds(t * TILE, TILE), pl.ds(row, TILE)
        for channel in range(c.count):
            e0[channel, to, :] = f_ref[channel, at, :]
        pairs = [(one_ref[m, at, :], two_ref[m, at, :]) for m in range(c.parts)]
        s.spread(
            row,
            [jnp.where(odd_lon, two, one) for one, two in pairs],
            [jnp.where(odd_lon, one, two) for one, two in pairs],
        )
        s.western(row)
    for row in places:
        s.diagonal(row)
    for n in range(STEPS):
        for row in places:
            s.forward(n, row)
    for n in range(STEPS - 1, 0, -1):
        for row in places:
            s.backward(n, row)
    for row in places[1:-1]:
        at = pl.ds(row - HALO, TILE)
        for k, value in s.source_gradient(row):
            gsource[k, at, :] = value
        for k, value in s.gradient(row):
            grad[k, at, :] = value


def edge_kernel(
    c, first_one, first_two, second_two, second_one, *refs,
):
    aliased = refs[: len(refs) // 2]
    del aliased
    e0, e1, w0, w1, d0, d1, x0, x1, m0, m1, adj, state, grad, gsource, state_hbm, grad_hbm, gsource_hbm, sems = refs[14:]
    rows = grad.shape[1]
    s = Sweeps(c, (e0, e1), (w0, w1), (d0, d1), (x0, x1), (m0, m1), adj, state)
    odd_lat = is_odd("lat")
    for row, low in ((0, True), (HALO + rows, False)):
        pole = lax.axis_index("lat") == (0 if low else lax.axis_size("lat") - 1)
        from_one = odd_lat if low else jnp.logical_not(odd_lat)
        to = pl.ds(row, TILE)

        def got(one, two, i):
            return jnp.where(pole, 0.0, jnp.where(from_one, one[i], two[i]))

        second = [got(second_one, second_two, i) for i in range(c.second)]
        for channel in range(c.first):
            e0[channel, to, :] = got(first_one, first_two, channel)
        e0[c.ce, to, :], e0[c.cn, to, :] = second[c.strips : c.cot_at]
        for k in range(c.levels):
            tile = second[c.cot_at + k // 2]
            if (k % 2 == 0) == low:
                tile = pltpu.roll(tile, TILE // 2, 0)
            e0[c.cot + k, to, :] = tile
        s.spread(row, second[: c.parts], second[c.parts : c.strips])
        s.western(row)
    top = lambda i: HALO + i - (DEPTH - 1)
    bottom = lambda i: HALO + rows - 1 - i
    places = lambda i: (top(i), bottom(i))
    for row in places(0):
        s.diagonal(row)
    for n in range(STEPS):
        for row in places(n):
            s.forward(n, row)
    own = pl.ds(HALO, rows)
    moves = [
        pltpu.make_async_copy(state.at[:, own, :], state_hbm, sems.at[0]),
        pltpu.make_async_copy(gsource, gsource_hbm, sems.at[1]),
        pltpu.make_async_copy(grad, grad_hbm, sems.at[2]),
    ]
    moves[0].start()
    for n in range(STEPS - 1, 0, -1):
        for row in places(2 * STEPS - 1 - n):
            s.backward(n, row)
    for row in places(DEPTH - 1):
        for k, value in s.source_gradient(row):
            gsource[k, pl.ds(row - HALO, TILE), :] = value
    moves[1].start()
    for row in places(DEPTH - 1):
        for k, value in s.gradient(row):
            grad[k, pl.ds(row - HALO, TILE), :] = value
    moves[2].start()
    for move in moves:
        move.wait()


def swaps(count, offset):
    pairs = [(i, (i + 1) % count) for i in range(offset, count, 2)]
    return pairs + [(j, i) for i, j in pairs]


def lat_swaps(lat, lon, offset):
    pairs, alone = [], set(range(lat))
    for i in range(offset, lat - 1, 2):
        alone -= {i, i + 1}
        pairs += [(i * lon + j, (i + 1) * lon + j) for j in range(lon)]
    for i in sorted(alone):
        pairs += [(i * lon + j, i * lon + j + 1) for j in range(0, lon, 2)]
    return pairs + [(j, i) for i, j in pairs]


def body(initial_state, source, cotangent, face_coefs, land_mask, bottom):
    arguments = (initial_state, source, cotangent, face_coefs, land_mask, bottom)
    levels, rows, lanes = initial_state.shape
    c = Names(levels)
    span = rows + 2 * HALO
    f32 = lambda *shape: jax.ShapeDtypeStruct(shape, jnp.float32)
    vmem, hbm = pl.BlockSpec(memory_space=pltpu.VMEM), pl.BlockSpec(memory_space=pltpu.HBM)
    params = pltpu.CompilerParams(vmem_limit_bytes=8 * 1024 * 1024)

    fields, one, two, lat_one, lat_two = pl.pallas_call(
        functools.partial(pack_kernel, c),
        out_shape=(f32(c.count, rows, lanes), *(f32(c.parts, rows, lanes),) * 2, *(f32(c.first, TILE, lanes),) * 2),
        in_specs=[hbm] * 6,
        out_specs=(vmem,) * 5,
        scratch_shapes=[
            pltpu.VMEM((levels, rows, lanes), jnp.float32),
            pltpu.VMEM((levels, rows, lanes), jnp.float32),
            pltpu.VMEM((2, rows, lanes), jnp.float32),
            pltpu.VMEM((levels, rows, lanes), jnp.int32),
            pltpu.VMEM((rows, lanes), jnp.int32),
            pltpu.SemaphoreType.DMA((6,)),
        ],
        compiler_params=params,
        name="pack",
    )(*(pltpu.with_memory_space_constraint(x, pltpu.HBM) for x in arguments))
    lon, lat = lax.axis_size("lon"), lax.axis_size("lat")
    one = lax.ppermute(one, "lon", swaps(lon, 0))
    two = lax.ppermute(two, "lon", swaps(lon, 1))
    both = ("lat", "lon")
    lat_pairs, other_pairs = lat_swaps(lat, lon, 0), lat_swaps(lat, lon, 1)
    first = lax.ppermute(lat_one, both, lat_pairs), lax.ppermute(lat_two, both, other_pairs)
    lat_one, lat_two = pl.pallas_call(
        functools.partial(corner_kernel, c),
        out_shape=(f32(c.second, TILE, lanes),) * 2,
        in_specs=[vmem] * 3,
        out_specs=(vmem,) * 2,
        compiler_params=params,
        name="corners",
    )(fields, one, two)
    second = lax.ppermute(lat_one, both, lat_pairs), lax.ppermute(lat_two, both, other_pairs)
    twice = lambda *shape: (f32(*shape), f32(*shape))
    shapes = (
        *twice(c.count, span, lanes),
        *twice(span, lanes),
        *twice(levels, span, lanes),
        *twice((2 * STEPS - 1) * levels, span, lanes),
        *twice((STEPS - 1) * levels, span, lanes),
        f32((STEPS - 1) * levels, span, lanes),
        f32(levels, span, lanes),
        f32(levels, rows, lanes),
        f32(levels, rows, lanes),
    )
    own = pl.pallas_call(
        functools.partial(own_kernel, c),
        out_shape=shapes,
        in_specs=[vmem] * 3,
        out_specs=(vmem,) * len(shapes),
        compiler_params=params,
        cost_estimate=pl.CostEstimate(
            flops=2 * STEPS * levels * rows * lanes * 40, bytes_accessed=16 * 2**20, transcendentals=0
        ),
        name="own_rows",
    )(fields, one, two)
    out = pl.pallas_call(
        functools.partial(edge_kernel, c),
        out_shape=(*shapes, *(f32(levels, rows, lanes),) * 3),
        in_specs=[vmem] * (4 + len(shapes)),
        out_specs=(*(vmem,) * len(shapes), hbm, hbm, hbm),
        input_output_aliases={4 + i: i for i in range(len(shapes))},
        scratch_shapes=[pltpu.SemaphoreType.DMA((3,))],
        compiler_params=params,
        name="edge_rows",
    )(*first, *second[::-1], *own)
    return tuple(out[len(shapes) :])


def solution(mesh):
    block = P(None, "lat", "lon")
    return jax.shard_map(
        body,
        mesh=mesh,
        in_specs=(block, block, block, block, block, P("lat", "lon")),
        out_specs=(block, block, block),
        check_vma=False,
    )
```

```python
import functools

import jax
import jax.numpy as jnp
from jax import lax
from jax.experimental import pallas as pl
from jax.experimental.pallas import tpu as pltpu
from jax.sharding import PartitionSpec as P

STEPS = 4
DEPTH = 2 * STEPS
TILE = 8
HALO = TILE

vertical_coef = 0.04


class Names:
    def __init__(self, levels):
        self.levels = levels
        self.u, self.s, self.wet = 0, levels, 2 * levels
        self.ce, self.cn, self.cot = 3 * levels, 3 * levels + 1, 3 * levels + 2
        self.count = 4 * levels + 2
        self.parts = -(-self.count // 16)
        self.strips = 2 * self.parts
        self.strips_at = self.ce
        self.faces_at = self.strips_at + self.strips
        self.cot_at = self.faces_at + 2
        self.late = self.cot_at + -(-levels // 2)
        self.early = max(self.count, self.late + 1)


def lane_iota(lanes):
    return lax.broadcasted_iota(jnp.int32, (TILE, lanes), 1)


def shift_of(channel):
    place = channel % 16
    return 2 * DEPTH * (place % 8) + DEPTH * (place // 8)


def even_groups(lanes):
    return lax.rem(lane_iota(lanes) // DEPTH, 2) == 0


def is_odd(axis):
    return lax.rem(lax.axis_index(axis), 2) == 1


def strip_rows(c, m):
    return range(16 * m, min(16 * m + 16, c.count))


def pack_kernel(
    c, u_hbm, s_hbm, a_hbm, c_hbm, land_hbm, bottom_hbm, f_ref, first_ref, second_ref, lat_ref,
    u_ref, s_ref, c_ref, land_ref, bottom_ref, sems,
):
    levels = c.levels
    _, rows, lanes = u_ref.shape
    moves = [
        pltpu.make_async_copy(source, target, sems.at[i])
        for i, (source, target) in enumerate(
            (
                (bottom_hbm, bottom_ref),
                (land_hbm, land_ref),
                (u_hbm, u_ref),
                (s_hbm, s_ref),
                (c_hbm, c_ref),
                (a_hbm, f_ref.at[pl.ds(c.cot, levels)]),
            )
        )
    ]
    for move in moves:
        move.start()
    for move in moves:
        move.wait()
    last_lat = lax.axis_index("lat") == lax.axis_size("lat") - 1
    for k in range(levels):
        wet = jnp.where(k < bottom_ref[...], land_ref[k], 0).astype(jnp.float32)
        f_ref[c.u + k] = wet * u_ref[k]
        f_ref[c.s + k] = wet * s_ref[k]
        f_ref[c.wet + k] = wet
    f_ref[c.ce] = c_ref[0]
    row = lax.broadcasted_iota(jnp.int32, (rows, lanes), 0)
    f_ref[c.cn] = jnp.where(jnp.logical_and(last_lat, row == rows - 1), 0.0, c_ref[1])
    odd = is_odd("lon")
    group, groups = lane_iota(lanes) // DEPTH, lanes // DEPTH
    for t in range(rows // TILE):
        at = pl.ds(t * TILE, TILE)
        for m in range(c.parts):
            east = jnp.zeros((TILE, lanes), jnp.float32)
            west = east
            for channel in strip_rows(c, m):
                shift = shift_of(channel)
                tile = f_ref[channel, at, :]
                if shift:
                    tile = pltpu.roll(tile, shift, 1)
                east = jnp.where(group == shift // DEPTH, tile, east)
                west = jnp.where(group == (shift // DEPTH - 1) % groups, tile, west)
            first_ref[m, at, :] = jnp.where(odd, east, west)
            second_ref[m, at, :] = jnp.where(odd, west, east)
    odd_lat = is_odd("lat")
    for channel in range(c.count):
        high, low = f_ref[channel, pl.ds(rows - TILE, TILE), :], f_ref[channel, pl.ds(0, TILE), :]
        lat_ref[channel] = jnp.where(odd_lat, low, high)
    for channel in range(c.count, c.early):
        lat_ref[channel] = jnp.zeros((TILE, lanes), jnp.float32)


def corner_kernel(c, f_ref, two_ref, one_ref, strips_ref, late_ref):
    odd_lat, odd_lon = is_odd("lat"), is_odd("lon")
    _, rows, lanes = f_ref.shape
    half = TILE // 2
    first_half = lax.broadcasted_iota(jnp.int32, (TILE, lanes), 0) < half
    low, high = pl.ds(0, TILE), pl.ds(rows - TILE, TILE)

    def late(i, low_tile, high_tile):
        late_ref[i] = jnp.where(odd_lat, high_tile, low_tile)

    def strips(i, low_tile, high_tile):
        strips_ref[i] = jnp.where(odd_lat, low_tile, high_tile)
        late(c.strips_at + i, low_tile, high_tile)

    for m in range(c.parts):
        ends = [(one_ref[m, at, :], two_ref[m, at, :]) for at in (low, high)]
        strips(m, *(jnp.where(odd_lon, two, one) for one, two in ends))
        strips(c.parts + m, *(jnp.where(odd_lon, one, two) for one, two in ends))
    for i, channel in (*((i, i) for i in range(c.strips_at)), (c.faces_at, c.ce), (c.faces_at + 1, c.cn)):
        late(i, f_ref[channel, low, :], f_ref[channel, high, :])
    for q in range(c.late - c.cot_at):
        one, two = c.cot + 2 * q, c.cot + min(2 * q + 1, c.levels - 1)
        late(
            c.cot_at + q,
            jnp.where(first_half, f_ref[one, low, :], pltpu.roll(f_ref[two, low, :], half, 0)),
            jnp.where(first_half, pltpu.roll(f_ref[one, high, :], half, 0), f_ref[two, high, :]),
        )


class Sweeps:
    def __init__(self, c, e, w, d, x, m, adj, state):
        self.c, self.e, self.w, self.d, self.x, self.m, self.adj, self.state = c, e, w, d, x, m, adj, state
        self.lanes = e[0].shape[-1]
        lane = lane_iota(self.lanes)
        self.at_first, self.at_last = lane == 0, lane == self.lanes - 1
        self.even_group = even_groups(self.lanes)

    def from_west(self, x0, x1):
        r0, r1 = pltpu.roll(x0, 1, 1), pltpu.roll(x1, 1, 1)
        return jnp.where(self.at_first, r1, r0), jnp.where(self.at_first, r0, r1)

    def from_east(self, x0, x1):
        r0, r1 = pltpu.roll(x0, self.lanes - 1, 1), pltpu.roll(x1, self.lanes - 1, 1)
        return jnp.where(self.at_last, r1, r0), jnp.where(self.at_last, r0, r1)

    def spread(self, row, easts, wests):
        for m, (east, west) in enumerate(zip(easts, wests)):
            both = jnp.where(self.even_group, east, west), jnp.where(self.even_group, west, east)
            for channel in strip_rows(self.c, m):
                shift = shift_of(channel)
                tile = both[(channel % 16) // 8]
                if shift:
                    tile = pltpu.roll(tile, self.lanes - shift, 1)
                self.e[1][channel, pl.ds(row, TILE), :] = tile

    def western(self, row):
        at = pl.ds(row, TILE)
        self.w[0][at, :], self.w[1][at, :] = self.from_west(self.e[0][self.c.ce, at, :], self.e[1][self.c.ce, at, :])

    def neighbours(self, load, row, halves=2):
        c, at = self.c, pl.ds(row, TILE)
        ce = [e[c.ce, at, :] for e in self.e]
        cw = [w[at, :] for w in self.w]
        cn = [e[c.cn, at, :] for e in self.e]
        cs = [e[c.cn, pl.ds(row - 1, TILE), :] for e in self.e]
        own = [(load(0, k, at), load(1, k, at)) for k in range(c.levels)]
        out = []
        for k in range(c.levels):
            east, west = self.from_east(*own[k]), self.from_west(*own[k])
            pair = []
            for h in range(halves):
                north, south = load(h, k, pl.ds(row + 1, TILE)), load(h, k, pl.ds(row - 1, TILE))
                total = (ce[h] * east[h] + cw[h] * west[h]) + (cn[h] * north + cs[h] * south)
                around = [own[j][h] for j in (k - 1, k + 1) if 0 <= j < c.levels]
                pair.append((own[k][h], total + vertical_coef * functools.reduce(jnp.add, around)))
            out.append(pair)
        return out

    def diagonal(self, row):
        load = lambda h, k, at: self.e[h][self.c.wet + k, at, :]
        for k, pair in enumerate(self.neighbours(load, row)):
            for h, (_, total) in enumerate(pair):
                self.d[h][k, pl.ds(row, TILE), :] = 1.0 - total

    def loader(self, index):
        if index == 0:
            return lambda h, k, at: self.e[h][self.c.u + k, at, :]
        base = (index - 1) * self.c.levels
        return lambda h, k, at: self.x[h][base + k, at, :]

    def forward(self, n, row):
        c, at = self.c, pl.ds(row, TILE)
        for k, pair in enumerate(self.neighbours(self.loader(n), row)):
            for h, (own, total) in enumerate(pair):
                e = self.e[h]
                wet = e[c.wet + k, at, :]
                bounded = wet * jnp.tanh(self.d[h][k, at, :] * own + total)
                slope = wet - bounded * bounded
                if n < STEPS - 1:
                    self.x[h][n * c.levels + k, at, :] = bounded + e[c.s + k, at, :]
                    self.m[h][n * c.levels + k, at, :] = slope
                else:
                    if h == 0:
                        self.state[k, at, :] = bounded + e[c.s + k, at, :]
                    self.x[h][n * c.levels + k, at, :] = slope * e[c.cot + k, at, :]

    def backward(self, n, row):
        c, at = self.c, pl.ds(row, TILE)
        index = 2 * STEPS - 1 - n
        for k, pair in enumerate(self.neighbours(self.loader(index), row)):
            for h, (own, total) in enumerate(pair):
                value = self.d[h][k, at, :] * own + total
                if h == 0:
                    self.adj[(n - 1) * c.levels + k, at, :] = value
                self.x[h][index * c.levels + k, at, :] = self.m[h][(n - 1) * c.levels + k, at, :] * value

    def gradient(self, row):
        c, at = self.c, pl.ds(row, TILE)
        for k, pair in enumerate(self.neighbours(self.loader(2 * STEPS - 1), row, 1)):
            own, total = pair[0]
            yield k, self.e[0][c.wet + k, at, :] * (self.d[0][k, at, :] * own + total)

    def source_gradient(self, row):
        c, at = self.c, pl.ds(row, TILE)
        for k in range(c.levels):
            total = self.e[0][c.cot + k, at, :]
            for n in range(STEPS - 1):
                total = total + self.adj[n * c.levels + k, at, :]
            yield k, self.e[0][c.wet + k, at, :] * total


def own_kernel(c, f_ref, two_ref, one_ref, e0, e1, w0, w1, d0, d1, x0, x1, m0, m1, adj, state, grad, gsource):
    rows = f_ref.shape[1]
    odd_lon = is_odd("lon")
    s = Sweeps(c, (e0, e1), (w0, w1), (d0, d1), (x0, x1), (m0, m1), adj, state)
    zero = jnp.zeros((TILE, f_ref.shape[2]), jnp.float32)
    for ref in (e0, e1):
        for end in (pl.ds(0, TILE), pl.ds(HALO + rows, TILE)):
            for channel in (*range(c.u, c.u + c.levels), *range(c.wet, c.wet + c.levels), c.cn):
                ref[channel, end, :] = zero
    tiles = rows // TILE
    places = [HALO + t * TILE for t in range(tiles)]
    for t, row in enumerate(places):
        at, to = pl.ds(t * TILE, TILE), pl.ds(row, TILE)
        for channel in range(c.count):
            e0[channel, to, :] = f_ref[channel, at, :]
        pairs = [(one_ref[m, at, :], two_ref[m, at, :]) for m in range(c.parts)]
        s.spread(
            row,
            [jnp.where(odd_lon, two, one) for one, two in pairs],
            [jnp.where(odd_lon, one, two) for one, two in pairs],
        )
        s.western(row)
    for row in places:
        s.diagonal(row)
    for n in range(STEPS):
        for row in places:
            s.forward(n, row)
    for n in range(STEPS - 1, 0, -1):
        for row in places:
            s.backward(n, row)
    for row in places[1:-1]:
        at = pl.ds(row - HALO, TILE)
        for k, value in s.source_gradient(row):
            gsource[k, at, :] = value
        for k, value in s.gradient(row):
            grad[k, at, :] = value


def edge_kernel(
    c, late, early, early_strips, *refs,
):
    aliased = refs[: len(refs) // 2]
    del aliased
    e0, e1, w0, w1, d0, d1, x0, x1, m0, m1, adj, state, grad, gsource, state_hbm, grad_hbm, gsource_hbm, sems = refs[14:]
    rows = grad.shape[1]
    s = Sweeps(c, (e0, e1), (w0, w1), (d0, d1), (x0, x1), (m0, m1), adj, state)
    odd_lat = is_odd("lat")
    for row, low in ((0, True), (HALO + rows, False)):
        pole = lax.axis_index("lat") == (0 if low else lax.axis_size("lat") - 1)
        from_early = odd_lat if low else jnp.logical_not(odd_lat)
        to = pl.ds(row, TILE)

        def got(early_tile, late_tile):
            return jnp.where(pole, 0.0, jnp.where(from_early, early_tile, late_tile))

        for channel in range(c.strips_at):
            e0[channel, to, :] = got(early[channel], late[channel])
        e0[c.ce, to, :] = got(early[c.ce], late[c.faces_at])
        e0[c.cn, to, :] = got(early[c.cn], late[c.faces_at + 1])
        for k in range(c.levels):
            tile = late[c.cot_at + k // 2]
            if (k % 2 == 0) == low:
                tile = pltpu.roll(tile, TILE // 2, 0)
            e0[c.cot + k, to, :] = got(early[c.cot + k], tile)
        strips = [got(early_strips[i], late[c.strips_at + i]) for i in range(c.strips)]
        s.spread(row, strips[: c.parts], strips[c.parts :])
        s.western(row)
    top = lambda i: HALO + i - (DEPTH - 1)
    bottom = lambda i: HALO + rows - 1 - i
    places = lambda i: (top(i), bottom(i))
    for row in places(0):
        s.diagonal(row)
    for n in range(STEPS):
        for row in places(n):
            s.forward(n, row)
    own = pl.ds(HALO, rows)
    moves = [
        pltpu.make_async_copy(state.at[:, own, :], state_hbm, sems.at[0]),
        pltpu.make_async_copy(gsource, gsource_hbm, sems.at[1]),
        pltpu.make_async_copy(grad, grad_hbm, sems.at[2]),
    ]
    moves[0].start()
    for n in range(STEPS - 1, 0, -1):
        for row in places(2 * STEPS - 1 - n):
            s.backward(n, row)
    for row in places(DEPTH - 1):
        for k, value in s.source_gradient(row):
            gsource[k, pl.ds(row - HALO, TILE), :] = value
    moves[1].start()
    for row in places(DEPTH - 1):
        for k, value in s.gradient(row):
            grad[k, pl.ds(row - HALO, TILE), :] = value
    moves[2].start()
    for move in moves:
        move.wait()


def swaps(count, offset):
    pairs = [(i, (i + 1) % count) for i in range(offset, count, 2)]
    return pairs + [(j, i) for i, j in pairs]


def lat_swaps(lat, lon, offset):
    pairs, alone = [], set(range(lat))
    for i in range(offset, lat - 1, 2):
        alone -= {i, i + 1}
        pairs += [(i * lon + j, (i + 1) * lon + j) for j in range(lon)]
    for i in sorted(alone):
        pairs += [(i * lon + j, i * lon + j + 1) for j in range(0, lon, 2)]
    return pairs + [(j, i) for i, j in pairs]


def body(initial_state, source, cotangent, face_coefs, land_mask, bottom):
    arguments = (initial_state, source, cotangent, face_coefs, land_mask, bottom)
    levels, rows, lanes = initial_state.shape
    c = Names(levels)
    span = rows + 2 * HALO
    f32 = lambda *shape: jax.ShapeDtypeStruct(shape, jnp.float32)
    vmem, hbm = pl.BlockSpec(memory_space=pltpu.VMEM), pl.BlockSpec(memory_space=pltpu.HBM)
    params = pltpu.CompilerParams(vmem_limit_bytes=8 * 1024 * 1024)

    fields, one, two, early = pl.pallas_call(
        functools.partial(pack_kernel, c),
        out_shape=(f32(c.count, rows, lanes), *(f32(c.parts, rows, lanes),) * 2, f32(c.early, TILE, lanes)),
        in_specs=[hbm] * 6,
        out_specs=(vmem,) * 4,
        scratch_shapes=[
            pltpu.VMEM((levels, rows, lanes), jnp.float32),
            pltpu.VMEM((levels, rows, lanes), jnp.float32),
            pltpu.VMEM((2, rows, lanes), jnp.float32),
            pltpu.VMEM((levels, rows, lanes), jnp.int32),
            pltpu.VMEM((rows, lanes), jnp.int32),
            pltpu.SemaphoreType.DMA((6,)),
        ],
        compiler_params=params,
        name="pack",
    )(*(pltpu.with_memory_space_constraint(x, pltpu.HBM) for x in arguments))
    lon, lat = lax.axis_size("lon"), lax.axis_size("lat")
    one = lax.ppermute(one, "lon", swaps(lon, 0))
    two = lax.ppermute(two, "lon", swaps(lon, 1))
    both = ("lat", "lon")
    early_pairs, late_pairs = lat_swaps(lat, lon, 0), lat_swaps(lat, lon, 1)
    early = lax.ppermute(early, both, early_pairs)
    early_strips, late = pl.pallas_call(
        functools.partial(corner_kernel, c),
        out_shape=(f32(c.strips, TILE, lanes), f32(c.late, TILE, lanes)),
        in_specs=[vmem] * 3,
        out_specs=(vmem,) * 2,
        compiler_params=params,
        name="late_rows",
    )(fields, two, one)
    late = lax.ppermute(late, both, late_pairs)
    early_strips = lax.ppermute(early_strips, both, early_pairs)
    twice = lambda *shape: (f32(*shape), f32(*shape))
    shapes = (
        *twice(c.count, span, lanes),
        *twice(span, lanes),
        *twice(levels, span, lanes),
        *twice((2 * STEPS - 1) * levels, span, lanes),
        *twice((STEPS - 1) * levels, span, lanes),
        f32((STEPS - 1) * levels, span, lanes),
        f32(levels, span, lanes),
        f32(levels, rows, lanes),
        f32(levels, rows, lanes),
    )
    own = pl.pallas_call(
        functools.partial(own_kernel, c),
        out_shape=shapes,
        in_specs=[vmem] * 3,
        out_specs=(vmem,) * len(shapes),
        compiler_params=params,
        cost_estimate=pl.CostEstimate(
            flops=2 * STEPS * levels * rows * lanes * 40, bytes_accessed=16 * 2**20, transcendentals=0
        ),
        name="own_rows",
    )(fields, two, one)
    out = pl.pallas_call(
        functools.partial(edge_kernel, c),
        out_shape=(*shapes, *(f32(levels, rows, lanes),) * 3),
        in_specs=[vmem] * (3 + len(shapes)),
        out_specs=(*(vmem,) * len(shapes), hbm, hbm, hbm),
        input_output_aliases={3 + i: i for i in range(len(shapes))},
        scratch_shapes=[pltpu.SemaphoreType.DMA((3,))],
        compiler_params=params,
        name="edge_rows",
    )(late, early, early_strips, *own)
    return tuple(out[len(shapes) :])


def solution(mesh):
    block = P(None, "lat", "lon")
    return jax.shard_map(
        body,
        mesh=mesh,
        in_specs=(block, block, block, block, block, P("lat", "lon")),
        out_specs=(block, block, block),
        check_vma=False,
    )
```

```python
import functools

import jax
import jax.numpy as jnp
from jax import lax
from jax.experimental import pallas as pl
from jax.experimental.pallas import tpu as pltpu
from jax.sharding import PartitionSpec as P

STEPS = 4
DEPTH = 2 * STEPS
TILE = 8
HALO = TILE
PIECE = 2

vertical_coef = 0.04


class Names:
    def __init__(self, levels):
        self.levels = levels
        self.u, self.s, self.wet = 0, levels, 2 * levels
        self.ce, self.cn, self.cot = 3 * levels, 3 * levels + 1, 3 * levels + 2
        self.count = 4 * levels + 2
        self.parts = -(-self.count // 16)
        self.strips = 2 * self.parts
        self.first = self.ce
        self.cot_at = self.strips + 2
        self.second = self.cot_at + -(-levels // 2)


def lane_iota(lanes):
    return lax.broadcasted_iota(jnp.int32, (TILE, lanes), 1)


def shift_of(channel):
    place = channel % 16
    return 2 * DEPTH * (place % 8) + DEPTH * (place // 8)


def even_groups(lanes):
    return lax.rem(lane_iota(lanes) // DEPTH, 2) == 0


def is_odd(axis):
    return lax.rem(lax.axis_index(axis), 2) == 1


def strip_rows(c, m):
    return range(16 * m, min(16 * m + 16, c.count))


def pack_kernel(
    c, u_hbm, s_hbm, a_hbm, c_hbm, land_hbm, bottom_hbm, f_ref, first_ref, second_ref, lat_one_ref, lat_two_ref,
    u_ref, s_ref, c_ref, land_ref, bottom_ref, sems,
):
    levels = c.levels
    _, rows, lanes = u_ref.shape
    pieces = [(bottom_hbm, bottom_ref)]
    groups = [range(k, min(k + PIECE, levels)) for k in range(0, levels, PIECE)]
    for held in groups:
        at = pl.ds(held.start, len(held))
        pieces += [(land_hbm.at[at], land_ref.at[at]), (u_hbm.at[at], u_ref.at[at]), (s_hbm.at[at], s_ref.at[at])]
    pieces.append((c_hbm, c_ref))
    for held in groups:
        pieces.append((a_hbm.at[pl.ds(held.start, len(held))], f_ref.at[pl.ds(c.cot + held.start, len(held))]))
    moves = [pltpu.make_async_copy(source, target, sems.at[i]) for i, (source, target) in enumerate(pieces)]
    for move in moves:
        move.start()
    last_lat = lax.axis_index("lat") == lax.axis_size("lat") - 1
    moves[0].wait()
    for i, held in enumerate(groups):
        for move in moves[1 + 3 * i : 4 + 3 * i]:
            move.wait()
        for k in held:
            wet = jnp.where(k < bottom_ref[...], land_ref[k], 0).astype(jnp.float32)
            f_ref[c.u + k] = wet * u_ref[k]
            f_ref[c.s + k] = wet * s_ref[k]
            f_ref[c.wet + k] = wet
    for move in moves[1 + 3 * len(groups) :]:
        move.wait()
    f_ref[c.ce] = c_ref[0]
    row = lax.broadcasted_iota(jnp.int32, (rows, lanes), 0)
    f_ref[c.cn] = jnp.where(jnp.logical_and(last_lat, row == rows - 1), 0.0, c_ref[1])
    odd = is_odd("lon")
    group, groups = lane_iota(lanes) // DEPTH, lanes // DEPTH
    for t in range(rows // TILE):
        at = pl.ds(t * TILE, TILE)
        for m in range(c.parts):
            east = jnp.zeros((TILE, lanes), jnp.float32)
            west = east
            for channel in strip_rows(c, m):
                shift = shift_of(channel)
                tile = f_ref[channel, at, :]
                if shift:
                    tile = pltpu.roll(tile, shift, 1)
                east = jnp.where(group == shift // DEPTH, tile, east)
                west = jnp.where(group == (shift // DEPTH - 1) % groups, tile, west)
            first_ref[m, at, :] = jnp.where(odd, east, west)
            second_ref[m, at, :] = jnp.where(odd, west, east)
    odd_lat = is_odd("lat")
    for channel in range(c.first):
        high, low = f_ref[channel, pl.ds(rows - TILE, TILE), :], f_ref[channel, pl.ds(0, TILE), :]
        lat_one_ref[channel] = jnp.where(odd_lat, low, high)
        lat_two_ref[channel] = jnp.where(odd_lat, high, low)


def corner_kernel(c, f_ref, one_ref, two_ref, lat_one_ref, lat_two_ref):
    odd_lat, odd_lon = is_odd("lat"), is_odd("lon")
    _, rows, lanes = f_ref.shape
    half = TILE // 2
    first_half = lax.broadcasted_iota(jnp.int32, (TILE, lanes), 0) < half
    low, high = pl.ds(0, TILE), pl.ds(rows - TILE, TILE)

    def put(i, low_tile, high_tile):
        lat_one_ref[i] = jnp.where(odd_lat, low_tile, high_tile)
        lat_two_ref[i] = jnp.where(odd_lat, high_tile, low_tile)

    for m in range(c.parts):
        ends = [(one_ref[m, at, :], two_ref[m, at, :]) for at in (low, high)]
        put(m, *(jnp.where(odd_lon, two, one) for one, two in ends))
        put(c.parts + m, *(jnp.where(odd_lon, one, two) for one, two in ends))
    put(c.strips, f_ref[c.ce, low, :], f_ref[c.ce, high, :])
    put(c.strips + 1, f_ref[c.cn, low, :], f_ref[c.cn, high, :])
    for q in range(c.second - c.cot_at):
        one, two = c.cot + 2 * q, c.cot + min(2 * q + 1, c.levels - 1)
        put(
            c.cot_at + q,
            jnp.where(first_half, f_ref[one, low, :], pltpu.roll(f_ref[two, low, :], half, 0)),
            jnp.where(first_half, pltpu.roll(f_ref[one, high, :], half, 0), f_ref[two, high, :]),
        )


class Sweeps:
    def __init__(self, c, e, w, d, x, m, adj, state):
        self.c, self.e, self.w, self.d, self.x, self.m, self.adj, self.state = c, e, w, d, x, m, adj, state
        self.lanes = e[0].shape[-1]
        lane = lane_iota(self.lanes)
        self.at_first, self.at_last = lane == 0, lane == self.lanes - 1
        self.even_group = even_groups(self.lanes)

    def from_west(self, x0, x1):
        r0, r1 = pltpu.roll(x0, 1, 1), pltpu.roll(x1, 1, 1)
        return jnp.where(self.at_first, r1, r0), jnp.where(self.at_first, r0, r1)

    def from_east(self, x0, x1):
        r0, r1 = pltpu.roll(x0, self.lanes - 1, 1), pltpu.roll(x1, self.lanes - 1, 1)
        return jnp.where(self.at_last, r1, r0), jnp.where(self.at_last, r0, r1)

    def spread(self, row, easts, wests):
        for m, (east, west) in enumerate(zip(easts, wests)):
            both = jnp.where(self.even_group, east, west), jnp.where(self.even_group, west, east)
            for channel in strip_rows(self.c, m):
                shift = shift_of(channel)
                tile = both[(channel % 16) // 8]
                if shift:
                    tile = pltpu.roll(tile, self.lanes - shift, 1)
                self.e[1][channel, pl.ds(row, TILE), :] = tile

    def western(self, row):
        at = pl.ds(row, TILE)
        self.w[0][at, :], self.w[1][at, :] = self.from_west(self.e[0][self.c.ce, at, :], self.e[1][self.c.ce, at, :])

    def neighbours(self, load, row, halves=2):
        c, at = self.c, pl.ds(row, TILE)
        ce = [e[c.ce, at, :] for e in self.e]
        cw = [w[at, :] for w in self.w]
        cn = [e[c.cn, at, :] for e in self.e]
        cs = [e[c.cn, pl.ds(row - 1, TILE), :] for e in self.e]
        own = [(load(0, k, at), load(1, k, at)) for k in range(c.levels)]
        out = []
        for k in range(c.levels):
            east, west = self.from_east(*own[k]), self.from_west(*own[k])
            pair = []
            for h in range(halves):
                north, south = load(h, k, pl.ds(row + 1, TILE)), load(h, k, pl.ds(row - 1, TILE))
                total = (ce[h] * east[h] + cw[h] * west[h]) + (cn[h] * north + cs[h] * south)
                around = [own[j][h] for j in (k - 1, k + 1) if 0 <= j < c.levels]
                pair.append((own[k][h], total + vertical_coef * functools.reduce(jnp.add, around)))
            out.append(pair)
        return out

    def diagonal(self, row):
        load = lambda h, k, at: self.e[h][self.c.wet + k, at, :]
        for k, pair in enumerate(self.neighbours(load, row)):
            for h, (_, total) in enumerate(pair):
                self.d[h][k, pl.ds(row, TILE), :] = 1.0 - total

    def loader(self, index):
        if index == 0:
            return lambda h, k, at: self.e[h][self.c.u + k, at, :]
        base = (index - 1) * self.c.levels
        return lambda h, k, at: self.x[h][base + k, at, :]

    def forward(self, n, row):
        c, at = self.c, pl.ds(row, TILE)
        for k, pair in enumerate(self.neighbours(self.loader(n), row)):
            for h, (own, total) in enumerate(pair):
                e = self.e[h]
                wet = e[c.wet + k, at, :]
                bounded = wet * jnp.tanh(self.d[h][k, at, :] * own + total)
                slope = wet - bounded * bounded
                if n < STEPS - 1:
                    self.x[h][n * c.levels + k, at, :] = bounded + e[c.s + k, at, :]
                    self.m[h][n * c.levels + k, at, :] = slope
                else:
                    if h == 0:
                        self.state[k, at, :] = bounded + e[c.s + k, at, :]
                    self.x[h][n * c.levels + k, at, :] = slope * e[c.cot + k, at, :]

    def backward(self, n, row):
        c, at = self.c, pl.ds(row, TILE)
        index = 2 * STEPS - 1 - n
        for k, pair in enumerate(self.neighbours(self.loader(index), row)):
            for h, (own, total) in enumerate(pair):
                value = self.d[h][k, at, :] * own + total
                if h == 0:
                    self.adj[(n - 1) * c.levels + k, at, :] = value
                self.x[h][index * c.levels + k, at, :] = self.m[h][(n - 1) * c.levels + k, at, :] * value

    def gradient(self, row):
        c, at = self.c, pl.ds(row, TILE)
        for k, pair in enumerate(self.neighbours(self.loader(2 * STEPS - 1), row, 1)):
            own, total = pair[0]
            yield k, self.e[0][c.wet + k, at, :] * (self.d[0][k, at, :] * own + total)

    def source_gradient(self, row):
        c, at = self.c, pl.ds(row, TILE)
        for k in range(c.levels):
            total = self.e[0][c.cot + k, at, :]
            for n in range(STEPS - 1):
                total = total + self.adj[n * c.levels + k, at, :]
            yield k, self.e[0][c.wet + k, at, :] * total


def own_kernel(c, f_ref, one_ref, two_ref, e0, e1, w0, w1, d0, d1, x0, x1, m0, m1, adj, state, grad, gsource):
    rows = f_ref.shape[1]
    odd_lon = is_odd("lon")
    s = Sweeps(c, (e0, e1), (w0, w1), (d0, d1), (x0, x1), (m0, m1), adj, state)
    zero = jnp.zeros((TILE, f_ref.shape[2]), jnp.float32)
    for ref in (e0, e1):
        for end in (pl.ds(0, TILE), pl.ds(HALO + rows, TILE)):
            for channel in (*range(c.u, c.u + c.levels), *range(c.wet, c.wet + c.levels), c.cn):
                ref[channel, end, :] = zero
    tiles = rows // TILE
    places = [HALO + t * TILE for t in range(tiles)]
    for t, row in enumerate(places):
        at, to = pl.ds(t * TILE, TILE), pl.ds(row, TILE)
        for channel in range(c.count):
            e0[channel, to, :] = f_ref[channel, at, :]
        pairs = [(one_ref[m, at, :], two_ref[m, at, :]) for m in range(c.parts)]
        s.spread(
            row,
            [jnp.where(odd_lon, two, one) for one, two in pairs],
            [jnp.where(odd_lon, one, two) for one, two in pairs],
        )
        s.western(row)
    for row in places:
        s.diagonal(row)
    for n in range(STEPS):
        for row in places:
            s.forward(n, row)
    for n in range(STEPS - 1, 0, -1):
        for row in places:
            s.backward(n, row)
    for row in places[1:-1]:
        at = pl.ds(row - HALO, TILE)
        for k, value in s.source_gradient(row):
            gsource[k, at, :] = value
        for k, value in s.gradient(row):
            grad[k, at, :] = value


def edge_kernel(
    c, first_one, first_two, second_two, second_one, *refs,
):
    aliased = refs[: len(refs) // 2]
    del aliased
    e0, e1, w0, w1, d0, d1, x0, x1, m0, m1, adj, state, grad, gsource, state_hbm, grad_hbm, gsource_hbm, sems = refs[14:]
    rows = grad.shape[1]
    s = Sweeps(c, (e0, e1), (w0, w1), (d0, d1), (x0, x1), (m0, m1), adj, state)
    moves = []

    def send(ref, skip, target, at, many):
        move = pltpu.make_async_copy(
            ref.at[:, pl.ds(skip + at, many), :], target.at[:, pl.ds(at, many), :], sems.at[len(moves)]
        )
        move.start()
        moves.append(move)

    def send_edges(ref, skip, target):
        send(ref, skip, target, 0, TILE)
        send(ref, skip, target, rows - TILE, TILE)

    inner = rows - 2 * TILE
    send(state, HALO, state_hbm, TILE, inner)
    send(gsource, 0, gsource_hbm, TILE, inner)
    send(grad, 0, grad_hbm, TILE, inner)
    odd_lat = is_odd("lat")
    for row, low in ((0, True), (HALO + rows, False)):
        pole = lax.axis_index("lat") == (0 if low else lax.axis_size("lat") - 1)
        from_one = odd_lat if low else jnp.logical_not(odd_lat)
        to = pl.ds(row, TILE)

        def got(one, two, i):
            return jnp.where(pole, 0.0, jnp.where(from_one, one[i], two[i]))

        second = [got(second_one, second_two, i) for i in range(c.second)]
        for channel in range(c.first):
            e0[channel, to, :] = got(first_one, first_two, channel)
        e0[c.ce, to, :], e0[c.cn, to, :] = second[c.strips : c.cot_at]
        for k in range(c.levels):
            tile = second[c.cot_at + k // 2]
            if (k % 2 == 0) == low:
                tile = pltpu.roll(tile, TILE // 2, 0)
            e0[c.cot + k, to, :] = tile
        s.spread(row, second[: c.parts], second[c.parts : c.strips])
        s.western(row)
    top = lambda i: HALO + i - (DEPTH - 1)
    bottom = lambda i: HALO + rows - 1 - i
    places = lambda i: (top(i), bottom(i))
    for row in places(0):
        s.diagonal(row)
    for n in range(STEPS):
        for row in places(n):
            s.forward(n, row)
    send_edges(state, HALO, state_hbm)
    for n in range(STEPS - 1, 0, -1):
        for row in places(2 * STEPS - 1 - n):
            s.backward(n, row)
    for row in places(DEPTH - 1):
        for k, value in s.source_gradient(row):
            gsource[k, pl.ds(row - HALO, TILE), :] = value
    send_edges(gsource, 0, gsource_hbm)
    for row in places(DEPTH - 1):
        for k, value in s.gradient(row):
            grad[k, pl.ds(row - HALO, TILE), :] = value
    send_edges(grad, 0, grad_hbm)
    for move in moves:
        move.wait()


def swaps(count, offset):
    pairs = [(i, (i + 1) % count) for i in range(offset, count, 2)]
    return pairs + [(j, i) for i, j in pairs]


def lat_swaps(lat, lon, offset):
    pairs, alone = [], set(range(lat))
    for i in range(offset, lat - 1, 2):
        alone -= {i, i + 1}
        pairs += [(i * lon + j, (i + 1) * lon + j) for j in range(lon)]
    for i in sorted(alone):
        pairs += [(i * lon + j, i * lon + j + 1) for j in range(0, lon, 2)]
    return pairs + [(j, i) for i, j in pairs]


def body(initial_state, source, cotangent, face_coefs, land_mask, bottom):
    arguments = (initial_state, source, cotangent, face_coefs, land_mask, bottom)
    levels, rows, lanes = initial_state.shape
    c = Names(levels)
    span = rows + 2 * HALO
    f32 = lambda *shape: jax.ShapeDtypeStruct(shape, jnp.float32)
    vmem, hbm = pl.BlockSpec(memory_space=pltpu.VMEM), pl.BlockSpec(memory_space=pltpu.HBM)
    params = pltpu.CompilerParams(vmem_limit_bytes=8 * 1024 * 1024)

    fields, one, two, lat_one, lat_two = pl.pallas_call(
        functools.partial(pack_kernel, c),
        out_shape=(f32(c.count, rows, lanes), *(f32(c.parts, rows, lanes),) * 2, *(f32(c.first, TILE, lanes),) * 2),
        in_specs=[hbm] * 6,
        out_specs=(vmem,) * 5,
        scratch_shapes=[
            pltpu.VMEM((levels, rows, lanes), jnp.float32),
            pltpu.VMEM((levels, rows, lanes), jnp.float32),
            pltpu.VMEM((2, rows, lanes), jnp.float32),
            pltpu.VMEM((levels, rows, lanes), jnp.int32),
            pltpu.VMEM((rows, lanes), jnp.int32),
            pltpu.SemaphoreType.DMA((2 + 4 * -(-levels // PIECE),)),
        ],
        compiler_params=params,
        name="pack",
    )(*(pltpu.with_memory_space_constraint(x, pltpu.HBM) for x in arguments))
    lon, lat = lax.axis_size("lon"), lax.axis_size("lat")
    one = lax.ppermute(one, "lon", swaps(lon, 0))
    two = lax.ppermute(two, "lon", swaps(lon, 1))
    both = ("lat", "lon")
    lat_pairs, other_pairs = lat_swaps(lat, lon, 0), lat_swaps(lat, lon, 1)
    first = lax.ppermute(lat_one, both, lat_pairs), lax.ppermute(lat_two, both, other_pairs)
    lat_one, lat_two = pl.pallas_call(
        functools.partial(corner_kernel, c),
        out_shape=(f32(c.second, TILE, lanes),) * 2,
        in_specs=[vmem] * 3,
        out_specs=(vmem,) * 2,
        compiler_params=params,
        name="corners",
    )(fields, one, two)
    second = lax.ppermute(lat_one, both, lat_pairs), lax.ppermute(lat_two, both, other_pairs)
    twice = lambda *shape: (f32(*shape), f32(*shape))
    shapes = (
        *twice(c.count, span, lanes),
        *twice(span, lanes),
        *twice(levels, span, lanes),
        *twice((2 * STEPS - 1) * levels, span, lanes),
        *twice((STEPS - 1) * levels, span, lanes),
        f32((STEPS - 1) * levels, span, lanes),
        f32(levels, span, lanes),
        f32(levels, rows, lanes),
        f32(levels, rows, lanes),
    )
    own = pl.pallas_call(
        functools.partial(own_kernel, c),
        out_shape=shapes,
        in_specs=[vmem] * 3,
        out_specs=(vmem,) * len(shapes),
        compiler_params=params,
        cost_estimate=pl.CostEstimate(
            flops=2 * STEPS * levels * rows * lanes * 40, bytes_accessed=16 * 2**20, transcendentals=0
        ),
        name="own_rows",
    )(fields, one, two)
    out = pl.pallas_call(
        functools.partial(edge_kernel, c),
        out_shape=(*shapes, *(f32(levels, rows, lanes),) * 3),
        in_specs=[vmem] * (4 + len(shapes)),
        out_specs=(*(vmem,) * len(shapes), hbm, hbm, hbm),
        input_output_aliases={4 + i: i for i in range(len(shapes))},
        scratch_shapes=[pltpu.SemaphoreType.DMA((9,))],
        compiler_params=params,
        name="edge_rows",
    )(*first, *second[::-1], *own)
    return tuple(out[len(shapes) :])


def solution(mesh):
    block = P(None, "lat", "lon")
    return jax.shard_map(
        body,
        mesh=mesh,
        in_specs=(block, block, block, block, block, P("lat", "lon")),
        out_specs=(block, block, block),
        check_vma=False,
    )
```

```python
import functools

import jax
import jax.numpy as jnp
from jax import lax
from jax.experimental import pallas as pl
from jax.experimental.pallas import tpu as pltpu
from jax.sharding import PartitionSpec as P

STEPS = 4
DEPTH = 2 * STEPS
TILE = 8
HALO = TILE
BLOCK = 2 * DEPTH
PIECE = 2

vertical_coef = 0.04


class Names:
    def __init__(self, levels):
        self.levels = levels
        self.u, self.s, self.wet = 0, levels, 2 * levels
        self.ce, self.cn, self.cot = 3 * levels, 3 * levels + 1, 3 * levels + 2
        self.count = 4 * levels + 2
        assert levels <= 6
        self.parts, self.face_place = 2, 6
        self.strips = 2 * self.parts
        self.first = self.ce
        self.cot_at = self.strips + 2
        self.second = self.cot_at + -(-levels // 2)

    def places(self, part):
        low, face, high = ((self.u, self.ce, self.s), (self.wet, self.cn, self.cot))[part]
        return [
            *((k, low + k) for k in range(self.levels)),
            (self.face_place, face),
            *((8 + k, high + k) for k in range(self.levels)),
        ]


def lane_iota(lanes):
    return lax.broadcasted_iota(jnp.int32, (TILE, lanes), 1)


def shift_of(place):
    return BLOCK * (place % 8) + DEPTH * (place // 8)


def even_groups(lanes):
    return lax.rem(lane_iota(lanes) // DEPTH, 2) == 0


def is_odd(axis):
    return lax.rem(lax.axis_index(axis), 2) == 1


def pack_kernel(
    c, u_hbm, s_hbm, a_hbm, c_hbm, land_hbm, bottom_hbm, f_ref, first_ref, second_ref, lat_one_ref, lat_two_ref,
    u_ref, s_ref, c_ref, land_ref, bottom_ref, sems,
):
    levels = c.levels
    _, rows, lanes = u_ref.shape
    pieces = [(bottom_hbm, bottom_ref)]
    groups = [range(k, min(k + PIECE, levels)) for k in range(0, levels, PIECE)]
    for held in groups:
        at = pl.ds(held.start, len(held))
        pieces += [(land_hbm.at[at], land_ref.at[at]), (u_hbm.at[at], u_ref.at[at]), (s_hbm.at[at], s_ref.at[at])]
    pieces.append((c_hbm, c_ref))
    for held in groups:
        pieces.append((a_hbm.at[pl.ds(held.start, len(held))], f_ref.at[pl.ds(c.cot + held.start, len(held))]))
    moves = [pltpu.make_async_copy(source, target, sems.at[i]) for i, (source, target) in enumerate(pieces)]
    for move in moves:
        move.start()
    last_lat = lax.axis_index("lat") == lax.axis_size("lat") - 1
    moves[0].wait()
    for i, held in enumerate(groups):
        for move in moves[1 + 3 * i : 4 + 3 * i]:
            move.wait()
        for k in held:
            wet = jnp.where(k < bottom_ref[...], land_ref[k], 0).astype(jnp.float32)
            f_ref[c.u + k] = wet * u_ref[k]
            f_ref[c.s + k] = wet * s_ref[k]
            f_ref[c.wet + k] = wet
    for move in moves[1 + 3 * len(groups) :]:
        move.wait()
    f_ref[c.ce] = c_ref[0]
    row = lax.broadcasted_iota(jnp.int32, (rows, lanes), 0)
    f_ref[c.cn] = jnp.where(jnp.logical_and(last_lat, row == rows - 1), 0.0, c_ref[1])
    odd = is_odd("lon")
    group, groups = lane_iota(lanes) // DEPTH, lanes // DEPTH
    for t in range(rows // TILE):
        at = pl.ds(t * TILE, TILE)
        for m in range(c.parts):
            east = jnp.zeros((TILE, lanes), jnp.float32)
            west = east
            for place, channel in c.places(m):
                shift = shift_of(place)
                tile = f_ref[channel, at, :]
                if shift:
                    tile = pltpu.roll(tile, shift, 1)
                east = jnp.where(group == shift // DEPTH, tile, east)
                west = jnp.where(group == (shift // DEPTH - 1) % groups, tile, west)
            first_ref[m, at, :] = jnp.where(odd, east, west)
            second_ref[m, at, :] = jnp.where(odd, west, east)
    odd_lat = is_odd("lat")
    for channel in range(c.first):
        high, low = f_ref[channel, pl.ds(rows - TILE, TILE), :], f_ref[channel, pl.ds(0, TILE), :]
        lat_one_ref[channel] = jnp.where(odd_lat, low, high)
        lat_two_ref[channel] = jnp.where(odd_lat, high, low)


def corner_kernel(c, f_ref, one_ref, two_ref, lat_one_ref, lat_two_ref):
    odd_lat, odd_lon = is_odd("lat"), is_odd("lon")
    _, rows, lanes = f_ref.shape
    half = TILE // 2
    first_half = lax.broadcasted_iota(jnp.int32, (TILE, lanes), 0) < half
    low, high = pl.ds(0, TILE), pl.ds(rows - TILE, TILE)

    def put(i, low_tile, high_tile):
        lat_one_ref[i] = jnp.where(odd_lat, low_tile, high_tile)
        lat_two_ref[i] = jnp.where(odd_lat, high_tile, low_tile)

    for m in range(c.parts):
        ends = [(one_ref[m, at, :], two_ref[m, at, :]) for at in (low, high)]
        put(m, *(jnp.where(odd_lon, two, one) for one, two in ends))
        put(c.parts + m, *(jnp.where(odd_lon, one, two) for one, two in ends))
    put(c.strips, f_ref[c.ce, low, :], f_ref[c.ce, high, :])
    put(c.strips + 1, f_ref[c.cn, low, :], f_ref[c.cn, high, :])
    for q in range(c.second - c.cot_at):
        one, two = c.cot + 2 * q, c.cot + min(2 * q + 1, c.levels - 1)
        put(
            c.cot_at + q,
            jnp.where(first_half, f_ref[one, low, :], pltpu.roll(f_ref[two, low, :], half, 0)),
            jnp.where(first_half, pltpu.roll(f_ref[one, high, :], half, 0), f_ref[two, high, :]),
        )


SU, SS, SWET, SCOT, SCE, SCN = range(6)


class Sweeps:
    def __init__(self, c, e, w, d, x, m, adj, state, direct):
        self.c, self.adj, self.state, self.direct = c, adj, state, direct
        (self.e, self.es), (self.w, self.ws), (self.d, self.ds), (self.x, self.xs), (self.m, self.ms) = e, w, d, x, m
        self.lanes = self.e.shape[-1]
        lane = lane_iota(self.lanes)
        self.lane = lane
        self.at_first, self.at_last = lane == 0, lane == self.lanes - 1
        self.even_group = even_groups(self.lanes)
        self.block_first, self.block_last = lax.rem(lane, BLOCK) == 0, lax.rem(lane, BLOCK) == BLOCK - 1
        self.used = jnp.logical_or(lane >= self.lanes - DEPTH, lane < BLOCK * (c.levels - 1) + DEPTH)

    def roll(self, tile, shift):
        shift %= self.lanes
        return pltpu.roll(tile, shift, 1) if shift else tile

    def repeat(self, tile):
        shift = BLOCK
        while shift < self.lanes:
            tile = tile + self.roll(tile, shift)
            shift *= 2
        return tile

    def spread(self, row, easts, wests):
        c, at = self.c, pl.ds(row, TILE)
        face = BLOCK * c.face_place
        in_face = jnp.logical_and(self.lane >= face - DEPTH, self.lane < face + DEPTH)
        for (low, high, coef), east, west in zip(((SU, SS, SCE), (SWET, SCOT, SCN)), easts, wests):
            near = jnp.where(self.even_group, east, west)
            far = self.roll(jnp.where(self.even_group, west, east), -DEPTH)
            self.es[low, at, :] = jnp.where(self.used, near, 0.0)
            self.es[high, at, :] = jnp.where(self.used, far, 0.0)
            self.es[coef, at, :] = self.repeat(jnp.where(in_face, near, 0.0))

    def western(self, row):
        at = pl.ds(row, TILE)
        own, strip = self.roll(self.e[self.c.ce, at, :], 1), self.roll(self.es[SCE, at, :], 1)
        self.w[at, :] = jnp.where(self.at_first, strip, own)
        self.ws[at, :] = jnp.where(self.block_first, self.repeat(jnp.where(self.at_first, own, 0.0)), strip)

    def blocks(self, tiles):
        out = tiles[0]
        for k in range(1, self.c.levels):
            begin = BLOCK * k - DEPTH
            here = jnp.logical_and(self.lane >= begin, self.lane < begin + BLOCK)
            out = jnp.where(here, tiles[k], out)
        return out

    def along_lon(self, own, strip, strips):
        levels = range(self.c.levels)
        if self.direct:
            east = [jnp.where(self.at_last, self.roll(strip, -1 - BLOCK * k), self.roll(own[k], -1)) for k in levels]
            west = [jnp.where(self.at_first, self.roll(strip, 1 - BLOCK * k), self.roll(own[k], 1)) for k in levels]
            if strips:
                inward = self.blocks([self.roll(own[k], BLOCK * k - 1) for k in levels])
                east.append(jnp.where(self.block_last, inward, self.roll(strip, -1)))
                inward = self.blocks([self.roll(own[k], BLOCK * k + 1) for k in levels])
                west.append(jnp.where(self.block_first, inward, self.roll(strip, 1)))
            return east, west
        outward = [self.roll(strip, -BLOCK * k) for k in levels]
        east = [self.roll(jnp.where(self.at_first, outward[k], own[k]), -1) for k in levels]
        west = [self.roll(jnp.where(self.at_last, outward[k], own[k]), 1) for k in levels]
        if strips:
            inward = self.blocks([self.roll(own[k], BLOCK * k) for k in levels])
            east.append(self.roll(jnp.where(self.block_first, inward, strip), -1))
            west.append(self.roll(jnp.where(self.block_last, inward, strip), 1))
        return east, west

    def neighbours(self, load, row, strips=True):
        c, at = self.c, pl.ds(row, TILE)
        levels = range(c.levels)
        north, south = pl.ds(row + 1, TILE), pl.ds(row - 1, TILE)
        own, strip = [load(k, at) for k in levels], load(None, at)
        east, west = self.along_lon(own, strip, strips)

        def total(faces, i, k, around):
            ce, cw, cn, cs = faces
            sides = (ce * east[i] + cw * west[i]) + (cn * load(k, north) + cs * load(k, south))
            return sides + vertical_coef * around

        faces = (self.e[c.ce, at, :], self.w[at, :], self.e[c.cn, at, :], self.e[c.cn, south, :])
        out = []
        for k in levels:
            around = functools.reduce(jnp.add, [own[j] for j in (k - 1, k + 1) if 0 <= j < c.levels])
            out.append((own[k], total(faces, k, k, around)))
        if strips:
            faces = (self.es[SCE, at, :], self.ws[at, :], self.es[SCN, at, :], self.es[SCN, south, :])
            around = self.roll(strip, BLOCK) + self.roll(strip, -BLOCK)
            out.append((strip, total(faces, c.levels, None, around)))
        return out

    def loader(self, own, base, strips, at_strip):
        return lambda k, at: strips[at_strip, at, :] if k is None else own[base + k, at, :]

    def state_loader(self, index):
        if index == 0:
            return self.loader(self.e, self.c.u, self.es, SU)
        return self.loader(self.x, (index - 1) * self.c.levels, self.xs, index - 1)

    def diagonal(self, row):
        at = pl.ds(row, TILE)
        *own, strip = self.neighbours(self.loader(self.e, self.c.wet, self.es, SWET), row)
        for k, (_, total) in enumerate(own):
            self.d[k, at, :] = 1.0 - total
        self.ds[at, :] = 1.0 - strip[1]

    def forward(self, n, row):
        c, at = self.c, pl.ds(row, TILE)

        def step(pair, d, wet):
            bounded = wet * jnp.tanh(d * pair[0] + pair[1])
            return bounded, wet - bounded * bounded

        *own, strip = self.neighbours(self.state_loader(n), row)
        for k, pair in enumerate(own):
            bounded, slope = step(pair, self.d[k, at, :], self.e[c.wet + k, at, :])
            value = bounded + self.e[c.s + k, at, :]
            if n < STEPS - 1:
                self.x[n * c.levels + k, at, :] = value
                self.m[n * c.levels + k, at, :] = slope
            else:
                self.state[k, at, :] = value
                self.x[n * c.levels + k, at, :] = slope * self.e[c.cot + k, at, :]
        bounded, slope = step(strip, self.ds[at, :], self.es[SWET, at, :])
        if n < STEPS - 1:
            self.xs[n, at, :] = bounded + self.es[SS, at, :]
            self.ms[n, at, :] = slope
        else:
            self.xs[n, at, :] = slope * self.es[SCOT, at, :]

    def backward(self, n, row):
        c, at = self.c, pl.ds(row, TILE)
        index = 2 * STEPS - 1 - n
        *own, strip = self.neighbours(self.state_loader(index), row)
        for k, (field, total) in enumerate(own):
            value = self.d[k, at, :] * field + total
            self.adj[(n - 1) * c.levels + k, at, :] = value
            self.x[index * c.levels + k, at, :] = self.m[(n - 1) * c.levels + k, at, :] * value
        self.xs[index, at, :] = self.ms[n - 1, at, :] * (self.ds[at, :] * strip[0] + strip[1])

    def gradient(self, row):
        c, at = self.c, pl.ds(row, TILE)
        for k, (field, total) in enumerate(self.neighbours(self.state_loader(2 * STEPS - 1), row, False)):
            yield k, self.e[c.wet + k, at, :] * (self.d[k, at, :] * field + total)

    def source_gradient(self, row):
        c, at = self.c, pl.ds(row, TILE)
        for k in range(c.levels):
            total = self.e[c.cot + k, at, :]
            for n in range(STEPS - 1):
                total = total + self.adj[n * c.levels + k, at, :]
            yield k, self.e[c.wet + k, at, :] * total


def own_kernel(c, f_ref, one_ref, two_ref, e0, e1, w0, w1, d0, d1, x0, x1, m0, m1, adj, state, grad, gsource):
    rows = f_ref.shape[1]
    odd_lon = is_odd("lon")
    s = Sweeps(c, (e0, e1), (w0, w1), (d0, d1), (x0, x1), (m0, m1), adj, state, False)
    zero = jnp.zeros((TILE, f_ref.shape[2]), jnp.float32)
    for end in (pl.ds(0, TILE), pl.ds(HALO + rows, TILE)):
        for channel in (*range(c.u, c.u + c.levels), *range(c.wet, c.wet + c.levels), c.cn):
            e0[channel, end, :] = zero
        for strip in (SU, SWET, SCN):
            e1[strip, end, :] = zero
    tiles = rows // TILE
    places = [HALO + t * TILE for t in range(tiles)]
    for t, row in enumerate(places):
        at, to = pl.ds(t * TILE, TILE), pl.ds(row, TILE)
        for channel in range(c.count):
            e0[channel, to, :] = f_ref[channel, at, :]
        pairs = [(one_ref[m, at, :], two_ref[m, at, :]) for m in range(c.parts)]
        s.spread(
            row,
            [jnp.where(odd_lon, two, one) for one, two in pairs],
            [jnp.where(odd_lon, one, two) for one, two in pairs],
        )
        s.western(row)
    for row in places:
        s.diagonal(row)
    for n in range(STEPS):
        for row in places:
            s.forward(n, row)
    for n in range(STEPS - 1, 0, -1):
        for row in places:
            s.backward(n, row)
    for row in places[1:-1]:
        at = pl.ds(row - HALO, TILE)
        for k, value in s.source_gradient(row):
            gsource[k, at, :] = value
        for k, value in s.gradient(row):
            grad[k, at, :] = value


def edge_kernel(
    c, first_one, first_two, second_two, second_one, *refs,
):
    aliased = refs[: len(refs) // 2]
    del aliased
    e0, e1, w0, w1, d0, d1, x0, x1, m0, m1, adj, state, grad, gsource, state_hbm, grad_hbm, gsource_hbm, sems = refs[14:]
    rows = grad.shape[1]
    s = Sweeps(c, (e0, e1), (w0, w1), (d0, d1), (x0, x1), (m0, m1), adj, state, True)
    moves = []

    def send(ref, skip, target, at, many):
        move = pltpu.make_async_copy(
            ref.at[:, pl.ds(skip + at, many), :], target.at[:, pl.ds(at, many), :], sems.at[len(moves)]
        )
        move.start()
        moves.append(move)

    def send_edges(ref, skip, target):
        send(ref, skip, target, 0, TILE)
        send(ref, skip, target, rows - TILE, TILE)

    inner = rows - 2 * TILE
    send(state, HALO, state_hbm, TILE, inner)
    send(gsource, 0, gsource_hbm, TILE, inner)
    send(grad, 0, grad_hbm, TILE, inner)
    odd_lat = is_odd("lat")
    for row, low in ((0, True), (HALO + rows, False)):
        pole = lax.axis_index("lat") == (0 if low else lax.axis_size("lat") - 1)
        from_one = odd_lat if low else jnp.logical_not(odd_lat)
        to = pl.ds(row, TILE)

        def got(one, two, i):
            return jnp.where(pole, 0.0, jnp.where(from_one, one[i], two[i]))

        second = [got(second_one, second_two, i) for i in range(c.second)]
        for channel in range(c.first):
            e0[channel, to, :] = got(first_one, first_two, channel)
        e0[c.ce, to, :], e0[c.cn, to, :] = second[c.strips : c.cot_at]
        for k in range(c.levels):
            tile = second[c.cot_at + k // 2]
            if (k % 2 == 0) == low:
                tile = pltpu.roll(tile, TILE // 2, 0)
            e0[c.cot + k, to, :] = tile
        s.spread(row, second[: c.parts], second[c.parts : c.strips])
        s.western(row)
    top = lambda i: HALO + i - (DEPTH - 1)
    bottom = lambda i: HALO + rows - 1 - i
    places = lambda i: (top(i), bottom(i))
    for row in places(0):
        s.diagonal(row)
    for n in range(STEPS):
        for row in places(n):
            s.forward(n, row)
    send_edges(state, HALO, state_hbm)
    for n in range(STEPS - 1, 0, -1):
        for row in places(2 * STEPS - 1 - n):
            s.backward(n, row)
    for row in places(DEPTH - 1):
        for k, value in s.source_gradient(row):
            gsource[k, pl.ds(row - HALO, TILE), :] = value
    send_edges(gsource, 0, gsource_hbm)
    for row in places(DEPTH - 1):
        for k, value in s.gradient(row):
            grad[k, pl.ds(row - HALO, TILE), :] = value
    send_edges(grad, 0, grad_hbm)
    for move in moves:
        move.wait()


def swaps(count, offset):
    pairs = [(i, (i + 1) % count) for i in range(offset, count, 2)]
    return pairs + [(j, i) for i, j in pairs]


def lat_swaps(lat, lon, offset):
    pairs, alone = [], set(range(lat))
    for i in range(offset, lat - 1, 2):
        alone -= {i, i + 1}
        pairs += [(i * lon + j, (i + 1) * lon + j) for j in range(lon)]
    for i in sorted(alone):
        pairs += [(i * lon + j, i * lon + j + 1) for j in range(0, lon, 2)]
    return pairs + [(j, i) for i, j in pairs]


def body(initial_state, source, cotangent, face_coefs, land_mask, bottom):
    arguments = (initial_state, source, cotangent, face_coefs, land_mask, bottom)
    levels, rows, lanes = initial_state.shape
    c = Names(levels)
    span = rows + 2 * HALO
    f32 = lambda *shape: jax.ShapeDtypeStruct(shape, jnp.float32)
    vmem, hbm = pl.BlockSpec(memory_space=pltpu.VMEM), pl.BlockSpec(memory_space=pltpu.HBM)
    params = pltpu.CompilerParams(vmem_limit_bytes=8 * 1024 * 1024)

    fields, one, two, lat_one, lat_two = pl.pallas_call(
        functools.partial(pack_kernel, c),
        out_shape=(f32(c.count, rows, lanes), *(f32(c.parts, rows, lanes),) * 2, *(f32(c.first, TILE, lanes),) * 2),
        in_specs=[hbm] * 6,
        out_specs=(vmem,) * 5,
        scratch_shapes=[
            pltpu.VMEM((levels, rows, lanes), jnp.float32),
            pltpu.VMEM((levels, rows, lanes), jnp.float32),
            pltpu.VMEM((2, rows, lanes), jnp.float32),
            pltpu.VMEM((levels, rows, lanes), jnp.int32),
            pltpu.VMEM((rows, lanes), jnp.int32),
            pltpu.SemaphoreType.DMA((2 + 4 * -(-levels // PIECE),)),
        ],
        compiler_params=params,
        name="pack",
    )(*(pltpu.with_memory_space_constraint(x, pltpu.HBM) for x in arguments))
    lon, lat = lax.axis_size("lon"), lax.axis_size("lat")
    one = lax.ppermute(one, "lon", swaps(lon, 0))
    two = lax.ppermute(two, "lon", swaps(lon, 1))
    both = ("lat", "lon")
    lat_pairs, other_pairs = lat_swaps(lat, lon, 0), lat_swaps(lat, lon, 1)
    first = lax.ppermute(lat_one, both, lat_pairs), lax.ppermute(lat_two, both, other_pairs)
    lat_one, lat_two = pl.pallas_call(
        functools.partial(corner_kernel, c),
        out_shape=(f32(c.second, TILE, lanes),) * 2,
        in_specs=[vmem] * 3,
        out_specs=(vmem,) * 2,
        compiler_params=params,
        name="corners",
    )(fields, one, two)
    second = lax.ppermute(lat_one, both, lat_pairs), lax.ppermute(lat_two, both, other_pairs)
    shapes = (
        f32(c.count, span, lanes),
        f32(6, span, lanes),
        f32(span, lanes),
        f32(span, lanes),
        f32(levels, span, lanes),
        f32(span, lanes),
        f32((2 * STEPS - 1) * levels, span, lanes),
        f32(2 * STEPS - 1, span, lanes),
        f32((STEPS - 1) * levels, span, lanes),
        f32(STEPS - 1, span, lanes),
        f32((STEPS - 1) * levels, span, lanes),
        f32(levels, span, lanes),
        f32(levels, rows, lanes),
        f32(levels, rows, lanes),
    )
    own = pl.pallas_call(
        functools.partial(own_kernel, c),
        out_shape=shapes,
        in_specs=[vmem] * 3,
        out_specs=(vmem,) * len(shapes),
        compiler_params=params,
        cost_estimate=pl.CostEstimate(
            flops=2 * STEPS * levels * rows * lanes * 40, bytes_accessed=16 * 2**20, transcendentals=0
        ),
        name="own_rows",
    )(fields, one, two)
    out = pl.pallas_call(
        functools.partial(edge_kernel, c),
        out_shape=(*shapes, *(f32(levels, rows, lanes),) * 3),
        in_specs=[vmem] * (4 + len(shapes)),
        out_specs=(*(vmem,) * len(shapes), hbm, hbm, hbm),
        input_output_aliases={4 + i: i for i in range(len(shapes))},
        scratch_shapes=[pltpu.SemaphoreType.DMA((9,))],
        compiler_params=params,
        name="edge_rows",
    )(*first, *second[::-1], *own)
    return tuple(out[len(shapes) :])


def solution(mesh):
    block = P(None, "lat", "lon")
    return jax.shard_map(
        body,
        mesh=mesh,
        in_specs=(block, block, block, block, block, P("lat", "lon")),
        out_specs=(block, block, block),
        check_vma=False,
    )
```

```python
import functools

import jax
import jax.numpy as jnp
from jax import lax
from jax.experimental import pallas as pl
from jax.experimental.pallas import tpu as pltpu
from jax.sharding import PartitionSpec as P

STEPS = 4
DEPTH = 2 * STEPS
TILE = 8
HALO = TILE
PIECE = 2

vertical_coef = 0.04


class Names:
    def __init__(self, levels):
        self.levels = levels
        self.u, self.s, self.wet = 0, levels, 2 * levels
        self.ce, self.cn, self.cot = 3 * levels, 3 * levels + 1, 3 * levels + 2
        self.count = 4 * levels + 2
        self.parts = -(-self.count // 16)
        self.strips = 2 * self.parts
        self.first = self.ce
        self.cot_at = self.strips + 2
        self.second = self.cot_at + -(-levels // 2)


def lane_iota(lanes):
    return lax.broadcasted_iota(jnp.int32, (TILE, lanes), 1)


def shift_of(channel):
    place = channel % 16
    return 2 * DEPTH * (place % 8) + DEPTH * (place // 8)


def even_groups(lanes):
    return lax.rem(lane_iota(lanes) // DEPTH, 2) == 0


def is_odd(axis):
    return lax.rem(lax.axis_index(axis), 2) == 1


def strip_rows(c, m):
    return range(16 * m, min(16 * m + 16, c.count))


def pack_kernel(
    c, u_hbm, s_hbm, a_hbm, c_hbm, land_hbm, bottom_hbm, f_ref, first_ref, second_ref, lat_one_ref, lat_two_ref,
    u_ref, s_ref, c_ref, land_ref, bottom_ref, sems,
):
    levels = c.levels
    _, rows, lanes = u_ref.shape
    pieces = [(bottom_hbm, bottom_ref)]
    groups = [range(k, min(k + PIECE, levels)) for k in range(0, levels, PIECE)]
    for held in groups:
        at = pl.ds(held.start, len(held))
        pieces += [(land_hbm.at[at], land_ref.at[at]), (u_hbm.at[at], u_ref.at[at]), (s_hbm.at[at], s_ref.at[at])]
    pieces.append((c_hbm, c_ref))
    for held in groups:
        pieces.append((a_hbm.at[pl.ds(held.start, len(held))], f_ref.at[pl.ds(c.cot + held.start, len(held))]))
    moves = [pltpu.make_async_copy(source, target, sems.at[i]) for i, (source, target) in enumerate(pieces)]
    for move in moves:
        move.start()
    last_lat = lax.axis_index("lat") == lax.axis_size("lat") - 1
    moves[0].wait()
    for i, held in enumerate(groups):
        for move in moves[1 + 3 * i : 4 + 3 * i]:
            move.wait()
        for k in held:
            wet = jnp.where(k < bottom_ref[...], land_ref[k], 0).astype(jnp.float32)
            f_ref[c.u + k] = wet * u_ref[k]
            f_ref[c.s + k] = wet * s_ref[k]
            f_ref[c.wet + k] = wet
    for move in moves[1 + 3 * len(groups) :]:
        move.wait()
    f_ref[c.ce] = c_ref[0]
    row = lax.broadcasted_iota(jnp.int32, (rows, lanes), 0)
    f_ref[c.cn] = jnp.where(jnp.logical_and(last_lat, row == rows - 1), 0.0, c_ref[1])
    odd = is_odd("lon")
    group, groups = lane_iota(lanes) // DEPTH, lanes // DEPTH
    for t in range(rows // TILE):
        at = pl.ds(t * TILE, TILE)
        for m in range(c.parts):
            east = jnp.zeros((TILE, lanes), jnp.float32)
            west = east
            for channel in strip_rows(c, m):
                shift = shift_of(channel)
                tile = f_ref[channel, at, :]
                if shift:
                    tile = pltpu.roll(tile, shift, 1)
                east = jnp.where(group == shift // DEPTH, tile, east)
                west = jnp.where(group == (shift // DEPTH - 1) % groups, tile, west)
            first_ref[m, at, :] = jnp.where(odd, east, west)
            second_ref[m, at, :] = jnp.where(odd, west, east)
    odd_lat = is_odd("lat")
    for channel in range(c.first):
        high, low = f_ref[channel, pl.ds(rows - TILE, TILE), :], f_ref[channel, pl.ds(0, TILE), :]
        lat_one_ref[channel] = jnp.where(odd_lat, low, high)
        lat_two_ref[channel] = jnp.where(odd_lat, high, low)


def corner_kernel(c, f_ref, one_ref, two_ref, lat_one_ref, lat_two_ref):
    odd_lat, odd_lon = is_odd("lat"), is_odd("lon")
    _, rows, lanes = f_ref.shape
    half = TILE // 2
    first_half = lax.broadcasted_iota(jnp.int32, (TILE, lanes), 0) < half
    low, high = pl.ds(0, TILE), pl.ds(rows - TILE, TILE)

    def put(i, low_tile, high_tile):
        lat_one_ref[i] = jnp.where(odd_lat, low_tile, high_tile)
        lat_two_ref[i] = jnp.where(odd_lat, high_tile, low_tile)

    for m in range(c.parts):
        ends = [(one_ref[m, at, :], two_ref[m, at, :]) for at in (low, high)]
        put(m, *(jnp.where(odd_lon, two, one) for one, two in ends))
        put(c.parts + m, *(jnp.where(odd_lon, one, two) for one, two in ends))
    put(c.strips, f_ref[c.ce, low, :], f_ref[c.ce, high, :])
    put(c.strips + 1, f_ref[c.cn, low, :], f_ref[c.cn, high, :])
    for q in range(c.second - c.cot_at):
        one, two = c.cot + 2 * q, c.cot + min(2 * q + 1, c.levels - 1)
        put(
            c.cot_at + q,
            jnp.where(first_half, f_ref[one, low, :], pltpu.roll(f_ref[two, low, :], half, 0)),
            jnp.where(first_half, pltpu.roll(f_ref[one, high, :], half, 0), f_ref[two, high, :]),
        )


class Sweeps:
    def __init__(self, c, e, w, d, x, m, adj, state):
        self.c, self.e, self.w, self.d, self.x, self.m, self.adj, self.state = c, e, w, d, x, m, adj, state
        self.held = []
        self.lanes = e[0].shape[-1]
        lane = lane_iota(self.lanes)
        self.at_first, self.at_last = lane == 0, lane == self.lanes - 1
        self.even_group = even_groups(self.lanes)

    def from_west(self, x0, x1):
        r0, r1 = pltpu.roll(x0, 1, 1), pltpu.roll(x1, 1, 1)
        return jnp.where(self.at_first, r1, r0), jnp.where(self.at_first, r0, r1)

    def from_east(self, x0, x1):
        r0, r1 = pltpu.roll(x0, self.lanes - 1, 1), pltpu.roll(x1, self.lanes - 1, 1)
        return jnp.where(self.at_last, r1, r0), jnp.where(self.at_last, r0, r1)

    def spread(self, row, easts, wests):
        for m, (east, west) in enumerate(zip(easts, wests)):
            both = jnp.where(self.even_group, east, west), jnp.where(self.even_group, west, east)
            for channel in strip_rows(self.c, m):
                shift = shift_of(channel)
                tile = both[(channel % 16) // 8]
                if shift:
                    tile = pltpu.roll(tile, self.lanes - shift, 1)
                self.e[1][channel, pl.ds(row, TILE), :] = tile

    def western(self, row):
        at = pl.ds(row, TILE)
        self.w[0][at, :], self.w[1][at, :] = self.from_west(self.e[0][self.c.ce, at, :], self.e[1][self.c.ce, at, :])

    def neighbours(self, load, row, halves=2):
        c, at = self.c, pl.ds(row, TILE)
        ce = [e[c.ce, at, :] for e in self.e]
        cw = [w[at, :] for w in self.w]
        cn = [e[c.cn, at, :] for e in self.e]
        cs = [e[c.cn, pl.ds(row - 1, TILE), :] for e in self.e]
        own = [(load(0, k, at), load(1, k, at)) for k in range(c.levels)]
        out = []
        for k in range(c.levels):
            east, west = self.from_east(*own[k]), self.from_west(*own[k])
            pair = []
            for h in range(halves):
                north, south = load(h, k, pl.ds(row + 1, TILE)), load(h, k, pl.ds(row - 1, TILE))
                total = (ce[h] * east[h] + cw[h] * west[h]) + (cn[h] * north + cs[h] * south)
                around = [own[j][h] for j in (k - 1, k + 1) if 0 <= j < c.levels]
                pair.append((own[k][h], total + vertical_coef * functools.reduce(jnp.add, around)))
            out.append(pair)
        return out

    def put(self, ref, k, at, value):
        self.held.append((ref, k, at, value))

    def flush(self):
        for ref, k, at, value in self.held:
            ref[k, at, :] = value
        self.held = []

    def diagonal(self, row):
        load = lambda h, k, at: self.e[h][self.c.wet + k, at, :]
        for k, pair in enumerate(self.neighbours(load, row)):
            for h, (_, total) in enumerate(pair):
                self.put(self.d[h], k, pl.ds(row, TILE), 1.0 - total)

    def loader(self, index):
        if index == 0:
            return lambda h, k, at: self.e[h][self.c.u + k, at, :]
        base = (index - 1) * self.c.levels
        return lambda h, k, at: self.x[h][base + k, at, :]

    def forward(self, n, row):
        c, at = self.c, pl.ds(row, TILE)
        for k, pair in enumerate(self.neighbours(self.loader(n), row)):
            for h, (own, total) in enumerate(pair):
                e = self.e[h]
                wet = e[c.wet + k, at, :]
                bounded = wet * jnp.tanh(self.d[h][k, at, :] * own + total)
                slope = wet - bounded * bounded
                if n < STEPS - 1:
                    self.put(self.x[h], n * c.levels + k, at, bounded + e[c.s + k, at, :])
                    self.put(self.m[h], n * c.levels + k, at, slope)
                else:
                    if h == 0:
                        self.put(self.state, k, at, bounded + e[c.s + k, at, :])
                    self.put(self.x[h], n * c.levels + k, at, slope * e[c.cot + k, at, :])

    def backward(self, n, row):
        c, at = self.c, pl.ds(row, TILE)
        index = 2 * STEPS - 1 - n
        for k, pair in enumerate(self.neighbours(self.loader(index), row)):
            for h, (own, total) in enumerate(pair):
                value = self.d[h][k, at, :] * own + total
                if h == 0:
                    self.put(self.adj, (n - 1) * c.levels + k, at, value)
                self.put(self.x[h], index * c.levels + k, at, self.m[h][(n - 1) * c.levels + k, at, :] * value)

    def over(self, step, rows, together):
        for i, row in enumerate(rows):
            step(row)
            if (i + 1) % together == 0:
                self.flush()
        self.flush()

    def gradient(self, row):
        c, at = self.c, pl.ds(row, TILE)
        for k, pair in enumerate(self.neighbours(self.loader(2 * STEPS - 1), row, 1)):
            own, total = pair[0]
            yield k, self.e[0][c.wet + k, at, :] * (self.d[0][k, at, :] * own + total)

    def source_gradient(self, row):
        c, at = self.c, pl.ds(row, TILE)
        for k in range(c.levels):
            total = self.e[0][c.cot + k, at, :]
            for n in range(STEPS - 1):
                total = total + self.adj[n * c.levels + k, at, :]
            yield k, self.e[0][c.wet + k, at, :] * total


def own_kernel(c, f_ref, one_ref, two_ref, e0, e1, w0, w1, d0, d1, x0, x1, m0, m1, adj, state, grad, gsource):
    rows = f_ref.shape[1]
    odd_lon = is_odd("lon")
    s = Sweeps(c, (e0, e1), (w0, w1), (d0, d1), (x0, x1), (m0, m1), adj, state)
    zero = jnp.zeros((TILE, f_ref.shape[2]), jnp.float32)
    for ref in (e0, e1):
        for end in (pl.ds(0, TILE), pl.ds(HALO + rows, TILE)):
            for channel in (*range(c.u, c.u + c.levels), *range(c.wet, c.wet + c.levels), c.cn):
                ref[channel, end, :] = zero
    tiles = rows // TILE
    places = [HALO + t * TILE for t in range(tiles)]
    for t, row in enumerate(places):
        at, to = pl.ds(t * TILE, TILE), pl.ds(row, TILE)
        for channel in range(c.count):
            e0[channel, to, :] = f_ref[channel, at, :]
        pairs = [(one_ref[m, at, :], two_ref[m, at, :]) for m in range(c.parts)]
        s.spread(
            row,
            [jnp.where(odd_lon, two, one) for one, two in pairs],
            [jnp.where(odd_lon, one, two) for one, two in pairs],
        )
        s.western(row)
    s.over(s.diagonal, places, 1)
    for n in range(STEPS):
        s.over(functools.partial(s.forward, n), places, 1)
    for n in range(STEPS - 1, 0, -1):
        s.over(functools.partial(s.backward, n), places, 1)
    for row in places[1:-1]:
        at = pl.ds(row - HALO, TILE)
        for k, value in s.source_gradient(row):
            gsource[k, at, :] = value
        for k, value in s.gradient(row):
            grad[k, at, :] = value


def edge_kernel(
    c, first_one, first_two, second_two, second_one, *refs,
):
    aliased = refs[: len(refs) // 2]
    del aliased
    e0, e1, w0, w1, d0, d1, x0, x1, m0, m1, adj, state, grad, gsource, state_hbm, grad_hbm, gsource_hbm, sems = refs[14:]
    rows = grad.shape[1]
    s = Sweeps(c, (e0, e1), (w0, w1), (d0, d1), (x0, x1), (m0, m1), adj, state)
    moves = []

    def send(ref, skip, target, at, many):
        move = pltpu.make_async_copy(
            ref.at[:, pl.ds(skip + at, many), :], target.at[:, pl.ds(at, many), :], sems.at[len(moves)]
        )
        move.start()
        moves.append(move)

    def send_edges(ref, skip, target):
        send(ref, skip, target, 0, TILE)
        send(ref, skip, target, rows - TILE, TILE)

    inner = rows - 2 * TILE
    send(state, HALO, state_hbm, TILE, inner)
    send(gsource, 0, gsource_hbm, TILE, inner)
    send(grad, 0, grad_hbm, TILE, inner)
    odd_lat = is_odd("lat")
    for row, low in ((0, True), (HALO + rows, False)):
        pole = lax.axis_index("lat") == (0 if low else lax.axis_size("lat") - 1)
        from_one = odd_lat if low else jnp.logical_not(odd_lat)
        to = pl.ds(row, TILE)

        def got(one, two, i):
            return jnp.where(pole, 0.0, jnp.where(from_one, one[i], two[i]))

        second = [got(second_one, second_two, i) for i in range(c.second)]
        for channel in range(c.first):
            e0[channel, to, :] = got(first_one, first_two, channel)
        e0[c.ce, to, :], e0[c.cn, to, :] = second[c.strips : c.cot_at]
        for k in range(c.levels):
            tile = second[c.cot_at + k // 2]
            if (k % 2 == 0) == low:
                tile = pltpu.roll(tile, TILE // 2, 0)
            e0[c.cot + k, to, :] = tile
        s.spread(row, second[: c.parts], second[c.parts : c.strips])
        s.western(row)
    top = lambda i: HALO + i - (DEPTH - 1)
    bottom = lambda i: HALO + rows - 1 - i
    places = lambda i: (top(i), bottom(i))
    s.over(s.diagonal, places(0), 2)
    for n in range(STEPS):
        s.over(functools.partial(s.forward, n), places(n), 2)
    send_edges(state, HALO, state_hbm)
    for n in range(STEPS - 1, 0, -1):
        s.over(functools.partial(s.backward, n), places(2 * STEPS - 1 - n), 2)
    for row in places(DEPTH - 1):
        for k, value in s.source_gradient(row):
            s.put(gsource, k, pl.ds(row - HALO, TILE), value)
    s.flush()
    send_edges(gsource, 0, gsource_hbm)
    for row in places(DEPTH - 1):
        for k, value in s.gradient(row):
            s.put(grad, k, pl.ds(row - HALO, TILE), value)
    s.flush()
    send_edges(grad, 0, grad_hbm)
    for move in moves:
        move.wait()


def swaps(count, offset):
    pairs = [(i, (i + 1) % count) for i in range(offset, count, 2)]
    return pairs + [(j, i) for i, j in pairs]


def lat_swaps(lat, lon, offset):
    pairs, alone = [], set(range(lat))
    for i in range(offset, lat - 1, 2):
        alone -= {i, i + 1}
        pairs += [(i * lon + j, (i + 1) * lon + j) for j in range(lon)]
    for i in sorted(alone):
        pairs += [(i * lon + j, i * lon + j + 1) for j in range(0, lon, 2)]
    return pairs + [(j, i) for i, j in pairs]


def body(initial_state, source, cotangent, face_coefs, land_mask, bottom):
    arguments = (initial_state, source, cotangent, face_coefs, land_mask, bottom)
    levels, rows, lanes = initial_state.shape
    c = Names(levels)
    span = rows + 2 * HALO
    f32 = lambda *shape: jax.ShapeDtypeStruct(shape, jnp.float32)
    vmem, hbm = pl.BlockSpec(memory_space=pltpu.VMEM), pl.BlockSpec(memory_space=pltpu.HBM)
    params = pltpu.CompilerParams(vmem_limit_bytes=8 * 1024 * 1024)

    fields, one, two, lat_one, lat_two = pl.pallas_call(
        functools.partial(pack_kernel, c),
        out_shape=(f32(c.count, rows, lanes), *(f32(c.parts, rows, lanes),) * 2, *(f32(c.first, TILE, lanes),) * 2),
        in_specs=[hbm] * 6,
        out_specs=(vmem,) * 5,
        scratch_shapes=[
            pltpu.VMEM((levels, rows, lanes), jnp.float32),
            pltpu.VMEM((levels, rows, lanes), jnp.float32),
            pltpu.VMEM((2, rows, lanes), jnp.float32),
            pltpu.VMEM((levels, rows, lanes), jnp.int32),
            pltpu.VMEM((rows, lanes), jnp.int32),
            pltpu.SemaphoreType.DMA((2 + 4 * -(-levels // PIECE),)),
        ],
        compiler_params=params,
        name="pack",
    )(*(pltpu.with_memory_space_constraint(x, pltpu.HBM) for x in arguments))
    lon, lat = lax.axis_size("lon"), lax.axis_size("lat")
    one = lax.ppermute(one, "lon", swaps(lon, 0))
    two = lax.ppermute(two, "lon", swaps(lon, 1))
    both = ("lat", "lon")
    lat_pairs, other_pairs = lat_swaps(lat, lon, 0), lat_swaps(lat, lon, 1)
    first = lax.ppermute(lat_one, both, lat_pairs), lax.ppermute(lat_two, both, other_pairs)
    lat_one, lat_two = pl.pallas_call(
        functools.partial(corner_kernel, c),
        out_shape=(f32(c.second, TILE, lanes),) * 2,
        in_specs=[vmem] * 3,
        out_specs=(vmem,) * 2,
        compiler_params=params,
        name="corners",
    )(fields, one, two)
    second = lax.ppermute(lat_one, both, lat_pairs), lax.ppermute(lat_two, both, other_pairs)
    twice = lambda *shape: (f32(*shape), f32(*shape))
    shapes = (
        *twice(c.count, span, lanes),
        *twice(span, lanes),
        *twice(levels, span, lanes),
        *twice((2 * STEPS - 1) * levels, span, lanes),
        *twice((STEPS - 1) * levels, span, lanes),
        f32((STEPS - 1) * levels, span, lanes),
        f32(levels, span, lanes),
        f32(levels, rows, lanes),
        f32(levels, rows, lanes),
    )
    own = pl.pallas_call(
        functools.partial(own_kernel, c),
        out_shape=shapes,
        in_specs=[vmem] * 3,
        out_specs=(vmem,) * len(shapes),
        compiler_params=params,
        cost_estimate=pl.CostEstimate(
            flops=2 * STEPS * levels * rows * lanes * 40, bytes_accessed=16 * 2**20, transcendentals=0
        ),
        name="own_rows",
    )(fields, one, two)
    out = pl.pallas_call(
        functools.partial(edge_kernel, c),
        out_shape=(*shapes, *(f32(levels, rows, lanes),) * 3),
        in_specs=[vmem] * (4 + len(shapes)),
        out_specs=(*(vmem,) * len(shapes), hbm, hbm, hbm),
        input_output_aliases={4 + i: i for i in range(len(shapes))},
        scratch_shapes=[pltpu.SemaphoreType.DMA((9,))],
        compiler_params=params,
        name="edge_rows",
    )(*first, *second[::-1], *own)
    return tuple(out[len(shapes) :])


def solution(mesh):
    block = P(None, "lat", "lon")
    return jax.shard_map(
        body,
        mesh=mesh,
        in_specs=(block, block, block, block, block, P("lat", "lon")),
        out_specs=(block, block, block),
        check_vma=False,
    )
```

```python
import functools

import jax
import jax.numpy as jnp
from jax import lax
from jax.experimental import pallas as pl
from jax.experimental.pallas import tpu as pltpu
from jax.sharding import PartitionSpec as P

STEPS = 4
DEPTH = 2 * STEPS
TILE = 8
HALO = TILE
PIECE = 2

vertical_coef = 0.04


class Names:
    def __init__(self, levels):
        self.levels = levels
        self.u, self.s, self.wet = 0, levels, 2 * levels
        self.ce, self.cn, self.cot = 3 * levels, 3 * levels + 1, 3 * levels + 2
        self.count = 4 * levels + 2
        self.parts = -(-self.count // 16)
        self.strips = 2 * self.parts
        self.first = self.ce
        self.cot_at = self.strips + 2
        self.second = self.cot_at + -(-levels // 2)

    def by_place(self):
        return sorted(range(self.count), key=lambda channel: (channel % 16, channel))


def lane_iota(lanes):
    return lax.broadcasted_iota(jnp.int32, (TILE, lanes), 1)


def shift_of(channel):
    place = channel % 16
    return 2 * DEPTH * (place % 8) + DEPTH * (place // 8)


def even_groups(lanes):
    return lax.rem(lane_iota(lanes) // DEPTH, 2) == 0


def is_odd(axis):
    return lax.rem(lax.axis_index(axis), 2) == 1


def pack_kernel(
    c, u_hbm, s_hbm, a_hbm, c_hbm, land_hbm, bottom_hbm, f_ref, first_ref, second_ref, lat_one_ref, lat_two_ref,
    u_ref, s_ref, c_ref, land_ref, bottom_ref, sems,
):
    levels = c.levels
    _, rows, lanes = u_ref.shape
    pieces = [(bottom_hbm, bottom_ref)]
    groups = [range(k, min(k + PIECE, levels)) for k in range(0, levels, PIECE)]
    for held in groups:
        at = pl.ds(held.start, len(held))
        pieces += [(land_hbm.at[at], land_ref.at[at]), (u_hbm.at[at], u_ref.at[at]), (s_hbm.at[at], s_ref.at[at])]
    pieces.append((c_hbm, c_ref))
    for held in groups:
        pieces.append((a_hbm.at[pl.ds(held.start, len(held))], f_ref.at[pl.ds(c.cot + held.start, len(held))]))
    moves = [pltpu.make_async_copy(source, target, sems.at[i]) for i, (source, target) in enumerate(pieces)]
    for move in moves:
        move.start()
    last_lat = lax.axis_index("lat") == lax.axis_size("lat") - 1
    moves[0].wait()
    for i, held in enumerate(groups):
        for move in moves[1 + 3 * i : 4 + 3 * i]:
            move.wait()
        for k in held:
            wet = jnp.where(k < bottom_ref[...], land_ref[k], 0).astype(jnp.float32)
            f_ref[c.u + k] = wet * u_ref[k]
            f_ref[c.s + k] = wet * s_ref[k]
            f_ref[c.wet + k] = wet
    for move in moves[1 + 3 * len(groups) :]:
        move.wait()
    f_ref[c.ce] = c_ref[0]
    row = lax.broadcasted_iota(jnp.int32, (rows, lanes), 0)
    f_ref[c.cn] = jnp.where(jnp.logical_and(last_lat, row == rows - 1), 0.0, c_ref[1])
    odd = is_odd("lon")
    group, groups = lane_iota(lanes) // DEPTH, lanes // DEPTH
    zero = jnp.zeros((TILE, lanes), jnp.float32)
    tiles = range(rows // TILE)
    easts = {(t, m): zero for t in tiles for m in range(c.parts)}
    wests = dict(easts)
    for channel in c.by_place():
        shift, m = shift_of(channel), channel // 16
        in_east, in_west = group == shift // DEPTH, group == (shift // DEPTH - 1) % groups
        for t in tiles:
            tile = f_ref[channel, pl.ds(t * TILE, TILE), :]
            if shift:
                tile = pltpu.roll(tile, shift, 1)
            easts[t, m] = jnp.where(in_east, tile, easts[t, m])
            wests[t, m] = jnp.where(in_west, tile, wests[t, m])
    for (t, m), east in easts.items():
        at, west = pl.ds(t * TILE, TILE), wests[t, m]
        first_ref[m, at, :] = jnp.where(odd, east, west)
        second_ref[m, at, :] = jnp.where(odd, west, east)
    odd_lat = is_odd("lat")
    for channel in range(c.first):
        high, low = f_ref[channel, pl.ds(rows - TILE, TILE), :], f_ref[channel, pl.ds(0, TILE), :]
        lat_one_ref[channel] = jnp.where(odd_lat, low, high)
        lat_two_ref[channel] = jnp.where(odd_lat, high, low)


def corner_kernel(c, f_ref, one_ref, two_ref, lat_one_ref, lat_two_ref):
    odd_lat, odd_lon = is_odd("lat"), is_odd("lon")
    _, rows, lanes = f_ref.shape
    half = TILE // 2
    first_half = lax.broadcasted_iota(jnp.int32, (TILE, lanes), 0) < half
    low, high = pl.ds(0, TILE), pl.ds(rows - TILE, TILE)

    def put(i, low_tile, high_tile):
        lat_one_ref[i] = jnp.where(odd_lat, low_tile, high_tile)
        lat_two_ref[i] = jnp.where(odd_lat, high_tile, low_tile)

    for m in range(c.parts):
        ends = [(one_ref[m, at, :], two_ref[m, at, :]) for at in (low, high)]
        put(m, *(jnp.where(odd_lon, two, one) for one, two in ends))
        put(c.parts + m, *(jnp.where(odd_lon, one, two) for one, two in ends))
    put(c.strips, f_ref[c.ce, low, :], f_ref[c.ce, high, :])
    put(c.strips + 1, f_ref[c.cn, low, :], f_ref[c.cn, high, :])
    for q in range(c.second - c.cot_at):
        one, two = c.cot + 2 * q, c.cot + min(2 * q + 1, c.levels - 1)
        put(
            c.cot_at + q,
            jnp.where(first_half, f_ref[one, low, :], pltpu.roll(f_ref[two, low, :], half, 0)),
            jnp.where(first_half, pltpu.roll(f_ref[one, high, :], half, 0), f_ref[two, high, :]),
        )


class Sweeps:
    def __init__(self, c, e, w, d, x, m, adj, state):
        self.c, self.e, self.w, self.d, self.x, self.m, self.adj, self.state = c, e, w, d, x, m, adj, state
        self.held = []
        self.lanes = e[0].shape[-1]
        lane = lane_iota(self.lanes)
        self.at_first, self.at_last = lane == 0, lane == self.lanes - 1
        self.even_group = even_groups(self.lanes)

    def from_west(self, x0, x1):
        r0, r1 = pltpu.roll(x0, 1, 1), pltpu.roll(x1, 1, 1)
        return jnp.where(self.at_first, r1, r0), jnp.where(self.at_first, r0, r1)

    def from_east(self, x0, x1):
        r0, r1 = pltpu.roll(x0, self.lanes - 1, 1), pltpu.roll(x1, self.lanes - 1, 1)
        return jnp.where(self.at_last, r1, r0), jnp.where(self.at_last, r0, r1)

    def mixed(self, east, west):
        return jnp.where(self.even_group, east, west), jnp.where(self.even_group, west, east)

    def spread(self, channel, row, both):
        shift = shift_of(channel)
        tile = both[(channel % 16) // 8]
        if shift:
            tile = pltpu.roll(tile, self.lanes - shift, 1)
        self.e[1][channel, pl.ds(row, TILE), :] = tile

    def western(self, row):
        at = pl.ds(row, TILE)
        self.w[0][at, :], self.w[1][at, :] = self.from_west(self.e[0][self.c.ce, at, :], self.e[1][self.c.ce, at, :])

    def neighbours(self, load, row, halves=2):
        c, at = self.c, pl.ds(row, TILE)
        ce = [e[c.ce, at, :] for e in self.e]
        cw = [w[at, :] for w in self.w]
        cn = [e[c.cn, at, :] for e in self.e]
        cs = [e[c.cn, pl.ds(row - 1, TILE), :] for e in self.e]
        own = [(load(0, k, at), load(1, k, at)) for k in range(c.levels)]
        easts = [self.from_east(*pair) for pair in own]
        wests = [self.from_west(*pair) for pair in own]
        out = []
        for k in range(c.levels):
            east, west = easts[k], wests[k]
            pair = []
            for h in range(halves):
                north, south = load(h, k, pl.ds(row + 1, TILE)), load(h, k, pl.ds(row - 1, TILE))
                total = (ce[h] * east[h] + cw[h] * west[h]) + (cn[h] * north + cs[h] * south)
                around = [own[j][h] for j in (k - 1, k + 1) if 0 <= j < c.levels]
                pair.append((own[k][h], total + vertical_coef * functools.reduce(jnp.add, around)))
            out.append(pair)
        return out

    def put(self, ref, k, at, value):
        self.held.append((ref, k, at, value))

    def flush(self):
        for ref, k, at, value in self.held:
            ref[k, at, :] = value
        self.held = []

    def diagonal(self, row):
        load = lambda h, k, at: self.e[h][self.c.wet + k, at, :]
        for k, pair in enumerate(self.neighbours(load, row)):
            for h, (_, total) in enumerate(pair):
                self.put(self.d[h], k, pl.ds(row, TILE), 1.0 - total)

    def loader(self, index):
        if index == 0:
            return lambda h, k, at: self.e[h][self.c.u + k, at, :]
        base = (index - 1) * self.c.levels
        return lambda h, k, at: self.x[h][base + k, at, :]

    def forward(self, n, row):
        c, at = self.c, pl.ds(row, TILE)
        for k, pair in enumerate(self.neighbours(self.loader(n), row)):
            for h, (own, total) in enumerate(pair):
                e = self.e[h]
                wet = e[c.wet + k, at, :]
                bounded = wet * jnp.tanh(self.d[h][k, at, :] * own + total)
                slope = wet - bounded * bounded
                if n < STEPS - 1:
                    self.put(self.x[h], n * c.levels + k, at, bounded + e[c.s + k, at, :])
                    self.put(self.m[h], n * c.levels + k, at, slope)
                else:
                    if h == 0:
                        self.put(self.state, k, at, bounded + e[c.s + k, at, :])
                    self.put(self.x[h], n * c.levels + k, at, slope * e[c.cot + k, at, :])

    def backward(self, n, row):
        c, at = self.c, pl.ds(row, TILE)
        index = 2 * STEPS - 1 - n
        for k, pair in enumerate(self.neighbours(self.loader(index), row)):
            for h, (own, total) in enumerate(pair):
                value = self.d[h][k, at, :] * own + total
                if h == 0:
                    self.put(self.adj, (n - 1) * c.levels + k, at, value)
                self.put(self.x[h], index * c.levels + k, at, self.m[h][(n - 1) * c.levels + k, at, :] * value)

    def over(self, step, rows, together):
        for i, row in enumerate(rows):
            step(row)
            if (i + 1) % together == 0:
                self.flush()
        self.flush()

    def gradient(self, row):
        c, at = self.c, pl.ds(row, TILE)
        for k, pair in enumerate(self.neighbours(self.loader(2 * STEPS - 1), row, 1)):
            own, total = pair[0]
            yield k, self.e[0][c.wet + k, at, :] * (self.d[0][k, at, :] * own + total)

    def source_gradient(self, row):
        c, at = self.c, pl.ds(row, TILE)
        for k in range(c.levels):
            total = self.e[0][c.cot + k, at, :]
            for n in range(STEPS - 1):
                total = total + self.adj[n * c.levels + k, at, :]
            yield k, self.e[0][c.wet + k, at, :] * total


def own_kernel(c, f_ref, one_ref, two_ref, e0, e1, w0, w1, d0, d1, x0, x1, m0, m1, adj, state, grad, gsource):
    rows = f_ref.shape[1]
    odd_lon = is_odd("lon")
    s = Sweeps(c, (e0, e1), (w0, w1), (d0, d1), (x0, x1), (m0, m1), adj, state)
    zero = jnp.zeros((TILE, f_ref.shape[2]), jnp.float32)
    for ref in (e0, e1):
        for end in (pl.ds(0, TILE), pl.ds(HALO + rows, TILE)):
            for channel in (*range(c.u, c.u + c.levels), *range(c.wet, c.wet + c.levels), c.cn):
                ref[channel, end, :] = zero
    tiles = rows // TILE
    places = [HALO + t * TILE for t in range(tiles)]
    both = {}
    for t in range(tiles):
        for m in range(c.parts):
            one, two = one_ref[m, pl.ds(t * TILE, TILE), :], two_ref[m, pl.ds(t * TILE, TILE), :]
            both[t, m] = s.mixed(jnp.where(odd_lon, two, one), jnp.where(odd_lon, one, two))
    for channel in c.by_place():
        for t, row in enumerate(places):
            e0[channel, pl.ds(row, TILE), :] = f_ref[channel, pl.ds(t * TILE, TILE), :]
            s.spread(channel, row, both[t, channel // 16])
    for row in places:
        s.western(row)
    s.over(s.diagonal, places, 1)
    for n in range(STEPS):
        s.over(functools.partial(s.forward, n), places, 1)
    for n in range(STEPS - 1, 0, -1):
        s.over(functools.partial(s.backward, n), places, 1)
    for row in places[1:-1]:
        at = pl.ds(row - HALO, TILE)
        for k, value in s.source_gradient(row):
            gsource[k, at, :] = value
        for k, value in s.gradient(row):
            grad[k, at, :] = value


def edge_kernel(
    c, first_one, first_two, second_two, second_one, *refs,
):
    aliased = refs[: len(refs) // 2]
    del aliased
    e0, e1, w0, w1, d0, d1, x0, x1, m0, m1, adj, state, grad, gsource, state_hbm, grad_hbm, gsource_hbm, sems = refs[14:]
    rows = grad.shape[1]
    s = Sweeps(c, (e0, e1), (w0, w1), (d0, d1), (x0, x1), (m0, m1), adj, state)
    moves = []

    def send(ref, skip, target, at, many):
        move = pltpu.make_async_copy(
            ref.at[:, pl.ds(skip + at, many), :], target.at[:, pl.ds(at, many), :], sems.at[len(moves)]
        )
        move.start()
        moves.append(move)

    def send_edges(ref, skip, target):
        send(ref, skip, target, 0, TILE)
        send(ref, skip, target, rows - TILE, TILE)

    inner = rows - 2 * TILE
    send(state, HALO, state_hbm, TILE, inner)
    send(gsource, 0, gsource_hbm, TILE, inner)
    send(grad, 0, grad_hbm, TILE, inner)
    odd_lat = is_odd("lat")
    both = {}
    for row, low in ((0, True), (HALO + rows, False)):
        pole = lax.axis_index("lat") == (0 if low else lax.axis_size("lat") - 1)
        from_one = odd_lat if low else jnp.logical_not(odd_lat)
        to = pl.ds(row, TILE)

        def got(one, two, i):
            return jnp.where(pole, 0.0, jnp.where(from_one, one[i], two[i]))

        second = [got(second_one, second_two, i) for i in range(c.second)]
        for channel in range(c.first):
            e0[channel, to, :] = got(first_one, first_two, channel)
        e0[c.ce, to, :], e0[c.cn, to, :] = second[c.strips : c.cot_at]
        for k in range(c.levels):
            tile = second[c.cot_at + k // 2]
            if (k % 2 == 0) == low:
                tile = pltpu.roll(tile, TILE // 2, 0)
            e0[c.cot + k, to, :] = tile
        for m in range(c.parts):
            both[row, m] = s.mixed(second[m], second[c.parts + m])
    for channel in c.by_place():
        for row in (0, HALO + rows):
            s.spread(channel, row, both[row, channel // 16])
    for row in (0, HALO + rows):
        s.western(row)
    top = lambda i: HALO + i - (DEPTH - 1)
    bottom = lambda i: HALO + rows - 1 - i
    places = lambda i: (top(i), bottom(i))
    s.over(s.diagonal, places(0), 2)
    for n in range(STEPS):
        s.over(functools.partial(s.forward, n), places(n), 2)
    send_edges(state, HALO, state_hbm)
    for n in range(STEPS - 1, 0, -1):
        s.over(functools.partial(s.backward, n), places(2 * STEPS - 1 - n), 2)
    for row in places(DEPTH - 1):
        for k, value in s.source_gradient(row):
            s.put(gsource, k, pl.ds(row - HALO, TILE), value)
    s.flush()
    send_edges(gsource, 0, gsource_hbm)
    for row in places(DEPTH - 1):
        for k, value in s.gradient(row):
            s.put(grad, k, pl.ds(row - HALO, TILE), value)
    s.flush()
    send_edges(grad, 0, grad_hbm)
    for move in moves:
        move.wait()


def swaps(count, offset):
    pairs = [(i, (i + 1) % count) for i in range(offset, count, 2)]
    return pairs + [(j, i) for i, j in pairs]


def lat_swaps(lat, lon, offset):
    pairs, alone = [], set(range(lat))
    for i in range(offset, lat - 1, 2):
        alone -= {i, i + 1}
        pairs += [(i * lon + j, (i + 1) * lon + j) for j in range(lon)]
    for i in sorted(alone):
        pairs += [(i * lon + j, i * lon + j + 1) for j in range(0, lon, 2)]
    return pairs + [(j, i) for i, j in pairs]


def body(initial_state, source, cotangent, face_coefs, land_mask, bottom):
    arguments = (initial_state, source, cotangent, face_coefs, land_mask, bottom)
    levels, rows, lanes = initial_state.shape
    c = Names(levels)
    span = rows + 2 * HALO
    f32 = lambda *shape: jax.ShapeDtypeStruct(shape, jnp.float32)
    vmem, hbm = pl.BlockSpec(memory_space=pltpu.VMEM), pl.BlockSpec(memory_space=pltpu.HBM)
    params = pltpu.CompilerParams(vmem_limit_bytes=8 * 1024 * 1024)

    fields, one, two, lat_one, lat_two = pl.pallas_call(
        functools.partial(pack_kernel, c),
        out_shape=(f32(c.count, rows, lanes), *(f32(c.parts, rows, lanes),) * 2, *(f32(c.first, TILE, lanes),) * 2),
        in_specs=[hbm] * 6,
        out_specs=(vmem,) * 5,
        scratch_shapes=[
            pltpu.VMEM((levels, rows, lanes), jnp.float32),
            pltpu.VMEM((levels, rows, lanes), jnp.float32),
            pltpu.VMEM((2, rows, lanes), jnp.float32),
            pltpu.VMEM((levels, rows, lanes), jnp.int32),
            pltpu.VMEM((rows, lanes), jnp.int32),
            pltpu.SemaphoreType.DMA((2 + 4 * -(-levels // PIECE),)),
        ],
        compiler_params=params,
        name="pack",
    )(*(pltpu.with_memory_space_constraint(x, pltpu.HBM) for x in arguments))
    lon, lat = lax.axis_size("lon"), lax.axis_size("lat")
    one = lax.ppermute(one, "lon", swaps(lon, 0))
    two = lax.ppermute(two, "lon", swaps(lon, 1))
    both = ("lat", "lon")
    lat_pairs, other_pairs = lat_swaps(lat, lon, 0), lat_swaps(lat, lon, 1)
    first = lax.ppermute(lat_one, both, lat_pairs), lax.ppermute(lat_two, both, other_pairs)
    lat_one, lat_two = pl.pallas_call(
        functools.partial(corner_kernel, c),
        out_shape=(f32(c.second, TILE, lanes),) * 2,
        in_specs=[vmem] * 3,
        out_specs=(vmem,) * 2,
        compiler_params=params,
        name="corners",
    )(fields, one, two)
    second = lax.ppermute(lat_one, both, lat_pairs), lax.ppermute(lat_two, both, other_pairs)
    twice = lambda *shape: (f32(*shape), f32(*shape))
    shapes = (
        *twice(c.count, span, lanes),
        *twice(span, lanes),
        *twice(levels, span, lanes),
        *twice((2 * STEPS - 1) * levels, span, lanes),
        *twice((STEPS - 1) * levels, span, lanes),
        f32((STEPS - 1) * levels, span, lanes),
        f32(levels, span, lanes),
        f32(levels, rows, lanes),
        f32(levels, rows, lanes),
    )
    own = pl.pallas_call(
        functools.partial(own_kernel, c),
        out_shape=shapes,
        in_specs=[vmem] * 3,
        out_specs=(vmem,) * len(shapes),
        compiler_params=params,
        cost_estimate=pl.CostEstimate(
            flops=2 * STEPS * levels * rows * lanes * 40, bytes_accessed=16 * 2**20, transcendentals=0
        ),
        name="own_rows",
    )(fields, one, two)
    out = pl.pallas_call(
        functools.partial(edge_kernel, c),
        out_shape=(*shapes, *(f32(levels, rows, lanes),) * 3),
        in_specs=[vmem] * (4 + len(shapes)),
        out_specs=(*(vmem,) * len(shapes), hbm, hbm, hbm),
        input_output_aliases={4 + i: i for i in range(len(shapes))},
        scratch_shapes=[pltpu.SemaphoreType.DMA((9,))],
        compiler_params=params,
        name="edge_rows",
    )(*first, *second[::-1], *own)
    return tuple(out[len(shapes) :])


def solution(mesh):
    block = P(None, "lat", "lon")
    return jax.shard_map(
        body,
        mesh=mesh,
        in_specs=(block, block, block, block, block, P("lat", "lon")),
        out_specs=(block, block, block),
        check_vma=False,
    )
```

```python
import functools

import jax
import jax.numpy as jnp
from jax import lax
from jax.experimental import pallas as pl
from jax.experimental.pallas import tpu as pltpu
from jax.sharding import PartitionSpec as P

STEPS = 4
DEPTH = 2 * STEPS
TILE = 8
HALO = TILE
PIECE = 2

vertical_coef = 0.04


class Names:
    def __init__(self, levels):
        self.levels = levels
        self.u, self.s, self.wet = 0, levels, 2 * levels
        self.ce, self.cn, self.cot = 3 * levels, 3 * levels + 1, 3 * levels + 2
        self.count = 4 * levels + 2
        self.parts, self.strips, self.paired = 2, 3, -(-levels // 2)
        self.pair_at = self.cot - 16
        assert 0 <= self.pair_at <= 8 - self.paired
        self.place = {channel: (channel // 16, channel % 16) for channel in range(self.cot)}
        self.place |= {self.cot + k: (1, self.pair_at + k // 2 + 8 * (k % 2)) for k in range(levels)}
        self.first = self.ce
        self.cot_at = self.strips + 2
        self.second = self.cot_at + self.paired


def lane_iota(lanes):
    return lax.broadcasted_iota(jnp.int32, (TILE, lanes), 1)


def clear_halo(c, ref, rows):
    zero = jnp.zeros((TILE, ref.shape[2]), jnp.float32)
    for end in (pl.ds(0, TILE), pl.ds(HALO + rows, TILE)):
        for channel in (*range(c.u, c.u + c.levels), *range(c.wet, c.wet + c.levels), c.cn):
            ref[channel, end, :] = zero


def shift_of(place):
    return 2 * DEPTH * (place % 8) + DEPTH * (place // 8)


def even_groups(lanes):
    return lax.rem(lane_iota(lanes) // DEPTH, 2) == 0


def is_odd(axis):
    return lax.rem(lax.axis_index(axis), 2) == 1


def pack_kernel(
    c, u_hbm, s_hbm, a_hbm, c_hbm, land_hbm, bottom_hbm, f_ref, first_ref, second_ref, lat_one_ref, lat_two_ref,
    u_ref, s_ref, c_ref, land_ref, bottom_ref, sems,
):
    levels = c.levels
    _, rows, lanes = u_ref.shape
    own = pl.ds(HALO, rows)
    pieces = [(bottom_hbm, bottom_ref)]
    groups = [range(k, min(k + PIECE, levels)) for k in range(0, levels, PIECE)]
    for held in groups:
        at = pl.ds(held.start, len(held))
        pieces += [(land_hbm.at[at], land_ref.at[at]), (u_hbm.at[at], u_ref.at[at]), (s_hbm.at[at], s_ref.at[at])]
    pieces.append((c_hbm, c_ref))
    for held in groups:
        pieces.append((a_hbm.at[pl.ds(held.start, len(held))], f_ref.at[pl.ds(c.cot + held.start, len(held)), own, :]))
    moves = [pltpu.make_async_copy(source, target, sems.at[i]) for i, (source, target) in enumerate(pieces)]
    for move in moves:
        move.start()
    clear_halo(c, f_ref, rows)
    last_lat = lax.axis_index("lat") == lax.axis_size("lat") - 1
    moves[0].wait()
    for i, held in enumerate(groups):
        for move in moves[1 + 3 * i : 4 + 3 * i]:
            move.wait()
        for k in held:
            wet = jnp.where(k < bottom_ref[...], land_ref[k], 0).astype(jnp.float32)
            f_ref[c.u + k, own, :] = wet * u_ref[k]
            f_ref[c.s + k, own, :] = wet * s_ref[k]
            f_ref[c.wet + k, own, :] = wet
    for move in moves[1 + 3 * len(groups) :]:
        move.wait()
    f_ref[c.ce, own, :] = c_ref[0]
    row = lax.broadcasted_iota(jnp.int32, (rows, lanes), 0)
    f_ref[c.cn, own, :] = jnp.where(jnp.logical_and(last_lat, row == rows - 1), 0.0, c_ref[1])
    odd = is_odd("lon")
    group, groups = lane_iota(lanes) // DEPTH, lanes // DEPTH
    for t in range(rows // TILE):
        at = pl.ds(t * TILE, TILE)
        for m in range(c.parts):
            east = jnp.zeros((TILE, lanes), jnp.float32)
            west = east
            for channel, (part, place) in c.place.items():
                if part != m:
                    continue
                shift = shift_of(place)
                tile = f_ref[channel, pl.ds(HALO + t * TILE, TILE), :]
                if shift:
                    tile = pltpu.roll(tile, shift, 1)
                east = jnp.where(group == shift // DEPTH, tile, east)
                west = jnp.where(group == (shift // DEPTH - 1) % groups, tile, west)
            first_ref[m, at, :] = jnp.where(odd, east, west)
            second_ref[m, at, :] = jnp.where(odd, west, east)
    odd_lat = is_odd("lat")
    for channel in range(c.first):
        high, low = f_ref[channel, pl.ds(HALO + rows - TILE, TILE), :], f_ref[channel, pl.ds(HALO, TILE), :]
        lat_one_ref[channel] = jnp.where(odd_lat, low, high)
        lat_two_ref[channel] = jnp.where(odd_lat, high, low)


def corner_kernel(c, f_ref, one_ref, two_ref, lat_one_ref, lat_two_ref):
    odd_lat, odd_lon = is_odd("lat"), is_odd("lon")
    _, rows, lanes = one_ref.shape
    half = TILE // 2
    first_half = lax.broadcasted_iota(jnp.int32, (TILE, lanes), 0) < half
    lane = lane_iota(lanes)
    pairs = 2 * DEPTH * c.pair_at - DEPTH
    in_pairs = jnp.logical_and(lane >= pairs, lane < pairs + 2 * DEPTH * c.paired)
    even_group = even_groups(lanes)

    def two_levels(even, odd, high):
        if high:
            return jnp.where(first_half, pltpu.roll(even, half, 0), odd)
        return jnp.where(first_half, even, pltpu.roll(odd, half, 0))

    def put(i, low, high):
        lat_one_ref[i] = jnp.where(odd_lat, low, high)
        lat_two_ref[i] = jnp.where(odd_lat, high, low)

    def strips(high):
        at = pl.ds(rows - TILE if high else 0, TILE)
        easts, wests = [], []
        for m in range(c.parts):
            one, two = one_ref[m, at, :], two_ref[m, at, :]
            easts.append(jnp.where(odd_lon, two, one))
            wests.append(jnp.where(odd_lon, one, two))
        folded = [
            jnp.where(in_pairs, two_levels(tile, pltpu.roll(tile, lanes - DEPTH, 1), high), tile)
            for tile in (easts[1], wests[1])
        ]
        return easts[0], wests[0], jnp.where(even_group, *folded)

    for i, (low, high) in enumerate(zip(strips(False), strips(True))):
        put(i, low, high)
    low, high = pl.ds(HALO, TILE), pl.ds(HALO + rows - TILE, TILE)
    put(c.strips, f_ref[c.ce, low, :], f_ref[c.ce, high, :])
    put(c.strips + 1, f_ref[c.cn, low, :], f_ref[c.cn, high, :])
    for q in range(c.paired):
        even, odd = c.cot + 2 * q, c.cot + min(2 * q + 1, c.levels - 1)
        put(c.cot_at + q, *(two_levels(f_ref[even, at, :], f_ref[odd, at, :], at is high) for at in (low, high)))


class Sweeps:
    def __init__(self, c, e, w, d, x, m, adj, state):
        self.c, self.e, self.w, self.d, self.x, self.m, self.adj, self.state = c, e, w, d, x, m, adj, state
        self.held = []
        self.lanes = e[0].shape[-1]
        lane = lane_iota(self.lanes)
        self.at_first, self.at_last = lane == 0, lane == self.lanes - 1
        self.even_group = even_groups(self.lanes)

    def from_west(self, x0, x1):
        r0, r1 = pltpu.roll(x0, 1, 1), pltpu.roll(x1, 1, 1)
        return jnp.where(self.at_first, r1, r0), jnp.where(self.at_first, r0, r1)

    def from_east(self, x0, x1):
        r0, r1 = pltpu.roll(x0, self.lanes - 1, 1), pltpu.roll(x1, self.lanes - 1, 1)
        return jnp.where(self.at_last, r1, r0), jnp.where(self.at_last, r0, r1)

    def mixed(self, east, west):
        return jnp.where(self.even_group, east, west), jnp.where(self.even_group, west, east)

    def ends(self, place, both):
        shift = shift_of(place)
        tile = both[place // 8]
        return pltpu.roll(tile, self.lanes - shift, 1) if shift else tile

    def western(self, row):
        at = pl.ds(row, TILE)
        self.w[0][at, :], self.w[1][at, :] = self.from_west(self.e[0][self.c.ce, at, :], self.e[1][self.c.ce, at, :])

    def neighbours(self, load, row, halves=2):
        c, at = self.c, pl.ds(row, TILE)
        ce = [e[c.ce, at, :] for e in self.e]
        cw = [w[at, :] for w in self.w]
        cn = [e[c.cn, at, :] for e in self.e]
        cs = [e[c.cn, pl.ds(row - 1, TILE), :] for e in self.e]
        own = [(load(0, k, at), load(1, k, at)) for k in range(c.levels)]
        out = []
        for k in range(c.levels):
            east, west = self.from_east(*own[k]), self.from_west(*own[k])
            pair = []
            for h in range(halves):
                north, south = load(h, k, pl.ds(row + 1, TILE)), load(h, k, pl.ds(row - 1, TILE))
                total = (ce[h] * east[h] + cw[h] * west[h]) + (cn[h] * north + cs[h] * south)
                around = [own[j][h] for j in (k - 1, k + 1) if 0 <= j < c.levels]
                pair.append((own[k][h], total + vertical_coef * functools.reduce(jnp.add, around)))
            out.append(pair)
        return out

    def put(self, ref, k, at, value):
        self.held.append((ref, k, at, value))

    def flush(self):
        for ref, k, at, value in self.held:
            ref[k, at, :] = value
        self.held = []

    def diagonal(self, row):
        load = lambda h, k, at: self.e[h][self.c.wet + k, at, :]
        for k, pair in enumerate(self.neighbours(load, row)):
            for h, (_, total) in enumerate(pair):
                self.put(self.d[h], k, pl.ds(row, TILE), 1.0 - total)

    def loader(self, index):
        if index == 0:
            return lambda h, k, at: self.e[h][self.c.u + k, at, :]
        base = (index - 1) * self.c.levels
        return lambda h, k, at: self.x[h][base + k, at, :]

    def forward(self, n, row):
        c, at = self.c, pl.ds(row, TILE)
        for k, pair in enumerate(self.neighbours(self.loader(n), row)):
            for h, (own, total) in enumerate(pair):
                e = self.e[h]
                wet = e[c.wet + k, at, :]
                bounded = wet * jnp.tanh(self.d[h][k, at, :] * own + total)
                slope = wet - bounded * bounded
                if n < STEPS - 1:
                    self.put(self.x[h], n * c.levels + k, at, bounded + e[c.s + k, at, :])
                    self.put(self.m[h], n * c.levels + k, at, slope)
                else:
                    if h == 0:
                        self.put(self.state, k, at, bounded + e[c.s + k, at, :])
                    self.put(self.x[h], n * c.levels + k, at, slope * e[c.cot + k, at, :])

    def backward(self, n, row):
        c, at = self.c, pl.ds(row, TILE)
        index = 2 * STEPS - 1 - n
        for k, pair in enumerate(self.neighbours(self.loader(index), row)):
            for h, (own, total) in enumerate(pair):
                value = self.d[h][k, at, :] * own + total
                if h == 0:
                    self.put(self.adj, (n - 1) * c.levels + k, at, value)
                self.put(self.x[h], index * c.levels + k, at, self.m[h][(n - 1) * c.levels + k, at, :] * value)

    def over(self, step, rows, together):
        for i, row in enumerate(rows):
            step(row)
            if (i + 1) % together == 0:
                self.flush()
        self.flush()

    def gradient(self, row):
        c, at = self.c, pl.ds(row, TILE)
        for k, pair in enumerate(self.neighbours(self.loader(2 * STEPS - 1), row, 1)):
            own, total = pair[0]
            yield k, self.e[0][c.wet + k, at, :] * (self.d[0][k, at, :] * own + total)

    def source_gradient(self, row):
        c, at = self.c, pl.ds(row, TILE)
        for k in range(c.levels):
            total = self.e[0][c.cot + k, at, :]
            for n in range(STEPS - 1):
                total = total + self.adj[n * c.levels + k, at, :]
            yield k, self.e[0][c.wet + k, at, :] * total


def own_kernel(c, e0, one_ref, two_ref, e1, w0, w1, d0, d1, x0, x1, m0, m1, adj, state, grad, gsource):
    rows, lanes = one_ref.shape[1:]
    odd_lon = is_odd("lon")
    s = Sweeps(c, (e0, e1), (w0, w1), (d0, d1), (x0, x1), (m0, m1), adj, state)
    clear_halo(c, e1, rows)
    tiles = rows // TILE
    places = [HALO + t * TILE for t in range(tiles)]
    for t, row in enumerate(places):
        at, to = pl.ds(t * TILE, TILE), pl.ds(row, TILE)
        both = []
        for m in range(c.parts):
            one, two = one_ref[m, at, :], two_ref[m, at, :]
            both.append(s.mixed(jnp.where(odd_lon, two, one), jnp.where(odd_lon, one, two)))
        for channel, (part, place) in c.place.items():
            e1[channel, to, :] = s.ends(place, both[part])
        s.western(row)
    s.over(s.diagonal, places, 1)
    for n in range(STEPS):
        s.over(functools.partial(s.forward, n), places, 1)
    for n in range(STEPS - 1, 0, -1):
        s.over(functools.partial(s.backward, n), places, 1)
    for row in places[1:-1]:
        at = pl.ds(row - HALO, TILE)
        for k, value in s.source_gradient(row):
            gsource[k, at, :] = value
        for k, value in s.gradient(row):
            grad[k, at, :] = value


def edge_kernel(
    c, first_one, first_two, second_two, second_one, *refs,
):
    e0, e1, w0, w1, d0, d1, x0, x1, m0, m1, adj, state, grad, gsource, state_hbm, grad_hbm, gsource_hbm, sems = refs[14:]
    rows = grad.shape[1]
    s = Sweeps(c, (e0, e1), (w0, w1), (d0, d1), (x0, x1), (m0, m1), adj, state)
    moves = []

    def send(ref, skip, target, at, many):
        move = pltpu.make_async_copy(
            ref.at[:, pl.ds(skip + at, many), :], target.at[:, pl.ds(at, many), :], sems.at[len(moves)]
        )
        move.start()
        moves.append(move)

    def send_edges(ref, skip, target):
        send(ref, skip, target, 0, TILE)
        send(ref, skip, target, rows - TILE, TILE)

    inner = rows - 2 * TILE
    send(state, HALO, state_hbm, TILE, inner)
    send(gsource, 0, gsource_hbm, TILE, inner)
    send(grad, 0, grad_hbm, TILE, inner)
    odd_lat = is_odd("lat")
    for row, low in ((0, True), (HALO + rows, False)):
        pole = lax.axis_index("lat") == (0 if low else lax.axis_size("lat") - 1)
        from_one = odd_lat if low else jnp.logical_not(odd_lat)
        to = pl.ds(row, TILE)

        def got(one, two, i):
            return jnp.where(pole, 0.0, jnp.where(from_one, one[i], two[i]))

        second = [got(second_one, second_two, i) for i in range(c.second)]
        for channel in range(c.first):
            e0[channel, to, :] = got(first_one, first_two, channel)
        e0[c.ce, to, :], e0[c.cn, to, :] = second[c.strips : c.cot_at]
        for k in range(c.levels):
            tile = second[c.cot_at + k // 2]
            if (k % 2 == 0) == low:
                tile = pltpu.roll(tile, TILE // 2, 0)
            e0[c.cot + k, to, :] = tile
        both = s.mixed(*second[:2]), (second[2],)
        for channel in range(c.cot):
            part, place = c.place[channel]
            e1[channel, to, :] = s.ends(place, both[part])
        for q in range(c.paired):
            tile = s.ends(c.pair_at + q, both[1])
            for k in range(2 * q, min(2 * q + 2, c.levels)):
                moved = (k % 2 == 0) == low
                e1[c.cot + k, to, :] = pltpu.roll(tile, TILE // 2, 0) if moved else tile
        s.western(row)
    top = lambda i: HALO + i - (DEPTH - 1)
    bottom = lambda i: HALO + rows - 1 - i
    places = lambda i: (top(i), bottom(i))
    s.over(s.diagonal, places(0), 2)
    for n in range(STEPS):
        s.over(functools.partial(s.forward, n), places(n), 2)
    send_edges(state, HALO, state_hbm)
    for n in range(STEPS - 1, 0, -1):
        s.over(functools.partial(s.backward, n), places(2 * STEPS - 1 - n), 2)
    for row in places(DEPTH - 1):
        for k, value in s.source_gradient(row):
            s.put(gsource, k, pl.ds(row - HALO, TILE), value)
    s.flush()
    send_edges(gsource, 0, gsource_hbm)
    for row in places(DEPTH - 1):
        for k, value in s.gradient(row):
            s.put(grad, k, pl.ds(row - HALO, TILE), value)
    s.flush()
    send_edges(grad, 0, grad_hbm)
    for move in moves:
        move.wait()


def swaps(count, offset):
    pairs = [(i, (i + 1) % count) for i in range(offset, count, 2)]
    return pairs + [(j, i) for i, j in pairs]


def lat_swaps(lat, lon, offset):
    pairs, alone = [], set(range(lat))
    for i in range(offset, lat - 1, 2):
        alone -= {i, i + 1}
        pairs += [(i * lon + j, (i + 1) * lon + j) for j in range(lon)]
    for i in sorted(alone):
        pairs += [(i * lon + j, i * lon + j + 1) for j in range(0, lon, 2)]
    return pairs + [(j, i) for i, j in pairs]


def body(initial_state, source, cotangent, face_coefs, land_mask, bottom):
    arguments = (initial_state, source, cotangent, face_coefs, land_mask, bottom)
    levels, rows, lanes = initial_state.shape
    c = Names(levels)
    span = rows + 2 * HALO
    f32 = lambda *shape: jax.ShapeDtypeStruct(shape, jnp.float32)
    vmem, hbm = pl.BlockSpec(memory_space=pltpu.VMEM), pl.BlockSpec(memory_space=pltpu.HBM)
    params = pltpu.CompilerParams(vmem_limit_bytes=8 * 1024 * 1024)

    fields, one, two, lat_one, lat_two = pl.pallas_call(
        functools.partial(pack_kernel, c),
        out_shape=(f32(c.count, span, lanes), *(f32(c.parts, rows, lanes),) * 2, *(f32(c.first, TILE, lanes),) * 2),
        in_specs=[hbm] * 6,
        out_specs=(vmem,) * 5,
        scratch_shapes=[
            pltpu.VMEM((levels, rows, lanes), jnp.float32),
            pltpu.VMEM((levels, rows, lanes), jnp.float32),
            pltpu.VMEM((2, rows, lanes), jnp.float32),
            pltpu.VMEM((levels, rows, lanes), jnp.int32),
            pltpu.VMEM((rows, lanes), jnp.int32),
            pltpu.SemaphoreType.DMA((2 + 4 * -(-levels // PIECE),)),
        ],
        compiler_params=params,
        name="pack",
    )(*(pltpu.with_memory_space_constraint(x, pltpu.HBM) for x in arguments))
    lon, lat = lax.axis_size("lon"), lax.axis_size("lat")
    one = lax.ppermute(one, "lon", swaps(lon, 0))
    two = lax.ppermute(two, "lon", swaps(lon, 1))
    both = ("lat", "lon")
    lat_pairs, other_pairs = lat_swaps(lat, lon, 0), lat_swaps(lat, lon, 1)
    first = lax.ppermute(lat_one, both, lat_pairs), lax.ppermute(lat_two, both, other_pairs)
    lat_one, lat_two = pl.pallas_call(
        functools.partial(corner_kernel, c),
        out_shape=(f32(c.second, TILE, lanes),) * 2,
        in_specs=[vmem] * 3,
        out_specs=(vmem,) * 2,
        compiler_params=params,
        name="corners",
    )(fields, one, two)
    second = lax.ppermute(lat_one, both, lat_pairs), lax.ppermute(lat_two, both, other_pairs)
    twice = lambda *shape: (f32(*shape), f32(*shape))
    shapes = (
        *twice(c.count, span, lanes),
        *twice(span, lanes),
        *twice(levels, span, lanes),
        *twice((2 * STEPS - 1) * levels, span, lanes),
        *twice((STEPS - 1) * levels, span, lanes),
        f32((STEPS - 1) * levels, span, lanes),
        f32(levels, span, lanes),
        f32(levels, rows, lanes),
        f32(levels, rows, lanes),
    )
    own = pl.pallas_call(
        functools.partial(own_kernel, c),
        out_shape=shapes[1:],
        in_specs=[vmem] * 3,
        out_specs=(vmem,) * (len(shapes) - 1),
        compiler_params=params,
        cost_estimate=pl.CostEstimate(
            flops=2 * STEPS * levels * rows * lanes * 40, bytes_accessed=16 * 2**20, transcendentals=0
        ),
        name="own_rows",
    )(fields, one, two)
    out = pl.pallas_call(
        functools.partial(edge_kernel, c),
        out_shape=(*shapes, *(f32(levels, rows, lanes),) * 3),
        in_specs=[vmem] * (4 + len(shapes)),
        out_specs=(*(vmem,) * len(shapes), hbm, hbm, hbm),
        input_output_aliases={4 + i: i for i in range(len(shapes))},
        scratch_shapes=[pltpu.SemaphoreType.DMA((9,))],
        compiler_params=params,
        name="edge_rows",
    )(*first, *second[::-1], fields, *own)
    return tuple(out[len(shapes) :])


def solution(mesh):
    block = P(None, "lat", "lon")
    return jax.shard_map(
        body,
        mesh=mesh,
        in_specs=(block, block, block, block, block, P("lat", "lon")),
        out_specs=(block, block, block),
        check_vma=False,
    )
```

```python
import functools

import jax
import jax.numpy as jnp
from jax import lax
from jax.experimental import pallas as pl
from jax.experimental.pallas import tpu as pltpu
from jax.sharding import PartitionSpec as P

STEPS = 4
DEPTH = 2 * STEPS
TILE = 8
HALO = TILE
PIECE = 2

vertical_coef = 0.04


class Names:
    def __init__(self, levels):
        assert levels % 2 == 0 and levels <= 6
        self.levels, self.half = levels, levels // 2
        self.u, self.s, self.wet = 0, levels, 2 * levels
        self.ce, self.cn, self.cot = 3 * levels, 3 * levels + 1, 3 * levels + 2
        self.count = 4 * levels + 2
        h = self.half
        self.su, self.ss, self.swet, self.sce, self.scn, self.scot = 0, h, 2 * h, 3 * h, 3 * h + 1, 3 * h + 2
        self.pairs = 4 * h + 2
        self.parts, self.strips = 2, 4
        self.place = {self.sce: (0, 3, 0), self.scn: (1, 3, 0)}
        for j in range(h):
            self.place |= {self.su + j: (0, j, 0), self.ss + j: (0, j, 1), self.swet + j: (1, j, 0), self.scot + j: (1, j, 1)}
        self.first = self.ce
        self.cot_at = self.strips + 2
        self.second = self.cot_at + h

    def levels_of(self, pair):
        for strip, channel in ((self.scot, self.cot), (self.scn, self.cn), (self.sce, self.ce)):
            if pair >= strip:
                break
        else:
            return pair % self.half + self.levels * (pair // self.half), pair % self.half + self.levels * (
                pair // self.half
            ) + self.half
        if channel != self.cot:
            return channel, channel
        return channel + pair - strip, channel + pair - strip + self.half


def lane_iota(lanes):
    return lax.broadcasted_iota(jnp.int32, (TILE, lanes), 1)


def clear_halo(ref, channels, rows):
    zero = jnp.zeros((TILE, ref.shape[2]), jnp.float32)
    for end in (pl.ds(0, TILE), pl.ds(HALO + rows, TILE)):
        for channel in channels:
            ref[channel, end, :] = zero


def turn(x):
    return pltpu.roll(x, x.shape[1] // 2, 1)


def middle(lanes):
    lane = lane_iota(lanes)
    return jnp.logical_and(lane >= lanes // 4, lane < lanes - lanes // 4)


def shift_of(place):
    return 2 * DEPTH * place[1] + DEPTH * place[2]


def even_groups(lanes):
    return lax.rem(lane_iota(lanes) // DEPTH, 2) == 0


def is_odd(axis):
    return lax.rem(lax.axis_index(axis), 2) == 1


def pack_kernel(
    c, u_hbm, s_hbm, a_hbm, c_hbm, land_hbm, bottom_hbm, f_ref, first_ref, second_ref, lat_one_ref, lat_two_ref,
    u_ref, s_ref, c_ref, land_ref, bottom_ref, sems,
):
    levels = c.levels
    _, rows, lanes = u_ref.shape
    own = pl.ds(HALO, rows)
    pieces = [(bottom_hbm, bottom_ref)]
    groups = [range(k, min(k + PIECE, levels)) for k in range(0, levels, PIECE)]
    for held in groups:
        at = pl.ds(held.start, len(held))
        pieces += [(land_hbm.at[at], land_ref.at[at]), (u_hbm.at[at], u_ref.at[at]), (s_hbm.at[at], s_ref.at[at])]
    pieces.append((c_hbm, c_ref))
    for held in groups:
        pieces.append((a_hbm.at[pl.ds(held.start, len(held))], f_ref.at[pl.ds(c.cot + held.start, len(held)), own, :]))
    moves = [pltpu.make_async_copy(source, target, sems.at[i]) for i, (source, target) in enumerate(pieces)]
    for move in moves:
        move.start()
    clear_halo(f_ref, (*range(c.u, c.u + levels), *range(c.wet, c.wet + levels), c.cn), rows)
    last_lat = lax.axis_index("lat") == lax.axis_size("lat") - 1
    moves[0].wait()
    for i, held in enumerate(groups):
        for move in moves[1 + 3 * i : 4 + 3 * i]:
            move.wait()
        for k in held:
            wet = jnp.where(k < bottom_ref[...], land_ref[k], 0).astype(jnp.float32)
            for at, value in ((c.u, wet * u_ref[k]), (c.s, wet * s_ref[k]), (c.wet, wet)):
                f_ref[at + k, own, :] = value if k < c.half else turn(value)
    for move in moves[1 + 3 * len(groups) :]:
        move.wait()
    for k in range(c.half, levels):
        f_ref[c.cot + k, own, :] = turn(f_ref[c.cot + k, own, :])
    f_ref[c.ce, own, :] = c_ref[0]
    row = lax.broadcasted_iota(jnp.int32, (rows, lanes), 0)
    f_ref[c.cn, own, :] = jnp.where(jnp.logical_and(last_lat, row == rows - 1), 0.0, c_ref[1])
    odd = is_odd("lon")
    group, groups = lax.rem(lane_iota(lanes) // DEPTH, lanes // DEPTH // 2), lanes // DEPTH // 2
    inside = middle(lanes)
    for t in range(rows // TILE):
        at = pl.ds(t * TILE, TILE)
        easts = [jnp.zeros((TILE, lanes), jnp.float32)] * c.parts
        wests = list(easts)
        for pair, place in c.place.items():
            lower, upper = (f_ref[channel, pl.ds(HALO + t * TILE, TILE), :] for channel in c.levels_of(pair))
            if pair in (c.sce, c.scn):
                upper = turn(upper)
            shift, m = shift_of(place), place[0]
            tile = jnp.where(inside, upper, lower)
            if shift:
                tile = pltpu.roll(tile, shift, 1)
            easts[m] = jnp.where(group == shift // DEPTH, tile, easts[m])
            wests[m] = jnp.where(group == (shift // DEPTH - 1) % groups, tile, wests[m])
        for m in range(c.parts):
            first_ref[m, at, :] = jnp.where(odd, easts[m], wests[m])
            second_ref[m, at, :] = jnp.where(odd, wests[m], easts[m])
    odd_lat = is_odd("lat")
    for channel in range(c.first):
        high, low = f_ref[channel, pl.ds(HALO + rows - TILE, TILE), :], f_ref[channel, pl.ds(HALO, TILE), :]
        lat_one_ref[channel] = jnp.where(odd_lat, low, high)
        lat_two_ref[channel] = jnp.where(odd_lat, high, low)


def corner_kernel(c, f_ref, one_ref, two_ref, lat_one_ref, lat_two_ref):
    odd_lat, odd_lon = is_odd("lat"), is_odd("lon")
    _, rows, lanes = one_ref.shape
    half = TILE // 2
    first_half = lax.broadcasted_iota(jnp.int32, (TILE, lanes), 0) < half
    low, high = pl.ds(HALO, TILE), pl.ds(HALO + rows - TILE, TILE)

    def put(i, low_tile, high_tile):
        lat_one_ref[i] = jnp.where(odd_lat, low_tile, high_tile)
        lat_two_ref[i] = jnp.where(odd_lat, high_tile, low_tile)

    for m in range(c.parts):
        ends = [(one_ref[m, at, :], two_ref[m, at, :]) for at in (pl.ds(0, TILE), pl.ds(rows - TILE, TILE))]
        put(m, *(jnp.where(odd_lon, two, one) for one, two in ends))
        put(c.parts + m, *(jnp.where(odd_lon, one, two) for one, two in ends))
    put(c.strips, f_ref[c.ce, low, :], f_ref[c.ce, high, :])
    put(c.strips + 1, f_ref[c.cn, low, :], f_ref[c.cn, high, :])
    for q in range(c.half):
        even, odd = c.cot + 2 * q, c.cot + 2 * q + 1
        put(
            c.cot_at + q,
            jnp.where(first_half, f_ref[even, low, :], pltpu.roll(f_ref[odd, low, :], half, 0)),
            jnp.where(first_half, pltpu.roll(f_ref[even, high, :], half, 0), f_ref[odd, high, :]),
        )


class Sweeps:
    def __init__(self, c, e, w, t, d, x, m, adj, state):
        self.c, self.e, self.w, self.t, self.d, self.x, self.m, self.adj, self.state = c, e, w, t, d, x, m, adj, state
        self.held = []
        self.lanes = lanes = e[0].shape[-1]
        lane = lane_iota(lanes)
        self.firsts = lane == 0, lane == lanes // 2
        self.lasts = lane == lanes - 1, lane == lanes // 2 - 1
        self.inside = middle(lanes)
        self.even_group = even_groups(lanes)
        self.tiles = [(0, k) for k in range(c.levels)] + [(1, j) for j in range(c.half)]

    def mixed(self, east, west):
        return jnp.where(self.even_group, east, west), jnp.where(self.even_group, west, east)

    def spread(self, row, easts, wests):
        both = [self.mixed(east, west) for east, west in zip(easts, wests)]
        for pair, place in self.c.place.items():
            shift = shift_of(place)
            tile = both[place[0]][place[2]]
            if shift:
                tile = pltpu.roll(tile, self.lanes - shift, 1)
            self.e[1][pair, pl.ds(row, TILE), :] = tile

    def western(self, row):
        c, at = self.c, pl.ds(row, TILE)
        own, halo = self.e[0][c.ce, at, :], self.e[1][c.sce, at, :]
        turned = turn(own)
        own_west, halo_west = pltpu.roll(own, 1, 1), pltpu.roll(halo, 1, 1)
        west = jnp.where(self.firsts[0], halo_west, own_west)
        self.w[0][at, :] = west
        upper = jnp.where(self.firsts[1], pltpu.roll(turned, 1, 1), halo_west)
        self.w[1][at, :] = jnp.where(self.firsts[0], own_west, upper)
        self.t[0, at, :], self.t[1, at, :], self.t[2, at, :] = turned, turn(west), turn(self.e[0][c.cn, at, :])

    def beside(self, own, halo, shift, ends):
        h = self.c.half
        own, halo = [pltpu.roll(x, shift, 1) for x in own], [pltpu.roll(x, shift, 1) for x in halo]
        tiles = [jnp.where(ends[k // h], halo[k % h], own[k]) for k in range(self.c.levels)]
        return tiles + [jnp.where(ends[0], own[j], jnp.where(ends[1], own[j + h], halo[j])) for j in range(h)]

    def around(self, own, halo):
        h, levels = self.c.half, self.c.levels
        out = []
        for k in range(levels):
            near = [turn(own[j]) if j // h != k // h else own[j] for j in (k - 1, k + 1) if 0 <= j < levels]
            out.append(functools.reduce(jnp.add, near))
        for j in range(h):
            near = [halo[i] for i in (j - 1, j + 1) if 0 <= i < h]
            if j == 0:
                near.append(jnp.where(self.inside, turn(halo[h - 1]), 0.0))
            if j == h - 1:
                near.append(jnp.where(self.inside, 0.0, turn(halo[0])))
            out.append(functools.reduce(jnp.add, near))
        return out

    def neighbours(self, load, row, halos=True):
        c, at = self.c, pl.ds(row, TILE)
        above, below = pl.ds(row + 1, TILE), pl.ds(row - 1, TILE)
        own, halo = [load(0, k, at) for k in range(c.levels)], [load(1, j, at) for j in range(c.half)]
        easts = self.beside(own, halo, self.lanes - 1, self.lasts)
        wests = self.beside(own, halo, 1, self.firsts)
        levels = self.around(own, halo)
        (e0, e1), (w0, w1), t = self.e, self.w, self.t
        faces = (
            (e0[c.ce, at, :], w0[at, :], e0[c.cn, at, :], e0[c.cn, below, :]),
            (t[0, at, :], t[1, at, :], t[2, at, :], t[2, below, :]),
            (e1[c.sce, at, :], w1[at, :], e1[c.scn, at, :], e1[c.scn, below, :]),
        )
        out = []
        for (part, k), field, east, west, around in zip(self.tiles, own + halo, easts, wests, levels):
            if part and not halos:
                break
            ce, cw, cn, cs = faces[2 if part else k // c.half]
            total = (ce * east + cw * west) + (cn * load(part, k, above) + cs * load(part, k, below))
            out.append((part, k, field, total + vertical_coef * around))
        return out

    def put(self, ref, k, at, value):
        self.held.append((ref, k, at, value))

    def flush(self):
        for ref, k, at, value in self.held:
            ref[k, at, :] = value
        self.held = []

    def plain(self, k, value):
        return value if k < self.c.half else turn(value)

    def many(self, part):
        return self.c.half if part else self.c.levels

    def field(self, own, halo):
        return lambda part, k, at: self.e[part][(halo if part else own) + k, at, :]

    def state_at(self, index):
        if index == 0:
            return self.field(self.c.u, self.c.su)
        return lambda part, k, at: self.x[part][(index - 1) * self.many(part) + k, at, :]

    def diagonal(self, row):
        at = pl.ds(row, TILE)
        for part, k, _, total in self.neighbours(self.field(self.c.wet, self.c.swet), row):
            self.put(self.d[part], k, at, 1.0 - total)

    def forward(self, n, row):
        c, at = self.c, pl.ds(row, TILE)
        wets, sources, cots = self.field(c.wet, c.swet), self.field(c.s, c.ss), self.field(c.cot, c.scot)
        for part, k, field, total in self.neighbours(self.state_at(n), row):
            wet = wets(part, k, at)
            bounded = wet * jnp.tanh(self.d[part][k, at, :] * field + total)
            slope = wet - bounded * bounded
            place = n * self.many(part) + k
            if n < STEPS - 1:
                self.put(self.x[part], place, at, bounded + sources(part, k, at))
                self.put(self.m[part], place, at, slope)
            else:
                if part == 0:
                    self.put(self.state, k, at, self.plain(k, bounded + sources(part, k, at)))
                self.put(self.x[part], place, at, slope * cots(part, k, at))

    def backward(self, n, row):
        at = pl.ds(row, TILE)
        index = 2 * STEPS - 1 - n
        for part, k, field, total in self.neighbours(self.state_at(index), row):
            value = self.d[part][k, at, :] * field + total
            many = self.many(part)
            if part == 0:
                self.put(self.adj, (n - 1) * many + k, at, value)
            self.put(self.x[part], index * many + k, at, self.m[part][(n - 1) * many + k, at, :] * value)

    def over(self, step, rows, together):
        for i, row in enumerate(rows):
            step(row)
            if (i + 1) % together == 0:
                self.flush()
        self.flush()

    def gradient(self, row):
        c, at = self.c, pl.ds(row, TILE)
        for _, k, field, total in self.neighbours(self.state_at(2 * STEPS - 1), row, False):
            yield k, self.plain(k, self.e[0][c.wet + k, at, :] * (self.d[0][k, at, :] * field + total))

    def source_gradient(self, row):
        c, at = self.c, pl.ds(row, TILE)
        for k in range(c.levels):
            total = self.e[0][c.cot + k, at, :]
            for n in range(STEPS - 1):
                total = total + self.adj[n * c.levels + k, at, :]
            yield k, self.plain(k, self.e[0][c.wet + k, at, :] * total)


def own_kernel(c, e0, one_ref, two_ref, e1, w0, w1, turned, d0, d1, x0, x1, m0, m1, adj, state, grad, gsource):
    rows, lanes = one_ref.shape[1:]
    odd_lon = is_odd("lon")
    s = Sweeps(c, (e0, e1), (w0, w1), turned, (d0, d1), (x0, x1), (m0, m1), adj, state)
    clear_halo(e1, (*range(c.su, c.su + c.half), *range(c.swet, c.swet + c.half), c.scn), rows)
    clear_halo(turned, (2,), rows)
    tiles = rows // TILE
    places = [HALO + t * TILE for t in range(tiles)]
    for t, row in enumerate(places):
        at = pl.ds(t * TILE, TILE)
        ends = [(one_ref[m, at, :], two_ref[m, at, :]) for m in range(c.parts)]
        s.spread(
            row,
            [jnp.where(odd_lon, two, one) for one, two in ends],
            [jnp.where(odd_lon, one, two) for one, two in ends],
        )
        s.western(row)
    s.over(s.diagonal, places, 1)
    for n in range(STEPS):
        s.over(functools.partial(s.forward, n), places, 1)
    for n in range(STEPS - 1, 0, -1):
        s.over(functools.partial(s.backward, n), places, 1)
    for row in places[1:-1]:
        at = pl.ds(row - HALO, TILE)
        for k, value in s.source_gradient(row):
            gsource[k, at, :] = value
        for k, value in s.gradient(row):
            grad[k, at, :] = value


def edge_kernel(
    c, first_one, first_two, second_two, second_one, *refs,
):
    e0, e1, w0, w1, turned, d0, d1, x0, x1, m0, m1, adj, state, grad, gsource, *outs, sems = refs[15:]
    state_hbm, grad_hbm, gsource_hbm = outs
    rows = grad.shape[1]
    s = Sweeps(c, (e0, e1), (w0, w1), turned, (d0, d1), (x0, x1), (m0, m1), adj, state)
    moves = []

    def send(ref, skip, target, at, many):
        move = pltpu.make_async_copy(
            ref.at[:, pl.ds(skip + at, many), :], target.at[:, pl.ds(at, many), :], sems.at[len(moves)]
        )
        move.start()
        moves.append(move)

    def send_edges(ref, skip, target):
        send(ref, skip, target, 0, TILE)
        send(ref, skip, target, rows - TILE, TILE)

    inner = rows - 2 * TILE
    send(state, HALO, state_hbm, TILE, inner)
    send(gsource, 0, gsource_hbm, TILE, inner)
    send(grad, 0, grad_hbm, TILE, inner)
    odd_lat = is_odd("lat")
    for row, low in ((0, True), (HALO + rows, False)):
        pole = lax.axis_index("lat") == (0 if low else lax.axis_size("lat") - 1)
        from_one = odd_lat if low else jnp.logical_not(odd_lat)
        to = pl.ds(row, TILE)

        def got(one, two, i):
            return jnp.where(pole, 0.0, jnp.where(from_one, one[i], two[i]))

        second = [got(second_one, second_two, i) for i in range(c.second)]
        for channel in range(c.first):
            e0[channel, to, :] = got(first_one, first_two, channel)
        e0[c.ce, to, :], e0[c.cn, to, :] = second[c.strips : c.cot_at]
        for k in range(c.levels):
            tile = second[c.cot_at + k // 2]
            if (k % 2 == 0) == low:
                tile = pltpu.roll(tile, TILE // 2, 0)
            e0[c.cot + k, to, :] = tile
        s.spread(row, second[: c.parts], second[c.parts : c.strips])
        s.western(row)
    top = lambda i: HALO + i - (DEPTH - 1)
    bottom = lambda i: HALO + rows - 1 - i
    places = lambda i: (top(i), bottom(i))
    s.over(s.diagonal, places(0), 2)
    for n in range(STEPS):
        s.over(functools.partial(s.forward, n), places(n), 2)
    send_edges(state, HALO, state_hbm)
    for n in range(STEPS - 1, 0, -1):
        s.over(functools.partial(s.backward, n), places(2 * STEPS - 1 - n), 2)
    for row in places(DEPTH - 1):
        for k, value in s.source_gradient(row):
            s.put(gsource, k, pl.ds(row - HALO, TILE), value)
    s.flush()
    send_edges(gsource, 0, gsource_hbm)
    for row in places(DEPTH - 1):
        for k, value in s.gradient(row):
            s.put(grad, k, pl.ds(row - HALO, TILE), value)
    s.flush()
    send_edges(grad, 0, grad_hbm)
    for move in moves:
        move.wait()


def swaps(count, offset):
    pairs = [(i, (i + 1) % count) for i in range(offset, count, 2)]
    return pairs + [(j, i) for i, j in pairs]


def lat_swaps(lat, lon, offset):
    pairs, alone = [], set(range(lat))
    for i in range(offset, lat - 1, 2):
        alone -= {i, i + 1}
        pairs += [(i * lon + j, (i + 1) * lon + j) for j in range(lon)]
    for i in sorted(alone):
        pairs += [(i * lon + j, i * lon + j + 1) for j in range(0, lon, 2)]
    return pairs + [(j, i) for i, j in pairs]


def body(initial_state, source, cotangent, face_coefs, land_mask, bottom):
    arguments = (initial_state, source, cotangent, face_coefs, land_mask, bottom)
    levels, rows, lanes = initial_state.shape
    c = Names(levels)
    span = rows + 2 * HALO
    f32 = lambda *shape: jax.ShapeDtypeStruct(shape, jnp.float32)
    vmem, hbm = pl.BlockSpec(memory_space=pltpu.VMEM), pl.BlockSpec(memory_space=pltpu.HBM)
    params = pltpu.CompilerParams(vmem_limit_bytes=8 * 1024 * 1024)

    fields, one, two, lat_one, lat_two = pl.pallas_call(
        functools.partial(pack_kernel, c),
        out_shape=(f32(c.count, span, lanes), *(f32(c.parts, rows, lanes),) * 2, *(f32(c.first, TILE, lanes),) * 2),
        in_specs=[hbm] * 6,
        out_specs=(vmem,) * 5,
        scratch_shapes=[
            pltpu.VMEM((levels, rows, lanes), jnp.float32),
            pltpu.VMEM((levels, rows, lanes), jnp.float32),
            pltpu.VMEM((2, rows, lanes), jnp.float32),
            pltpu.VMEM((levels, rows, lanes), jnp.int32),
            pltpu.VMEM((rows, lanes), jnp.int32),
            pltpu.SemaphoreType.DMA((2 + 4 * -(-levels // PIECE),)),
        ],
        compiler_params=params,
        name="pack",
    )(*(pltpu.with_memory_space_constraint(x, pltpu.HBM) for x in arguments))
    lon, lat = lax.axis_size("lon"), lax.axis_size("lat")
    one = lax.ppermute(one, "lon", swaps(lon, 0))
    two = lax.ppermute(two, "lon", swaps(lon, 1))
    both = ("lat", "lon")
    lat_pairs, other_pairs = lat_swaps(lat, lon, 0), lat_swaps(lat, lon, 1)
    first = lax.ppermute(lat_one, both, lat_pairs), lax.ppermute(lat_two, both, other_pairs)
    lat_one, lat_two = pl.pallas_call(
        functools.partial(corner_kernel, c),
        out_shape=(f32(c.second, TILE, lanes),) * 2,
        in_specs=[vmem] * 3,
        out_specs=(vmem,) * 2,
        compiler_params=params,
        name="corners",
    )(fields, one, two)
    second = lax.ppermute(lat_one, both, lat_pairs), lax.ppermute(lat_two, both, other_pairs)
    both = lambda many: (f32(many * levels, span, lanes), f32(many * c.half, span, lanes))
    shapes = (
        f32(c.count, span, lanes),
        f32(c.pairs, span, lanes),
        f32(span, lanes),
        f32(span, lanes),
        f32(3, span, lanes),
        *both(1),
        *both(2 * STEPS - 1),
        *both(STEPS - 1),
        f32((STEPS - 1) * levels, span, lanes),
        f32(levels, span, lanes),
        f32(levels, rows, lanes),
        f32(levels, rows, lanes),
    )
    own = pl.pallas_call(
        functools.partial(own_kernel, c),
        out_shape=shapes[1:],
        in_specs=[vmem] * 3,
        out_specs=(vmem,) * (len(shapes) - 1),
        compiler_params=params,
        cost_estimate=pl.CostEstimate(
            flops=2 * STEPS * levels * rows * lanes * 40, bytes_accessed=16 * 2**20, transcendentals=0
        ),
        name="own_rows",
    )(fields, one, two)
    out = pl.pallas_call(
        functools.partial(edge_kernel, c),
        out_shape=(*shapes, *(f32(levels, rows, lanes),) * 3),
        in_specs=[vmem] * (4 + len(shapes)),
        out_specs=(*(vmem,) * len(shapes), hbm, hbm, hbm),
        input_output_aliases={4 + i: i for i in range(len(shapes))},
        scratch_shapes=[pltpu.SemaphoreType.DMA((9,))],
        compiler_params=params,
        name="edge_rows",
    )(*first, *second[::-1], fields, *own)
    return tuple(out[len(shapes) :])


def solution(mesh):
    block = P(None, "lat", "lon")
    return jax.shard_map(
        body,
        mesh=mesh,
        in_specs=(block, block, block, block, block, P("lat", "lon")),
        out_specs=(block, block, block),
        check_vma=False,
    )
```

```python
import functools

import jax
import jax.numpy as jnp
from jax import lax
from jax.experimental import pallas as pl
from jax.experimental.pallas import tpu as pltpu
from jax.sharding import PartitionSpec as P

STEPS = 4
DEPTH = 2 * STEPS
TILE = 8
HALO = TILE
PIECE = 2

vertical_coef = 0.04


class Names:
    def __init__(self, levels):
        self.levels = levels
        self.u, self.s, self.wet = 0, levels, 2 * levels
        self.ce, self.cn, self.cot = 3 * levels, 3 * levels + 1, 3 * levels + 2
        self.count = 4 * levels + 2
        self.parts = -(-self.count // 16)
        self.strips = 2 * self.parts
        self.first = self.ce
        self.cot_at = self.strips + 2
        self.second = self.cot_at + -(-levels // 2)


def lane_iota(lanes):
    return lax.broadcasted_iota(jnp.int32, (TILE, lanes), 1)


def shift_of(channel):
    place = channel % 16
    return 2 * DEPTH * (place % 8) + DEPTH * (place // 8)


def even_groups(lanes):
    return lax.rem(lane_iota(lanes) // DEPTH, 2) == 0


def is_odd(axis):
    return lax.rem(lax.axis_index(axis), 2) == 1


def strip_rows(c, m):
    return range(16 * m, min(16 * m + 16, c.count))


def pack_kernel(
    c, u_hbm, s_hbm, a_hbm, c_hbm, land_hbm, bottom_hbm, f_ref, first_ref, second_ref, lat_one_ref, lat_two_ref,
    u_ref, s_ref, c_ref, land_ref, bottom_ref, sems,
):
    levels = c.levels
    _, rows, lanes = u_ref.shape
    pieces = [(bottom_hbm, bottom_ref)]
    groups = [range(k, min(k + PIECE, levels)) for k in range(0, levels, PIECE)]
    for held in groups:
        at = pl.ds(held.start, len(held))
        pieces += [(land_hbm.at[at], land_ref.at[at]), (u_hbm.at[at], u_ref.at[at]), (s_hbm.at[at], s_ref.at[at])]
    pieces.append((c_hbm, c_ref))
    for held in groups:
        pieces.append((a_hbm.at[pl.ds(held.start, len(held))], f_ref.at[pl.ds(c.cot + held.start, len(held))]))
    moves = [pltpu.make_async_copy(source, target, sems.at[i]) for i, (source, target) in enumerate(pieces)]
    for move in moves:
        move.start()
    last_lat = lax.axis_index("lat") == lax.axis_size("lat") - 1
    moves[0].wait()
    for i, held in enumerate(groups):
        for move in moves[1 + 3 * i : 4 + 3 * i]:
            move.wait()
        for k in held:
            wet = jnp.where(k < bottom_ref[...], land_ref[k], 0).astype(jnp.float32)
            f_ref[c.u + k] = wet * u_ref[k]
            f_ref[c.s + k] = wet * s_ref[k]
            f_ref[c.wet + k] = wet
    for move in moves[1 + 3 * len(groups) :]:
        move.wait()
    f_ref[c.ce] = c_ref[0]
    row = lax.broadcasted_iota(jnp.int32, (rows, lanes), 0)
    f_ref[c.cn] = jnp.where(jnp.logical_and(last_lat, row == rows - 1), 0.0, c_ref[1])
    odd = is_odd("lon")
    group, groups = lane_iota(lanes) // DEPTH, lanes // DEPTH
    for t in range(rows // TILE):
        at = pl.ds(t * TILE, TILE)
        for m in range(c.parts):
            east = jnp.zeros((TILE, lanes), jnp.float32)
            west = east
            for channel in strip_rows(c, m):
                shift = shift_of(channel)
                tile = f_ref[channel, at, :]
                if shift:
                    tile = pltpu.roll(tile, shift, 1)
                east = jnp.where(group == shift // DEPTH, tile, east)
                west = jnp.where(group == (shift // DEPTH - 1) % groups, tile, west)
            first_ref[m, at, :] = jnp.where(odd, east, west)
            second_ref[m, at, :] = jnp.where(odd, west, east)
    odd_lat = is_odd("lat")
    for channel in range(c.first):
        high, low = f_ref[channel, pl.ds(rows - TILE, TILE), :], f_ref[channel, pl.ds(0, TILE), :]
        lat_one_ref[channel] = jnp.where(odd_lat, low, high)
        lat_two_ref[channel] = jnp.where(odd_lat, high, low)


def corner_kernel(c, f_ref, one_ref, two_ref, lat_one_ref, lat_two_ref):
    odd_lat, odd_lon = is_odd("lat"), is_odd("lon")
    _, rows, lanes = f_ref.shape
    half = TILE // 2
    first_half = lax.broadcasted_iota(jnp.int32, (TILE, lanes), 0) < half
    low, high = pl.ds(0, TILE), pl.ds(rows - TILE, TILE)

    def put(i, low_tile, high_tile):
        lat_one_ref[i] = jnp.where(odd_lat, low_tile, high_tile)
        lat_two_ref[i] = jnp.where(odd_lat, high_tile, low_tile)

    for m in range(c.parts):
        ends = [(one_ref[m, at, :], two_ref[m, at, :]) for at in (low, high)]
        put(m, *(jnp.where(odd_lon, two, one) for one, two in ends))
        put(c.parts + m, *(jnp.where(odd_lon, one, two) for one, two in ends))
    put(c.strips, f_ref[c.ce, low, :], f_ref[c.ce, high, :])
    put(c.strips + 1, f_ref[c.cn, low, :], f_ref[c.cn, high, :])
    for q in range(c.second - c.cot_at):
        one, two = c.cot + 2 * q, c.cot + min(2 * q + 1, c.levels - 1)
        put(
            c.cot_at + q,
            jnp.where(first_half, f_ref[one, low, :], pltpu.roll(f_ref[two, low, :], half, 0)),
            jnp.where(first_half, pltpu.roll(f_ref[one, high, :], half, 0), f_ref[two, high, :]),
        )


class Sweeps:
    def __init__(self, c, e, w, d, x, m, adj, state):
        self.c, self.e, self.w, self.d, self.x, self.m, self.adj, self.state = c, e, w, d, x, m, adj, state
        self.held = []
        self.lanes = e[0].shape[-1]
        lane = lane_iota(self.lanes)
        self.at_first, self.at_last = lane == 0, lane == self.lanes - 1
        self.even_group = even_groups(self.lanes)

    def from_west(self, x0, x1, halves=2):
        tiles = [jnp.where(self.at_last, x1, x0), jnp.where(self.at_last, x0, x1)]
        return [pltpu.roll(tile, 1, 1) for tile in tiles[:halves]]

    def from_east(self, x0, x1, halves=2):
        tiles = [jnp.where(self.at_first, x1, x0), jnp.where(self.at_first, x0, x1)]
        return [pltpu.roll(tile, self.lanes - 1, 1) for tile in tiles[:halves]]

    def spread(self, row, easts, wests):
        for m, (east, west) in enumerate(zip(easts, wests)):
            both = jnp.where(self.even_group, east, west), jnp.where(self.even_group, west, east)
            for channel in strip_rows(self.c, m):
                shift = shift_of(channel)
                tile = both[(channel % 16) // 8]
                if shift:
                    tile = pltpu.roll(tile, self.lanes - shift, 1)
                self.e[1][channel, pl.ds(row, TILE), :] = tile

    def western(self, row):
        at = pl.ds(row, TILE)
        self.w[0][at, :], self.w[1][at, :] = self.from_west(self.e[0][self.c.ce, at, :], self.e[1][self.c.ce, at, :])

    def neighbours(self, load, row, halves=2):
        c, at = self.c, pl.ds(row, TILE)
        ce = [e[c.ce, at, :] for e in self.e]
        cw = [w[at, :] for w in self.w]
        cn = [e[c.cn, at, :] for e in self.e]
        cs = [e[c.cn, pl.ds(row - 1, TILE), :] for e in self.e]
        own = [(load(0, k, at), load(1, k, at)) for k in range(c.levels)]
        out = []
        for k in range(c.levels):
            east, west = self.from_east(*own[k], halves), self.from_west(*own[k], halves)
            pair = []
            for h in range(halves):
                north, south = load(h, k, pl.ds(row + 1, TILE)), load(h, k, pl.ds(row - 1, TILE))
                total = (ce[h] * east[h] + cw[h] * west[h]) + (cn[h] * north + cs[h] * south)
                around = [own[j][h] for j in (k - 1, k + 1) if 0 <= j < c.levels]
                pair.append((own[k][h], total + vertical_coef * functools.reduce(jnp.add, around)))
            out.append(pair)
        return out

    def put(self, ref, k, at, value):
        self.held.append((ref, k, at, value))

    def flush(self):
        for ref, k, at, value in self.held:
            ref[k, at, :] = value
        self.held = []

    def diagonal(self, row):
        load = lambda h, k, at: self.e[h][self.c.wet + k, at, :]
        for k, pair in enumerate(self.neighbours(load, row)):
            for h, (_, total) in enumerate(pair):
                self.put(self.d[h], k, pl.ds(row, TILE), 1.0 - total)

    def loader(self, index):
        if index == 0:
            return lambda h, k, at: self.e[h][self.c.u + k, at, :]
        base = (index - 1) * self.c.levels
        return lambda h, k, at: self.x[h][base + k, at, :]

    def forward(self, n, row):
        c, at = self.c, pl.ds(row, TILE)
        for k, pair in enumerate(self.neighbours(self.loader(n), row)):
            for h, (own, total) in enumerate(pair):
                e = self.e[h]
                wet = e[c.wet + k, at, :]
                bounded = wet * jnp.tanh(self.d[h][k, at, :] * own + total)
                slope = wet - bounded * bounded
                if n < STEPS - 1:
                    self.put(self.x[h], n * c.levels + k, at, bounded + e[c.s + k, at, :])
                    self.put(self.m[h], n * c.levels + k, at, slope)
                else:
                    if h == 0:
                        self.put(self.state, k, at, bounded + e[c.s + k, at, :])
                    self.put(self.x[h], n * c.levels + k, at, slope * e[c.cot + k, at, :])

    def backward(self, n, row):
        c, at = self.c, pl.ds(row, TILE)
        index = 2 * STEPS - 1 - n
        for k, pair in enumerate(self.neighbours(self.loader(index), row)):
            for h, (own, total) in enumerate(pair):
                value = self.d[h][k, at, :] * own + total
                if h == 0:
                    self.put(self.adj, (n - 1) * c.levels + k, at, value)
                self.put(self.x[h], index * c.levels + k, at, self.m[h][(n - 1) * c.levels + k, at, :] * value)

    def over(self, step, rows, together):
        for i, row in enumerate(rows):
            step(row)
            if (i + 1) % together == 0:
                self.flush()
        self.flush()

    def gradient(self, row):
        c, at = self.c, pl.ds(row, TILE)
        for k, pair in enumerate(self.neighbours(self.loader(2 * STEPS - 1), row, 1)):
            own, total = pair[0]
            yield k, self.e[0][c.wet + k, at, :] * (self.d[0][k, at, :] * own + total)

    def source_gradient(self, row):
        c, at = self.c, pl.ds(row, TILE)
        for k in range(c.levels):
            total = self.e[0][c.cot + k, at, :]
            for n in range(STEPS - 1):
                total = total + self.adj[n * c.levels + k, at, :]
            yield k, self.e[0][c.wet + k, at, :] * total


def own_kernel(c, f_ref, one_ref, two_ref, e0, e1, w0, w1, d0, d1, x0, x1, m0, m1, adj, state, grad, gsource):
    rows = f_ref.shape[1]
    odd_lon = is_odd("lon")
    s = Sweeps(c, (e0, e1), (w0, w1), (d0, d1), (x0, x1), (m0, m1), adj, state)
    zero = jnp.zeros((TILE, f_ref.shape[2]), jnp.float32)
    for ref in (e0, e1):
        for end in (pl.ds(0, TILE), pl.ds(HALO + rows, TILE)):
            for channel in (*range(c.u, c.u + c.levels), *range(c.wet, c.wet + c.levels), c.cn):
                ref[channel, end, :] = zero
    tiles = rows // TILE
    places = [HALO + t * TILE for t in range(tiles)]
    for t, row in enumerate(places):
        at, to = pl.ds(t * TILE, TILE), pl.ds(row, TILE)
        for channel in range(c.count):
            e0[channel, to, :] = f_ref[channel, at, :]
        pairs = [(one_ref[m, at, :], two_ref[m, at, :]) for m in range(c.parts)]
        s.spread(
            row,
            [jnp.where(odd_lon, two, one) for one, two in pairs],
            [jnp.where(odd_lon, one, two) for one, two in pairs],
        )
        s.western(row)
    s.over(s.diagonal, places, 1)
    for n in range(STEPS):
        s.over(functools.partial(s.forward, n), places, 1)
    for n in range(STEPS - 1, 0, -1):
        s.over(functools.partial(s.backward, n), places, 1)
    for row in places[1:-1]:
        at = pl.ds(row - HALO, TILE)
        for k, value in s.source_gradient(row):
            gsource[k, at, :] = value
        for k, value in s.gradient(row):
            grad[k, at, :] = value


def edge_kernel(
    c, first_one, first_two, second_two, second_one, *refs,
):
    aliased = refs[: len(refs) // 2]
    del aliased
    e0, e1, w0, w1, d0, d1, x0, x1, m0, m1, adj, state, grad, gsource, state_hbm, grad_hbm, gsource_hbm, sems = refs[14:]
    rows = grad.shape[1]
    s = Sweeps(c, (e0, e1), (w0, w1), (d0, d1), (x0, x1), (m0, m1), adj, state)
    moves = []

    def send(ref, skip, target, at, many):
        move = pltpu.make_async_copy(
            ref.at[:, pl.ds(skip + at, many), :], target.at[:, pl.ds(at, many), :], sems.at[len(moves)]
        )
        move.start()
        moves.append(move)

    def send_edges(ref, skip, target):
        send(ref, skip, target, 0, TILE)
        send(ref, skip, target, rows - TILE, TILE)

    inner = rows - 2 * TILE
    send(state, HALO, state_hbm, TILE, inner)
    send(gsource, 0, gsource_hbm, TILE, inner)
    send(grad, 0, grad_hbm, TILE, inner)
    odd_lat = is_odd("lat")
    for row, low in ((0, True), (HALO + rows, False)):
        pole = lax.axis_index("lat") == (0 if low else lax.axis_size("lat") - 1)
        from_one = odd_lat if low else jnp.logical_not(odd_lat)
        to = pl.ds(row, TILE)

        def got(one, two, i):
            return jnp.where(pole, 0.0, jnp.where(from_one, one[i], two[i]))

        second = [got(second_one, second_two, i) for i in range(c.second)]
        for channel in range(c.first):
            e0[channel, to, :] = got(first_one, first_two, channel)
        e0[c.ce, to, :], e0[c.cn, to, :] = second[c.strips : c.cot_at]
        for k in range(c.levels):
            tile = second[c.cot_at + k // 2]
            if (k % 2 == 0) == low:
                tile = pltpu.roll(tile, TILE // 2, 0)
            e0[c.cot + k, to, :] = tile
        s.spread(row, second[: c.parts], second[c.parts : c.strips])
        s.western(row)
    top = lambda i: HALO + i - (DEPTH - 1)
    bottom = lambda i: HALO + rows - 1 - i
    places = lambda i: (top(i), bottom(i))
    s.over(s.diagonal, places(0), 2)
    for n in range(STEPS):
        s.over(functools.partial(s.forward, n), places(n), 2)
    send_edges(state, HALO, state_hbm)
    for n in range(STEPS - 1, 0, -1):
        s.over(functools.partial(s.backward, n), places(2 * STEPS - 1 - n), 2)
    for row in places(DEPTH - 1):
        for k, value in s.source_gradient(row):
            s.put(gsource, k, pl.ds(row - HALO, TILE), value)
    s.flush()
    send_edges(gsource, 0, gsource_hbm)
    for row in places(DEPTH - 1):
        for k, value in s.gradient(row):
            s.put(grad, k, pl.ds(row - HALO, TILE), value)
    s.flush()
    send_edges(grad, 0, grad_hbm)
    for move in moves:
        move.wait()


def swaps(count, offset):
    pairs = [(i, (i + 1) % count) for i in range(offset, count, 2)]
    return pairs + [(j, i) for i, j in pairs]


def lat_swaps(lat, lon, offset):
    pairs, alone = [], set(range(lat))
    for i in range(offset, lat - 1, 2):
        alone -= {i, i + 1}
        pairs += [(i * lon + j, (i + 1) * lon + j) for j in range(lon)]
    for i in sorted(alone):
        pairs += [(i * lon + j, i * lon + j + 1) for j in range(0, lon, 2)]
    return pairs + [(j, i) for i, j in pairs]


def body(initial_state, source, cotangent, face_coefs, land_mask, bottom):
    arguments = (initial_state, source, cotangent, face_coefs, land_mask, bottom)
    levels, rows, lanes = initial_state.shape
    c = Names(levels)
    span = rows + 2 * HALO
    f32 = lambda *shape: jax.ShapeDtypeStruct(shape, jnp.float32)
    vmem, hbm = pl.BlockSpec(memory_space=pltpu.VMEM), pl.BlockSpec(memory_space=pltpu.HBM)
    params = pltpu.CompilerParams(vmem_limit_bytes=8 * 1024 * 1024)

    fields, one, two, lat_one, lat_two = pl.pallas_call(
        functools.partial(pack_kernel, c),
        out_shape=(f32(c.count, rows, lanes), *(f32(c.parts, rows, lanes),) * 2, *(f32(c.first, TILE, lanes),) * 2),
        in_specs=[hbm] * 6,
        out_specs=(vmem,) * 5,
        scratch_shapes=[
            pltpu.VMEM((levels, rows, lanes), jnp.float32),
            pltpu.VMEM((levels, rows, lanes), jnp.float32),
            pltpu.VMEM((2, rows, lanes), jnp.float32),
            pltpu.VMEM((levels, rows, lanes), jnp.int32),
            pltpu.VMEM((rows, lanes), jnp.int32),
            pltpu.SemaphoreType.DMA((2 + 4 * -(-levels // PIECE),)),
        ],
        compiler_params=params,
        name="pack",
    )(*(pltpu.with_memory_space_constraint(x, pltpu.HBM) for x in arguments))
    lon, lat = lax.axis_size("lon"), lax.axis_size("lat")
    one = lax.ppermute(one, "lon", swaps(lon, 0))
    two = lax.ppermute(two, "lon", swaps(lon, 1))
    both = ("lat", "lon")
    lat_pairs, other_pairs = lat_swaps(lat, lon, 0), lat_swaps(lat, lon, 1)
    first = lax.ppermute(lat_one, both, lat_pairs), lax.ppermute(lat_two, both, other_pairs)
    lat_one, lat_two = pl.pallas_call(
        functools.partial(corner_kernel, c),
        out_shape=(f32(c.second, TILE, lanes),) * 2,
        in_specs=[vmem] * 3,
        out_specs=(vmem,) * 2,
        compiler_params=params,
        name="corners",
    )(fields, one, two)
    second = lax.ppermute(lat_one, both, lat_pairs), lax.ppermute(lat_two, both, other_pairs)
    twice = lambda *shape: (f32(*shape), f32(*shape))
    shapes = (
        *twice(c.count, span, lanes),
        *twice(span, lanes),
        *twice(levels, span, lanes),
        *twice((2 * STEPS - 1) * levels, span, lanes),
        *twice((STEPS - 1) * levels, span, lanes),
        f32((STEPS - 1) * levels, span, lanes),
        f32(levels, span, lanes),
        f32(levels, rows, lanes),
        f32(levels, rows, lanes),
    )
    own = pl.pallas_call(
        functools.partial(own_kernel, c),
        out_shape=shapes,
        in_specs=[vmem] * 3,
        out_specs=(vmem,) * len(shapes),
        compiler_params=params,
        cost_estimate=pl.CostEstimate(
            flops=2 * STEPS * levels * rows * lanes * 40, bytes_accessed=16 * 2**20, transcendentals=0
        ),
        name="own_rows",
    )(fields, one, two)
    out = pl.pallas_call(
        functools.partial(edge_kernel, c),
        out_shape=(*shapes, *(f32(levels, rows, lanes),) * 3),
        in_specs=[vmem] * (4 + len(shapes)),
        out_specs=(*(vmem,) * len(shapes), hbm, hbm, hbm),
        input_output_aliases={4 + i: i for i in range(len(shapes))},
        scratch_shapes=[pltpu.SemaphoreType.DMA((9,))],
        compiler_params=params,
        name="edge_rows",
    )(*first, *second[::-1], *own)
    return tuple(out[len(shapes) :])


def solution(mesh):
    block = P(None, "lat", "lon")
    return jax.shard_map(
        body,
        mesh=mesh,
        in_specs=(block, block, block, block, block, P("lat", "lon")),
        out_specs=(block, block, block),
        check_vma=False,
    )
```

```python
import functools

import jax
import jax.numpy as jnp
from jax import lax
from jax.experimental import pallas as pl
from jax.experimental.pallas import tpu as pltpu
from jax.sharding import PartitionSpec as P

STEPS = 4
DEPTH = 2 * STEPS
TILE = 8
HALO = TILE
PIECE = 2

vertical_coef = 0.04


class Names:
    def __init__(self, levels):
        self.levels = levels
        self.u, self.s, self.wet = 0, levels, 2 * levels
        self.ce, self.cn, self.cot = 3 * levels, 3 * levels + 1, 3 * levels + 2
        self.count = 4 * levels + 2
        self.parts = -(-self.count // 16)
        self.strips = 2 * self.parts
        self.first = self.ce
        self.cot_at = self.strips + 2
        self.second = self.cot_at + -(-levels // 2)


def lane_iota(lanes):
    return lax.broadcasted_iota(jnp.int32, (TILE, lanes), 1)


def shift_of(channel):
    place = channel % 16
    return 2 * DEPTH * (place % 8) + DEPTH * (place // 8)


def even_groups(lanes):
    return lax.rem(lane_iota(lanes) // DEPTH, 2) == 0


def is_odd(axis):
    return lax.rem(lax.axis_index(axis), 2) == 1


def strip_rows(c, m):
    return range(16 * m, min(16 * m + 16, c.count))


def pack_kernel(
    c, u_hbm, s_hbm, a_hbm, c_hbm, land_hbm, bottom_hbm, f_ref, first_ref, second_ref, lat_one_ref, lat_two_ref,
    u_ref, s_ref, c_ref, land_ref, bottom_ref, sems,
):
    levels = c.levels
    _, rows, lanes = u_ref.shape
    pieces = [(bottom_hbm, bottom_ref)]
    groups = [range(k, min(k + PIECE, levels)) for k in range(0, levels, PIECE)]
    for held in groups:
        at = pl.ds(held.start, len(held))
        pieces += [(land_hbm.at[at], land_ref.at[at]), (u_hbm.at[at], u_ref.at[at]), (s_hbm.at[at], s_ref.at[at])]
    pieces.append((c_hbm, c_ref))
    for held in groups:
        pieces.append((a_hbm.at[pl.ds(held.start, len(held))], f_ref.at[pl.ds(c.cot + held.start, len(held))]))
    moves = [pltpu.make_async_copy(source, target, sems.at[i]) for i, (source, target) in enumerate(pieces)]
    for move in moves:
        move.start()
    last_lat = lax.axis_index("lat") == lax.axis_size("lat") - 1
    moves[0].wait()
    for i, held in enumerate(groups):
        for move in moves[1 + 3 * i : 4 + 3 * i]:
            move.wait()
        for k in held:
            wet = jnp.where(k < bottom_ref[...], land_ref[k], 0).astype(jnp.float32)
            f_ref[c.u + k] = wet * u_ref[k]
            f_ref[c.s + k] = wet * s_ref[k]
            f_ref[c.wet + k] = wet
    odd_lat = is_odd("lat")
    for channel in range(c.first):
        high, low = f_ref[channel, pl.ds(rows - TILE, TILE), :], f_ref[channel, pl.ds(0, TILE), :]
        lat_one_ref[channel] = jnp.where(odd_lat, low, high)
        lat_two_ref[channel] = jnp.where(odd_lat, high, low)
    odd = is_odd("lon")
    group, lane_groups = lane_iota(lanes) // DEPTH, lanes // DEPTH

    def strips(m):
        for t in range(rows // TILE):
            at = pl.ds(t * TILE, TILE)
            east = jnp.zeros((TILE, lanes), jnp.float32)
            west = east
            for channel in strip_rows(c, m):
                shift = shift_of(channel)
                tile = f_ref[channel, at, :]
                if shift:
                    tile = pltpu.roll(tile, shift, 1)
                east = jnp.where(group == shift // DEPTH, tile, east)
                west = jnp.where(group == (shift // DEPTH - 1) % lane_groups, tile, west)
            first_ref[m, at, :] = jnp.where(odd, east, west)
            second_ref[m, at, :] = jnp.where(odd, west, east)

    ready = c.ce // 16
    for m in range(ready):
        strips(m)
    for move in moves[1 + 3 * len(groups) :]:
        move.wait()
    f_ref[c.ce] = c_ref[0]
    row = lax.broadcasted_iota(jnp.int32, (rows, lanes), 0)
    f_ref[c.cn] = jnp.where(jnp.logical_and(last_lat, row == rows - 1), 0.0, c_ref[1])
    for m in range(ready, c.parts):
        strips(m)


def corner_kernel(c, f_ref, one_ref, two_ref, lat_one_ref, lat_two_ref):
    odd_lat, odd_lon = is_odd("lat"), is_odd("lon")
    _, rows, lanes = f_ref.shape
    half = TILE // 2
    first_half = lax.broadcasted_iota(jnp.int32, (TILE, lanes), 0) < half
    low, high = pl.ds(0, TILE), pl.ds(rows - TILE, TILE)

    def put(i, low_tile, high_tile):
        lat_one_ref[i] = jnp.where(odd_lat, low_tile, high_tile)
        lat_two_ref[i] = jnp.where(odd_lat, high_tile, low_tile)

    for m in range(c.parts):
        ends = [(one_ref[m, at, :], two_ref[m, at, :]) for at in (low, high)]
        put(m, *(jnp.where(odd_lon, two, one) for one, two in ends))
        put(c.parts + m, *(jnp.where(odd_lon, one, two) for one, two in ends))
    put(c.strips, f_ref[c.ce, low, :], f_ref[c.ce, high, :])
    put(c.strips + 1, f_ref[c.cn, low, :], f_ref[c.cn, high, :])
    for q in range(c.second - c.cot_at):
        one, two = c.cot + 2 * q, c.cot + min(2 * q + 1, c.levels - 1)
        put(
            c.cot_at + q,
            jnp.where(first_half, f_ref[one, low, :], pltpu.roll(f_ref[two, low, :], half, 0)),
            jnp.where(first_half, pltpu.roll(f_ref[one, high, :], half, 0), f_ref[two, high, :]),
        )


class Sweeps:
    def __init__(self, c, e, w, d, x, m, adj, state):
        self.c, self.e, self.w, self.d, self.x, self.m, self.adj, self.state = c, e, w, d, x, m, adj, state
        self.held = []
        self.lanes = e[0].shape[-1]
        lane = lane_iota(self.lanes)
        self.at_first, self.at_last = lane == 0, lane == self.lanes - 1
        self.even_group = even_groups(self.lanes)

    def from_west(self, x0, x1):
        r0, r1 = pltpu.roll(x0, 1, 1), pltpu.roll(x1, 1, 1)
        return jnp.where(self.at_first, r1, r0), jnp.where(self.at_first, r0, r1)

    def from_east(self, x0, x1):
        r0, r1 = pltpu.roll(x0, self.lanes - 1, 1), pltpu.roll(x1, self.lanes - 1, 1)
        return jnp.where(self.at_last, r1, r0), jnp.where(self.at_last, r0, r1)

    def spread(self, row, easts, wests):
        for m, (east, west) in enumerate(zip(easts, wests)):
            both = jnp.where(self.even_group, east, west), jnp.where(self.even_group, west, east)
            for channel in strip_rows(self.c, m):
                shift = shift_of(channel)
                tile = both[(channel % 16) // 8]
                if shift:
                    tile = pltpu.roll(tile, self.lanes - shift, 1)
                self.e[1][channel, pl.ds(row, TILE), :] = tile

    def western(self, row):
        at = pl.ds(row, TILE)
        self.w[0][at, :], self.w[1][at, :] = self.from_west(self.e[0][self.c.ce, at, :], self.e[1][self.c.ce, at, :])

    def neighbours(self, load, row, halves=2):
        c, at = self.c, pl.ds(row, TILE)
        ce = [e[c.ce, at, :] for e in self.e]
        cw = [w[at, :] for w in self.w]
        cn = [e[c.cn, at, :] for e in self.e]
        cs = [e[c.cn, pl.ds(row - 1, TILE), :] for e in self.e]
        own = [(load(0, k, at), load(1, k, at)) for k in range(c.levels)]
        out = []
        for k in range(c.levels):
            east, west = self.from_east(*own[k]), self.from_west(*own[k])
            pair = []
            for h in range(halves):
                north, south = load(h, k, pl.ds(row + 1, TILE)), load(h, k, pl.ds(row - 1, TILE))
                total = (ce[h] * east[h] + cw[h] * west[h]) + (cn[h] * north + cs[h] * south)
                around = [own[j][h] for j in (k - 1, k + 1) if 0 <= j < c.levels]
                pair.append((own[k][h], total + vertical_coef * functools.reduce(jnp.add, around)))
            out.append(pair)
        return out

    def put(self, ref, k, at, value):
        self.held.append((ref, k, at, value))

    def flush(self):
        for ref, k, at, value in self.held:
            ref[k, at, :] = value
        self.held = []

    def diagonal(self, row):
        load = lambda h, k, at: self.e[h][self.c.wet + k, at, :]
        for k, pair in enumerate(self.neighbours(load, row)):
            for h, (_, total) in enumerate(pair):
                self.put(self.d[h], k, pl.ds(row, TILE), 1.0 - total)

    def loader(self, index):
        if index == 0:
            return lambda h, k, at: self.e[h][self.c.u + k, at, :]
        base = (index - 1) * self.c.levels
        return lambda h, k, at: self.x[h][base + k, at, :]

    def forward(self, n, row):
        c, at = self.c, pl.ds(row, TILE)
        for k, pair in enumerate(self.neighbours(self.loader(n), row)):
            for h, (own, total) in enumerate(pair):
                e = self.e[h]
                wet = e[c.wet + k, at, :]
                bounded = wet * jnp.tanh(self.d[h][k, at, :] * own + total)
                slope = wet - bounded * bounded
                if n < STEPS - 1:
                    self.put(self.x[h], n * c.levels + k, at, bounded + e[c.s + k, at, :])
                    self.put(self.m[h], n * c.levels + k, at, slope)
                else:
                    if h == 0:
                        self.put(self.state, k, at, bounded + e[c.s + k, at, :])
                    self.put(self.x[h], n * c.levels + k, at, slope * e[c.cot + k, at, :])

    def backward(self, n, row):
        c, at = self.c, pl.ds(row, TILE)
        index = 2 * STEPS - 1 - n
        for k, pair in enumerate(self.neighbours(self.loader(index), row)):
            for h, (own, total) in enumerate(pair):
                value = self.d[h][k, at, :] * own + total
                if h == 0:
                    self.put(self.adj, (n - 1) * c.levels + k, at, value)
                self.put(self.x[h], index * c.levels + k, at, self.m[h][(n - 1) * c.levels + k, at, :] * value)

    def over(self, step, rows, together):
        for i, row in enumerate(rows):
            step(row)
            if (i + 1) % together == 0:
                self.flush()
        self.flush()

    def gradient(self, row):
        c, at = self.c, pl.ds(row, TILE)
        for k, pair in enumerate(self.neighbours(self.loader(2 * STEPS - 1), row, 1)):
            own, total = pair[0]
            yield k, self.e[0][c.wet + k, at, :] * (self.d[0][k, at, :] * own + total)

    def source_gradient(self, row):
        c, at = self.c, pl.ds(row, TILE)
        for k in range(c.levels):
            total = self.e[0][c.cot + k, at, :]
            for n in range(STEPS - 1):
                total = total + self.adj[n * c.levels + k, at, :]
            yield k, self.e[0][c.wet + k, at, :] * total


def own_kernel(c, f_ref, one_ref, two_ref, e0, e1, w0, w1, d0, d1, x0, x1, m0, m1, adj, state, grad, gsource):
    rows = f_ref.shape[1]
    odd_lon = is_odd("lon")
    s = Sweeps(c, (e0, e1), (w0, w1), (d0, d1), (x0, x1), (m0, m1), adj, state)
    zero = jnp.zeros((TILE, f_ref.shape[2]), jnp.float32)
    for ref in (e0, e1):
        for end in (pl.ds(0, TILE), pl.ds(HALO + rows, TILE)):
            for channel in (*range(c.u, c.u + c.levels), *range(c.wet, c.wet + c.levels), c.cn):
                ref[channel, end, :] = zero
    tiles = rows // TILE
    places = [HALO + t * TILE for t in range(tiles)]
    for t, row in enumerate(places):
        at, to = pl.ds(t * TILE, TILE), pl.ds(row, TILE)
        for channel in range(c.count):
            e0[channel, to, :] = f_ref[channel, at, :]
        pairs = [(one_ref[m, at, :], two_ref[m, at, :]) for m in range(c.parts)]
        s.spread(
            row,
            [jnp.where(odd_lon, two, one) for one, two in pairs],
            [jnp.where(odd_lon, one, two) for one, two in pairs],
        )
        s.western(row)
    s.over(s.diagonal, places, 1)
    for n in range(STEPS):
        s.over(functools.partial(s.forward, n), places, 1)
    for n in range(STEPS - 1, 0, -1):
        s.over(functools.partial(s.backward, n), places, 1)
    for row in places[1:-1]:
        at = pl.ds(row - HALO, TILE)
        for k, value in s.source_gradient(row):
            gsource[k, at, :] = value
        for k, value in s.gradient(row):
            grad[k, at, :] = value


def edge_kernel(
    c, first_one, first_two, second_two, second_one, *refs,
):
    aliased = refs[: len(refs) // 2]
    del aliased
    e0, e1, w0, w1, d0, d1, x0, x1, m0, m1, adj, state, grad, gsource, state_hbm, grad_hbm, gsource_hbm, sems = refs[14:]
    rows = grad.shape[1]
    s = Sweeps(c, (e0, e1), (w0, w1), (d0, d1), (x0, x1), (m0, m1), adj, state)
    moves = []

    def send(ref, skip, target, at, many):
        move = pltpu.make_async_copy(
            ref.at[:, pl.ds(skip + at, many), :], target.at[:, pl.ds(at, many), :], sems.at[len(moves)]
        )
        move.start()
        moves.append(move)

    def send_edges(ref, skip, target):
        send(ref, skip, target, 0, TILE)
        send(ref, skip, target, rows - TILE, TILE)

    inner = rows - 2 * TILE
    send(state, HALO, state_hbm, TILE, inner)
    send(gsource, 0, gsource_hbm, TILE, inner)
    send(grad, 0, grad_hbm, TILE, inner)
    odd_lat = is_odd("lat")
    for row, low in ((0, True), (HALO + rows, False)):
        pole = lax.axis_index("lat") == (0 if low else lax.axis_size("lat") - 1)
        from_one = odd_lat if low else jnp.logical_not(odd_lat)
        to = pl.ds(row, TILE)

        def got(one, two, i):
            return jnp.where(pole, 0.0, jnp.where(from_one, one[i], two[i]))

        second = [got(second_one, second_two, i) for i in range(c.second)]
        for channel in range(c.first):
            e0[channel, to, :] = got(first_one, first_two, channel)
        e0[c.ce, to, :], e0[c.cn, to, :] = second[c.strips : c.cot_at]
        for k in range(c.levels):
            tile = second[c.cot_at + k // 2]
            if (k % 2 == 0) == low:
                tile = pltpu.roll(tile, TILE // 2, 0)
            e0[c.cot + k, to, :] = tile
        s.spread(row, second[: c.parts], second[c.parts : c.strips])
        s.western(row)
    top = lambda i: HALO + i - (DEPTH - 1)
    bottom = lambda i: HALO + rows - 1 - i
    places = lambda i: (top(i), bottom(i))
    s.over(s.diagonal, places(0), 2)
    for n in range(STEPS):
        s.over(functools.partial(s.forward, n), places(n), 2)
    send_edges(state, HALO, state_hbm)
    for n in range(STEPS - 1, 0, -1):
        s.over(functools.partial(s.backward, n), places(2 * STEPS - 1 - n), 2)
    for row in places(DEPTH - 1):
        for k, value in s.source_gradient(row):
            s.put(gsource, k, pl.ds(row - HALO, TILE), value)
    s.flush()
    send_edges(gsource, 0, gsource_hbm)
    for row in places(DEPTH - 1):
        for k, value in s.gradient(row):
            s.put(grad, k, pl.ds(row - HALO, TILE), value)
    s.flush()
    send_edges(grad, 0, grad_hbm)
    for move in moves:
        move.wait()


def swaps(count, offset):
    pairs = [(i, (i + 1) % count) for i in range(offset, count, 2)]
    return pairs + [(j, i) for i, j in pairs]


def lat_swaps(lat, lon, offset):
    pairs, alone = [], set(range(lat))
    for i in range(offset, lat - 1, 2):
        alone -= {i, i + 1}
        pairs += [(i * lon + j, (i + 1) * lon + j) for j in range(lon)]
    for i in sorted(alone):
        pairs += [(i * lon + j, i * lon + j + 1) for j in range(0, lon, 2)]
    return pairs + [(j, i) for i, j in pairs]


def body(initial_state, source, cotangent, face_coefs, land_mask, bottom):
    arguments = (initial_state, source, cotangent, face_coefs, land_mask, bottom)
    levels, rows, lanes = initial_state.shape
    c = Names(levels)
    span = rows + 2 * HALO
    f32 = lambda *shape: jax.ShapeDtypeStruct(shape, jnp.float32)
    vmem, hbm = pl.BlockSpec(memory_space=pltpu.VMEM), pl.BlockSpec(memory_space=pltpu.HBM)
    params = pltpu.CompilerParams(vmem_limit_bytes=8 * 1024 * 1024)

    fields, one, two, lat_one, lat_two = pl.pallas_call(
        functools.partial(pack_kernel, c),
        out_shape=(f32(c.count, rows, lanes), *(f32(c.parts, rows, lanes),) * 2, *(f32(c.first, TILE, lanes),) * 2),
        in_specs=[hbm] * 6,
        out_specs=(vmem,) * 5,
        scratch_shapes=[
            pltpu.VMEM((levels, rows, lanes), jnp.float32),
            pltpu.VMEM((levels, rows, lanes), jnp.float32),
            pltpu.VMEM((2, rows, lanes), jnp.float32),
            pltpu.VMEM((levels, rows, lanes), jnp.int32),
            pltpu.VMEM((rows, lanes), jnp.int32),
            pltpu.SemaphoreType.DMA((2 + 4 * -(-levels // PIECE),)),
        ],
        compiler_params=params,
        name="pack",
    )(*(pltpu.with_memory_space_constraint(x, pltpu.HBM) for x in arguments))
    lon, lat = lax.axis_size("lon"), lax.axis_size("lat")
    one = lax.ppermute(one, "lon", swaps(lon, 0))
    two = lax.ppermute(two, "lon", swaps(lon, 1))
    both = ("lat", "lon")
    lat_pairs, other_pairs = lat_swaps(lat, lon, 0), lat_swaps(lat, lon, 1)
    first = lax.ppermute(lat_one, both, lat_pairs), lax.ppermute(lat_two, both, other_pairs)
    lat_one, lat_two = pl.pallas_call(
        functools.partial(corner_kernel, c),
        out_shape=(f32(c.second, TILE, lanes),) * 2,
        in_specs=[vmem] * 3,
        out_specs=(vmem,) * 2,
        compiler_params=params,
        name="corners",
    )(fields, one, two)
    second = lax.ppermute(lat_one, both, lat_pairs), lax.ppermute(lat_two, both, other_pairs)
    twice = lambda *shape: (f32(*shape), f32(*shape))
    shapes = (
        *twice(c.count, span, lanes),
        *twice(span, lanes),
        *twice(levels, span, lanes),
        *twice((2 * STEPS - 1) * levels, span, lanes),
        *twice((STEPS - 1) * levels, span, lanes),
        f32((STEPS - 1) * levels, span, lanes),
        f32(levels, span, lanes),
        f32(levels, rows, lanes),
        f32(levels, rows, lanes),
    )
    own = pl.pallas_call(
        functools.partial(own_kernel, c),
        out_shape=shapes,
        in_specs=[vmem] * 3,
        out_specs=(vmem,) * len(shapes),
        compiler_params=params,
        cost_estimate=pl.CostEstimate(
            flops=2 * STEPS * levels * rows * lanes * 40, bytes_accessed=16 * 2**20, transcendentals=0
        ),
        name="own_rows",
    )(fields, one, two)
    out = pl.pallas_call(
        functools.partial(edge_kernel, c),
        out_shape=(*shapes, *(f32(levels, rows, lanes),) * 3),
        in_specs=[vmem] * (4 + len(shapes)),
        out_specs=(*(vmem,) * len(shapes), hbm, hbm, hbm),
        input_output_aliases={4 + i: i for i in range(len(shapes))},
        scratch_shapes=[pltpu.SemaphoreType.DMA((9,))],
        compiler_params=params,
        name="edge_rows",
    )(*first, *second[::-1], *own)
    return tuple(out[len(shapes) :])


def solution(mesh):
    block = P(None, "lat", "lon")
    return jax.shard_map(
        body,
        mesh=mesh,
        in_specs=(block, block, block, block, block, P("lat", "lon")),
        out_specs=(block, block, block),
        check_vma=False,
    )
```

```python
import functools

import jax
import jax.numpy as jnp
from jax import lax
from jax.experimental import pallas as pl
from jax.experimental.pallas import tpu as pltpu
from jax.sharding import PartitionSpec as P

STEPS = 4
DEPTH = 2 * STEPS
TILE = 8
HALO = TILE
PIECE = 2

vertical_coef = 0.04


class Names:
    def __init__(self, levels):
        self.levels = levels
        self.u, self.s, self.wet = 0, levels, 2 * levels
        self.ce, self.cn, self.cot = 3 * levels, 3 * levels + 1, 3 * levels + 2
        self.count = 4 * levels + 2
        self.parts = -(-self.count // 16)
        self.strips = 2 * self.parts
        self.first = self.ce
        self.cot_at = self.strips + 2
        self.second = self.cot_at + -(-levels // 2)


def lane_iota(lanes):
    return lax.broadcasted_iota(jnp.int32, (TILE, lanes), 1)


def shift_of(channel):
    place = channel % 16
    return 2 * DEPTH * (place % 8) + DEPTH * (place // 8)


def even_groups(lanes):
    return lax.rem(lane_iota(lanes) // DEPTH, 2) == 0


def is_odd(axis):
    return lax.rem(lax.axis_index(axis), 2) == 1


def strip_rows(c, m):
    return range(16 * m, min(16 * m + 16, c.count))


def pack_kernel(
    c, u_hbm, s_hbm, a_hbm, c_hbm, land_hbm, bottom_hbm, f_ref, first_ref, second_ref, lat_one_ref, lat_two_ref,
    u_ref, s_ref, c_ref, land_ref, bottom_ref, sems,
):
    levels = c.levels
    _, rows, lanes = u_ref.shape
    pieces = [(bottom_hbm, bottom_ref)]
    groups = [range(k, min(k + PIECE, levels)) for k in range(0, levels, PIECE)]
    for held in groups:
        at = pl.ds(held.start, len(held))
        pieces += [(land_hbm.at[at], land_ref.at[at]), (u_hbm.at[at], u_ref.at[at]), (s_hbm.at[at], s_ref.at[at])]
    pieces.append((c_hbm, c_ref))
    for held in groups:
        pieces.append((a_hbm.at[pl.ds(held.start, len(held))], f_ref.at[pl.ds(c.cot + held.start, len(held))]))
    moves = [pltpu.make_async_copy(source, target, sems.at[i]) for i, (source, target) in enumerate(pieces)]
    for move in moves:
        move.start()
    last_lat = lax.axis_index("lat") == lax.axis_size("lat") - 1
    moves[0].wait()
    for i, held in enumerate(groups):
        for move in moves[1 + 3 * i : 4 + 3 * i]:
            move.wait()
        for k in held:
            wet = jnp.where(k < bottom_ref[...], land_ref[k], 0).astype(jnp.float32)
            f_ref[c.u + k] = wet * u_ref[k]
            f_ref[c.s + k] = wet * s_ref[k]
            f_ref[c.wet + k] = wet
    for move in moves[1 + 3 * len(groups) :]:
        move.wait()
    f_ref[c.ce] = c_ref[0]
    row = lax.broadcasted_iota(jnp.int32, (rows, lanes), 0)
    f_ref[c.cn] = jnp.where(jnp.logical_and(last_lat, row == rows - 1), 0.0, c_ref[1])
    odd = is_odd("lon")
    group, groups = lane_iota(lanes) // DEPTH, lanes // DEPTH
    for t in range(rows // TILE):
        at = pl.ds(t * TILE, TILE)
        for m in range(c.parts):
            east = jnp.zeros((TILE, lanes), jnp.float32)
            west = east
            for channel in strip_rows(c, m):
                shift = shift_of(channel)
                tile = f_ref[channel, at, :]
                if shift:
                    tile = pltpu.roll(tile, shift, 1)
                east = jnp.where(group == shift // DEPTH, tile, east)
                west = jnp.where(group == (shift // DEPTH - 1) % groups, tile, west)
            first_ref[m, at, :] = jnp.where(odd, east, west)
            second_ref[m, at, :] = jnp.where(odd, west, east)
    odd_lat = is_odd("lat")
    for channel in range(c.first):
        high, low = f_ref[channel, pl.ds(rows - TILE, TILE), :], f_ref[channel, pl.ds(0, TILE), :]
        lat_one_ref[channel] = jnp.where(odd_lat, low, high)
        lat_two_ref[channel] = jnp.where(odd_lat, high, low)


def corner_kernel(c, f_ref, one_ref, two_ref, lat_one_ref, lat_two_ref):
    odd_lat, odd_lon = is_odd("lat"), is_odd("lon")
    _, rows, lanes = f_ref.shape
    half = TILE // 2
    first_half = lax.broadcasted_iota(jnp.int32, (TILE, lanes), 0) < half
    low, high = pl.ds(0, TILE), pl.ds(rows - TILE, TILE)

    def put(i, low_tile, high_tile):
        lat_one_ref[i] = jnp.where(odd_lat, low_tile, high_tile)
        lat_two_ref[i] = jnp.where(odd_lat, high_tile, low_tile)

    for m in range(c.parts):
        ends = [(one_ref[m, at, :], two_ref[m, at, :]) for at in (low, high)]
        put(m, *(jnp.where(odd_lon, two, one) for one, two in ends))
        put(c.parts + m, *(jnp.where(odd_lon, one, two) for one, two in ends))
    put(c.strips, f_ref[c.ce, low, :], f_ref[c.ce, high, :])
    put(c.strips + 1, f_ref[c.cn, low, :], f_ref[c.cn, high, :])
    for q in range(c.second - c.cot_at):
        one, two = c.cot + 2 * q, c.cot + min(2 * q + 1, c.levels - 1)
        put(
            c.cot_at + q,
            jnp.where(first_half, f_ref[one, low, :], pltpu.roll(f_ref[two, low, :], half, 0)),
            jnp.where(first_half, pltpu.roll(f_ref[one, high, :], half, 0), f_ref[two, high, :]),
        )


class Sweeps:
    def __init__(self, c, e, w, d, x, m, adj, state):
        self.c, self.e, self.w, self.d, self.x, self.m, self.adj, self.state = c, e, w, d, x, m, adj, state
        self.lanes = e[0].shape[-1]
        lane = lane_iota(self.lanes)
        self.at_first, self.at_last = lane == 0, lane == self.lanes - 1
        self.even_group = even_groups(self.lanes)

    def from_west(self, x0, x1):
        r0, r1 = pltpu.roll(x0, 1, 1), pltpu.roll(x1, 1, 1)
        return jnp.where(self.at_first, r1, r0), jnp.where(self.at_first, r0, r1)

    def from_east(self, x0, x1):
        r0, r1 = pltpu.roll(x0, self.lanes - 1, 1), pltpu.roll(x1, self.lanes - 1, 1)
        return jnp.where(self.at_last, r1, r0), jnp.where(self.at_last, r0, r1)

    def spread(self, row, easts, wests):
        for m, (east, west) in enumerate(zip(easts, wests)):
            both = jnp.where(self.even_group, east, west), jnp.where(self.even_group, west, east)
            for channel in strip_rows(self.c, m):
                shift = shift_of(channel)
                tile = both[(channel % 16) // 8]
                if shift:
                    tile = pltpu.roll(tile, self.lanes - shift, 1)
                self.e[1][channel, pl.ds(row, TILE), :] = tile

    def western(self, row):
        at = pl.ds(row, TILE)
        self.w[0][at, :], self.w[1][at, :] = self.from_west(self.e[0][self.c.ce, at, :], self.e[1][self.c.ce, at, :])

    def neighbours(self, load, row, halves=2):
        c, at = self.c, pl.ds(row, TILE)
        ce = [e[c.ce, at, :] for e in self.e]
        cw = [w[at, :] for w in self.w]
        cn = [e[c.cn, at, :] for e in self.e]
        cs = [e[c.cn, pl.ds(row - 1, TILE), :] for e in self.e]
        pick = lambda k: (load(0, k, at), load(1, k, at))
        before, own, after = None, pick(0), None
        for k in range(c.levels):
            after = pick(k + 1) if k + 1 < c.levels else None
            east, west = self.from_east(*own), self.from_west(*own)
            pair = []
            for h in range(halves):
                north, south = load(h, k, pl.ds(row + 1, TILE)), load(h, k, pl.ds(row - 1, TILE))
                total = (ce[h] * east[h] + cw[h] * west[h]) + (cn[h] * north + cs[h] * south)
                around = [other[h] for other in (before, after) if other]
                pair.append((own[h], total + vertical_coef * functools.reduce(jnp.add, around)))
            yield pair
            before, own = own, after

    def diagonal(self, row):
        load = lambda h, k, at: self.e[h][self.c.wet + k, at, :]
        for k, pair in enumerate(self.neighbours(load, row)):
            for h, (_, total) in enumerate(pair):
                self.d[h][k, pl.ds(row, TILE), :] = 1.0 - total

    def loader(self, index):
        if index == 0:
            return lambda h, k, at: self.e[h][self.c.u + k, at, :]
        base = (index - 1) * self.c.levels
        return lambda h, k, at: self.x[h][base + k, at, :]

    def forward(self, n, row):
        c, at = self.c, pl.ds(row, TILE)
        for k, pair in enumerate(self.neighbours(self.loader(n), row)):
            for h, (own, total) in enumerate(pair):
                e = self.e[h]
                wet = e[c.wet + k, at, :]
                bounded = wet * jnp.tanh(self.d[h][k, at, :] * own + total)
                slope = wet - bounded * bounded
                if n < STEPS - 1:
                    self.x[h][n * c.levels + k, at, :] = bounded + e[c.s + k, at, :]
                    self.m[h][n * c.levels + k, at, :] = slope
                else:
                    if h == 0:
                        self.state[k, at, :] = bounded + e[c.s + k, at, :]
                    self.x[h][n * c.levels + k, at, :] = slope * e[c.cot + k, at, :]

    def backward(self, n, row):
        c, at = self.c, pl.ds(row, TILE)
        index = 2 * STEPS - 1 - n
        for k, pair in enumerate(self.neighbours(self.loader(index), row)):
            for h, (own, total) in enumerate(pair):
                value = self.d[h][k, at, :] * own + total
                if h == 0:
                    self.adj[(n - 1) * c.levels + k, at, :] = value
                self.x[h][index * c.levels + k, at, :] = self.m[h][(n - 1) * c.levels + k, at, :] * value

    def gradient(self, row):
        c, at = self.c, pl.ds(row, TILE)
        for k, pair in enumerate(self.neighbours(self.loader(2 * STEPS - 1), row, 1)):
            own, total = pair[0]
            yield k, self.e[0][c.wet + k, at, :] * (self.d[0][k, at, :] * own + total)

    def source_gradient(self, row):
        c, at = self.c, pl.ds(row, TILE)
        for k in range(c.levels):
            total = self.e[0][c.cot + k, at, :]
            for n in range(STEPS - 1):
                total = total + self.adj[n * c.levels + k, at, :]
            yield k, self.e[0][c.wet + k, at, :] * total


def own_kernel(c, f_ref, one_ref, two_ref, e0, e1, w0, w1, d0, d1, x0, x1, m0, m1, adj, state, grad, gsource):
    rows = f_ref.shape[1]
    odd_lon = is_odd("lon")
    s = Sweeps(c, (e0, e1), (w0, w1), (d0, d1), (x0, x1), (m0, m1), adj, state)
    zero = jnp.zeros((TILE, f_ref.shape[2]), jnp.float32)
    for ref in (e0, e1):
        for end in (pl.ds(0, TILE), pl.ds(HALO + rows, TILE)):
            for channel in (*range(c.u, c.u + c.levels), *range(c.wet, c.wet + c.levels), c.cn):
                ref[channel, end, :] = zero
    tiles = rows // TILE
    places = [HALO + t * TILE for t in range(tiles)]
    for t, row in enumerate(places):
        at, to = pl.ds(t * TILE, TILE), pl.ds(row, TILE)
        for channel in range(c.count):
            e0[channel, to, :] = f_ref[channel, at, :]
        pairs = [(one_ref[m, at, :], two_ref[m, at, :]) for m in range(c.parts)]
        s.spread(
            row,
            [jnp.where(odd_lon, two, one) for one, two in pairs],
            [jnp.where(odd_lon, one, two) for one, two in pairs],
        )
        s.western(row)
    for row in places:
        s.diagonal(row)
    for n in range(STEPS):
        for row in places:
            s.forward(n, row)
    for n in range(STEPS - 1, 0, -1):
        for row in places:
            s.backward(n, row)
    for row in places[1:-1]:
        at = pl.ds(row - HALO, TILE)
        for k, value in s.source_gradient(row):
            gsource[k, at, :] = value
        for k, value in s.gradient(row):
            grad[k, at, :] = value


def edge_kernel(
    c, first_one, first_two, second_two, second_one, *refs,
):
    aliased = refs[: len(refs) // 2]
    del aliased
    e0, e1, w0, w1, d0, d1, x0, x1, m0, m1, adj, state, grad, gsource, state_hbm, grad_hbm, gsource_hbm, sems = refs[14:]
    rows = grad.shape[1]
    s = Sweeps(c, (e0, e1), (w0, w1), (d0, d1), (x0, x1), (m0, m1), adj, state)
    moves = []

    def send(ref, skip, target, at, many):
        move = pltpu.make_async_copy(
            ref.at[:, pl.ds(skip + at, many), :], target.at[:, pl.ds(at, many), :], sems.at[len(moves)]
        )
        move.start()
        moves.append(move)

    def send_edges(ref, skip, target):
        send(ref, skip, target, 0, TILE)
        send(ref, skip, target, rows - TILE, TILE)

    inner = rows - 2 * TILE
    send(state, HALO, state_hbm, TILE, inner)
    send(gsource, 0, gsource_hbm, TILE, inner)
    send(grad, 0, grad_hbm, TILE, inner)
    odd_lat = is_odd("lat")
    for row, low in ((0, True), (HALO + rows, False)):
        pole = lax.axis_index("lat") == (0 if low else lax.axis_size("lat") - 1)
        from_one = odd_lat if low else jnp.logical_not(odd_lat)
        to = pl.ds(row, TILE)

        def got(one, two, i):
            return jnp.where(pole, 0.0, jnp.where(from_one, one[i], two[i]))

        second = [got(second_one, second_two, i) for i in range(c.second)]
        for channel in range(c.first):
            e0[channel, to, :] = got(first_one, first_two, channel)
        e0[c.ce, to, :], e0[c.cn, to, :] = second[c.strips : c.cot_at]
        for k in range(c.levels):
            tile = second[c.cot_at + k // 2]
            if (k % 2 == 0) == low:
                tile = pltpu.roll(tile, TILE // 2, 0)
            e0[c.cot + k, to, :] = tile
        s.spread(row, second[: c.parts], second[c.parts : c.strips])
        s.western(row)
    top = lambda i: HALO + i - (DEPTH - 1)
    bottom = lambda i: HALO + rows - 1 - i
    places = lambda i: (top(i), bottom(i))
    for row in places(0):
        s.diagonal(row)
    for n in range(STEPS):
        for row in places(n):
            s.forward(n, row)
    send_edges(state, HALO, state_hbm)
    for n in range(STEPS - 1, 0, -1):
        for row in places(2 * STEPS - 1 - n):
            s.backward(n, row)
    for row in places(DEPTH - 1):
        for k, value in s.source_gradient(row):
            gsource[k, pl.ds(row - HALO, TILE), :] = value
    send_edges(gsource, 0, gsource_hbm)
    for row in places(DEPTH - 1):
        for k, value in s.gradient(row):
            grad[k, pl.ds(row - HALO, TILE), :] = value
    send_edges(grad, 0, grad_hbm)
    for move in moves:
        move.wait()


def swaps(count, offset):
    pairs = [(i, (i + 1) % count) for i in range(offset, count, 2)]
    return pairs + [(j, i) for i, j in pairs]


def lat_swaps(lat, lon, offset):
    pairs, alone = [], set(range(lat))
    for i in range(offset, lat - 1, 2):
        alone -= {i, i + 1}
        pairs += [(i * lon + j, (i + 1) * lon + j) for j in range(lon)]
    for i in sorted(alone):
        pairs += [(i * lon + j, i * lon + j + 1) for j in range(0, lon, 2)]
    return pairs + [(j, i) for i, j in pairs]


def body(initial_state, source, cotangent, face_coefs, land_mask, bottom):
    arguments = (initial_state, source, cotangent, face_coefs, land_mask, bottom)
    levels, rows, lanes = initial_state.shape
    c = Names(levels)
    span = rows + 2 * HALO
    f32 = lambda *shape: jax.ShapeDtypeStruct(shape, jnp.float32)
    vmem, hbm = pl.BlockSpec(memory_space=pltpu.VMEM), pl.BlockSpec(memory_space=pltpu.HBM)
    params = pltpu.CompilerParams(vmem_limit_bytes=8 * 1024 * 1024)

    fields, one, two, lat_one, lat_two = pl.pallas_call(
        functools.partial(pack_kernel, c),
        out_shape=(f32(c.count, rows, lanes), *(f32(c.parts, rows, lanes),) * 2, *(f32(c.first, TILE, lanes),) * 2),
        in_specs=[hbm] * 6,
        out_specs=(vmem,) * 5,
        scratch_shapes=[
            pltpu.VMEM((levels, rows, lanes), jnp.float32),
            pltpu.VMEM((levels, rows, lanes), jnp.float32),
            pltpu.VMEM((2, rows, lanes), jnp.float32),
            pltpu.VMEM((levels, rows, lanes), jnp.int32),
            pltpu.VMEM((rows, lanes), jnp.int32),
            pltpu.SemaphoreType.DMA((2 + 4 * -(-levels // PIECE),)),
        ],
        compiler_params=params,
        name="pack",
    )(*(pltpu.with_memory_space_constraint(x, pltpu.HBM) for x in arguments))
    lon, lat = lax.axis_size("lon"), lax.axis_size("lat")
    one = lax.ppermute(one, "lon", swaps(lon, 0))
    two = lax.ppermute(two, "lon", swaps(lon, 1))
    both = ("lat", "lon")
    lat_pairs, other_pairs = lat_swaps(lat, lon, 0), lat_swaps(lat, lon, 1)
    first = lax.ppermute(lat_one, both, lat_pairs), lax.ppermute(lat_two, both, other_pairs)
    lat_one, lat_two = pl.pallas_call(
        functools.partial(corner_kernel, c),
        out_shape=(f32(c.second, TILE, lanes),) * 2,
        in_specs=[vmem] * 3,
        out_specs=(vmem,) * 2,
        compiler_params=params,
        name="corners",
    )(fields, one, two)
    second = lax.ppermute(lat_one, both, lat_pairs), lax.ppermute(lat_two, both, other_pairs)
    twice = lambda *shape: (f32(*shape), f32(*shape))
    shapes = (
        *twice(c.count, span, lanes),
        *twice(span, lanes),
        *twice(levels, span, lanes),
        *twice((2 * STEPS - 1) * levels, span, lanes),
        *twice((STEPS - 1) * levels, span, lanes),
        f32((STEPS - 1) * levels, span, lanes),
        f32(levels, span, lanes),
        f32(levels, rows, lanes),
        f32(levels, rows, lanes),
    )
    own = pl.pallas_call(
        functools.partial(own_kernel, c),
        out_shape=shapes,
        in_specs=[vmem] * 3,
        out_specs=(vmem,) * len(shapes),
        compiler_params=params,
        cost_estimate=pl.CostEstimate(
            flops=2 * STEPS * levels * rows * lanes * 40, bytes_accessed=16 * 2**20, transcendentals=0
        ),
        name="own_rows",
    )(fields, one, two)
    out = pl.pallas_call(
        functools.partial(edge_kernel, c),
        out_shape=(*shapes, *(f32(levels, rows, lanes),) * 3),
        in_specs=[vmem] * (4 + len(shapes)),
        out_specs=(*(vmem,) * len(shapes), hbm, hbm, hbm),
        input_output_aliases={4 + i: i for i in range(len(shapes))},
        scratch_shapes=[pltpu.SemaphoreType.DMA((9,))],
        compiler_params=params,
        name="edge_rows",
    )(*first, *second[::-1], *own)
    return tuple(out[len(shapes) :])


def solution(mesh):
    block = P(None, "lat", "lon")
    return jax.shard_map(
        body,
        mesh=mesh,
        in_specs=(block, block, block, block, block, P("lat", "lon")),
        out_specs=(block, block, block),
        check_vma=False,
    )
```

```python
import functools

import jax
import jax.numpy as jnp
from jax import lax
from jax.experimental import pallas as pl
from jax.experimental.pallas import tpu as pltpu
from jax.sharding import PartitionSpec as P

STEPS = 4
DEPTH = 2 * STEPS
TILE = 8
HALO = TILE
PIECE = 2

vertical_coef = 0.04


class Names:
    def __init__(self, levels):
        self.levels = levels
        self.u, self.s, self.wet = 0, levels, 2 * levels
        self.ce, self.cn, self.cot = 3 * levels, 3 * levels + 1, 3 * levels + 2
        self.count = 4 * levels + 2
        self.parts = -(-self.count // 16)
        self.strips = 2 * self.parts
        self.first = self.ce
        self.cot_at = self.strips + 2
        self.second = self.cot_at + -(-levels // 2)


def lane_iota(lanes):
    return lax.broadcasted_iota(jnp.int32, (TILE, lanes), 1)


def shift_of(channel):
    place = channel % 16
    return 2 * DEPTH * (place % 8) + DEPTH * (place // 8)


def even_groups(lanes):
    return lax.rem(lane_iota(lanes) // DEPTH, 2) == 0


def is_odd(axis):
    return lax.rem(lax.axis_index(axis), 2) == 1


def strip_rows(c, m):
    return range(16 * m, min(16 * m + 16, c.count))


def pack_kernel(
    c, u_hbm, s_hbm, a_hbm, c_hbm, land_hbm, bottom_hbm, f_ref, first_ref, second_ref, lat_one_ref, lat_two_ref,
    u_ref, s_ref, c_ref, land_ref, bottom_ref, sems,
):
    levels = c.levels
    _, rows, lanes = u_ref.shape
    pieces = [(bottom_hbm, bottom_ref)]
    groups = [range(k, min(k + PIECE, levels)) for k in range(0, levels, PIECE)]
    for held in groups:
        at = pl.ds(held.start, len(held))
        pieces += [(land_hbm.at[at], land_ref.at[at]), (u_hbm.at[at], u_ref.at[at]), (s_hbm.at[at], s_ref.at[at])]
    pieces.append((c_hbm, c_ref))
    for held in groups:
        pieces.append((a_hbm.at[pl.ds(held.start, len(held))], f_ref.at[pl.ds(c.cot + held.start, len(held))]))
    moves = [pltpu.make_async_copy(source, target, sems.at[i]) for i, (source, target) in enumerate(pieces)]
    for move in moves:
        move.start()
    last_lat = lax.axis_index("lat") == lax.axis_size("lat") - 1
    moves[0].wait()
    for i, held in enumerate(groups):
        for move in moves[1 + 3 * i : 4 + 3 * i]:
            move.wait()
        for k in held:
            wet = jnp.where(k < bottom_ref[...], land_ref[k], 0).astype(jnp.float32)
            f_ref[c.u + k] = wet * u_ref[k]
            f_ref[c.s + k] = wet * s_ref[k]
            f_ref[c.wet + k] = wet
    for move in moves[1 + 3 * len(groups) :]:
        move.wait()
    f_ref[c.ce] = c_ref[0]
    row = lax.broadcasted_iota(jnp.int32, (rows, lanes), 0)
    f_ref[c.cn] = jnp.where(jnp.logical_and(last_lat, row == rows - 1), 0.0, c_ref[1])
    odd = is_odd("lon")
    group, groups = lane_iota(lanes) // DEPTH, lanes // DEPTH
    for t in range(rows // TILE):
        at = pl.ds(t * TILE, TILE)
        for m in range(c.parts):
            east = jnp.zeros((TILE, lanes), jnp.float32)
            west = east
            for channel in strip_rows(c, m):
                shift = shift_of(channel)
                tile = f_ref[channel, at, :]
                if shift:
                    tile = pltpu.roll(tile, shift, 1)
                east = jnp.where(group == shift // DEPTH, tile, east)
                west = jnp.where(group == (shift // DEPTH - 1) % groups, tile, west)
            first_ref[m, at, :] = jnp.where(odd, east, west)
            second_ref[m, at, :] = jnp.where(odd, west, east)
    odd_lat = is_odd("lat")
    for channel in range(c.first):
        high, low = f_ref[channel, pl.ds(rows - TILE, TILE), :], f_ref[channel, pl.ds(0, TILE), :]
        lat_one_ref[channel] = jnp.where(odd_lat, low, high)
        lat_two_ref[channel] = jnp.where(odd_lat, high, low)


def corner_kernel(c, f_ref, two_ref, one_ref, lat_one_ref, lat_two_ref):
    odd_lat, odd_lon = is_odd("lat"), is_odd("lon")
    _, rows, lanes = f_ref.shape
    half = TILE // 2
    first_half = lax.broadcasted_iota(jnp.int32, (TILE, lanes), 0) < half
    low, high = pl.ds(0, TILE), pl.ds(rows - TILE, TILE)

    def put(i, low_tile, high_tile):
        lat_one_ref[i] = jnp.where(odd_lat, low_tile, high_tile)
        lat_two_ref[i] = jnp.where(odd_lat, high_tile, low_tile)

    for m in range(c.parts):
        ends = [(one_ref[m, at, :], two_ref[m, at, :]) for at in (low, high)]
        put(m, *(jnp.where(odd_lon, two, one) for one, two in ends))
        put(c.parts + m, *(jnp.where(odd_lon, one, two) for one, two in ends))
    put(c.strips, f_ref[c.ce, low, :], f_ref[c.ce, high, :])
    put(c.strips + 1, f_ref[c.cn, low, :], f_ref[c.cn, high, :])
    for q in range(c.second - c.cot_at):
        one, two = c.cot + 2 * q, c.cot + min(2 * q + 1, c.levels - 1)
        put(
            c.cot_at + q,
            jnp.where(first_half, f_ref[one, low, :], pltpu.roll(f_ref[two, low, :], half, 0)),
            jnp.where(first_half, pltpu.roll(f_ref[one, high, :], half, 0), f_ref[two, high, :]),
        )


class Sweeps:
    def __init__(self, c, e, w, d, x, m, adj, state):
        self.c, self.e, self.w, self.d, self.x, self.m, self.adj, self.state = c, e, w, d, x, m, adj, state
        self.lanes = e[0].shape[-1]
        lane = lane_iota(self.lanes)
        self.at_first, self.at_last = lane == 0, lane == self.lanes - 1
        self.even_group = even_groups(self.lanes)

    def from_west(self, x0, x1):
        r0, r1 = pltpu.roll(x0, 1, 1), pltpu.roll(x1, 1, 1)
        return jnp.where(self.at_first, r1, r0), jnp.where(self.at_first, r0, r1)

    def from_east(self, x0, x1):
        r0, r1 = pltpu.roll(x0, self.lanes - 1, 1), pltpu.roll(x1, self.lanes - 1, 1)
        return jnp.where(self.at_last, r1, r0), jnp.where(self.at_last, r0, r1)

    def spread(self, row, easts, wests):
        for m, (east, west) in enumerate(zip(easts, wests)):
            both = jnp.where(self.even_group, east, west), jnp.where(self.even_group, west, east)
            for channel in strip_rows(self.c, m):
                shift = shift_of(channel)
                tile = both[(channel % 16) // 8]
                if shift:
                    tile = pltpu.roll(tile, self.lanes - shift, 1)
                self.e[1][channel, pl.ds(row, TILE), :] = tile

    def western(self, row):
        at = pl.ds(row, TILE)
        self.w[0][at, :], self.w[1][at, :] = self.from_west(self.e[0][self.c.ce, at, :], self.e[1][self.c.ce, at, :])

    def neighbours(self, load, row, halves=2):
        c, at = self.c, pl.ds(row, TILE)
        ce = [e[c.ce, at, :] for e in self.e]
        cw = [w[at, :] for w in self.w]
        cn = [e[c.cn, at, :] for e in self.e]
        cs = [e[c.cn, pl.ds(row - 1, TILE), :] for e in self.e]
        pick = lambda k: (load(0, k, at), load(1, k, at))
        before, own, after = None, pick(0), None
        for k in range(c.levels):
            after = pick(k + 1) if k + 1 < c.levels else None
            east, west = self.from_east(*own), self.from_west(*own)
            pair = []
            for h in range(halves):
                north, south = load(h, k, pl.ds(row + 1, TILE)), load(h, k, pl.ds(row - 1, TILE))
                total = (ce[h] * east[h] + cw[h] * west[h]) + (cn[h] * north + cs[h] * south)
                around = [other[h] for other in (before, after) if other]
                pair.append((own[h], total + vertical_coef * functools.reduce(jnp.add, around)))
            yield pair
            before, own = own, after

    def diagonal(self, row):
        load = lambda h, k, at: self.e[h][self.c.wet + k, at, :]
        for k, pair in enumerate(self.neighbours(load, row)):
            for h, (_, total) in enumerate(pair):
                self.d[h][k, pl.ds(row, TILE), :] = 1.0 - total

    def loader(self, index):
        if index == 0:
            return lambda h, k, at: self.e[h][self.c.u + k, at, :]
        base = (index - 1) * self.c.levels
        return lambda h, k, at: self.x[h][base + k, at, :]

    def forward(self, n, row):
        c, at = self.c, pl.ds(row, TILE)
        for k, pair in enumerate(self.neighbours(self.loader(n), row)):
            for h, (own, total) in enumerate(pair):
                e = self.e[h]
                wet = e[c.wet + k, at, :]
                bounded = wet * jnp.tanh(self.d[h][k, at, :] * own + total)
                slope = wet - bounded * bounded
                if n < STEPS - 1:
                    self.x[h][n * c.levels + k, at, :] = bounded + e[c.s + k, at, :]
                    self.m[h][n * c.levels + k, at, :] = slope
                else:
                    if h == 0:
                        self.state[k, at, :] = bounded + e[c.s + k, at, :]
                    self.x[h][n * c.levels + k, at, :] = slope * e[c.cot + k, at, :]

    def backward(self, n, row):
        c, at = self.c, pl.ds(row, TILE)
        index = 2 * STEPS - 1 - n
        for k, pair in enumerate(self.neighbours(self.loader(index), row)):
            for h, (own, total) in enumerate(pair):
                value = self.d[h][k, at, :] * own + total
                if h == 0:
                    self.adj[(n - 1) * c.levels + k, at, :] = value
                self.x[h][index * c.levels + k, at, :] = self.m[h][(n - 1) * c.levels + k, at, :] * value

    def gradient(self, row):
        c, at = self.c, pl.ds(row, TILE)
        for k, pair in enumerate(self.neighbours(self.loader(2 * STEPS - 1), row, 1)):
            own, total = pair[0]
            yield k, self.e[0][c.wet + k, at, :] * (self.d[0][k, at, :] * own + total)

    def source_gradient(self, row):
        c, at = self.c, pl.ds(row, TILE)
        for k in range(c.levels):
            total = self.e[0][c.cot + k, at, :]
            for n in range(STEPS - 1):
                total = total + self.adj[n * c.levels + k, at, :]
            yield k, self.e[0][c.wet + k, at, :] * total


def own_kernel(c, f_ref, two_ref, one_ref, e0, e1, w0, w1, d0, d1, x0, x1, m0, m1, adj, state, grad, gsource):
    rows = f_ref.shape[1]
    odd_lon = is_odd("lon")
    s = Sweeps(c, (e0, e1), (w0, w1), (d0, d1), (x0, x1), (m0, m1), adj, state)
    zero = jnp.zeros((TILE, f_ref.shape[2]), jnp.float32)
    for ref in (e0, e1):
        for end in (pl.ds(0, TILE), pl.ds(HALO + rows, TILE)):
            for channel in (*range(c.u, c.u + c.levels), *range(c.wet, c.wet + c.levels), c.cn):
                ref[channel, end, :] = zero
    tiles = rows // TILE
    places = [HALO + t * TILE for t in range(tiles)]
    for t, row in enumerate(places):
        at, to = pl.ds(t * TILE, TILE), pl.ds(row, TILE)
        for channel in range(c.count):
            e0[channel, to, :] = f_ref[channel, at, :]
        pairs = [(one_ref[m, at, :], two_ref[m, at, :]) for m in range(c.parts)]
        s.spread(
            row,
            [jnp.where(odd_lon, two, one) for one, two in pairs],
            [jnp.where(odd_lon, one, two) for one, two in pairs],
        )
        s.western(row)
    for row in places:
        s.diagonal(row)
    for n in range(STEPS):
        for row in places:
            s.forward(n, row)
    for n in range(STEPS - 1, 0, -1):
        for row in places:
            s.backward(n, row)
    for row in places[1:-1]:
        at = pl.ds(row - HALO, TILE)
        for k, value in s.source_gradient(row):
            gsource[k, at, :] = value
        for k, value in s.gradient(row):
            grad[k, at, :] = value


def edge_kernel(
    c, first_one, first_two, second_two, second_one, *refs,
):
    aliased = refs[: len(refs) // 2]
    del aliased
    e0, e1, w0, w1, d0, d1, x0, x1, m0, m1, adj, state, grad, gsource, state_hbm, grad_hbm, gsource_hbm, sems = refs[14:]
    rows = grad.shape[1]
    s = Sweeps(c, (e0, e1), (w0, w1), (d0, d1), (x0, x1), (m0, m1), adj, state)
    moves = []

    def send(ref, skip, target, at, many):
        move = pltpu.make_async_copy(
            ref.at[:, pl.ds(skip + at, many), :], target.at[:, pl.ds(at, many), :], sems.at[len(moves)]
        )
        move.start()
        moves.append(move)

    def send_edges(ref, skip, target):
        send(ref, skip, target, 0, TILE)
        send(ref, skip, target, rows - TILE, TILE)

    inner = rows - 2 * TILE
    send(state, HALO, state_hbm, TILE, inner)
    send(gsource, 0, gsource_hbm, TILE, inner)
    send(grad, 0, grad_hbm, TILE, inner)
    odd_lat = is_odd("lat")
    for row, low in ((0, True), (HALO + rows, False)):
        pole = lax.axis_index("lat") == (0 if low else lax.axis_size("lat") - 1)
        from_one = odd_lat if low else jnp.logical_not(odd_lat)
        to = pl.ds(row, TILE)

        def got(one, two, i):
            return jnp.where(pole, 0.0, jnp.where(from_one, one[i], two[i]))

        second = [got(second_one, second_two, i) for i in range(c.second)]
        for channel in range(c.first):
            e0[channel, to, :] = got(first_one, first_two, channel)
        e0[c.ce, to, :], e0[c.cn, to, :] = second[c.strips : c.cot_at]
        for k in range(c.levels):
            tile = second[c.cot_at + k // 2]
            if (k % 2 == 0) == low:
                tile = pltpu.roll(tile, TILE // 2, 0)
            e0[c.cot + k, to, :] = tile
        s.spread(row, second[: c.parts], second[c.parts : c.strips])
        s.western(row)
    top = lambda i: HALO + i - (DEPTH - 1)
    bottom = lambda i: HALO + rows - 1 - i
    places = lambda i: (top(i), bottom(i))
    for row in places(0):
        s.diagonal(row)
    for n in range(STEPS):
        for row in places(n):
            s.forward(n, row)
    send_edges(state, HALO, state_hbm)
    for n in range(STEPS - 1, 0, -1):
        for row in places(2 * STEPS - 1 - n):
            s.backward(n, row)
    for row in places(DEPTH - 1):
        for k, value in s.source_gradient(row):
            gsource[k, pl.ds(row - HALO, TILE), :] = value
    send_edges(gsource, 0, gsource_hbm)
    for row in places(DEPTH - 1):
        for k, value in s.gradient(row):
            grad[k, pl.ds(row - HALO, TILE), :] = value
    send_edges(grad, 0, grad_hbm)
    for move in moves:
        move.wait()


def swaps(count, offset):
    pairs = [(i, (i + 1) % count) for i in range(offset, count, 2)]
    return pairs + [(j, i) for i, j in pairs]


def lat_swaps(lat, lon, offset):
    pairs, alone = [], set(range(lat))
    for i in range(offset, lat - 1, 2):
        alone -= {i, i + 1}
        pairs += [(i * lon + j, (i + 1) * lon + j) for j in range(lon)]
    for i in sorted(alone):
        pairs += [(i * lon + j, i * lon + j + 1) for j in range(0, lon, 2)]
    return pairs + [(j, i) for i, j in pairs]


def body(initial_state, source, cotangent, face_coefs, land_mask, bottom):
    arguments = (initial_state, source, cotangent, face_coefs, land_mask, bottom)
    levels, rows, lanes = initial_state.shape
    c = Names(levels)
    span = rows + 2 * HALO
    f32 = lambda *shape: jax.ShapeDtypeStruct(shape, jnp.float32)
    vmem, hbm = pl.BlockSpec(memory_space=pltpu.VMEM), pl.BlockSpec(memory_space=pltpu.HBM)
    params = pltpu.CompilerParams(vmem_limit_bytes=8 * 1024 * 1024)

    fields, one, two, lat_one, lat_two = pl.pallas_call(
        functools.partial(pack_kernel, c),
        out_shape=(f32(c.count, rows, lanes), *(f32(c.parts, rows, lanes),) * 2, *(f32(c.first, TILE, lanes),) * 2),
        in_specs=[hbm] * 6,
        out_specs=(vmem,) * 5,
        scratch_shapes=[
            pltpu.VMEM((levels, rows, lanes), jnp.float32),
            pltpu.VMEM((levels, rows, lanes), jnp.float32),
            pltpu.VMEM((2, rows, lanes), jnp.float32),
            pltpu.VMEM((levels, rows, lanes), jnp.int32),
            pltpu.VMEM((rows, lanes), jnp.int32),
            pltpu.SemaphoreType.DMA((2 + 4 * -(-levels // PIECE),)),
        ],
        compiler_params=params,
        name="pack",
    )(*(pltpu.with_memory_space_constraint(x, pltpu.HBM) for x in arguments))
    lon, lat = lax.axis_size("lon"), lax.axis_size("lat")
    one = lax.ppermute(one, "lon", swaps(lon, 0))
    two = lax.ppermute(two, "lon", swaps(lon, 1))
    both = ("lat", "lon")
    lat_pairs, other_pairs = lat_swaps(lat, lon, 0), lat_swaps(lat, lon, 1)
    first = lax.ppermute(lat_one, both, lat_pairs), lax.ppermute(lat_two, both, other_pairs)
    lat_one, lat_two = pl.pallas_call(
        functools.partial(corner_kernel, c),
        out_shape=(f32(c.second, TILE, lanes),) * 2,
        in_specs=[vmem] * 3,
        out_specs=(vmem,) * 2,
        compiler_params=params,
        name="corners",
    )(fields, two, one)
    second = lax.ppermute(lat_one, both, lat_pairs), lax.ppermute(lat_two, both, other_pairs)
    twice = lambda *shape: (f32(*shape), f32(*shape))
    shapes = (
        *twice(c.count, span, lanes),
        *twice(span, lanes),
        *twice(levels, span, lanes),
        *twice((2 * STEPS - 1) * levels, span, lanes),
        *twice((STEPS - 1) * levels, span, lanes),
        f32((STEPS - 1) * levels, span, lanes),
        f32(levels, span, lanes),
        f32(levels, rows, lanes),
        f32(levels, rows, lanes),
    )
    own = pl.pallas_call(
        functools.partial(own_kernel, c),
        out_shape=shapes,
        in_specs=[vmem] * 3,
        out_specs=(vmem,) * len(shapes),
        compiler_params=params,
        cost_estimate=pl.CostEstimate(
            flops=2 * STEPS * levels * rows * lanes * 40, bytes_accessed=16 * 2**20, transcendentals=0
        ),
        name="own_rows",
    )(fields, two, one)
    out = pl.pallas_call(
        functools.partial(edge_kernel, c),
        out_shape=(*shapes, *(f32(levels, rows, lanes),) * 3),
        in_specs=[vmem] * (4 + len(shapes)),
        out_specs=(*(vmem,) * len(shapes), hbm, hbm, hbm),
        input_output_aliases={4 + i: i for i in range(len(shapes))},
        scratch_shapes=[pltpu.SemaphoreType.DMA((9,))],
        compiler_params=params,
        name="edge_rows",
    )(*first, *second[::-1], *own)
    return tuple(out[len(shapes) :])


def solution(mesh):
    block = P(None, "lat", "lon")
    return jax.shard_map(
        body,
        mesh=mesh,
        in_specs=(block, block, block, block, block, P("lat", "lon")),
        out_specs=(block, block, block),
        check_vma=False,
    )
```

```python
import functools

import jax
import jax.numpy as jnp
from jax import lax
from jax.experimental import pallas as pl
from jax.experimental.pallas import tpu as pltpu
from jax.sharding import PartitionSpec as P

STEPS = 4
DEPTH = 2 * STEPS
TILE = 8
HALO = TILE

vertical_coef = 0.04


class Names:
    def __init__(self, levels):
        self.levels = levels
        self.u, self.s, self.wet = 0, levels, 2 * levels
        self.ce, self.cn, self.cot = 3 * levels, 3 * levels + 1, 3 * levels + 2
        self.count = 4 * levels + 2
        self.parts = -(-self.count // 16)
        self.strips = 2 * self.parts
        self.first = self.ce
        self.cot_at = self.strips + 2
        self.second = self.cot_at + -(-levels // 2)


def lane_iota(lanes):
    return lax.broadcasted_iota(jnp.int32, (TILE, lanes), 1)


def shift_of(channel):
    place = channel % 16
    return 2 * DEPTH * (place % 8) + DEPTH * (place // 8)


def even_groups(lanes):
    return lax.rem(lane_iota(lanes) // DEPTH, 2) == 0


def is_odd(axis):
    return lax.rem(lax.axis_index(axis), 2) == 1


def strip_rows(c, m):
    return range(16 * m, min(16 * m + 16, c.count))


def pack_kernel(
    c, u_hbm, s_hbm, a_hbm, c_hbm, land_hbm, bottom_hbm, f_ref, first_ref, second_ref, lat_one_ref, lat_two_ref,
    u_ref, s_ref, c_ref, land_ref, bottom_ref, sems,
):
    levels = c.levels
    _, rows, lanes = u_ref.shape
    moves = [
        pltpu.make_async_copy(source, target, sems.at[i])
        for i, (source, target) in enumerate(
            (
                (bottom_hbm, bottom_ref),
                (land_hbm, land_ref),
                (u_hbm, u_ref),
                (s_hbm, s_ref),
                (c_hbm, c_ref),
                (a_hbm, f_ref.at[pl.ds(c.cot, levels)]),
            )
        )
    ]
    for move in moves:
        move.start()
    for move in moves:
        move.wait()
    last_lat = lax.axis_index("lat") == lax.axis_size("lat") - 1
    for k in range(levels):
        wet = jnp.where(k < bottom_ref[...], land_ref[k], 0).astype(jnp.float32)
        f_ref[c.u + k] = wet * u_ref[k]
        f_ref[c.s + k] = wet * s_ref[k]
        f_ref[c.wet + k] = wet
    f_ref[c.ce] = c_ref[0]
    row = lax.broadcasted_iota(jnp.int32, (rows, lanes), 0)
    f_ref[c.cn] = jnp.where(jnp.logical_and(last_lat, row == rows - 1), 0.0, c_ref[1])
    odd = is_odd("lon")
    group, groups = lane_iota(lanes) // DEPTH, lanes // DEPTH
    for t in range(rows // TILE):
        at = pl.ds(t * TILE, TILE)
        for m in range(c.parts):
            east = jnp.zeros((TILE, lanes), jnp.float32)
            west = east
            for channel in strip_rows(c, m):
                shift = shift_of(channel)
                tile = f_ref[channel, at, :]
                if shift:
                    tile = pltpu.roll(tile, shift, 1)
                east = jnp.where(group == shift // DEPTH, tile, east)
                west = jnp.where(group == (shift // DEPTH - 1) % groups, tile, west)
            first_ref[m, at, :] = jnp.where(odd, east, west)
            second_ref[m, at, :] = jnp.where(odd, west, east)
    odd_lat = is_odd("lat")
    for channel in range(c.first):
        high, low = f_ref[channel, pl.ds(rows - TILE, TILE), :], f_ref[channel, pl.ds(0, TILE), :]
        lat_one_ref[channel] = jnp.where(odd_lat, low, high)
        lat_two_ref[channel] = jnp.where(odd_lat, high, low)


def corner_kernel(c, f_ref, one_ref, two_ref, lat_one_ref, lat_two_ref):
    odd_lat, odd_lon = is_odd("lat"), is_odd("lon")
    _, rows, lanes = f_ref.shape
    half = TILE // 2
    first_half = lax.broadcasted_iota(jnp.int32, (TILE, lanes), 0) < half
    low, high = pl.ds(0, TILE), pl.ds(rows - TILE, TILE)

    def put(i, low_tile, high_tile):
        lat_one_ref[i] = jnp.where(odd_lat, low_tile, high_tile)
        lat_two_ref[i] = jnp.where(odd_lat, high_tile, low_tile)

    for m in range(c.parts):
        ends = [(one_ref[m, at, :], two_ref[m, at, :]) for at in (low, high)]
        put(m, *(jnp.where(odd_lon, two, one) for one, two in ends))
        put(c.parts + m, *(jnp.where(odd_lon, one, two) for one, two in ends))
    put(c.strips, f_ref[c.ce, low, :], f_ref[c.ce, high, :])
    put(c.strips + 1, f_ref[c.cn, low, :], f_ref[c.cn, high, :])
    for q in range(c.second - c.cot_at):
        one, two = c.cot + 2 * q, c.cot + min(2 * q + 1, c.levels - 1)
        put(
            c.cot_at + q,
            jnp.where(first_half, f_ref[one, low, :], pltpu.roll(f_ref[two, low, :], half, 0)),
            jnp.where(first_half, pltpu.roll(f_ref[one, high, :], half, 0), f_ref[two, high, :]),
        )


class Sweeps:
    def __init__(self, c, e, w, d, x, m, adj, state):
        self.c, self.e, self.w, self.d, self.x, self.m, self.adj, self.state = c, e, w, d, x, m, adj, state
        self.lanes = e[0].shape[-1]
        lane = lane_iota(self.lanes)
        self.at_first, self.at_last = lane == 0, lane == self.lanes - 1
        self.even_group = even_groups(self.lanes)

    def from_west(self, x0, x1):
        r0, r1 = pltpu.roll(x0, 1, 1), pltpu.roll(x1, 1, 1)
        return jnp.where(self.at_first, r1, r0), jnp.where(self.at_first, r0, r1)

    def from_east(self, x0, x1):
        r0, r1 = pltpu.roll(x0, self.lanes - 1, 1), pltpu.roll(x1, self.lanes - 1, 1)
        return jnp.where(self.at_last, r1, r0), jnp.where(self.at_last, r0, r1)

    def spread(self, row, easts, wests):
        for m, (east, west) in enumerate(zip(easts, wests)):
            both = jnp.where(self.even_group, east, west), jnp.where(self.even_group, west, east)
            for channel in strip_rows(self.c, m):
                shift = shift_of(channel)
                tile = both[(channel % 16) // 8]
                if shift:
                    tile = pltpu.roll(tile, self.lanes - shift, 1)
                self.e[1][channel, pl.ds(row, TILE), :] = tile

    def western(self, row):
        at = pl.ds(row, TILE)
        self.w[0][at, :], self.w[1][at, :] = self.from_west(self.e[0][self.c.ce, at, :], self.e[1][self.c.ce, at, :])

    def neighbours(self, load, row, halves=2):
        c, at = self.c, pl.ds(row, TILE)
        ce = [e[c.ce, at, :] for e in self.e]
        cw = [w[at, :] for w in self.w]
        cn = [e[c.cn, at, :] for e in self.e]
        cs = [e[c.cn, pl.ds(row - 1, TILE), :] for e in self.e]
        own = [(load(0, k, at), load(1, k, at)) for k in range(c.levels)]
        out = []
        for k in range(c.levels):
            east, west = self.from_east(*own[k]), self.from_west(*own[k])
            pair = []
            for h in range(halves):
                north, south = load(h, k, pl.ds(row + 1, TILE)), load(h, k, pl.ds(row - 1, TILE))
                total = (ce[h] * east[h] + cw[h] * west[h]) + (cn[h] * north + cs[h] * south)
                around = [own[j][h] for j in (k - 1, k + 1) if 0 <= j < c.levels]
                pair.append((own[k][h], total + vertical_coef * functools.reduce(jnp.add, around)))
            out.append(pair)
        return out

    def diagonal(self, row):
        load = lambda h, k, at: self.e[h][self.c.wet + k, at, :]
        for k, pair in enumerate(self.neighbours(load, row)):
            for h, (_, total) in enumerate(pair):
                self.d[h][k, pl.ds(row, TILE), :] = 1.0 - total

    def loader(self, index):
        if index == 0:
            return lambda h, k, at: self.e[h][self.c.u + k, at, :]
        base = (index - 1) * self.c.levels
        return lambda h, k, at: self.x[h][base + k, at, :]

    def forward(self, n, row):
        c, at = self.c, pl.ds(row, TILE)
        for k, pair in enumerate(self.neighbours(self.loader(n), row)):
            for h, (own, total) in enumerate(pair):
                e = self.e[h]
                wet = e[c.wet + k, at, :]
                bounded = wet * jnp.tanh(self.d[h][k, at, :] * own + total)
                slope = wet - bounded * bounded
                if n < STEPS - 1:
                    self.x[h][n * c.levels + k, at, :] = bounded + e[c.s + k, at, :]
                    self.m[h][n * c.levels + k, at, :] = slope
                else:
                    if h == 0:
                        self.state[k, at, :] = bounded + e[c.s + k, at, :]
                    self.x[h][n * c.levels + k, at, :] = slope * e[c.cot + k, at, :]

    def backward(self, n, row):
        c, at = self.c, pl.ds(row, TILE)
        index = 2 * STEPS - 1 - n
        for k, pair in enumerate(self.neighbours(self.loader(index), row)):
            for h, (own, total) in enumerate(pair):
                value = self.d[h][k, at, :] * own + total
                if h == 0:
                    self.adj[(n - 1) * c.levels + k, at, :] = value
                self.x[h][index * c.levels + k, at, :] = self.m[h][(n - 1) * c.levels + k, at, :] * value

    def gradient(self, row):
        c, at = self.c, pl.ds(row, TILE)
        for k, pair in enumerate(self.neighbours(self.loader(2 * STEPS - 1), row, 1)):
            own, total = pair[0]
            yield k, self.e[0][c.wet + k, at, :] * (self.d[0][k, at, :] * own + total)

    def source_gradient(self, row):
        c, at = self.c, pl.ds(row, TILE)
        for k in range(c.levels):
            total = self.e[0][c.cot + k, at, :]
            for n in range(STEPS - 1):
                total = total + self.adj[n * c.levels + k, at, :]
            yield k, self.e[0][c.wet + k, at, :] * total


def own_kernel(c, f_ref, one_ref, two_ref, e0, e1, w0, w1, d0, d1, x0, x1, m0, m1, adj, state, grad, gsource):
    rows = f_ref.shape[1]
    odd_lon = is_odd("lon")
    s = Sweeps(c, (e0, e1), (w0, w1), (d0, d1), (x0, x1), (m0, m1), adj, state)
    zero = jnp.zeros((TILE, f_ref.shape[2]), jnp.float32)
    for ref in (e0, e1):
        for end in (pl.ds(0, TILE), pl.ds(HALO + rows, TILE)):
            for channel in (*range(c.u, c.u + c.levels), *range(c.wet, c.wet + c.levels), c.cn):
                ref[channel, end, :] = zero
    tiles = rows // TILE
    places = [HALO + t * TILE for t in range(tiles)]
    for t, row in enumerate(places):
        at, to = pl.ds(t * TILE, TILE), pl.ds(row, TILE)
        for channel in range(c.count):
            e0[channel, to, :] = f_ref[channel, at, :]
        pairs = [(one_ref[m, at, :], two_ref[m, at, :]) for m in range(c.parts)]
        s.spread(
            row,
            [jnp.where(odd_lon, two, one) for one, two in pairs],
            [jnp.where(odd_lon, one, two) for one, two in pairs],
        )
        s.western(row)
    for row in places:
        s.diagonal(row)
    for n in range(STEPS):
        for row in places:
            s.forward(n, row)
    for n in range(STEPS - 1, 0, -1):
        for row in places:
            s.backward(n, row)
    for row in places[1:-1]:
        at = pl.ds(row - HALO, TILE)
        for k, value in s.source_gradient(row):
            gsource[k, at, :] = value
        for k, value in s.gradient(row):
            grad[k, at, :] = value


def edge_kernel(
    c, first_two, first_one, second_one, second_two, *refs,
):
    aliased = refs[: len(refs) // 2]
    del aliased
    e0, e1, w0, w1, d0, d1, x0, x1, m0, m1, adj, state, grad, gsource, state_hbm, grad_hbm, gsource_hbm, sems = refs[14:]
    rows = grad.shape[1]
    s = Sweeps(c, (e0, e1), (w0, w1), (d0, d1), (x0, x1), (m0, m1), adj, state)
    odd_lat = is_odd("lat")
    for row, low in ((0, True), (HALO + rows, False)):
        pole = lax.axis_index("lat") == (0 if low else lax.axis_size("lat") - 1)
        from_one = odd_lat if low else jnp.logical_not(odd_lat)
        to = pl.ds(row, TILE)

        def got(one, two, i):
            return jnp.where(pole, 0.0, jnp.where(from_one, one[i], two[i]))

        second = [got(second_one, second_two, i) for i in range(c.second)]
        for channel in range(c.first):
            e0[channel, to, :] = got(first_one, first_two, channel)
        e0[c.ce, to, :], e0[c.cn, to, :] = second[c.strips : c.cot_at]
        for k in range(c.levels):
            tile = second[c.cot_at + k // 2]
            if (k % 2 == 0) == low:
                tile = pltpu.roll(tile, TILE // 2, 0)
            e0[c.cot + k, to, :] = tile
        s.spread(row, second[: c.parts], second[c.parts : c.strips])
        s.western(row)
    top = lambda i: HALO + i - (DEPTH - 1)
    bottom = lambda i: HALO + rows - 1 - i
    places = lambda i: (top(i), bottom(i))
    for row in places(0):
        s.diagonal(row)
    for n in range(STEPS):
        for row in places(n):
            s.forward(n, row)
    own = pl.ds(HALO, rows)
    moves = [
        pltpu.make_async_copy(state.at[:, own, :], state_hbm, sems.at[0]),
        pltpu.make_async_copy(gsource, gsource_hbm, sems.at[1]),
        pltpu.make_async_copy(grad, grad_hbm, sems.at[2]),
    ]
    moves[0].start()
    for n in range(STEPS - 1, 0, -1):
        for row in places(2 * STEPS - 1 - n):
            s.backward(n, row)
    for row in places(DEPTH - 1):
        for k, value in s.source_gradient(row):
            gsource[k, pl.ds(row - HALO, TILE), :] = value
    moves[1].start()
    for row in places(DEPTH - 1):
        for k, value in s.gradient(row):
            grad[k, pl.ds(row - HALO, TILE), :] = value
    moves[2].start()
    for move in moves:
        move.wait()


def swaps(count, offset):
    pairs = [(i, (i + 1) % count) for i in range(offset, count, 2)]
    return pairs + [(j, i) for i, j in pairs]


def lat_swaps(lat, lon, offset):
    pairs, alone = [], set(range(lat))
    for i in range(offset, lat - 1, 2):
        alone -= {i, i + 1}
        pairs += [(i * lon + j, (i + 1) * lon + j) for j in range(lon)]
    for i in sorted(alone):
        pairs += [(i * lon + j, i * lon + j + 1) for j in range(0, lon, 2)]
    return pairs + [(j, i) for i, j in pairs]


def body(initial_state, source, cotangent, face_coefs, land_mask, bottom):
    arguments = (initial_state, source, cotangent, face_coefs, land_mask, bottom)
    levels, rows, lanes = initial_state.shape
    c = Names(levels)
    span = rows + 2 * HALO
    f32 = lambda *shape: jax.ShapeDtypeStruct(shape, jnp.float32)
    vmem, hbm = pl.BlockSpec(memory_space=pltpu.VMEM), pl.BlockSpec(memory_space=pltpu.HBM)
    params = pltpu.CompilerParams(vmem_limit_bytes=8 * 1024 * 1024)

    fields, one, two, lat_one, lat_two = pl.pallas_call(
        functools.partial(pack_kernel, c),
        out_shape=(f32(c.count, rows, lanes), *(f32(c.parts, rows, lanes),) * 2, *(f32(c.first, TILE, lanes),) * 2),
        in_specs=[hbm] * 6,
        out_specs=(vmem,) * 5,
        scratch_shapes=[
            pltpu.VMEM((levels, rows, lanes), jnp.float32),
            pltpu.VMEM((levels, rows, lanes), jnp.float32),
            pltpu.VMEM((2, rows, lanes), jnp.float32),
            pltpu.VMEM((levels, rows, lanes), jnp.int32),
            pltpu.VMEM((rows, lanes), jnp.int32),
            pltpu.SemaphoreType.DMA((6,)),
        ],
        compiler_params=params,
        name="pack",
    )(*(pltpu.with_memory_space_constraint(x, pltpu.HBM) for x in arguments))
    lon, lat = lax.axis_size("lon"), lax.axis_size("lat")
    one = lax.ppermute(one, "lon", swaps(lon, 0))
    two = lax.ppermute(two, "lon", swaps(lon, 1))
    both = ("lat", "lon")
    lat_pairs, other_pairs = lat_swaps(lat, lon, 0), lat_swaps(lat, lon, 1)
    first = lax.ppermute(lat_one, both, lat_pairs), lax.ppermute(lat_two, both, other_pairs)
    lat_one, lat_two = pl.pallas_call(
        functools.partial(corner_kernel, c),
        out_shape=(f32(c.second, TILE, lanes),) * 2,
        in_specs=[vmem] * 3,
        out_specs=(vmem,) * 2,
        compiler_params=params,
        name="corners",
    )(fields, one, two)
    second = lax.ppermute(lat_one, both, lat_pairs), lax.ppermute(lat_two, both, other_pairs)
    twice = lambda *shape: (f32(*shape), f32(*shape))
    shapes = (
        *twice(c.count, span, lanes),
        *twice(span, lanes),
        *twice(levels, span, lanes),
        *twice((2 * STEPS - 1) * levels, span, lanes),
        *twice((STEPS - 1) * levels, span, lanes),
        f32((STEPS - 1) * levels, span, lanes),
        f32(levels, span, lanes),
        f32(levels, rows, lanes),
        f32(levels, rows, lanes),
    )
    own = pl.pallas_call(
        functools.partial(own_kernel, c),
        out_shape=shapes,
        in_specs=[vmem] * 3,
        out_specs=(vmem,) * len(shapes),
        compiler_params=params,
        cost_estimate=pl.CostEstimate(
            flops=2 * STEPS * levels * rows * lanes * 40, bytes_accessed=16 * 2**20, transcendentals=0
        ),
        name="own_rows",
    )(fields, one, two)
    out = pl.pallas_call(
        functools.partial(edge_kernel, c),
        out_shape=(*shapes, *(f32(levels, rows, lanes),) * 3),
        in_specs=[vmem] * (4 + len(shapes)),
        out_specs=(*(vmem,) * len(shapes), hbm, hbm, hbm),
        input_output_aliases={4 + i: i for i in range(len(shapes))},
        scratch_shapes=[pltpu.SemaphoreType.DMA((3,))],
        compiler_params=params,
        name="edge_rows",
    )(*first[::-1], *second, *own)
    return tuple(out[len(shapes) :])


def solution(mesh):
    block = P(None, "lat", "lon")
    return jax.shard_map(
        body,
        mesh=mesh,
        in_specs=(block, block, block, block, block, P("lat", "lon")),
        out_specs=(block, block, block),
        check_vma=False,
    )
```
